32 devices in a mesh: wide: 16 (over z, x, core), grp: 2 (over y).
Axes of the slice: x: 2, y: 2, z: 4, core: 2. Of those that a mesh axis runs over, the one named last changes fastest.
Arguments:
- measured: float32 [512, 16, 2048], P(('wide', 'grp')), may hold values from -192 to 192
- drift: int32 [512], replicated, may hold values from -4 to 4
- start_volume: float32 [16, 8, 2048], P('wide', 'grp'), may hold values from -6 to 6
Outputs:
- estimate: float32 [16, 8, 2048], P('wide', 'grp')
The draws below stay inside these ranges and needn't reach their ends.
All inputs are finite; a program needn't handle non-finite values.
Results may differ from the reference program's by a relative error of at most 0.0001.
Values sent between devices are 32-bit elements; how exact they have to be, the bound alone decides.
No kernel may reach another device: no remote copies, remote signals or barrier semaphores. Data moves between devices by JAX's collectives and lax.ppermute only.
A program may use at most 128 MiB of HBM per device.

```python
import math
from functools import reduce
import jax
import jax.numpy as jnp
from jax import lax

A = 512
C = 2048
ITERS = 2
DMAX = 4
Z = 16
NR = 8
MAX_BIN_SHIFT = 10


def touch_ends(entries, stream_key, low, top_value):
    index_at = [jax.random.randint(jax.random.fold_in(stream_key, axis), (), 0, length) for axis, length in enumerate(entries.shape)]
    longest = entries.shape.index(max(entries.shape))
    beside = index_at[:longest] + [(index_at[longest] + 1) % entries.shape[longest]] + index_at[longest + 1:]
    return entries.at[tuple(index_at)].set(low).at[tuple(beside)].set(top_value)


def levels(stream_key, shape, shards, least, largest):
    gain, own = 1.0, jax.random.fold_in(stream_key, 6)
    for dim, blocks in shards:
        steps = jnp.exp(jax.random.uniform(jax.random.fold_in(own, dim), (blocks,), jnp.float32, least / len(shards), largest / len(shards)))
        gain = gain * jnp.repeat(steps, shape[dim] // blocks).reshape([-1 if axis == dim else 1 for axis in range(len(shape))])
    return gain


def noise(rng, dims, width, reach, split=(), kind=jnp.bfloat16):
    drawn = width * jax.random.normal(rng, dims, jnp.float32)
    if split:
        drawn = drawn * levels(rng, dims, split, -0.22, 0.18)
    return jnp.clip(drawn, -reach, reach).astype(kind)


def setup_inputs(seed: int = 0) -> dict:
    key_list = jax.random.split(jax.random.key(seed), 4)
    measured = noise(key_list[0], (A, Z, C), (4 * NR), 192.0, ((0, 32),), jnp.float32)
    drift = touch_ends(jax.random.randint(key_list[1], (A,), 0 - DMAX, DMAX + 1), jax.random.fold_in(key_list[1], 1), 0 - DMAX, DMAX).astype(jnp.int32)
    start_volume = noise(key_list[2], (Z, NR, C), 1.0, 6.0, ((0, 16), (1, 2)), jnp.float32)
    return dict(measured=measured, drift=drift, start_volume=start_volume)


TILT_MAX = math.pi / 4
SMOOTH_EPS = 0.05
TV_STEP = 0.1

def geometry(angle_ids, drift_vals, total_angles, rows, band_extent):
    angle_rad = TILT_MAX * (2.0 * angle_ids.astype(jnp.float32) / (total_angles - 1) - 1.0)
    secant = 1.0 / jnp.cos(angle_rad)
    height = jnp.arange(rows, dtype=jnp.float32) - (rows - 1) / 2.0
    offsets = jnp.arange(2 * band_extent + 1, dtype=jnp.float32) - band_extent
    shifts = height[None, :] * jnp.tan(angle_rad)[:, None] - drift_vals.astype(jnp.float32)[:, None]
    weight_factors = secant[:, None, None] * jnp.maximum(0.0, 1.0 - jnp.abs(shifts[:, :, None] - offsets[None, None, :]))
    return (weight_factors, jnp.cos(angle_rad) / rows)

def secant_sum(total_angles):
    angle_rad = TILT_MAX * (2.0 * jnp.arange(total_angles, dtype=jnp.float32) / (total_angles - 1) - 1.0)
    return jnp.sum(1.0 / jnp.cos(angle_rad))

def apply_correction(row_band_strip, measurement_part, weight_factors, residual_scale, global_scale, band_extent):
    col_count = row_band_strip.shape[2]
    span = 2 * band_extent + 1
    padded = jnp.pad(row_band_strip, ((0, 0), (0, 0), (band_extent, band_extent)))
    shifted = jnp.stack([padded[:, :, shift_id:shift_id + col_count] for shift_id in range(span)], axis=2)
    forward_projected = jnp.einsum('ark,zrku->azu', weight_factors, shifted, precision=lax.Precision.HIGHEST)
    residual_error = residual_scale[:, None, None] * (measurement_part - forward_projected)
    spread = jnp.einsum('ark,azu->kzru', weight_factors, residual_error, precision=lax.Precision.HIGHEST)
    spread = jnp.pad(spread, ((0, 0), (0, 0), (0, 0), (band_extent, band_extent)))
    pieces = [spread[shift_id, :, :, 2 * band_extent - shift_id:2 * band_extent - shift_id + col_count] for shift_id in range(span)]
    return global_scale * reduce(lambda left, right: left + right, pieces)

def divergence(extended, z_first, r_first, zcount, rcount):
    plane_count, height, col_count = extended.shape
    z_index = z_first + jnp.arange(plane_count, dtype=jnp.int32)[:, None, None]
    row_index = r_first + jnp.arange(height, dtype=jnp.int32)[None, :, None]
    col_index = jnp.arange(col_count, dtype=jnp.int32)[None, None, :]
    diff_z = jnp.concatenate([extended[1:] - extended[:-1], jnp.zeros_like(extended[:1])], axis=0)
    diff_z = jnp.where((z_index >= 0) & (z_index < zcount - 1), diff_z, 0.0)
    diff_r = jnp.concatenate([extended[:, 1:] - extended[:, :-1], jnp.zeros_like(extended[:, :1])], axis=1)
    diff_r = jnp.where((row_index >= 0) & (row_index < rcount - 1), diff_r, 0.0)
    diff_c = jnp.concatenate([extended[:, :, 1:] - extended[:, :, :-1], jnp.zeros_like(extended[:, :, :1])], axis=2)
    diff_c = jnp.where(col_index < col_count - 1, diff_c, 0.0)
    magnitude = jnp.sqrt(diff_z * diff_z + diff_r * diff_r + diff_c * diff_c + SMOOTH_EPS * SMOOTH_EPS)
    unit_z = diff_z / magnitude
    unit_r = diff_r / magnitude
    unit_c = diff_c / magnitude
    back_c = unit_c - jnp.concatenate([jnp.zeros_like(unit_c[:, :, :1]), unit_c[:, :, :-1]], axis=2)
    return unit_z[1:-1, 1:-1] - unit_z[:-2, 1:-1] + (unit_r[1:-1, 1:-1] - unit_r[1:-1, :-2]) + back_c[1:-1, 1:-1]

def reference(measured, drift, start_volume):
    angle_ids = jnp.arange(A, dtype=jnp.int32)
    weight_factors, residual_scale = geometry(angle_ids, drift, A, NR, MAX_BIN_SHIFT)
    global_scale = 1.0 / secant_sum(A)
    sinograms = jnp.moveaxis(measured, 1, 0)
    volume = start_volume
    for sweep in range(ITERS):

        def per_slice(packed_stack):
            rows_of_slice, slice_measurement = packed_stack
            return apply_correction(rows_of_slice[None], slice_measurement[:, None, :], weight_factors, residual_scale, global_scale, MAX_BIN_SHIFT)[0]
        volume = volume + lax.map(per_slice, (volume, sinograms))
        extended = jnp.pad(volume, ((1, 1), (1, 1), (0, 0)))
        volume = volume + TV_STEP * divergence(extended, -1, -1, Z, NR)
    return volume
```

```python
import functools
from functools import reduce
import math

import jax
import jax.numpy as jnp
import numpy as np
from jax import lax
from jax.experimental import pallas as pl
from jax.experimental.pallas import tpu as pltpu
from jax.sharding import PartitionSpec as P

ITERS = 2
DMAX = 4


TILT_MAX = math.pi / 4
SMOOTH_EPS = 0.05
TV_STEP = 0.1


def with_halo(block, sides, width):
    for axis, dim in sides:
        count = lax.axis_size(axis)
        forward = [(i, i + 1) for i in range(count - 1)]
        backward = [(target, source) for source, target in forward]
        low = lax.ppermute(
            lax.slice_in_dim(block, block.shape[dim] - width, None, axis=dim), axis, forward
        )
        high = lax.ppermute(lax.slice_in_dim(block, 0, width, axis=dim), axis, backward)
        block = jnp.concatenate([low, block, high], axis=dim)
    return block


def geometry(angle_ids, drift_vals, total_angles, rows, band_extent):
    angle_rad = TILT_MAX * (2.0 * angle_ids.astype(jnp.float32) / (total_angles - 1) - 1.0)
    secant = 1.0 / jnp.cos(angle_rad)
    height = jnp.arange(rows, dtype=jnp.float32) - (rows - 1) / 2.0
    offsets = jnp.arange(2 * band_extent + 1, dtype=jnp.float32) - band_extent
    shifts = height[None, :] * jnp.tan(angle_rad)[:, None] - drift_vals.astype(jnp.float32)[:, None]
    weight_factors = secant[:, None, None] * jnp.maximum(
        0.0, 1.0 - jnp.abs(shifts[:, :, None] - offsets[None, None, :])
    )
    return (weight_factors, jnp.cos(angle_rad) / rows)


def secant_sum(total_angles):
    angle_rad = TILT_MAX * (
        2.0 * jnp.arange(total_angles, dtype=jnp.float32) / (total_angles - 1) - 1.0
    )
    return jnp.sum(1.0 / jnp.cos(angle_rad))


def local_geometry(angle_ids, drift, total_angles, rows_all, band_extent):
    matches = angle_ids[:, None] == jnp.arange(total_angles, dtype=jnp.int32)[None, :]
    local_drift = jnp.sum(jnp.where(matches, drift[None, :], 0), axis=1)
    return geometry(angle_ids, local_drift, total_angles, rows_all, band_extent)


def apply_correction(
    row_band_strip, measurement_part, weight_factors, residual_scale, global_scale, band_extent
):
    col_count = row_band_strip.shape[2]
    span = 2 * band_extent + 1
    padded = jnp.pad(row_band_strip, ((0, 0), (0, 0), (band_extent, band_extent)))
    shifted = jnp.stack(
        [padded[:, :, shift_id : shift_id + col_count] for shift_id in range(span)], axis=2
    )
    forward_projected = jnp.einsum(
        "ark,zrku->azu", weight_factors, shifted, precision=lax.Precision.HIGHEST
    )
    residual_error = residual_scale[:, None, None] * (measurement_part - forward_projected)
    spread = jnp.einsum(
        "ark,azu->kzru", weight_factors, residual_error, precision=lax.Precision.HIGHEST
    )
    spread = jnp.pad(spread, ((0, 0), (0, 0), (0, 0), (band_extent, band_extent)))
    pieces = [
        spread[shift_id, :, :, 2 * band_extent - shift_id : 2 * band_extent - shift_id + col_count]
        for shift_id in range(span)
    ]
    return global_scale * reduce(lambda left, right: left + right, pieces)


def divergence(extended, z_first, r_first, zcount, rcount):
    plane_count, height, col_count = extended.shape
    z_index = z_first + jnp.arange(plane_count, dtype=jnp.int32)[:, None, None]
    row_index = r_first + jnp.arange(height, dtype=jnp.int32)[None, :, None]
    col_index = jnp.arange(col_count, dtype=jnp.int32)[None, None, :]
    diff_z = jnp.concatenate([extended[1:] - extended[:-1], jnp.zeros_like(extended[:1])], axis=0)
    diff_z = jnp.where((z_index >= 0) & (z_index < zcount - 1), diff_z, 0.0)
    diff_r = jnp.concatenate(
        [extended[:, 1:] - extended[:, :-1], jnp.zeros_like(extended[:, :1])], axis=1
    )
    diff_r = jnp.where((row_index >= 0) & (row_index < rcount - 1), diff_r, 0.0)
    diff_c = jnp.concatenate(
        [extended[:, :, 1:] - extended[:, :, :-1], jnp.zeros_like(extended[:, :, :1])], axis=2
    )
    diff_c = jnp.where(col_index < col_count - 1, diff_c, 0.0)
    magnitude = jnp.sqrt(
        diff_z * diff_z + diff_r * diff_r + diff_c * diff_c + SMOOTH_EPS * SMOOTH_EPS
    )
    unit_z = diff_z / magnitude
    unit_r = diff_r / magnitude
    unit_c = diff_c / magnitude
    back_c = unit_c - jnp.concatenate([jnp.zeros_like(unit_c[:, :, :1]), unit_c[:, :, :-1]], axis=2)
    return (
        unit_z[1:-1, 1:-1]
        - unit_z[:-2, 1:-1]
        + (unit_r[1:-1, 1:-1] - unit_r[1:-1, :-2])
        + back_c[1:-1, 1:-1]
    )


def on_device(measured, drift, start_volume):
    wide_count = lax.axis_size("wide")
    groups = lax.axis_size("grp")
    slab_count, rows_tile, col_count = start_volume.shape
    rows_all = rows_tile * groups
    band_extent = rows_all // 2 + DMAX + 2
    per_device = measured.shape[0]
    total_angles = per_device * wide_count * groups
    global_scale = 1.0 / secant_sum(total_angles)
    z_first = lax.axis_index("wide") * slab_count - 1
    zcount = slab_count * wide_count
    local_measurement = lax.all_to_all(measured, "wide", split_axis=1, concat_axis=0, tiled=True)
    bin_position = jnp.arange(local_measurement.shape[0], dtype=jnp.int32)
    angle_ids = (
        bin_position // per_device * groups + lax.axis_index("grp")
    ) * per_device + bin_position % per_device
    weight_factors, residual_scale = local_geometry(
        angle_ids, drift, total_angles, rows_all, band_extent
    )
    own_tile = start_volume
    r_first = lax.axis_index("grp") * rows_tile - 1
    for sweep in range(ITERS):
        row_band_strip = lax.all_gather(own_tile, "grp", axis=1, tiled=True)
        volume_update = apply_correction(
            row_band_strip,
            local_measurement,
            weight_factors,
            residual_scale,
            global_scale,
            band_extent,
        )
        own_tile = own_tile + lax.psum_scatter(
            volume_update, "grp", scatter_dimension=1, tiled=True
        )
        extended = with_halo(own_tile, (("wide", 0), ("grp", 1)), 1)
        own_tile = own_tile + TV_STEP * divergence(extended, z_first, r_first, zcount, rows_all)
    return own_tile


LANES = 128
SUB = 8
HALO = 64


def tan_and_secant(total_angles):
    angle = TILT_MAX * (2.0 * np.arange(total_angles) / (total_angles - 1) - 1.0)
    return np.tan(angle), 1.0 / np.cos(angle)


def coords():
    wide, y = lax.axis_index("wide"), lax.axis_index("grp")
    return wide // 4, wide // 2 % 2, wide % 2, y


def move(value, target):
    pairs = []
    for z in range(4):
        for x in range(2):
            for c in range(2):
                for y in range(2):
                    to = target(z, x, c, y)
                    if to is not None and 0 <= to[0] < 4:
                        tz, tx, tc, ty = to
                        pairs.append((((z * 2 + x) * 2 + c) * 2 + y, ((tz * 2 + tx) * 2 + tc) * 2 + ty))
    return lax.ppermute(value, ("wide", "grp"), pairs)


def split_rows(value):
    high = value.astype(jnp.bfloat16).astype(jnp.float32)
    return jnp.concatenate([high, value - high], axis=0)


def split_terms(value):
    high = value.astype(jnp.bfloat16)
    low = (value - high.astype(jnp.float32)).astype(jnp.bfloat16)
    return jnp.concatenate([high, low], axis=0)


def lane_iota(shape):
    return lax.broadcasted_iota(jnp.int32, shape, len(shape) - 1)


def row_iota(shape):
    return lax.broadcasted_iota(jnp.int32, shape, len(shape) - 2)


def back_project_kernel(
    sibling, views, slices, rows, half_cols, band, scale, tan_ref, drift_ref, meas_ref, out_ref, buf, sem
):
    in_cols = half_cols + LANES
    z, x, c, y = coords()
    half = 1 - c if sibling else c
    first = pl.multiple_of(half * (half_cols - LANES), LANES)
    tiles = in_cols // LANES
    copies = [
        pltpu.make_async_copy(meas_ref.at[:, pl.ds(first + t * LANES, LANES)], buf.at[t + 1], sem.at[t])
        for t in range(tiles)
    ]
    for copy in copies:
        copy.start()
    buf[0] = jnp.zeros((views * slices, LANES), jnp.float32)
    buf[tiles + 1] = jnp.zeros((views * slices, LANES), jnp.float32)
    first_view = (((z * 2 + x) * 2 + c) * 2 + y) * views
    step = 7
    parts = 2 * band // step + 1
    shape = (parts * rows, step * views)
    lane, row = lane_iota(shape), row_iota(shape)
    view_of = lane % views
    tan_lane = jnp.zeros(shape, jnp.float32)
    drift_lane = jnp.zeros(shape, jnp.float32)
    for a in range(views):
        tan_lane = jnp.where(view_of == a, tan_ref[first_view + a], tan_lane)
        drift_lane = jnp.where(view_of == a, drift_ref[first_view + a].astype(jnp.float32), drift_lane)
    shift = ((row % rows).astype(jnp.float32) - (rows - 1) / 2.0) * tan_lane - drift_lane
    offset = ((row // rows) * step + lane // views - band).astype(jnp.float32)
    weights = (scale / rows) * jnp.maximum(0.0, 1.0 - jnp.abs(shift - offset))
    weights = split_rows(weights)
    weights = jnp.concatenate([weights, weights], axis=1).astype(jnp.bfloat16)
    width = in_cols + LANES
    for copy in copies:
        copy.wait()

    def one_slice(s, carry):
        strip = jnp.concatenate([buf[half + t, pl.ds(s, views, stride=slices), :] for t in range(tiles + 1)], axis=1)
        moved = jnp.concatenate(
            [pltpu.roll(strip, width - (HALO + band - j), 1) for j in range(step)], axis=0
        )
        spread = jnp.dot(weights, split_terms(moved), preferred_element_type=jnp.float32)
        spread = spread[: parts * rows] + spread[parts * rows :]
        total = spread[0:rows]
        for i in range(1, parts):
            total = total + pltpu.roll(spread[i * rows : (i + 1) * rows], step * i, 1)
        out_ref[s] = total[:, :in_cols]
        return carry

    lax.fori_loop(0, slices, one_slice, 0, unroll=2)


def plane_pack_kernel(block, own_ref, got_ref, vol_ref, halo_ref, mine, to_x, to_y, to_xy, acc, vbuf):
    slices, rows, half_cols = own_ref.shape
    width = block + 2 * HALO
    z, x, c, y = coords()
    acc[...] = own_ref[...] + got_ref[...]
    part = vol_ref.shape[1]
    cols = vol_ref.shape[2]
    vbuf[:, 0:LANES] = jnp.zeros((2 * part, LANES), jnp.float32)
    vbuf[:, cols + LANES :] = jnp.zeros((2 * part, LANES), jnp.float32)
    both = jnp.concatenate([vol_ref[0], halo_ref[0]], axis=0)
    vbuf[:, LANES : LANES + cols] = both
    for out, (px, py) in ((mine, (x, y)), (to_x, (1 - x, y)), (to_y, (x, 1 - y)), (to_xy, (1 - x, 1 - y))):
        q = 2 * px + py
        out[0:slices] = acc[:, :, pl.ds(pl.multiple_of(q * block, LANES), width)]
        for h in range(2):
            begin = pl.multiple_of((4 * h + q) * block, LANES)
            window = vbuf[:, pl.ds(begin, width + LANES)]
            window = pltpu.roll(window, width + LANES - HALO, 1)
            out[slices + h] = window[:, :width]


def depth_pack_kernel(mine, got_x, got_y, got_xy, own_win, to_1, to_2, to_3, vol_own, vol_sib, acc):
    slices = mine.shape[0] - 2
    rows = mine.shape[1]
    part = rows // 2
    z, x, c, y = coords()
    acc[0:2] = jnp.zeros((2,) + acc.shape[1:], jnp.float32)
    acc[slices + 2 :] = jnp.zeros((2,) + acc.shape[1:], jnp.float32)
    acc[2 : slices + 2] = (mine[0:slices] + got_x[0:slices]) + (got_y[0:slices] + got_xy[0:slices])
    for out, zz in (
        (own_win, z),
        (to_1, jnp.where(z % 2 == 0, z + 1, z - 1)),
        (to_2, jnp.where(z < 2, z + 2, z - 2)),
        (to_3, 3 - z),
    ):
        out[...] = acc[pl.ds(4 * zz, 8)]
    for out, h in ((vol_own, c), (vol_sib, 1 - c)):
        here, there = mine[slices + h], got_y[slices + h]
        x_here, x_there = got_x[slices + h], got_xy[slices + h]
        for source_x in range(2):
            same = x == source_x
            a = jnp.where(same, here, x_here)
            b = jnp.where(same, there, x_there)
            upper = jnp.where(y == 0, a, b)
            lower = jnp.where(y == 0, b, a)
            own_slice = jnp.concatenate([upper[:part], lower[:part]], axis=0)
            halo_slice = jnp.concatenate([upper[part:], lower[part:]], axis=0)
            out[1 + source_x] = own_slice
            out[3 * source_x] = halo_slice


def gram_kernel(rows, band, scale, tan_ref, sec_ref, drift_ref, after_ref, conv_ref, low_ref, high_ref):
    views = tan_ref.shape[1]
    span = 2 * band + 1
    shape = (span * rows, views)
    row = row_iota(shape)
    shift = ((row % rows).astype(jnp.float32) - (rows - 1) / 2.0) * tan_ref[...] - drift_ref[...].astype(jnp.float32)
    hat = jnp.maximum(0.0, 1.0 - jnp.abs(shift - (row // rows - band).astype(jnp.float32)))
    gram = lax.dot_general(
        hat * ((scale / rows) * sec_ref[...]),
        hat,
        (((1,), (1,)), ((), ())),
        precision=lax.Precision.HIGHEST,
        preferred_element_type=jnp.float32,
    )
    edge = band * rows
    low_ref[...] = gram[edge + rows :, edge + rows :]
    high_ref[...] = gram[:edge, :edge]
    width = conv_ref.shape[1] // 2 * 3
    padded = jnp.concatenate([gram, jnp.zeros((span * rows, width - span * rows), jnp.float32)], axis=1)
    total = jnp.zeros((rows, width), jnp.float32)
    for k in range(span):
        total = total + pltpu.roll(padded[k * rows : (k + 1) * rows], rows * (2 * band - k), 1)
    lanes = width // 3
    stacked = jnp.concatenate([total[:, i * lanes : (i + 1) * lanes] for i in range(3)], axis=0)
    stacked = split_rows(stacked)
    conv_ref[...] = jnp.concatenate([stacked, stacked], axis=1)


def normal(volumes, conv, low_ref, high_ref, out, band, is_low, is_high):
    rows, width = volumes[0].shape
    count = len(volumes)
    step = conv.shape[1] // 2 // rows
    parts = conv.shape[0] // 2 // rows
    for s in range(count):
        moved = jnp.concatenate(
            [pltpu.roll(volumes[s], (2 * band - j) % width, 1) for j in range(step)], axis=0
        )
        spread = jnp.dot(conv, split_terms(moved), preferred_element_type=jnp.float32)
        spread = spread[: parts * rows] + spread[parts * rows :]
        total = spread[0:rows]
        for i in range(1, parts):
            total = total + pltpu.roll(spread[i * rows : (i + 1) * rows], width - step * i, 1)
        out[s] = total

    lane = lane_iota((rows, LANES))

    @pl.when(is_low)
    def _():
        tiles = [v[:, :LANES] for v in volumes]
        moved = jnp.concatenate(
            [jnp.concatenate([pltpu.roll(t, LANES - k, 1) for k in range(1, band + 1)], axis=0) for t in tiles], axis=1
        )
        spread = jnp.dot(low_ref[...], moved, precision=lax.Precision.HIGHEST, preferred_element_type=jnp.float32)
        for s in range(count):
            total = jnp.zeros((rows, LANES), jnp.float32)
            for k in range(1, band + 1):
                piece = spread[(k - 1) * rows : k * rows, s * LANES : (s + 1) * LANES]
                piece = jnp.where((lane >= HALO - band) & (lane < HALO), piece, 0.0)
                total = total + pltpu.roll(piece, k, 1)
            out[s, :, 0:LANES] = out[s, :, 0:LANES] - total

    @pl.when(is_high)
    def _():
        tiles = [v[:, width - LANES :] for v in volumes]
        moved = jnp.concatenate(
            [jnp.concatenate([pltpu.roll(t, k, 1) for k in range(band, 0, -1)], axis=0) for t in tiles], axis=1
        )
        spread = jnp.dot(high_ref[...], moved, precision=lax.Precision.HIGHEST, preferred_element_type=jnp.float32)
        for s in range(count):
            total = jnp.zeros((rows, LANES), jnp.float32)
            for k in range(band, 0, -1):
                piece = spread[(band - k) * rows : (band - k + 1) * rows, s * LANES : (s + 1) * LANES]
                piece = jnp.where((lane >= LANES - HALO) & (lane < LANES - HALO + band), piece, 0.0)
                total = total + pltpu.roll(piece, LANES - k, 1)
            out[s, :, width - LANES :] = out[s, :, width - LANES :] - total


def block_place(block, total_cols):
    z, x, c, y = coords()
    index = (c * 2 + x) * 2 + y
    return z, index * block - HALO, index == 0, index == total_cols // block - 1


def first_normal_kernel(band, block, total_cols, vol_own, vol_sib, conv_ref, low_ref, high_ref, out, vols, work):
    _, _, is_low, is_high = block_place(block, total_cols)
    _, _, c, _ = coords()
    for m in range(4):
        vols[2 * m + c] = vol_own[m]
        vols[2 * m + 1 - c] = vol_sib[m]
    volumes = [vols[s] for s in range(8)]
    normal(volumes, conv_ref[...].astype(jnp.bfloat16), low_ref, high_ref, work, band, is_low, is_high)
    for s in range(8):
        out[s] = volumes[s] - work[s]


def variation_step(half, z_of, first_col, depth, total_cols):
    rows, width = half[0].shape
    col = first_col + lane_iota((rows, width))
    row = row_iota((rows, width))
    inside = (col >= 0) & (col < total_cols - 1)
    units = []
    for w in range(len(half) - 1):
        v = half[w]
        keep = (z_of(w) >= 0) & (z_of(w) < depth - 1)
        dz = jnp.where(keep, half[w + 1] - v, 0.0)
        dr = jnp.where(row < rows - 1, pltpu.roll(v, rows - 1, 0) - v, 0.0)
        dc = jnp.where(inside, pltpu.roll(v, width - 1, 1) - v, 0.0)
        inverse = 1.0 / jnp.sqrt(dz * dz + dr * dr + dc * dc + SMOOTH_EPS * SMOOTH_EPS)
        units.append((dz * inverse, dr * inverse, dc * inverse))
    result = []
    for w in range(1, len(half) - 1):
        uz, ur, uc = units[w]
        div = (uz - units[w - 1][0]) + (ur - pltpu.roll(ur, 1, 0)) + (uc - pltpu.roll(uc, 1, 1))
        result.append(jnp.where((col >= 0) & (col < total_cols), half[w] + TV_STEP * div, 0.0))
    return result


def finish_kernel(
    band, block, depth, total_cols,
    first_ref, own_win, got_1, got_2, got_3, conv_ref, low_ref, high_ref, keep_ref, send_ref, corr, work, done,
):
    z, first_col, is_low, is_high = block_place(block, total_cols)
    _, _, c, _ = coords()
    corr[...] = (own_win[...] + got_1[...]) + (got_2[...] + got_3[...])
    half = [first_ref[s] + corr[s] for s in range(8)]
    volumes = variation_step(half, lambda w: 4 * z - 2 + w, first_col, depth, total_cols)
    normal(volumes, conv_ref[...].astype(jnp.bfloat16), low_ref, high_ref, work, band, is_low, is_high)
    half = [volumes[s] + corr[s + 1] - work[s] for s in range(6)]
    volumes = variation_step(half, lambda w: 4 * z - 1 + w, first_col, depth, total_cols)
    width = volumes[0].shape[1]
    for s in range(4):
        done[s] = pltpu.roll(volumes[s], width - HALO, 1)[:, :block]
    for px in range(2):
        keep_ref[px] = done[2 * px + c]
        send_ref[px] = done[2 * px + 1 - c]


def result_pack_kernel(own_ref, got_ref, mine, to_x, to_y, to_xy):
    z, x, c, y = coords()
    part = own_ref.shape[1] // 2
    for out, (px, py) in ((mine, (x, y)), (to_x, (1 - x, y)), (to_y, (x, 1 - y)), (to_xy, (1 - x, 1 - y))):
        own, got = own_ref[px], got_ref[px]
        out[c] = jnp.where(py == 0, own[:part], own[part:])
        out[1 - c] = jnp.where(py == 0, got[:part], got[part:])


def result_kernel(mine, got_x, got_y, got_xy, out):
    z, x, c, y = coords()
    block = mine.shape[2]
    for ref, (px, py) in ((mine, (x, y)), (got_x, (1 - x, y)), (got_y, (x, 1 - y)), (got_xy, (1 - x, 1 - y))):
        for h in range(2):
            begin = pl.multiple_of((4 * h + 2 * px + py) * block, LANES)
            out[0, :, pl.ds(begin, block)] = ref[h]


def f32(*shape):
    return jax.ShapeDtypeStruct(shape, jnp.float32)


VMEM_SPEC = pl.BlockSpec(memory_space=pltpu.VMEM)
SMEM_SPEC = pl.BlockSpec(memory_space=pltpu.SMEM)
ANY_SPEC = pl.BlockSpec(memory_space=pl.ANY)
PARAMS = pltpu.CompilerParams(vmem_limit_bytes=40 * 1024 * 1024)


def kernel_call(body, outs, in_specs, scratch, name, flops=0, size=0):
    many = isinstance(outs, (list, tuple))
    return pl.pallas_call(
        body,
        out_shape=outs,
        in_specs=in_specs,
        out_specs=[VMEM_SPEC] * len(outs) if many else VMEM_SPEC,
        scratch_shapes=scratch,
        compiler_params=PARAMS,
        name=name,
        cost_estimate=pl.CostEstimate(flops=flops, bytes_accessed=size, transcendentals=0),
    )


def summed_plan(measured, drift, start_volume):
    views, slices, cols = measured.shape
    part = start_volume.shape[1]
    rows = 2 * part
    band = rows // 2 + DMAX + 2
    total_angles = drift.shape[0]
    block = cols // 8
    half_cols = cols // 2
    half_width = half_cols + LANES
    width = block + 2 * HALO
    tangent, secant = tan_and_secant(total_angles)
    scale = float(1.0 / np.sum(secant))
    tangent, secant = tangent.astype(np.float32), secant.astype(np.float32)

    flat = measured.reshape(views * slices, cols)
    halo = move(start_volume, lambda z, x, c, y: (z + 1, 0, c, y) if x else (z - 1, 1, c, y))

    def back_project(sibling):
        return kernel_call(
            functools.partial(back_project_kernel, sibling, views, slices, rows, half_cols, band, scale),
            f32(slices, rows, half_width),
            [SMEM_SPEC, SMEM_SPEC, ANY_SPEC],
            [
                pltpu.VMEM((half_width // LANES + 2, views * slices, LANES), jnp.float32),
                pltpu.SemaphoreType.DMA((half_width // LANES,)),
            ],
            "back_project_sibling" if sibling else "back_project_own",
            flops=2 * 10**9,
            size=2**21,
        )(tangent, drift, flat)

    got = move(back_project(True), lambda z, x, c, y: (z, x, 1 - c, y))
    own = back_project(False)

    message = f32(slices + 2, rows, width)
    mine, to_x, to_y, to_xy = kernel_call(
        functools.partial(plane_pack_kernel, block),
        [message] * 4,
        [VMEM_SPEC] * 4,
        [pltpu.VMEM((slices, rows, half_width), jnp.float32), pltpu.VMEM((2 * part, cols + 2 * LANES), jnp.float32)],
        "plane_pack",
    )(own, got, start_volume, halo)
    got_xy = move(to_xy, lambda z, x, c, y: (z, 1 - x, c, 1 - y))
    got_x = move(to_x, lambda z, x, c, y: (z, 1 - x, c, y))
    got_y = move(to_y, lambda z, x, c, y: (z, x, c, 1 - y))

    edge = band * rows
    conv, low, high = kernel_call(
        functools.partial(gram_kernel, rows, band, scale),
        [f32(6 * rows, 2 * LANES), f32(edge, edge), f32(edge, edge)],
        [VMEM_SPEC] * 3 + [ANY_SPEC],
        [],
        "gram",
        flops=10**9,
    )(tangent[None], secant[None], drift[None], mine)

    window = f32(8, rows, width)
    own_win, to_1, to_2, to_3, vol_own, vol_sib = kernel_call(
        depth_pack_kernel,
        [window] * 4 + [f32(4, rows, width)] * 2,
        [VMEM_SPEC] * 4,
        [pltpu.VMEM((slices + 4, rows, width), jnp.float32)],
        "depth_pack",
    )(mine, got_x, got_y, got_xy)
    got_2 = move(to_2, lambda z, x, c, y: (z ^ 2, x, c, y))
    got_1 = move(to_1, lambda z, x, c, y: (z ^ 1, x, c, y))
    got_3 = move(to_3, lambda z, x, c, y: (z ^ 3, x, c, y))
    vol_got = move(vol_sib, lambda z, x, c, y: (z, x, 1 - c, y))

    work = pltpu.VMEM((8, rows, width), jnp.float32)
    first = kernel_call(
        functools.partial(first_normal_kernel, band, block, cols),
        window,
        [VMEM_SPEC] * 5,
        [work, work],
        "first_normal",
        flops=10**9,
    )(vol_own, vol_got, conv, low, high)

    piece = f32(2, rows, block)
    keep, send = kernel_call(
        functools.partial(finish_kernel, band, block, slices, cols),
        [piece, piece],
        [VMEM_SPEC] * 8,
        [work, work, pltpu.VMEM((4, rows, block), jnp.float32)],
        "finish",
    )(first, own_win, got_1, got_2, got_3, conv, low, high)
    swapped = move(send, lambda z, x, c, y: (z, x, 1 - c, y))
    small = f32(2, part, block)
    mine, to_x, to_y, to_xy = kernel_call(result_pack_kernel, [small] * 4, [VMEM_SPEC] * 2, [], "result_pack")(
        keep, swapped
    )
    got_xy = move(to_xy, lambda z, x, c, y: (z, 1 - x, c, 1 - y))
    got_x = move(to_x, lambda z, x, c, y: (z, 1 - x, c, y))
    got_y = move(to_y, lambda z, x, c, y: (z, x, c, 1 - y))
    return kernel_call(result_kernel, f32(1, part, cols), [VMEM_SPEC] * 4, [], "result")(mine, got_x, got_y, got_xy)


def summed_plan_fits(mesh, measured, start_volume):
    rows = start_volume.shape[1]
    cols = measured.shape[2]
    return (
        ITERS == 2
        and dict(mesh.shape) == {"wide": 16, "grp": 2}
        and measured.shape[1] == start_volume.shape[0] == 16
        and rows == SUB
        and cols % (16 * LANES) == 0
        and measured.shape[0] % 256 == 0
    )


def solution(mesh):
    in_specs = (P(("wide", "grp"), None, None), P(), P("wide", "grp", None))
    out_specs = P("wide", "grp", None)

    def run(measured, drift, start_volume):
        plan = summed_plan if summed_plan_fits(mesh, measured, start_volume) else on_device
        return jax.shard_map(plan, mesh=mesh, in_specs=in_specs, out_specs=out_specs, check_vma=False)(
            measured, drift, start_volume
        )

    return run
```

```python
import functools
from functools import reduce
import math

import jax
import jax.numpy as jnp
import numpy as np
from jax import lax
from jax.experimental import pallas as pl
from jax.experimental.pallas import tpu as pltpu
from jax.sharding import PartitionSpec as P

ITERS = 2
DMAX = 4


TILT_MAX = math.pi / 4
SMOOTH_EPS = 0.05
TV_STEP = 0.1


def with_halo(block, sides, width):
    for axis, dim in sides:
        count = lax.axis_size(axis)
        forward = [(i, i + 1) for i in range(count - 1)]
        backward = [(target, source) for source, target in forward]
        low = lax.ppermute(
            lax.slice_in_dim(block, block.shape[dim] - width, None, axis=dim), axis, forward
        )
        high = lax.ppermute(lax.slice_in_dim(block, 0, width, axis=dim), axis, backward)
        block = jnp.concatenate([low, block, high], axis=dim)
    return block


def geometry(angle_ids, drift_vals, total_angles, rows, band_extent):
    angle_rad = TILT_MAX * (2.0 * angle_ids.astype(jnp.float32) / (total_angles - 1) - 1.0)
    secant = 1.0 / jnp.cos(angle_rad)
    height = jnp.arange(rows, dtype=jnp.float32) - (rows - 1) / 2.0
    offsets = jnp.arange(2 * band_extent + 1, dtype=jnp.float32) - band_extent
    shifts = height[None, :] * jnp.tan(angle_rad)[:, None] - drift_vals.astype(jnp.float32)[:, None]
    weight_factors = secant[:, None, None] * jnp.maximum(
        0.0, 1.0 - jnp.abs(shifts[:, :, None] - offsets[None, None, :])
    )
    return (weight_factors, jnp.cos(angle_rad) / rows)


def secant_sum(total_angles):
    angle_rad = TILT_MAX * (
        2.0 * jnp.arange(total_angles, dtype=jnp.float32) / (total_angles - 1) - 1.0
    )
    return jnp.sum(1.0 / jnp.cos(angle_rad))


def local_geometry(angle_ids, drift, total_angles, rows_all, band_extent):
    matches = angle_ids[:, None] == jnp.arange(total_angles, dtype=jnp.int32)[None, :]
    local_drift = jnp.sum(jnp.where(matches, drift[None, :], 0), axis=1)
    return geometry(angle_ids, local_drift, total_angles, rows_all, band_extent)


def apply_correction(
    row_band_strip, measurement_part, weight_factors, residual_scale, global_scale, band_extent
):
    col_count = row_band_strip.shape[2]
    span = 2 * band_extent + 1
    padded = jnp.pad(row_band_strip, ((0, 0), (0, 0), (band_extent, band_extent)))
    shifted = jnp.stack(
        [padded[:, :, shift_id : shift_id + col_count] for shift_id in range(span)], axis=2
    )
    forward_projected = jnp.einsum(
        "ark,zrku->azu", weight_factors, shifted, precision=lax.Precision.HIGHEST
    )
    residual_error = residual_scale[:, None, None] * (measurement_part - forward_projected)
    spread = jnp.einsum(
        "ark,azu->kzru", weight_factors, residual_error, precision=lax.Precision.HIGHEST
    )
    spread = jnp.pad(spread, ((0, 0), (0, 0), (0, 0), (band_extent, band_extent)))
    pieces = [
        spread[shift_id, :, :, 2 * band_extent - shift_id : 2 * band_extent - shift_id + col_count]
        for shift_id in range(span)
    ]
    return global_scale * reduce(lambda left, right: left + right, pieces)


def divergence(extended, z_first, r_first, zcount, rcount):
    plane_count, height, col_count = extended.shape
    z_index = z_first + jnp.arange(plane_count, dtype=jnp.int32)[:, None, None]
    row_index = r_first + jnp.arange(height, dtype=jnp.int32)[None, :, None]
    col_index = jnp.arange(col_count, dtype=jnp.int32)[None, None, :]
    diff_z = jnp.concatenate([extended[1:] - extended[:-1], jnp.zeros_like(extended[:1])], axis=0)
    diff_z = jnp.where((z_index >= 0) & (z_index < zcount - 1), diff_z, 0.0)
    diff_r = jnp.concatenate(
        [extended[:, 1:] - extended[:, :-1], jnp.zeros_like(extended[:, :1])], axis=1
    )
    diff_r = jnp.where((row_index >= 0) & (row_index < rcount - 1), diff_r, 0.0)
    diff_c = jnp.concatenate(
        [extended[:, :, 1:] - extended[:, :, :-1], jnp.zeros_like(extended[:, :, :1])], axis=2
    )
    diff_c = jnp.where(col_index < col_count - 1, diff_c, 0.0)
    magnitude = jnp.sqrt(
        diff_z * diff_z + diff_r * diff_r + diff_c * diff_c + SMOOTH_EPS * SMOOTH_EPS
    )
    unit_z = diff_z / magnitude
    unit_r = diff_r / magnitude
    unit_c = diff_c / magnitude
    back_c = unit_c - jnp.concatenate([jnp.zeros_like(unit_c[:, :, :1]), unit_c[:, :, :-1]], axis=2)
    return (
        unit_z[1:-1, 1:-1]
        - unit_z[:-2, 1:-1]
        + (unit_r[1:-1, 1:-1] - unit_r[1:-1, :-2])
        + back_c[1:-1, 1:-1]
    )


def on_device(measured, drift, start_volume):
    wide_count = lax.axis_size("wide")
    groups = lax.axis_size("grp")
    slab_count, rows_tile, col_count = start_volume.shape
    rows_all = rows_tile * groups
    band_extent = rows_all // 2 + DMAX + 2
    per_device = measured.shape[0]
    total_angles = per_device * wide_count * groups
    global_scale = 1.0 / secant_sum(total_angles)
    z_first = lax.axis_index("wide") * slab_count - 1
    zcount = slab_count * wide_count
    local_measurement = lax.all_to_all(measured, "wide", split_axis=1, concat_axis=0, tiled=True)
    bin_position = jnp.arange(local_measurement.shape[0], dtype=jnp.int32)
    angle_ids = (
        bin_position // per_device * groups + lax.axis_index("grp")
    ) * per_device + bin_position % per_device
    weight_factors, residual_scale = local_geometry(
        angle_ids, drift, total_angles, rows_all, band_extent
    )
    own_tile = start_volume
    r_first = lax.axis_index("grp") * rows_tile - 1
    for sweep in range(ITERS):
        row_band_strip = lax.all_gather(own_tile, "grp", axis=1, tiled=True)
        volume_update = apply_correction(
            row_band_strip,
            local_measurement,
            weight_factors,
            residual_scale,
            global_scale,
            band_extent,
        )
        own_tile = own_tile + lax.psum_scatter(
            volume_update, "grp", scatter_dimension=1, tiled=True
        )
        extended = with_halo(own_tile, (("wide", 0), ("grp", 1)), 1)
        own_tile = own_tile + TV_STEP * divergence(extended, z_first, r_first, zcount, rows_all)
    return own_tile


LANES = 128
SUB = 8
HALO = 64


def tan_and_secant(total_angles):
    angle = TILT_MAX * (2.0 * np.arange(total_angles) / (total_angles - 1) - 1.0)
    return np.tan(angle), 1.0 / np.cos(angle)


def coords():
    wide, y = lax.axis_index("wide"), lax.axis_index("grp")
    return wide // 4, wide // 2 % 2, wide % 2, y


def move(value, target):
    pairs = []
    for z in range(4):
        for x in range(2):
            for c in range(2):
                for y in range(2):
                    to = target(z, x, c, y)
                    if to is not None and 0 <= to[0] < 4:
                        tz, tx, tc, ty = to
                        pairs.append((((z * 2 + x) * 2 + c) * 2 + y, ((tz * 2 + tx) * 2 + tc) * 2 + ty))
    return lax.ppermute(value, ("wide", "grp"), pairs)


def split_rows(value):
    high = value.astype(jnp.bfloat16).astype(jnp.float32)
    return jnp.concatenate([high, value - high], axis=0)


def split_terms(value):
    high = value.astype(jnp.bfloat16)
    low = (value - high.astype(jnp.float32)).astype(jnp.bfloat16)
    return jnp.concatenate([high, low], axis=0)


def lane_iota(shape):
    return lax.broadcasted_iota(jnp.int32, shape, len(shape) - 1)


def row_iota(shape):
    return lax.broadcasted_iota(jnp.int32, shape, len(shape) - 2)


STEP = 3


def view_weights(views, rows, band, scale, tan_ref, drift_ref):
    z, x, c, y = coords()
    first_view = (((z * 2 + x) * 2 + c) * 2 + y) * views
    parts = 2 * band // STEP + 1
    shape = (parts * rows, STEP * views)
    lane, row = lane_iota(shape), row_iota(shape)
    view_of = lane_iota((1, STEP * views)) % views
    tan_lane = jnp.zeros((1, STEP * views), jnp.float32)
    drift_lane = tan_lane
    for a in range(views):
        tan_lane = jnp.where(view_of == a, tan_ref[first_view + a], tan_lane)
        drift_lane = jnp.where(view_of == a, drift_ref[first_view + a].astype(jnp.float32), drift_lane)
    shift = ((row % rows).astype(jnp.float32) - (rows - 1) / 2.0) * tan_lane - drift_lane
    offset = ((row // rows) * STEP + lane // views - band).astype(jnp.float32)
    weights = (scale / rows) * jnp.maximum(0.0, 1.0 - jnp.abs(shift - offset))
    weights = split_rows(weights)
    return jnp.concatenate([weights, weights], axis=1).astype(jnp.bfloat16)


def back_project(views, slices, rows, band, weights, load_strip, out_ref, terms):
    out_cols = out_ref.shape[2]
    width = terms.shape[2]
    parts = 2 * band // STEP + 1

    def prepare(s, buf):
        strip = load_strip(s)
        high = strip.astype(jnp.bfloat16)
        low = (strip - high.astype(jnp.float32)).astype(jnp.bfloat16)
        for j in range(STEP):
            buf[j * views : (j + 1) * views] = pltpu.roll(high, j, 1) if j else high
            buf[(STEP + j) * views : (STEP + j + 1) * views] = pltpu.roll(low, j, 1) if j else low

    prepare(0, terms.at[0])
    for s in range(slices):
        if s + 1 < slices:
            prepare(s + 1, terms.at[(s + 1) % 2])
        spread = jnp.dot(weights, terms[s % 2], preferred_element_type=jnp.float32)
        spread = spread[: parts * rows] + spread[parts * rows :]
        total = None
        for i in range(parts):
            piece = pltpu.roll(spread[i * rows : (i + 1) * rows], width - HALO - band + STEP * i, 1)
            total = piece if total is None else total + piece
        out_ref[s] = total[:, :out_cols]


def strip_loader(buf, half, views, tiles):
    def load(s):
        return jnp.concatenate(
            [buf[s // SUB, half + t, pl.ds(s % SUB, views, stride=SUB), :] for t in range(tiles + 1)], axis=1
        )

    return load


def sibling_kernel(views, slices, rows, band, scale, tan_hbm, drift_hbm, meas_ref, out_ref, own_buf, weights_ref,
                   tan_ref, drift_ref, buf, terms, table_sem, sem, own_sem):
    _, _, c, _ = coords()
    tiles = out_ref.shape[2] // LANES
    groups = slices // SUB

    def fetch(half, g, t, target, semaphore):
        first = pl.multiple_of((half * (tiles - 1) + t - half) * LANES, LANES)
        return pltpu.make_async_copy(
            meas_ref.at[:, pl.ds(g * SUB, SUB), pl.ds(first, LANES)], target.at[g, t + 1], semaphore
        )

    tables = [
        pltpu.make_async_copy(tan_hbm, tan_ref, table_sem.at[0]),
        pltpu.make_async_copy(drift_hbm, drift_ref, table_sem.at[1]),
    ]
    first = [[fetch(1 - c, g, t, buf, sem.at[g, t]) for t in range(tiles)] for g in range(groups)]
    later = [[fetch(c, g, t, own_buf, own_sem.at[g, t]) for t in range(tiles)] for g in range(groups)]
    for copy in tables + first[0] + first[1] + later[0] + later[1]:
        copy.start()
    zero = jnp.zeros((views, SUB, LANES), jnp.float32)
    for g in range(groups):
        for target in (buf, own_buf):
            target[g, 0] = zero
            target[g, tiles + 1] = zero
    for copy in tables:
        copy.wait()
    weights = view_weights(views, rows, band, scale, tan_ref, drift_ref)
    weights_ref[...] = weights.astype(jnp.float32)
    flat = buf.reshape(groups, tiles + 2, views * SUB, LANES)
    load = strip_loader(flat, 1 - c, views, tiles)

    def load_strip(s):
        if s % SUB == 0:
            for copy in first[s // SUB]:
                copy.wait()
        return load(s)

    back_project(views, slices, rows, band, weights, load_strip, out_ref, terms)
    for group in later:
        for copy in group:
            copy.wait()


def own_kernel(views, slices, rows, band, buf, weights_ref, out_ref, terms):
    _, _, c, _ = coords()
    tiles = out_ref.shape[2] // LANES
    flat = buf.reshape(slices // SUB, tiles + 2, views * SUB, LANES)
    load = strip_loader(flat, c, views, tiles)
    back_project(views, slices, rows, band, weights_ref[...].astype(jnp.bfloat16), load, out_ref, terms)


def plane_pack_kernel(block, own_ref, got_ref, vol_ref, halo_ref, mine, to_x, to_y, to_xy, acc, vbuf):
    slices, rows, half_cols = own_ref.shape
    width = block + 2 * HALO
    z, x, c, y = coords()
    acc[...] = own_ref[...] + got_ref[...]
    part = vol_ref.shape[1]
    cols = vol_ref.shape[2]
    vbuf[:, 0:LANES] = jnp.zeros((2 * part, LANES), jnp.float32)
    vbuf[:, cols + LANES :] = jnp.zeros((2 * part, LANES), jnp.float32)
    both = jnp.concatenate([vol_ref[0], halo_ref[0]], axis=0)
    vbuf[:, LANES : LANES + cols] = both
    for out, (px, py) in ((mine, (x, y)), (to_x, (1 - x, y)), (to_y, (x, 1 - y)), (to_xy, (1 - x, 1 - y))):
        q = 2 * px + py
        out[0:slices] = acc[:, :, pl.ds(pl.multiple_of(q * block, LANES), width)]
        for h in range(2):
            begin = pl.multiple_of((4 * h + q) * block, LANES)
            window = vbuf[:, pl.ds(begin, width + LANES)]
            window = pltpu.roll(window, width + LANES - HALO, 1)
            out[slices + h] = window[:, :width]


def depth_pack_kernel(mine, got_x, got_y, got_xy, own_win, to_1, to_2, to_3, vol_own, vol_sib, acc):
    slices = mine.shape[0] - 2
    rows = mine.shape[1]
    part = rows // 2
    z, x, c, y = coords()
    acc[0:2] = jnp.zeros((2,) + acc.shape[1:], jnp.float32)
    acc[slices + 2 :] = jnp.zeros((2,) + acc.shape[1:], jnp.float32)
    acc[2 : slices + 2] = (mine[0:slices] + got_x[0:slices]) + (got_y[0:slices] + got_xy[0:slices])
    for out, zz in (
        (own_win, z),
        (to_1, jnp.where(z % 2 == 0, z + 1, z - 1)),
        (to_2, jnp.where(z < 2, z + 2, z - 2)),
        (to_3, 3 - z),
    ):
        out[...] = acc[pl.ds(4 * zz, 8)]
    for out, h in ((vol_own, c), (vol_sib, 1 - c)):
        here, there = mine[slices + h], got_y[slices + h]
        x_here, x_there = got_x[slices + h], got_xy[slices + h]
        for source_x in range(2):
            same = x == source_x
            a = jnp.where(same, here, x_here)
            b = jnp.where(same, there, x_there)
            upper = jnp.where(y == 0, a, b)
            lower = jnp.where(y == 0, b, a)
            own_slice = jnp.concatenate([upper[:part], lower[:part]], axis=0)
            halo_slice = jnp.concatenate([upper[part:], lower[part:]], axis=0)
            out[1 + source_x] = own_slice
            out[3 * source_x] = halo_slice


def gram_kernel(rows, band, scale, tan_ref, sec_ref, drift_ref, after_ref, conv_ref, low_ref, high_ref):
    views = tan_ref.shape[1]
    span = 2 * band + 1
    shape = (span * rows, views)
    row = row_iota(shape)
    shift = ((row % rows).astype(jnp.float32) - (rows - 1) / 2.0) * tan_ref[...] - drift_ref[...].astype(jnp.float32)
    hat = jnp.maximum(0.0, 1.0 - jnp.abs(shift - (row // rows - band).astype(jnp.float32)))
    gram = lax.dot_general(
        hat * ((scale / rows) * sec_ref[...]),
        hat,
        (((1,), (1,)), ((), ())),
        precision=lax.Precision.HIGHEST,
        preferred_element_type=jnp.float32,
    )
    edge = band * rows
    low_ref[...] = gram[edge + rows :, edge + rows :]
    high_ref[...] = gram[:edge, :edge]
    width = conv_ref.shape[1] // 2 * 3
    padded = jnp.concatenate([gram, jnp.zeros((span * rows, width - span * rows), jnp.float32)], axis=1)
    total = jnp.zeros((rows, width), jnp.float32)
    for k in range(span):
        total = total + pltpu.roll(padded[k * rows : (k + 1) * rows], rows * (2 * band - k), 1)
    lanes = width // 3
    stacked = jnp.concatenate([total[:, i * lanes : (i + 1) * lanes] for i in range(3)], axis=0)
    stacked = split_rows(stacked)
    conv_ref[...] = jnp.concatenate([stacked, stacked], axis=1)


def normal(volumes, conv, low_ref, high_ref, out, band, is_low, is_high):
    rows, width = volumes[0].shape
    count = len(volumes)
    step = conv.shape[1] // 2 // rows
    parts = conv.shape[0] // 2 // rows
    for s in range(count):
        moved = jnp.concatenate(
            [pltpu.roll(volumes[s], (2 * band - j) % width, 1) for j in range(step)], axis=0
        )
        spread = jnp.dot(conv, split_terms(moved), preferred_element_type=jnp.float32)
        spread = spread[: parts * rows] + spread[parts * rows :]
        total = spread[0:rows]
        for i in range(1, parts):
            total = total + pltpu.roll(spread[i * rows : (i + 1) * rows], width - step * i, 1)
        out[s] = total

    lane = lane_iota((rows, LANES))

    @pl.when(is_low)
    def _():
        tiles = [v[:, :LANES] for v in volumes]
        moved = jnp.concatenate(
            [jnp.concatenate([pltpu.roll(t, LANES - k, 1) for k in range(1, band + 1)], axis=0) for t in tiles], axis=1
        )
        spread = jnp.dot(low_ref[...], moved, precision=lax.Precision.HIGHEST, preferred_element_type=jnp.float32)
        for s in range(count):
            total = jnp.zeros((rows, LANES), jnp.float32)
            for k in range(1, band + 1):
                piece = spread[(k - 1) * rows : k * rows, s * LANES : (s + 1) * LANES]
                piece = jnp.where((lane >= HALO - band) & (lane < HALO), piece, 0.0)
                total = total + pltpu.roll(piece, k, 1)
            out[s, :, 0:LANES] = out[s, :, 0:LANES] - total

    @pl.when(is_high)
    def _():
        tiles = [v[:, width - LANES :] for v in volumes]
        moved = jnp.concatenate(
            [jnp.concatenate([pltpu.roll(t, k, 1) for k in range(band, 0, -1)], axis=0) for t in tiles], axis=1
        )
        spread = jnp.dot(high_ref[...], moved, precision=lax.Precision.HIGHEST, preferred_element_type=jnp.float32)
        for s in range(count):
            total = jnp.zeros((rows, LANES), jnp.float32)
            for k in range(band, 0, -1):
                piece = spread[(band - k) * rows : (band - k + 1) * rows, s * LANES : (s + 1) * LANES]
                piece = jnp.where((lane >= LANES - HALO) & (lane < LANES - HALO + band), piece, 0.0)
                total = total + pltpu.roll(piece, LANES - k, 1)
            out[s, :, width - LANES :] = out[s, :, width - LANES :] - total


def block_place(block, total_cols):
    z, x, c, y = coords()
    index = (c * 2 + x) * 2 + y
    return z, index * block - HALO, index == 0, index == total_cols // block - 1


def first_normal_kernel(band, block, total_cols, vol_own, vol_sib, conv_ref, low_ref, high_ref, out, vols, work):
    _, _, is_low, is_high = block_place(block, total_cols)
    _, _, c, _ = coords()
    for m in range(4):
        vols[2 * m + c] = vol_own[m]
        vols[2 * m + 1 - c] = vol_sib[m]
    volumes = [vols[s] for s in range(8)]
    normal(volumes, conv_ref[...].astype(jnp.bfloat16), low_ref, high_ref, work, band, is_low, is_high)
    for s in range(8):
        out[s] = volumes[s] - work[s]


def variation_step(half, z_of, first_col, depth, total_cols):
    rows, width = half[0].shape
    col = first_col + lane_iota((rows, width))
    row = row_iota((rows, width))
    inside = (col >= 0) & (col < total_cols - 1)
    units = []
    for w in range(len(half) - 1):
        v = half[w]
        keep = (z_of(w) >= 0) & (z_of(w) < depth - 1)
        dz = jnp.where(keep, half[w + 1] - v, 0.0)
        dr = jnp.where(row < rows - 1, pltpu.roll(v, rows - 1, 0) - v, 0.0)
        dc = jnp.where(inside, pltpu.roll(v, width - 1, 1) - v, 0.0)
        inverse = 1.0 / jnp.sqrt(dz * dz + dr * dr + dc * dc + SMOOTH_EPS * SMOOTH_EPS)
        units.append((dz * inverse, dr * inverse, dc * inverse))
    result = []
    for w in range(1, len(half) - 1):
        uz, ur, uc = units[w]
        div = (uz - units[w - 1][0]) + (ur - pltpu.roll(ur, 1, 0)) + (uc - pltpu.roll(uc, 1, 1))
        result.append(jnp.where((col >= 0) & (col < total_cols), half[w] + TV_STEP * div, 0.0))
    return result


def finish_kernel(
    band, block, depth, total_cols,
    first_ref, own_win, got_1, got_2, got_3, conv_ref, low_ref, high_ref, keep_ref, send_ref, corr, work, done,
):
    z, first_col, is_low, is_high = block_place(block, total_cols)
    _, _, c, _ = coords()
    corr[...] = (own_win[...] + got_1[...]) + (got_2[...] + got_3[...])
    half = [first_ref[s] + corr[s] for s in range(8)]
    volumes = variation_step(half, lambda w: 4 * z - 2 + w, first_col, depth, total_cols)
    normal(volumes, conv_ref[...].astype(jnp.bfloat16), low_ref, high_ref, work, band, is_low, is_high)
    half = [volumes[s] + corr[s + 1] - work[s] for s in range(6)]
    volumes = variation_step(half, lambda w: 4 * z - 1 + w, first_col, depth, total_cols)
    width = volumes[0].shape[1]
    for s in range(4):
        done[s] = pltpu.roll(volumes[s], width - HALO, 1)[:, :block]
    for px in range(2):
        keep_ref[px] = done[2 * px + c]
        send_ref[px] = done[2 * px + 1 - c]


def result_pack_kernel(own_ref, got_ref, mine, to_x, to_y, to_xy):
    z, x, c, y = coords()
    part = own_ref.shape[1] // 2
    for out, (px, py) in ((mine, (x, y)), (to_x, (1 - x, y)), (to_y, (x, 1 - y)), (to_xy, (1 - x, 1 - y))):
        own, got = own_ref[px], got_ref[px]
        out[c] = jnp.where(py == 0, own[:part], own[part:])
        out[1 - c] = jnp.where(py == 0, got[:part], got[part:])


def result_kernel(mine, got_x, got_y, got_xy, out):
    z, x, c, y = coords()
    block = mine.shape[2]
    for ref, (px, py) in ((mine, (x, y)), (got_x, (1 - x, y)), (got_y, (x, 1 - y)), (got_xy, (1 - x, 1 - y))):
        for h in range(2):
            begin = pl.multiple_of((4 * h + 2 * px + py) * block, LANES)
            out[0, :, pl.ds(begin, block)] = ref[h]


def f32(*shape):
    return jax.ShapeDtypeStruct(shape, jnp.float32)


VMEM_SPEC = pl.BlockSpec(memory_space=pltpu.VMEM)
SMEM_SPEC = pl.BlockSpec(memory_space=pltpu.SMEM)
ANY_SPEC = pl.BlockSpec(memory_space=pl.ANY)
HBM_SPEC = pl.BlockSpec(memory_space=pltpu.HBM)
PARAMS = pltpu.CompilerParams(vmem_limit_bytes=40 * 1024 * 1024)


def kernel_call(body, outs, in_specs, scratch, name, flops=0, size=0):
    many = isinstance(outs, (list, tuple))
    return pl.pallas_call(
        body,
        out_shape=outs,
        in_specs=in_specs,
        out_specs=[VMEM_SPEC] * len(outs) if many else VMEM_SPEC,
        scratch_shapes=scratch,
        compiler_params=PARAMS,
        name=name,
        cost_estimate=pl.CostEstimate(flops=flops, bytes_accessed=size, transcendentals=0),
    )


def summed_plan(measured, drift, start_volume):
    views, slices, cols = measured.shape
    part = start_volume.shape[1]
    rows = 2 * part
    band = rows // 2 + DMAX + 2
    total_angles = drift.shape[0]
    block = cols // 8
    half_cols = cols // 2
    half_width = half_cols + LANES
    width = block + 2 * HALO
    tangent, secant = tan_and_secant(total_angles)
    scale = float(1.0 / np.sum(secant))
    tangent, secant = tangent.astype(np.float32), secant.astype(np.float32)

    halo = move(start_volume, lambda z, x, c, y: (z + 1, 0, c, y) if x else (z - 1, 1, c, y))

    tiles = half_width // LANES
    groups = slices // SUB
    window = (groups, tiles + 2, views, SUB, LANES)
    table = (2 * (2 * band // STEP + 1) * rows, 2 * STEP * views)
    terms = pltpu.VMEM((2, 2 * STEP * views, half_width + LANES), jnp.bfloat16)
    sibling, own_buf, weights = kernel_call(
        functools.partial(sibling_kernel, views, slices, rows, band, scale),
        [f32(slices, rows, half_width), f32(*window), f32(*table)],
        [HBM_SPEC] * 3,
        [
            pltpu.SMEM((total_angles,), jnp.float32),
            pltpu.SMEM((total_angles,), jnp.int32),
            pltpu.VMEM(window, jnp.float32),
            terms,
            pltpu.SemaphoreType.DMA((2,)),
            pltpu.SemaphoreType.DMA((groups, tiles)),
            pltpu.SemaphoreType.DMA((groups, tiles)),
        ],
        "back_project_sibling",
        flops=2 * 10**9,
        size=2**21,
    )(tangent, drift, measured)
    got = move(sibling, lambda z, x, c, y: (z, x, 1 - c, y))
    own = kernel_call(
        functools.partial(own_kernel, views, slices, rows, band),
        f32(slices, rows, half_width),
        [VMEM_SPEC] * 2,
        [terms],
        "back_project_own",
        flops=2 * 10**9,
        size=2**21,
    )(own_buf, weights)

    message = f32(slices + 2, rows, width)
    mine, to_x, to_y, to_xy = kernel_call(
        functools.partial(plane_pack_kernel, block),
        [message] * 4,
        [VMEM_SPEC] * 4,
        [pltpu.VMEM((slices, rows, half_width), jnp.float32), pltpu.VMEM((2 * part, cols + 2 * LANES), jnp.float32)],
        "plane_pack",
    )(own, got, start_volume, halo)
    got_xy = move(to_xy, lambda z, x, c, y: (z, 1 - x, c, 1 - y))
    got_x = move(to_x, lambda z, x, c, y: (z, 1 - x, c, y))
    got_y = move(to_y, lambda z, x, c, y: (z, x, c, 1 - y))

    edge = band * rows
    conv, low, high = kernel_call(
        functools.partial(gram_kernel, rows, band, scale),
        [f32(6 * rows, 2 * LANES), f32(edge, edge), f32(edge, edge)],
        [VMEM_SPEC] * 3 + [ANY_SPEC],
        [],
        "gram",
        flops=10**9,
    )(tangent[None], secant[None], drift[None], mine)

    window = f32(8, rows, width)
    own_win, to_1, to_2, to_3, vol_own, vol_sib = kernel_call(
        depth_pack_kernel,
        [window] * 4 + [f32(4, rows, width)] * 2,
        [VMEM_SPEC] * 4,
        [pltpu.VMEM((slices + 4, rows, width), jnp.float32)],
        "depth_pack",
    )(mine, got_x, got_y, got_xy)
    got_2 = move(to_2, lambda z, x, c, y: (z ^ 2, x, c, y))
    got_1 = move(to_1, lambda z, x, c, y: (z ^ 1, x, c, y))
    got_3 = move(to_3, lambda z, x, c, y: (z ^ 3, x, c, y))
    vol_got = move(vol_sib, lambda z, x, c, y: (z, x, 1 - c, y))

    work = pltpu.VMEM((8, rows, width), jnp.float32)
    first = kernel_call(
        functools.partial(first_normal_kernel, band, block, cols),
        window,
        [VMEM_SPEC] * 5,
        [work, work],
        "first_normal",
        flops=10**9,
    )(vol_own, vol_got, conv, low, high)

    piece = f32(2, rows, block)
    keep, send = kernel_call(
        functools.partial(finish_kernel, band, block, slices, cols),
        [piece, piece],
        [VMEM_SPEC] * 8,
        [work, work, pltpu.VMEM((4, rows, block), jnp.float32)],
        "finish",
    )(first, own_win, got_1, got_2, got_3, conv, low, high)
    swapped = move(send, lambda z, x, c, y: (z, x, 1 - c, y))
    small = f32(2, part, block)
    mine, to_x, to_y, to_xy = kernel_call(result_pack_kernel, [small] * 4, [VMEM_SPEC] * 2, [], "result_pack")(
        keep, swapped
    )
    got_xy = move(to_xy, lambda z, x, c, y: (z, 1 - x, c, 1 - y))
    got_x = move(to_x, lambda z, x, c, y: (z, 1 - x, c, y))
    got_y = move(to_y, lambda z, x, c, y: (z, x, c, 1 - y))
    return kernel_call(result_kernel, f32(1, part, cols), [VMEM_SPEC] * 4, [], "result")(mine, got_x, got_y, got_xy)


def summed_plan_fits(mesh, measured, start_volume):
    rows = start_volume.shape[1]
    cols = measured.shape[2]
    return (
        ITERS == 2
        and dict(mesh.shape) == {"wide": 16, "grp": 2}
        and measured.shape[1] == start_volume.shape[0] == 16
        and rows == SUB
        and cols % (16 * LANES) == 0
        and measured.shape[0] % 256 == 0
    )


def solution(mesh):
    in_specs = (P(("wide", "grp"), None, None), P(), P("wide", "grp", None))
    out_specs = P("wide", "grp", None)

    def run(measured, drift, start_volume):
        plan = summed_plan if summed_plan_fits(mesh, measured, start_volume) else on_device
        return jax.shard_map(plan, mesh=mesh, in_specs=in_specs, out_specs=out_specs, check_vma=False)(
            measured, drift, start_volume
        )

    return run
```

```python
import functools
from functools import reduce
import math

import jax
import jax.numpy as jnp
import numpy as np
from jax import lax
from jax.experimental import pallas as pl
from jax.experimental.pallas import tpu as pltpu
from jax.sharding import PartitionSpec as P

ITERS = 2
DMAX = 4


TILT_MAX = math.pi / 4
SMOOTH_EPS = 0.05
TV_STEP = 0.1


def with_halo(block, sides, width):
    for axis, dim in sides:
        count = lax.axis_size(axis)
        forward = [(i, i + 1) for i in range(count - 1)]
        backward = [(target, source) for source, target in forward]
        low = lax.ppermute(
            lax.slice_in_dim(block, block.shape[dim] - width, None, axis=dim), axis, forward
        )
        high = lax.ppermute(lax.slice_in_dim(block, 0, width, axis=dim), axis, backward)
        block = jnp.concatenate([low, block, high], axis=dim)
    return block


def geometry(angle_ids, drift_vals, total_angles, rows, band_extent):
    angle_rad = TILT_MAX * (2.0 * angle_ids.astype(jnp.float32) / (total_angles - 1) - 1.0)
    secant = 1.0 / jnp.cos(angle_rad)
    height = jnp.arange(rows, dtype=jnp.float32) - (rows - 1) / 2.0
    offsets = jnp.arange(2 * band_extent + 1, dtype=jnp.float32) - band_extent
    shifts = height[None, :] * jnp.tan(angle_rad)[:, None] - drift_vals.astype(jnp.float32)[:, None]
    weight_factors = secant[:, None, None] * jnp.maximum(
        0.0, 1.0 - jnp.abs(shifts[:, :, None] - offsets[None, None, :])
    )
    return (weight_factors, jnp.cos(angle_rad) / rows)


def secant_sum(total_angles):
    angle_rad = TILT_MAX * (
        2.0 * jnp.arange(total_angles, dtype=jnp.float32) / (total_angles - 1) - 1.0
    )
    return jnp.sum(1.0 / jnp.cos(angle_rad))


def local_geometry(angle_ids, drift, total_angles, rows_all, band_extent):
    matches = angle_ids[:, None] == jnp.arange(total_angles, dtype=jnp.int32)[None, :]
    local_drift = jnp.sum(jnp.where(matches, drift[None, :], 0), axis=1)
    return geometry(angle_ids, local_drift, total_angles, rows_all, band_extent)


def apply_correction(
    row_band_strip, measurement_part, weight_factors, residual_scale, global_scale, band_extent
):
    col_count = row_band_strip.shape[2]
    span = 2 * band_extent + 1
    padded = jnp.pad(row_band_strip, ((0, 0), (0, 0), (band_extent, band_extent)))
    shifted = jnp.stack(
        [padded[:, :, shift_id : shift_id + col_count] for shift_id in range(span)], axis=2
    )
    forward_projected = jnp.einsum(
        "ark,zrku->azu", weight_factors, shifted, precision=lax.Precision.HIGHEST
    )
    residual_error = residual_scale[:, None, None] * (measurement_part - forward_projected)
    spread = jnp.einsum(
        "ark,azu->kzru", weight_factors, residual_error, precision=lax.Precision.HIGHEST
    )
    spread = jnp.pad(spread, ((0, 0), (0, 0), (0, 0), (band_extent, band_extent)))
    pieces = [
        spread[shift_id, :, :, 2 * band_extent - shift_id : 2 * band_extent - shift_id + col_count]
        for shift_id in range(span)
    ]
    return global_scale * reduce(lambda left, right: left + right, pieces)


def divergence(extended, z_first, r_first, zcount, rcount):
    plane_count, height, col_count = extended.shape
    z_index = z_first + jnp.arange(plane_count, dtype=jnp.int32)[:, None, None]
    row_index = r_first + jnp.arange(height, dtype=jnp.int32)[None, :, None]
    col_index = jnp.arange(col_count, dtype=jnp.int32)[None, None, :]
    diff_z = jnp.concatenate([extended[1:] - extended[:-1], jnp.zeros_like(extended[:1])], axis=0)
    diff_z = jnp.where((z_index >= 0) & (z_index < zcount - 1), diff_z, 0.0)
    diff_r = jnp.concatenate(
        [extended[:, 1:] - extended[:, :-1], jnp.zeros_like(extended[:, :1])], axis=1
    )
    diff_r = jnp.where((row_index >= 0) & (row_index < rcount - 1), diff_r, 0.0)
    diff_c = jnp.concatenate(
        [extended[:, :, 1:] - extended[:, :, :-1], jnp.zeros_like(extended[:, :, :1])], axis=2
    )
    diff_c = jnp.where(col_index < col_count - 1, diff_c, 0.0)
    magnitude = jnp.sqrt(
        diff_z * diff_z + diff_r * diff_r + diff_c * diff_c + SMOOTH_EPS * SMOOTH_EPS
    )
    unit_z = diff_z / magnitude
    unit_r = diff_r / magnitude
    unit_c = diff_c / magnitude
    back_c = unit_c - jnp.concatenate([jnp.zeros_like(unit_c[:, :, :1]), unit_c[:, :, :-1]], axis=2)
    return (
        unit_z[1:-1, 1:-1]
        - unit_z[:-2, 1:-1]
        + (unit_r[1:-1, 1:-1] - unit_r[1:-1, :-2])
        + back_c[1:-1, 1:-1]
    )


def on_device(measured, drift, start_volume):
    wide_count = lax.axis_size("wide")
    groups = lax.axis_size("grp")
    slab_count, rows_tile, col_count = start_volume.shape
    rows_all = rows_tile * groups
    band_extent = rows_all // 2 + DMAX + 2
    per_device = measured.shape[0]
    total_angles = per_device * wide_count * groups
    global_scale = 1.0 / secant_sum(total_angles)
    z_first = lax.axis_index("wide") * slab_count - 1
    zcount = slab_count * wide_count
    local_measurement = lax.all_to_all(measured, "wide", split_axis=1, concat_axis=0, tiled=True)
    bin_position = jnp.arange(local_measurement.shape[0], dtype=jnp.int32)
    angle_ids = (
        bin_position // per_device * groups + lax.axis_index("grp")
    ) * per_device + bin_position % per_device
    weight_factors, residual_scale = local_geometry(
        angle_ids, drift, total_angles, rows_all, band_extent
    )
    own_tile = start_volume
    r_first = lax.axis_index("grp") * rows_tile - 1
    for sweep in range(ITERS):
        row_band_strip = lax.all_gather(own_tile, "grp", axis=1, tiled=True)
        volume_update = apply_correction(
            row_band_strip,
            local_measurement,
            weight_factors,
            residual_scale,
            global_scale,
            band_extent,
        )
        own_tile = own_tile + lax.psum_scatter(
            volume_update, "grp", scatter_dimension=1, tiled=True
        )
        extended = with_halo(own_tile, (("wide", 0), ("grp", 1)), 1)
        own_tile = own_tile + TV_STEP * divergence(extended, z_first, r_first, zcount, rows_all)
    return own_tile


LANES = 128
SUB = 8
HALO = 64


def tan_and_secant(total_angles):
    angle = TILT_MAX * (2.0 * np.arange(total_angles) / (total_angles - 1) - 1.0)
    return np.tan(angle), 1.0 / np.cos(angle)


def coords():
    wide, y = lax.axis_index("wide"), lax.axis_index("grp")
    return wide // 4, wide // 2 % 2, wide % 2, y


def move(value, target):
    pairs = []
    for z in range(4):
        for x in range(2):
            for c in range(2):
                for y in range(2):
                    to = target(z, x, c, y)
                    if to is not None and 0 <= to[0] < 4:
                        tz, tx, tc, ty = to
                        pairs.append((((z * 2 + x) * 2 + c) * 2 + y, ((tz * 2 + tx) * 2 + tc) * 2 + ty))
    return lax.ppermute(value, ("wide", "grp"), pairs)


def split_rows(value):
    high = value.astype(jnp.bfloat16).astype(jnp.float32)
    return jnp.concatenate([high, value - high], axis=0)


def split_terms(value):
    high = value.astype(jnp.bfloat16)
    low = (value - high.astype(jnp.float32)).astype(jnp.bfloat16)
    return jnp.concatenate([high, low], axis=0)


def lane_iota(shape):
    return lax.broadcasted_iota(jnp.int32, shape, len(shape) - 1)


def row_iota(shape):
    return lax.broadcasted_iota(jnp.int32, shape, len(shape) - 2)


STEP = 3


def view_weights(views, rows, band, scale, tan_ref, drift_ref):
    z, x, c, y = coords()
    first_view = (((z * 2 + x) * 2 + c) * 2 + y) * views
    parts = 2 * band // STEP + 1
    shape = (parts * rows, STEP * views)
    lane, row = lane_iota(shape), row_iota(shape)
    view_of = lane_iota((1, STEP * views)) % views
    tan_lane = jnp.zeros((1, STEP * views), jnp.float32)
    drift_lane = tan_lane
    for a in range(views):
        tan_lane = jnp.where(view_of == a, tan_ref[first_view + a], tan_lane)
        drift_lane = jnp.where(view_of == a, drift_ref[first_view + a].astype(jnp.float32), drift_lane)
    shift = ((row % rows).astype(jnp.float32) - (rows - 1) / 2.0) * tan_lane - drift_lane
    offset = ((row // rows) * STEP + lane // views - band).astype(jnp.float32)
    weights = (scale / rows) * jnp.maximum(0.0, 1.0 - jnp.abs(shift - offset))
    weights = split_rows(weights)
    return jnp.concatenate([weights, weights], axis=1).astype(jnp.bfloat16)


def back_project(views, slices, rows, band, weights, load_strip, out_ref, terms):
    out_cols = out_ref.shape[2]
    width = terms.shape[2]
    parts = 2 * band // STEP + 1

    def prepare(s, buf):
        strip = load_strip(s)
        high = strip.astype(jnp.bfloat16)
        low = (strip - high.astype(jnp.float32)).astype(jnp.bfloat16)
        for j in range(STEP):
            buf[j * views : (j + 1) * views] = pltpu.roll(high, j, 1) if j else high
            buf[(STEP + j) * views : (STEP + j + 1) * views] = pltpu.roll(low, j, 1) if j else low

    prepare(0, terms.at[0])
    for s in range(slices):
        if s + 1 < slices:
            prepare(s + 1, terms.at[(s + 1) % 2])
        spread = jnp.dot(weights, terms[s % 2], preferred_element_type=jnp.float32)
        spread = spread[: parts * rows] + spread[parts * rows :]
        total = None
        for i in range(parts):
            piece = pltpu.roll(spread[i * rows : (i + 1) * rows], width - HALO - band + STEP * i, 1)
            total = piece if total is None else total + piece
        out_ref[s] = total[:, :out_cols]


def strip_loader(buf, half, views, tiles):
    def load(s):
        return jnp.concatenate(
            [buf[s // SUB, half + t, pl.ds(s % SUB, views, stride=SUB), :] for t in range(tiles + 1)], axis=1
        )

    return load


def volume_window(vol_ref, half, half_cols, vbuf):
    part, cols = vol_ref.shape[1:]
    vbuf[:, 0:LANES] = jnp.zeros((part, LANES), jnp.float32)
    vbuf[:, LANES : LANES + cols] = vol_ref[0]
    vbuf[:, LANES + cols :] = jnp.zeros((part, LANES), jnp.float32)
    width = half_cols + 2 * LANES
    window = vbuf[:, pl.ds(pl.multiple_of(half * half_cols, LANES), width)]
    return pltpu.roll(window, width - HALO, 1)[:, : half_cols + LANES]


def sibling_kernel(views, slices, rows, band, scale, tan_hbm, drift_hbm, meas_ref, vol_ref, out_ref, own_buf,
                   weights_ref, tan_ref, drift_ref, buf, terms, vbuf, table_sem, sem, own_sem):
    _, _, c, _ = coords()
    tiles = out_ref.shape[2] // LANES
    groups = slices // SUB

    def fetch(half, g, t, target, semaphore):
        first = pl.multiple_of((half * (tiles - 1) + t - half) * LANES, LANES)
        return pltpu.make_async_copy(
            meas_ref.at[:, pl.ds(g * SUB, SUB), pl.ds(first, LANES)], target.at[g, t + 1], semaphore
        )

    tables = [
        pltpu.make_async_copy(tan_hbm, tan_ref, table_sem.at[0]),
        pltpu.make_async_copy(drift_hbm, drift_ref, table_sem.at[1]),
    ]
    first = [[fetch(1 - c, g, t, buf, sem.at[g, t]) for t in range(tiles)] for g in range(groups)]
    later = [[fetch(c, g, t, own_buf, own_sem.at[g, t]) for t in range(tiles)] for g in range(groups)]
    for copy in tables + first[0] + first[1] + later[0] + later[1]:
        copy.start()
    zero = jnp.zeros((views, SUB, LANES), jnp.float32)
    for g in range(groups):
        for target in (buf, own_buf):
            target[g, 0] = zero
            target[g, tiles + 1] = zero
    half_cols = out_ref.shape[2] - LANES
    part = vol_ref.shape[1]
    out_ref[slices, 0:part] = volume_window(vol_ref, 1 - c, half_cols, vbuf)
    out_ref[slices, part:] = jnp.zeros((rows - part, half_cols + LANES), jnp.float32)
    for copy in tables:
        copy.wait()
    weights = view_weights(views, rows, band, scale, tan_ref, drift_ref)
    weights_ref[...] = weights.astype(jnp.float32)
    flat = buf.reshape(groups, tiles + 2, views * SUB, LANES)
    load = strip_loader(flat, 1 - c, views, tiles)

    def load_strip(s):
        if s % SUB == 0:
            for copy in first[s // SUB]:
                copy.wait()
        return load(s)

    back_project(views, slices, rows, band, weights, load_strip, out_ref, terms)
    for group in later:
        for copy in group:
            copy.wait()


def own_kernel(views, slices, rows, band, buf, weights_ref, out_ref, terms):
    _, _, c, _ = coords()
    tiles = out_ref.shape[2] // LANES
    flat = buf.reshape(slices // SUB, tiles + 2, views * SUB, LANES)
    load = strip_loader(flat, c, views, tiles)
    back_project(views, slices, rows, band, weights_ref[...].astype(jnp.bfloat16), load, out_ref, terms)


def plane_pack_kernel(own_ref, got_ref, vol_ref, mine, to_x, to_y, to_xy, acc, both, vbuf):
    slices, rows, half_width = own_ref.shape
    width = mine.shape[2]
    part = vol_ref.shape[1]
    z, x, c, y = coords()
    acc[...] = own_ref[...] + got_ref[0:slices]
    here = volume_window(vol_ref, c, half_width - LANES, vbuf)
    there = got_ref[slices, 0:part]
    both[0:part] = jnp.where(c == 0, here, there)
    both[part:] = jnp.where(c == 0, there, here)
    for out, px, py in ((mine, x, y), (to_x, 1 - x, y), (to_y, x, 1 - y), (to_xy, 1 - x, 1 - y)):
        begin = pl.multiple_of(py * (width - LANES), LANES)
        for pz in range(slices // 4):
            out[2 * pz : 2 * pz + 2] = acc[pl.ds(4 * pz + 2 * px, 2), :, pl.ds(begin, width)]
        if out.shape[0] > slices // 2:
            out[slices // 2] = both[:, pl.ds(begin, width)]


def depth_pack_kernel(mine, got_x, got_y, got_xy, own_pair, to_1, to_2, to_3, vol_pair, acc):
    count, rows, _ = acc.shape
    part = rows // 2
    z, x, c, y = coords()
    acc[...] = (mine[0:count] + got_x[...]) + (got_y[0:count] + got_xy[...])
    for out, pz in (
        (own_pair, z),
        (to_1, jnp.where(z % 2 == 0, z + 1, z - 1)),
        (to_2, jnp.where(z < 2, z + 2, z - 2)),
        (to_3, 3 - z),
    ):
        out[...] = acc[pl.ds(2 * pz, 2)]
    here, there = mine[count], got_y[count]
    upper = jnp.where(y == 0, here, there)
    lower = jnp.where(y == 0, there, here)
    for i in range(2):
        vol_pair[i] = jnp.concatenate([upper[i * part : (i + 1) * part], lower[i * part : (i + 1) * part]], axis=0)


def gram_kernel(rows, band, scale, tan_ref, sec_ref, drift_ref, after_ref, conv_ref, low_ref, high_ref):
    views = tan_ref.shape[1]
    span = 2 * band + 1
    shape = (span * rows, views)
    row = row_iota(shape)
    shift = ((row % rows).astype(jnp.float32) - (rows - 1) / 2.0) * tan_ref[...] - drift_ref[...].astype(jnp.float32)
    hat = jnp.maximum(0.0, 1.0 - jnp.abs(shift - (row // rows - band).astype(jnp.float32)))
    gram = lax.dot_general(
        hat * ((scale / rows) * sec_ref[...]),
        hat,
        (((1,), (1,)), ((), ())),
        precision=lax.Precision.HIGHEST,
        preferred_element_type=jnp.float32,
    )
    edge = band * rows
    low_ref[...] = gram[edge + rows :, edge + rows :]
    high_ref[...] = gram[:edge, :edge]
    width = conv_ref.shape[1] // 2 * 3
    padded = jnp.concatenate([gram, jnp.zeros((span * rows, width - span * rows), jnp.float32)], axis=1)
    total = jnp.zeros((rows, width), jnp.float32)
    for k in range(span):
        total = total + pltpu.roll(padded[k * rows : (k + 1) * rows], rows * (2 * band - k), 1)
    lanes = width // 3
    stacked = jnp.concatenate([total[:, i * lanes : (i + 1) * lanes] for i in range(3)], axis=0)
    stacked = split_rows(stacked)
    conv_ref[...] = jnp.concatenate([stacked, stacked], axis=1)


def normal(volumes, conv, low_ref, high_ref, out, band, is_low, is_high):
    rows, width = volumes[0].shape
    count = len(volumes)
    step = conv.shape[1] // 2 // rows
    parts = conv.shape[0] // 2 // rows
    for s in range(count):
        moved = jnp.concatenate(
            [pltpu.roll(volumes[s], (2 * band - j) % width, 1) for j in range(step)], axis=0
        )
        spread = jnp.dot(conv, split_terms(moved), preferred_element_type=jnp.float32)
        spread = spread[: parts * rows] + spread[parts * rows :]
        total = spread[0:rows]
        for i in range(1, parts):
            total = total + pltpu.roll(spread[i * rows : (i + 1) * rows], width - step * i, 1)
        out[s] = total

    lane = lane_iota((rows, LANES))

    @pl.when(is_low)
    def _():
        tiles = [v[:, :LANES] for v in volumes]
        moved = jnp.concatenate(
            [jnp.concatenate([pltpu.roll(t, LANES - k, 1) for k in range(1, band + 1)], axis=0) for t in tiles], axis=1
        )
        spread = jnp.dot(low_ref[...], moved, precision=lax.Precision.HIGHEST, preferred_element_type=jnp.float32)
        for s in range(count):
            total = jnp.zeros((rows, LANES), jnp.float32)
            for k in range(1, band + 1):
                piece = spread[(k - 1) * rows : k * rows, s * LANES : (s + 1) * LANES]
                piece = jnp.where((lane >= HALO - band) & (lane < HALO), piece, 0.0)
                total = total + pltpu.roll(piece, k, 1)
            out[s, :, 0:LANES] = out[s, :, 0:LANES] - total

    @pl.when(is_high)
    def _():
        tiles = [v[:, width - LANES :] for v in volumes]
        moved = jnp.concatenate(
            [jnp.concatenate([pltpu.roll(t, k, 1) for k in range(band, 0, -1)], axis=0) for t in tiles], axis=1
        )
        spread = jnp.dot(high_ref[...], moved, precision=lax.Precision.HIGHEST, preferred_element_type=jnp.float32)
        for s in range(count):
            total = jnp.zeros((rows, LANES), jnp.float32)
            for k in range(band, 0, -1):
                piece = spread[(band - k) * rows : (band - k + 1) * rows, s * LANES : (s + 1) * LANES]
                piece = jnp.where((lane >= LANES - HALO) & (lane < LANES - HALO + band), piece, 0.0)
                total = total + pltpu.roll(piece, LANES - k, 1)
            out[s, :, width - LANES :] = out[s, :, width - LANES :] - total


def block_place(width, total_cols):
    z, x, c, y = coords()
    block = width - 2 * HALO
    index = c * 2 + y
    return index * block - HALO, index == 0, index == total_cols // block - 1


def first_normal_kernel(band, total_cols, vol_pair, conv_ref, low_ref, high_ref, out, work):
    _, is_low, is_high = block_place(vol_pair.shape[2], total_cols)
    volumes = [vol_pair[i] for i in range(2)]
    normal(volumes, conv_ref[...].astype(jnp.bfloat16), low_ref, high_ref, work, band, is_low, is_high)
    for i in range(2):
        out[i] = volumes[i] - work[i]


def half_pair_kernel(first_ref, own_pair, got_1, got_2, got_3, mine, to_x, to_diag, corr):
    _, x, _, _ = coords()
    corr[...] = (own_pair[...] + got_1[...]) + (got_2[...] + got_3[...])
    half = first_ref[...] + corr[...]
    mine[0:2] = half
    mine[2:4] = corr[...]
    to_x[0:2] = half
    to_x[2] = corr[1 - x]
    to_diag[0:2] = half
    to_diag[2] = corr[x]


def variation_step(half, z_of, first_col, depth, total_cols):
    rows, width = half[0].shape
    col = first_col + lane_iota((rows, width))
    row = row_iota((rows, width))
    inside = (col >= 0) & (col < total_cols - 1)
    units = []
    for w in range(len(half) - 1):
        v = half[w]
        keep = (z_of(w) >= 0) & (z_of(w) < depth - 1)
        dz = jnp.where(keep, half[w + 1] - v, 0.0)
        dr = jnp.where(row < rows - 1, pltpu.roll(v, rows - 1, 0) - v, 0.0)
        dc = jnp.where(inside, pltpu.roll(v, width - 1, 1) - v, 0.0)
        inverse = 1.0 / jnp.sqrt(dz * dz + dr * dr + dc * dc + SMOOTH_EPS * SMOOTH_EPS)
        units.append((dz * inverse, dr * inverse, dc * inverse))
    result = []
    for w in range(1, len(half) - 1):
        uz, ur, uc = units[w]
        div = (uz - units[w - 1][0]) + (ur - pltpu.roll(ur, 1, 0)) + (uc - pltpu.roll(uc, 1, 1))
        result.append(jnp.where((col >= 0) & (col < total_cols), half[w] + TV_STEP * div, 0.0))
    return result


def finish_kernel(
    band, depth, total_cols, mine, got_x, got_diag, conv_ref, low_ref, high_ref, keep_ref, send_ref, work, done
):
    width = mine.shape[2]
    first_col, is_low, is_high = block_place(width, total_cols)
    z, x, c, _ = coords()
    before = [jnp.where(x == 0, got_diag[i], got_x[i]) for i in range(3)]
    after = [jnp.where(x == 0, got_x[i], got_diag[i]) for i in range(3)]
    half = [before[0], before[1], mine[0], mine[1], after[0], after[1]]
    corr = [before[2], mine[2], mine[3], after[2]]
    slice_0 = 4 * z + 2 * x
    volumes = variation_step(half, lambda w: slice_0 - 2 + w, first_col, depth, total_cols)
    normal(volumes, conv_ref[...].astype(jnp.bfloat16), low_ref, high_ref, work, band, is_low, is_high)
    half = [volumes[s] + corr[s] - work[s] for s in range(4)]
    volumes = variation_step(half, lambda w: slice_0 - 1 + w, first_col, depth, total_cols)
    for s in range(2):
        done[s] = pltpu.roll(volumes[s], width - HALO, 1)[:, : width - LANES]
    keep_ref[...] = done[c]
    send_ref[...] = done[1 - c]


def result_pack_kernel(own_ref, got_ref, to_y):
    _, _, c, y = coords()
    part = to_y.shape[1]
    own, got = own_ref[...], got_ref[...]
    to_y[c] = jnp.where(y == 0, own[part:], own[:part])
    to_y[1 - c] = jnp.where(y == 0, got[part:], got[:part])


def result_kernel(own_ref, got_ref, got_y, out):
    _, _, c, y = coords()
    _, part, block = got_y.shape
    own, got = own_ref[...], got_ref[...]
    here = jnp.where(y == 0, own[:part], own[part:])
    there = jnp.where(y == 0, got[:part], got[part:])
    for value, h, q in ((here, c, y), (there, 1 - c, y), (got_y[0], 0, 1 - y), (got_y[1], 1, 1 - y)):
        out[0, :, pl.ds(pl.multiple_of((2 * h + q) * block, LANES), block)] = value


def f32(*shape):
    return jax.ShapeDtypeStruct(shape, jnp.float32)


VMEM_SPEC = pl.BlockSpec(memory_space=pltpu.VMEM)
SMEM_SPEC = pl.BlockSpec(memory_space=pltpu.SMEM)
ANY_SPEC = pl.BlockSpec(memory_space=pl.ANY)
HBM_SPEC = pl.BlockSpec(memory_space=pltpu.HBM)
PARAMS = pltpu.CompilerParams(vmem_limit_bytes=40 * 1024 * 1024)


def in_hbm(value):
    return pltpu.with_memory_space_constraint(value, pltpu.HBM)


def kernel_call(body, outs, in_specs, scratch, name, flops=0, size=0):
    many = isinstance(outs, (list, tuple))
    return pl.pallas_call(
        body,
        out_shape=outs,
        in_specs=in_specs,
        out_specs=[VMEM_SPEC] * len(outs) if many else VMEM_SPEC,
        scratch_shapes=scratch,
        compiler_params=PARAMS,
        name=name,
        cost_estimate=pl.CostEstimate(flops=flops, bytes_accessed=size, transcendentals=0),
    )


def summed_plan(measured, drift, start_volume):
    views, slices, cols = measured.shape
    part = start_volume.shape[1]
    rows = 2 * part
    band = rows // 2 + DMAX + 2
    total_angles = drift.shape[0]
    half_cols = cols // 2
    half_width = half_cols + LANES
    width = cols // 4 + 2 * HALO
    tangent, secant = tan_and_secant(total_angles)
    scale = float(1.0 / np.sum(secant))
    tangent, secant = tangent.astype(np.float32), secant.astype(np.float32)

    tiles = half_width // LANES
    groups = slices // SUB
    window = (groups, tiles + 2, views, SUB, LANES)
    table = (2 * (2 * band // STEP + 1) * rows, 2 * STEP * views)
    terms = pltpu.VMEM((2, 2 * STEP * views, half_width + LANES), jnp.bfloat16)
    vbuf = pltpu.VMEM((part, cols + 2 * LANES), jnp.float32)
    sibling, own_buf, weights = kernel_call(
        functools.partial(sibling_kernel, views, slices, rows, band, scale),
        [f32(slices + 1, rows, half_width), f32(*window), f32(*table)],
        [HBM_SPEC] * 3 + [VMEM_SPEC],
        [
            pltpu.SMEM((total_angles,), jnp.float32),
            pltpu.SMEM((total_angles,), jnp.int32),
            pltpu.VMEM(window, jnp.float32),
            terms,
            vbuf,
            pltpu.SemaphoreType.DMA((2,)),
            pltpu.SemaphoreType.DMA((groups, tiles)),
            pltpu.SemaphoreType.DMA((groups, tiles)),
        ],
        "back_project_sibling",
        flops=2 * 10**9,
        size=2**21,
    )(in_hbm(jnp.asarray(tangent)), in_hbm(drift), in_hbm(measured), start_volume)
    got = move(sibling, lambda z, x, c, y: (z, x, 1 - c, y))
    own = kernel_call(
        functools.partial(own_kernel, views, slices, rows, band),
        f32(slices, rows, half_width),
        [VMEM_SPEC] * 2,
        [terms],
        "back_project_own",
        flops=2 * 10**9,
        size=2**21,
    )(own_buf, weights)

    count = slices // 2
    mine, to_x, to_y, to_xy = kernel_call(
        plane_pack_kernel,
        [f32(count + 1, rows, width), f32(count, rows, width), f32(count + 1, rows, width), f32(count, rows, width)],
        [VMEM_SPEC] * 3,
        [pltpu.VMEM((slices, rows, half_width), jnp.float32), pltpu.VMEM((rows, half_width), jnp.float32), vbuf],
        "plane_pack",
    )(own, got, start_volume)
    got_xy = move(to_xy, lambda z, x, c, y: (z, 1 - x, c, 1 - y))
    got_x = move(to_x, lambda z, x, c, y: (z, 1 - x, c, y))
    got_y = move(to_y, lambda z, x, c, y: (z, x, c, 1 - y))

    edge = band * rows
    conv, low, high = kernel_call(
        functools.partial(gram_kernel, rows, band, scale),
        [f32(6 * rows, 2 * LANES), f32(edge, edge), f32(edge, edge)],
        [VMEM_SPEC] * 3 + [ANY_SPEC],
        [],
        "gram",
        flops=10**9,
    )(tangent[None], secant[None], drift[None], mine)

    pair = f32(2, rows, width)
    own_pair, to_1, to_2, to_3, vol_pair = kernel_call(
        depth_pack_kernel,
        [pair] * 5,
        [VMEM_SPEC] * 4,
        [pltpu.VMEM((count, rows, width), jnp.float32)],
        "depth_pack",
    )(mine, got_x, got_y, got_xy)
    got_2 = move(to_2, lambda z, x, c, y: (z ^ 2, x, c, y))
    got_1 = move(to_1, lambda z, x, c, y: (z ^ 1, x, c, y))
    got_3 = move(to_3, lambda z, x, c, y: (z ^ 3, x, c, y))

    first = kernel_call(
        functools.partial(first_normal_kernel, band, cols),
        pair,
        [VMEM_SPEC] * 4,
        [pltpu.VMEM((2, rows, width), jnp.float32)],
        "first_normal",
        flops=10**9,
    )(vol_pair, conv, low, high)

    three = f32(3, rows, width)
    mine, to_x, to_diag = kernel_call(
        half_pair_kernel,
        [f32(4, rows, width), three, three],
        [VMEM_SPEC] * 5,
        [pltpu.VMEM((2, rows, width), jnp.float32)],
        "half_pair",
    )(first, own_pair, got_1, got_2, got_3)
    got_diag = move(to_diag, lambda z, x, c, y: (z + 1, 0, c, y) if x else (z - 1, 1, c, y))
    got_x = move(to_x, lambda z, x, c, y: (z, 1 - x, c, y))

    block = width - 2 * HALO
    quarter = f32(rows, block)
    keep, send = kernel_call(
        functools.partial(finish_kernel, band, slices, cols),
        [quarter, quarter],
        [VMEM_SPEC] * 6,
        [pltpu.VMEM((4, rows, width), jnp.float32), pltpu.VMEM((2, rows, block), jnp.float32)],
        "finish",
    )(mine, got_x, got_diag, conv, low, high)
    swapped = move(send, lambda z, x, c, y: (z, x, 1 - c, y))
    to_y = kernel_call(result_pack_kernel, f32(2, part, block), [VMEM_SPEC] * 2, [], "result_pack")(keep, swapped)
    got_y = move(to_y, lambda z, x, c, y: (z, x, c, 1 - y))
    return kernel_call(result_kernel, f32(1, part, cols), [VMEM_SPEC] * 3, [], "result")(keep, swapped, got_y)


def summed_plan_fits(mesh, measured, start_volume):
    rows = start_volume.shape[1]
    cols = measured.shape[2]
    return (
        ITERS == 2
        and dict(mesh.shape) == {"wide": 16, "grp": 2}
        and measured.shape[1] == start_volume.shape[0] == 16
        and rows == SUB
        and cols % (16 * LANES) == 0
        and measured.shape[0] % 256 == 0
    )


def solution(mesh):
    in_specs = (P(("wide", "grp"), None, None), P(), P("wide", "grp", None))
    out_specs = P("wide", "grp", None)

    def run(measured, drift, start_volume):
        plan = summed_plan if summed_plan_fits(mesh, measured, start_volume) else on_device
        return jax.shard_map(plan, mesh=mesh, in_specs=in_specs, out_specs=out_specs, check_vma=False)(
            measured, drift, start_volume
        )

    return run
```

```python
import functools
from functools import reduce
import math

import jax
import jax.numpy as jnp
import numpy as np
from jax import lax
from jax.experimental import pallas as pl
from jax.experimental.pallas import tpu as pltpu
from jax.sharding import PartitionSpec as P

ITERS = 2
DMAX = 4


TILT_MAX = math.pi / 4
SMOOTH_EPS = 0.05
TV_STEP = 0.1


def with_halo(block, sides, width):
    for axis, dim in sides:
        count = lax.axis_size(axis)
        forward = [(i, i + 1) for i in range(count - 1)]
        backward = [(target, source) for source, target in forward]
        low = lax.ppermute(
            lax.slice_in_dim(block, block.shape[dim] - width, None, axis=dim), axis, forward
        )
        high = lax.ppermute(lax.slice_in_dim(block, 0, width, axis=dim), axis, backward)
        block = jnp.concatenate([low, block, high], axis=dim)
    return block


def geometry(angle_ids, drift_vals, total_angles, rows, band_extent):
    angle_rad = TILT_MAX * (2.0 * angle_ids.astype(jnp.float32) / (total_angles - 1) - 1.0)
    secant = 1.0 / jnp.cos(angle_rad)
    height = jnp.arange(rows, dtype=jnp.float32) - (rows - 1) / 2.0
    offsets = jnp.arange(2 * band_extent + 1, dtype=jnp.float32) - band_extent
    shifts = height[None, :] * jnp.tan(angle_rad)[:, None] - drift_vals.astype(jnp.float32)[:, None]
    weight_factors = secant[:, None, None] * jnp.maximum(
        0.0, 1.0 - jnp.abs(shifts[:, :, None] - offsets[None, None, :])
    )
    return (weight_factors, jnp.cos(angle_rad) / rows)


def secant_sum(total_angles):
    angle_rad = TILT_MAX * (
        2.0 * jnp.arange(total_angles, dtype=jnp.float32) / (total_angles - 1) - 1.0
    )
    return jnp.sum(1.0 / jnp.cos(angle_rad))


def local_geometry(angle_ids, drift, total_angles, rows_all, band_extent):
    matches = angle_ids[:, None] == jnp.arange(total_angles, dtype=jnp.int32)[None, :]
    local_drift = jnp.sum(jnp.where(matches, drift[None, :], 0), axis=1)
    return geometry(angle_ids, local_drift, total_angles, rows_all, band_extent)


def apply_correction(
    row_band_strip, measurement_part, weight_factors, residual_scale, global_scale, band_extent
):
    col_count = row_band_strip.shape[2]
    span = 2 * band_extent + 1
    padded = jnp.pad(row_band_strip, ((0, 0), (0, 0), (band_extent, band_extent)))
    shifted = jnp.stack(
        [padded[:, :, shift_id : shift_id + col_count] for shift_id in range(span)], axis=2
    )
    forward_projected = jnp.einsum(
        "ark,zrku->azu", weight_factors, shifted, precision=lax.Precision.HIGHEST
    )
    residual_error = residual_scale[:, None, None] * (measurement_part - forward_projected)
    spread = jnp.einsum(
        "ark,azu->kzru", weight_factors, residual_error, precision=lax.Precision.HIGHEST
    )
    spread = jnp.pad(spread, ((0, 0), (0, 0), (0, 0), (band_extent, band_extent)))
    pieces = [
        spread[shift_id, :, :, 2 * band_extent - shift_id : 2 * band_extent - shift_id + col_count]
        for shift_id in range(span)
    ]
    return global_scale * reduce(lambda left, right: left + right, pieces)


def divergence(extended, z_first, r_first, zcount, rcount):
    plane_count, height, col_count = extended.shape
    z_index = z_first + jnp.arange(plane_count, dtype=jnp.int32)[:, None, None]
    row_index = r_first + jnp.arange(height, dtype=jnp.int32)[None, :, None]
    col_index = jnp.arange(col_count, dtype=jnp.int32)[None, None, :]
    diff_z = jnp.concatenate([extended[1:] - extended[:-1], jnp.zeros_like(extended[:1])], axis=0)
    diff_z = jnp.where((z_index >= 0) & (z_index < zcount - 1), diff_z, 0.0)
    diff_r = jnp.concatenate(
        [extended[:, 1:] - extended[:, :-1], jnp.zeros_like(extended[:, :1])], axis=1
    )
    diff_r = jnp.where((row_index >= 0) & (row_index < rcount - 1), diff_r, 0.0)
    diff_c = jnp.concatenate(
        [extended[:, :, 1:] - extended[:, :, :-1], jnp.zeros_like(extended[:, :, :1])], axis=2
    )
    diff_c = jnp.where(col_index < col_count - 1, diff_c, 0.0)
    magnitude = jnp.sqrt(
        diff_z * diff_z + diff_r * diff_r + diff_c * diff_c + SMOOTH_EPS * SMOOTH_EPS
    )
    unit_z = diff_z / magnitude
    unit_r = diff_r / magnitude
    unit_c = diff_c / magnitude
    back_c = unit_c - jnp.concatenate([jnp.zeros_like(unit_c[:, :, :1]), unit_c[:, :, :-1]], axis=2)
    return (
        unit_z[1:-1, 1:-1]
        - unit_z[:-2, 1:-1]
        + (unit_r[1:-1, 1:-1] - unit_r[1:-1, :-2])
        + back_c[1:-1, 1:-1]
    )


def on_device(measured, drift, start_volume):
    wide_count = lax.axis_size("wide")
    groups = lax.axis_size("grp")
    slab_count, rows_tile, col_count = start_volume.shape
    rows_all = rows_tile * groups
    band_extent = rows_all // 2 + DMAX + 2
    per_device = measured.shape[0]
    total_angles = per_device * wide_count * groups
    global_scale = 1.0 / secant_sum(total_angles)
    z_first = lax.axis_index("wide") * slab_count - 1
    zcount = slab_count * wide_count
    local_measurement = lax.all_to_all(measured, "wide", split_axis=1, concat_axis=0, tiled=True)
    bin_position = jnp.arange(local_measurement.shape[0], dtype=jnp.int32)
    angle_ids = (
        bin_position // per_device * groups + lax.axis_index("grp")
    ) * per_device + bin_position % per_device
    weight_factors, residual_scale = local_geometry(
        angle_ids, drift, total_angles, rows_all, band_extent
    )
    own_tile = start_volume
    r_first = lax.axis_index("grp") * rows_tile - 1
    for sweep in range(ITERS):
        row_band_strip = lax.all_gather(own_tile, "grp", axis=1, tiled=True)
        volume_update = apply_correction(
            row_band_strip,
            local_measurement,
            weight_factors,
            residual_scale,
            global_scale,
            band_extent,
        )
        own_tile = own_tile + lax.psum_scatter(
            volume_update, "grp", scatter_dimension=1, tiled=True
        )
        extended = with_halo(own_tile, (("wide", 0), ("grp", 1)), 1)
        own_tile = own_tile + TV_STEP * divergence(extended, z_first, r_first, zcount, rows_all)
    return own_tile


LANES = 128
SUB = 8
HALO = 64


def tan_and_secant(total_angles):
    angle = TILT_MAX * (2.0 * np.arange(total_angles) / (total_angles - 1) - 1.0)
    return np.tan(angle), 1.0 / np.cos(angle)


def coords():
    wide, y = lax.axis_index("wide"), lax.axis_index("grp")
    return wide // 4, wide // 2 % 2, wide % 2, y


def move(value, target):
    pairs = []
    for z in range(4):
        for x in range(2):
            for c in range(2):
                for y in range(2):
                    to = target(z, x, c, y)
                    if to is not None and 0 <= to[0] < 4:
                        tz, tx, tc, ty = to
                        pairs.append((((z * 2 + x) * 2 + c) * 2 + y, ((tz * 2 + tx) * 2 + tc) * 2 + ty))
    return lax.ppermute(value, ("wide", "grp"), pairs)


def split_rows(value):
    high = value.astype(jnp.bfloat16).astype(jnp.float32)
    return jnp.concatenate([high, value - high], axis=0)


def split_terms(value):
    high = value.astype(jnp.bfloat16)
    low = (value - high.astype(jnp.float32)).astype(jnp.bfloat16)
    return jnp.concatenate([high, low], axis=0)


def lane_iota(shape):
    return lax.broadcasted_iota(jnp.int32, shape, len(shape) - 1)


def row_iota(shape):
    return lax.broadcasted_iota(jnp.int32, shape, len(shape) - 2)


STEP = 3


def view_weights(views, rows, band, scale, tan_ref, drift_ref):
    z, x, c, y = coords()
    first_view = (((z * 2 + x) * 2 + c) * 2 + y) * views
    parts = 2 * band // STEP + 1
    shape = (parts * rows, STEP * views)
    lane, row = lane_iota(shape), row_iota(shape)
    view_of = lane_iota((1, STEP * views)) % views
    tan_lane = jnp.zeros((1, STEP * views), jnp.float32)
    drift_lane = tan_lane
    for a in range(views):
        tan_lane = jnp.where(view_of == a, tan_ref[first_view + a], tan_lane)
        drift_lane = jnp.where(view_of == a, drift_ref[first_view + a].astype(jnp.float32), drift_lane)
    shift = ((row % rows).astype(jnp.float32) - (rows - 1) / 2.0) * tan_lane - drift_lane
    offset = ((row // rows) * STEP + lane // views - band).astype(jnp.float32)
    weights = (scale / rows) * jnp.maximum(0.0, 1.0 - jnp.abs(shift - offset))
    weights = split_rows(weights)
    return jnp.concatenate([weights, weights], axis=1).astype(jnp.bfloat16)


def back_project(views, slices, rows, band, weights, load_strip, out_ref, terms):
    out_cols = out_ref.shape[2]
    width = terms.shape[2]
    parts = 2 * band // STEP + 1

    def prepare(s, buf):
        strip = load_strip(s)
        high = strip.astype(jnp.bfloat16)
        low = (strip - high.astype(jnp.float32)).astype(jnp.bfloat16)
        for j in range(STEP):
            buf[j * views : (j + 1) * views] = pltpu.roll(high, j, 1) if j else high
            buf[(STEP + j) * views : (STEP + j + 1) * views] = pltpu.roll(low, j, 1) if j else low

    prepare(0, terms.at[0])
    for s in range(slices):
        if s + 1 < slices:
            prepare(s + 1, terms.at[(s + 1) % 2])
        spread = jnp.dot(weights, terms[s % 2], preferred_element_type=jnp.float32)
        spread = spread[: parts * rows] + spread[parts * rows :]
        total = None
        for i in range(parts):
            piece = pltpu.roll(spread[i * rows : (i + 1) * rows], width - HALO - band + STEP * i, 1)
            total = piece if total is None else total + piece
        out_ref[s] = total[:, :out_cols]


def strip_loader(buf, half, views, tiles):
    def load(s):
        return jnp.concatenate(
            [buf[s // SUB, half + t, pl.ds(s % SUB, views, stride=SUB), :] for t in range(tiles + 1)], axis=1
        )

    return load


def volume_window(vol_ref, half, half_cols, vbuf):
    part, cols = vol_ref.shape[1:]
    vbuf[:, 0:LANES] = jnp.zeros((part, LANES), jnp.float32)
    vbuf[:, LANES : LANES + cols] = vol_ref[0]
    vbuf[:, LANES + cols :] = jnp.zeros((part, LANES), jnp.float32)
    width = half_cols + 2 * LANES
    window = vbuf[:, pl.ds(pl.multiple_of(half * half_cols, LANES), width)]
    return pltpu.roll(window, width - HALO, 1)[:, : half_cols + LANES]


def sibling_kernel(views, slices, rows, band, scale, tan_hbm, drift_hbm, meas_ref, vol_hbm, out_ref, own_buf,
                   weights_ref, tan_ref, drift_ref, vol_ref, buf, terms, vbuf, table_sem, sem, own_sem):
    _, _, c, _ = coords()
    tiles = out_ref.shape[2] // LANES
    groups = slices // SUB

    def fetch(half, g, t, target, semaphore):
        first = pl.multiple_of((half * (tiles - 1) + t - half) * LANES, LANES)
        return pltpu.make_async_copy(
            meas_ref.at[:, pl.ds(g * SUB, SUB), pl.ds(first, LANES)], target.at[g, t + 1], semaphore
        )

    tables = [
        pltpu.make_async_copy(tan_hbm, tan_ref, table_sem.at[0]),
        pltpu.make_async_copy(drift_hbm, drift_ref, table_sem.at[1]),
    ]
    vol_copy = pltpu.make_async_copy(vol_hbm, vol_ref, table_sem.at[2])
    first = [[fetch(1 - c, g, t, buf, sem.at[g, t]) for t in range(tiles)] for g in range(groups)]
    later = [[fetch(c, g, t, own_buf, own_sem.at[g, t]) for t in range(tiles)] for g in range(groups)]
    for copy in tables + first[0] + first[1] + [vol_copy] + later[0] + later[1]:
        copy.start()
    zero = jnp.zeros((views, SUB, LANES), jnp.float32)
    for g in range(groups):
        for target in (buf, own_buf):
            target[g, 0] = zero
            target[g, tiles + 1] = zero
    for copy in tables:
        copy.wait()
    weights = view_weights(views, rows, band, scale, tan_ref, drift_ref)
    weights_ref[...] = weights.astype(jnp.float32)
    flat = buf.reshape(groups, tiles + 2, views * SUB, LANES)
    load = strip_loader(flat, 1 - c, views, tiles)

    def load_strip(s):
        if s % SUB == 0:
            for copy in first[s // SUB]:
                copy.wait()
        return load(s)

    back_project(views, slices, rows, band, weights, load_strip, out_ref, terms)
    half_cols = out_ref.shape[2] - LANES
    part = vol_ref.shape[1]
    vol_copy.wait()
    out_ref[slices, 0:part] = volume_window(vol_ref, 1 - c, half_cols, vbuf)
    out_ref[slices, part:] = jnp.zeros((rows - part, half_cols + LANES), jnp.float32)
    for group in later:
        for copy in group:
            copy.wait()


def own_kernel(views, slices, rows, band, buf, weights_ref, out_ref, terms):
    _, _, c, _ = coords()
    tiles = out_ref.shape[2] // LANES
    flat = buf.reshape(slices // SUB, tiles + 2, views * SUB, LANES)
    load = strip_loader(flat, c, views, tiles)
    back_project(views, slices, rows, band, weights_ref[...].astype(jnp.bfloat16), load, out_ref, terms)


def plane_pack_kernel(own_ref, got_ref, vol_ref, mine, to_x, to_y, to_xy, acc, both, vbuf):
    slices, rows, half_width = own_ref.shape
    width = mine.shape[2]
    part = vol_ref.shape[1]
    z, x, c, y = coords()
    acc[...] = own_ref[...] + got_ref[0:slices]
    here = volume_window(vol_ref, c, half_width - LANES, vbuf)
    there = got_ref[slices, 0:part]
    both[0:part] = jnp.where(c == 0, here, there)
    both[part:] = jnp.where(c == 0, there, here)
    for out, px, py in ((mine, x, y), (to_x, 1 - x, y), (to_y, x, 1 - y), (to_xy, 1 - x, 1 - y)):
        begin = pl.multiple_of(py * (width - LANES), LANES)
        for pz in range(slices // 4):
            out[2 * pz : 2 * pz + 2] = acc[pl.ds(4 * pz + 2 * px, 2), :, pl.ds(begin, width)]
        if out.shape[0] > slices // 2:
            out[slices // 2] = both[:, pl.ds(begin, width)]


def depth_pack_kernel(mine, got_xy, got_x, got_y, own_pair, to_1, to_2, to_3, vol_pair, acc):
    count, rows, _ = acc.shape
    part = rows // 2
    z, x, c, y = coords()
    acc[...] = (mine[0:count] + got_x[...]) + (got_y[0:count] + got_xy[...])
    for out, pz in (
        (own_pair, z),
        (to_1, jnp.where(z % 2 == 0, z + 1, z - 1)),
        (to_2, jnp.where(z < 2, z + 2, z - 2)),
        (to_3, 3 - z),
    ):
        out[...] = acc[pl.ds(2 * pz, 2)]
    here, there = mine[count], got_y[count]
    upper = jnp.where(y == 0, here, there)
    lower = jnp.where(y == 0, there, here)
    for i in range(2):
        vol_pair[i] = jnp.concatenate([upper[i * part : (i + 1) * part], lower[i * part : (i + 1) * part]], axis=0)


def gram_kernel(rows, band, scale, tan_ref, sec_ref, drift_ref, after_ref, conv_ref, low_ref, high_ref):
    views = tan_ref.shape[1]
    span = 2 * band + 1
    shape = (span * rows, views)
    row = row_iota(shape)
    shift = ((row % rows).astype(jnp.float32) - (rows - 1) / 2.0) * tan_ref[...] - drift_ref[...].astype(jnp.float32)
    hat = jnp.maximum(0.0, 1.0 - jnp.abs(shift - (row // rows - band).astype(jnp.float32)))
    gram = lax.dot_general(
        hat * ((scale / rows) * sec_ref[...]),
        hat,
        (((1,), (1,)), ((), ())),
        precision=lax.Precision.HIGHEST,
        preferred_element_type=jnp.float32,
    )
    edge = band * rows
    low_ref[...] = gram[edge + rows :, edge + rows :]
    high_ref[...] = gram[:edge, :edge]
    width = conv_ref.shape[1] // 2 * 3
    padded = jnp.concatenate([gram, jnp.zeros((span * rows, width - span * rows), jnp.float32)], axis=1)
    total = jnp.zeros((rows, width), jnp.float32)
    for k in range(span):
        total = total + pltpu.roll(padded[k * rows : (k + 1) * rows], rows * (2 * band - k), 1)
    lanes = width // 3
    stacked = jnp.concatenate([total[:, i * lanes : (i + 1) * lanes] for i in range(3)], axis=0)
    stacked = split_rows(stacked)
    conv_ref[...] = jnp.concatenate([stacked, stacked], axis=1)


def normal(volumes, conv, low_ref, high_ref, out, band, is_low, is_high):
    rows, width = volumes[0].shape
    count = len(volumes)
    step = conv.shape[1] // 2 // rows
    parts = conv.shape[0] // 2 // rows
    for s in range(count):
        moved = jnp.concatenate(
            [pltpu.roll(volumes[s], (2 * band - j) % width, 1) for j in range(step)], axis=0
        )
        spread = jnp.dot(conv, split_terms(moved), preferred_element_type=jnp.float32)
        spread = spread[: parts * rows] + spread[parts * rows :]
        total = spread[0:rows]
        for i in range(1, parts):
            total = total + pltpu.roll(spread[i * rows : (i + 1) * rows], width - step * i, 1)
        out[s] = total

    lane = lane_iota((rows, LANES))

    @pl.when(is_low)
    def _():
        tiles = [v[:, :LANES] for v in volumes]
        moved = jnp.concatenate(
            [jnp.concatenate([pltpu.roll(t, LANES - k, 1) for k in range(1, band + 1)], axis=0) for t in tiles], axis=1
        )
        spread = jnp.dot(low_ref[...], moved, precision=lax.Precision.HIGHEST, preferred_element_type=jnp.float32)
        for s in range(count):
            total = jnp.zeros((rows, LANES), jnp.float32)
            for k in range(1, band + 1):
                piece = spread[(k - 1) * rows : k * rows, s * LANES : (s + 1) * LANES]
                piece = jnp.where((lane >= HALO - band) & (lane < HALO), piece, 0.0)
                total = total + pltpu.roll(piece, k, 1)
            out[s, :, 0:LANES] = out[s, :, 0:LANES] - total

    @pl.when(is_high)
    def _():
        tiles = [v[:, width - LANES :] for v in volumes]
        moved = jnp.concatenate(
            [jnp.concatenate([pltpu.roll(t, k, 1) for k in range(band, 0, -1)], axis=0) for t in tiles], axis=1
        )
        spread = jnp.dot(high_ref[...], moved, precision=lax.Precision.HIGHEST, preferred_element_type=jnp.float32)
        for s in range(count):
            total = jnp.zeros((rows, LANES), jnp.float32)
            for k in range(band, 0, -1):
                piece = spread[(band - k) * rows : (band - k + 1) * rows, s * LANES : (s + 1) * LANES]
                piece = jnp.where((lane >= LANES - HALO) & (lane < LANES - HALO + band), piece, 0.0)
                total = total + pltpu.roll(piece, LANES - k, 1)
            out[s, :, width - LANES :] = out[s, :, width - LANES :] - total


def block_place(width, total_cols):
    z, x, c, y = coords()
    block = width - 2 * HALO
    index = c * 2 + y
    return index * block - HALO, index == 0, index == total_cols // block - 1


def first_normal_kernel(band, total_cols, vol_pair, conv_ref, low_ref, high_ref, out, work):
    _, is_low, is_high = block_place(vol_pair.shape[2], total_cols)
    volumes = [vol_pair[i] for i in range(2)]
    normal(volumes, conv_ref[...].astype(jnp.bfloat16), low_ref, high_ref, work, band, is_low, is_high)
    for i in range(2):
        out[i] = volumes[i] - work[i]


def half_pair_kernel(first_ref, own_pair, got_3, got_2, got_1, mine, to_x, to_diag, corr):
    _, x, _, _ = coords()
    corr[...] = (own_pair[...] + got_1[...]) + (got_2[...] + got_3[...])
    half = first_ref[...] + corr[...]
    mine[0:2] = half
    mine[2:4] = corr[...]
    to_x[0:2] = half
    to_x[2] = corr[1 - x]
    to_diag[0:2] = half
    to_diag[2] = corr[x]


def variation_step(half, z_of, first_col, depth, total_cols):
    rows, width = half[0].shape
    col = first_col + lane_iota((rows, width))
    row = row_iota((rows, width))
    inside = (col >= 0) & (col < total_cols - 1)
    units = []
    for w in range(len(half) - 1):
        v = half[w]
        keep = (z_of(w) >= 0) & (z_of(w) < depth - 1)
        dz = jnp.where(keep, half[w + 1] - v, 0.0)
        dr = jnp.where(row < rows - 1, pltpu.roll(v, rows - 1, 0) - v, 0.0)
        dc = jnp.where(inside, pltpu.roll(v, width - 1, 1) - v, 0.0)
        inverse = 1.0 / jnp.sqrt(dz * dz + dr * dr + dc * dc + SMOOTH_EPS * SMOOTH_EPS)
        units.append((dz * inverse, dr * inverse, dc * inverse))
    result = []
    for w in range(1, len(half) - 1):
        uz, ur, uc = units[w]
        div = (uz - units[w - 1][0]) + (ur - pltpu.roll(ur, 1, 0)) + (uc - pltpu.roll(uc, 1, 1))
        result.append(jnp.where((col >= 0) & (col < total_cols), half[w] + TV_STEP * div, 0.0))
    return result


def finish_kernel(
    band, depth, total_cols, mine, got_diag, got_x, conv_ref, low_ref, high_ref, keep_ref, send_ref, work, done
):
    width = mine.shape[2]
    first_col, is_low, is_high = block_place(width, total_cols)
    z, x, c, _ = coords()
    before = [jnp.where(x == 0, got_diag[i], got_x[i]) for i in range(3)]
    after = [jnp.where(x == 0, got_x[i], got_diag[i]) for i in range(3)]
    half = [before[0], before[1], mine[0], mine[1], after[0], after[1]]
    corr = [before[2], mine[2], mine[3], after[2]]
    slice_0 = 4 * z + 2 * x
    volumes = variation_step(half, lambda w: slice_0 - 2 + w, first_col, depth, total_cols)
    normal(volumes, conv_ref[...].astype(jnp.bfloat16), low_ref, high_ref, work, band, is_low, is_high)
    half = [volumes[s] + corr[s] - work[s] for s in range(4)]
    volumes = variation_step(half, lambda w: slice_0 - 1 + w, first_col, depth, total_cols)
    for s in range(2):
        done[s] = pltpu.roll(volumes[s], width - HALO, 1)[:, : width - LANES]
    keep_ref[...] = done[c]
    send_ref[...] = done[1 - c]


def result_pack_kernel(own_ref, got_ref, to_y):
    _, _, c, y = coords()
    part = to_y.shape[1]
    own, got = own_ref[...], got_ref[...]
    to_y[c] = jnp.where(y == 0, own[part:], own[:part])
    to_y[1 - c] = jnp.where(y == 0, got[part:], got[:part])


def result_kernel(own_ref, got_ref, got_y, out):
    _, _, c, y = coords()
    _, part, block = got_y.shape
    own, got = own_ref[...], got_ref[...]
    here = jnp.where(y == 0, own[:part], own[part:])
    there = jnp.where(y == 0, got[:part], got[part:])
    for value, h, q in ((here, c, y), (there, 1 - c, y), (got_y[0], 0, 1 - y), (got_y[1], 1, 1 - y)):
        out[0, :, pl.ds(pl.multiple_of((2 * h + q) * block, LANES), block)] = value


def f32(*shape):
    return jax.ShapeDtypeStruct(shape, jnp.float32)


VMEM_SPEC = pl.BlockSpec(memory_space=pltpu.VMEM)
SMEM_SPEC = pl.BlockSpec(memory_space=pltpu.SMEM)
ANY_SPEC = pl.BlockSpec(memory_space=pl.ANY)
HBM_SPEC = pl.BlockSpec(memory_space=pltpu.HBM)
PARAMS = pltpu.CompilerParams(vmem_limit_bytes=40 * 1024 * 1024)


def in_hbm(value):
    return pltpu.with_memory_space_constraint(value, pltpu.HBM)


def kernel_call(body, outs, in_specs, scratch, name, flops=0, size=0):
    many = isinstance(outs, (list, tuple))
    return pl.pallas_call(
        body,
        out_shape=outs,
        in_specs=in_specs,
        out_specs=[VMEM_SPEC] * len(outs) if many else VMEM_SPEC,
        scratch_shapes=scratch,
        compiler_params=PARAMS,
        name=name,
        cost_estimate=pl.CostEstimate(flops=flops, bytes_accessed=size, transcendentals=0),
    )


def summed_plan(measured, drift, start_volume):
    views, slices, cols = measured.shape
    part = start_volume.shape[1]
    rows = 2 * part
    band = rows // 2 + DMAX + 2
    total_angles = drift.shape[0]
    half_cols = cols // 2
    half_width = half_cols + LANES
    width = cols // 4 + 2 * HALO
    tangent, secant = tan_and_secant(total_angles)
    scale = float(1.0 / np.sum(secant))
    tangent, secant = tangent.astype(np.float32), secant.astype(np.float32)

    tiles = half_width // LANES
    groups = slices // SUB
    window = (groups, tiles + 2, views, SUB, LANES)
    table = (2 * (2 * band // STEP + 1) * rows, 2 * STEP * views)
    terms = pltpu.VMEM((2, 2 * STEP * views, half_width + LANES), jnp.bfloat16)
    vbuf = pltpu.VMEM((part, cols + 2 * LANES), jnp.float32)
    sibling, own_buf, weights = kernel_call(
        functools.partial(sibling_kernel, views, slices, rows, band, scale),
        [f32(slices + 1, rows, half_width), f32(*window), f32(*table)],
        [HBM_SPEC] * 4,
        [
            pltpu.SMEM((total_angles,), jnp.float32),
            pltpu.SMEM((total_angles,), jnp.int32),
            pltpu.VMEM((1, part, cols), jnp.float32),
            pltpu.VMEM(window, jnp.float32),
            terms,
            vbuf,
            pltpu.SemaphoreType.DMA((3,)),
            pltpu.SemaphoreType.DMA((groups, tiles)),
            pltpu.SemaphoreType.DMA((groups, tiles)),
        ],
        "back_project_sibling",
        flops=2 * 10**9,
        size=2**21,
    )(in_hbm(jnp.asarray(tangent)), in_hbm(drift), in_hbm(measured), in_hbm(start_volume))
    got = move(sibling, lambda z, x, c, y: (z, x, 1 - c, y))
    own = kernel_call(
        functools.partial(own_kernel, views, slices, rows, band),
        f32(slices, rows, half_width),
        [VMEM_SPEC] * 2,
        [terms],
        "back_project_own",
        flops=2 * 10**9,
        size=2**21,
    )(own_buf, weights)

    count = slices // 2
    mine, to_x, to_y, to_xy = kernel_call(
        plane_pack_kernel,
        [f32(count + 1, rows, width), f32(count, rows, width), f32(count + 1, rows, width), f32(count, rows, width)],
        [VMEM_SPEC] * 3,
        [pltpu.VMEM((slices, rows, half_width), jnp.float32), pltpu.VMEM((rows, half_width), jnp.float32), vbuf],
        "plane_pack",
    )(own, got, start_volume)
    got_xy = move(to_xy, lambda z, x, c, y: (z, 1 - x, c, 1 - y))
    got_x = move(to_x, lambda z, x, c, y: (z, 1 - x, c, y))
    got_y = move(to_y, lambda z, x, c, y: (z, x, c, 1 - y))

    edge = band * rows
    conv, low, high = kernel_call(
        functools.partial(gram_kernel, rows, band, scale),
        [f32(6 * rows, 2 * LANES), f32(edge, edge), f32(edge, edge)],
        [VMEM_SPEC] * 3 + [ANY_SPEC],
        [],
        "gram",
        flops=10**9,
    )(tangent[None], secant[None], drift[None], mine)

    pair = f32(2, rows, width)
    own_pair, to_1, to_2, to_3, vol_pair = kernel_call(
        depth_pack_kernel,
        [pair] * 5,
        [VMEM_SPEC] * 4,
        [pltpu.VMEM((count, rows, width), jnp.float32)],
        "depth_pack",
    )(mine, got_xy, got_x, got_y)
    got_2 = move(to_2, lambda z, x, c, y: (z ^ 2, x, c, y))
    got_1 = move(to_1, lambda z, x, c, y: (z ^ 1, x, c, y))
    got_3 = move(to_3, lambda z, x, c, y: (z ^ 3, x, c, y))

    first = kernel_call(
        functools.partial(first_normal_kernel, band, cols),
        pair,
        [VMEM_SPEC] * 4,
        [pltpu.VMEM((2, rows, width), jnp.float32)],
        "first_normal",
        flops=10**9,
    )(vol_pair, conv, low, high)

    three = f32(3, rows, width)
    mine, to_x, to_diag = kernel_call(
        half_pair_kernel,
        [f32(4, rows, width), three, three],
        [VMEM_SPEC] * 5,
        [pltpu.VMEM((2, rows, width), jnp.float32)],
        "half_pair",
    )(first, own_pair, got_3, got_2, got_1)
    got_diag = move(to_diag, lambda z, x, c, y: (z + 1, 0, c, y) if x else (z - 1, 1, c, y))
    got_x = move(to_x, lambda z, x, c, y: (z, 1 - x, c, y))

    block = width - 2 * HALO
    quarter = f32(rows, block)
    keep, send = kernel_call(
        functools.partial(finish_kernel, band, slices, cols),
        [quarter, quarter],
        [VMEM_SPEC] * 6,
        [pltpu.VMEM((4, rows, width), jnp.float32), pltpu.VMEM((2, rows, block), jnp.float32)],
        "finish",
    )(mine, got_diag, got_x, conv, low, high)
    swapped = move(send, lambda z, x, c, y: (z, x, 1 - c, y))
    to_y = kernel_call(result_pack_kernel, f32(2, part, block), [VMEM_SPEC] * 2, [], "result_pack")(keep, swapped)
    got_y = move(to_y, lambda z, x, c, y: (z, x, c, 1 - y))
    return kernel_call(result_kernel, f32(1, part, cols), [VMEM_SPEC] * 3, [], "result")(keep, swapped, got_y)


def summed_plan_fits(mesh, measured, start_volume):
    rows = start_volume.shape[1]
    cols = measured.shape[2]
    return (
        ITERS == 2
        and dict(mesh.shape) == {"wide": 16, "grp": 2}
        and measured.shape[1] == start_volume.shape[0] == 16
        and rows == SUB
        and cols % (16 * LANES) == 0
        and measured.shape[0] % 256 == 0
    )


def solution(mesh):
    in_specs = (P(("wide", "grp"), None, None), P(), P("wide", "grp", None))
    out_specs = P("wide", "grp", None)

    def run(measured, drift, start_volume):
        plan = summed_plan if summed_plan_fits(mesh, measured, start_volume) else on_device
        return jax.shard_map(plan, mesh=mesh, in_specs=in_specs, out_specs=out_specs, check_vma=False)(
            measured, drift, start_volume
        )

    return run
```

```python
import functools
from functools import reduce
import math

import jax
import jax.numpy as jnp
import numpy as np
from jax import lax
from jax.experimental import pallas as pl
from jax.experimental.pallas import tpu as pltpu
from jax.sharding import PartitionSpec as P

ITERS = 2
DMAX = 4


TILT_MAX = math.pi / 4
SMOOTH_EPS = 0.05
TV_STEP = 0.1


def with_halo(block, sides, width):
    for axis, dim in sides:
        count = lax.axis_size(axis)
        forward = [(i, i + 1) for i in range(count - 1)]
        backward = [(target, source) for source, target in forward]
        low = lax.ppermute(
            lax.slice_in_dim(block, block.shape[dim] - width, None, axis=dim), axis, forward
        )
        high = lax.ppermute(lax.slice_in_dim(block, 0, width, axis=dim), axis, backward)
        block = jnp.concatenate([low, block, high], axis=dim)
    return block


def geometry(angle_ids, drift_vals, total_angles, rows, band_extent):
    angle_rad = TILT_MAX * (2.0 * angle_ids.astype(jnp.float32) / (total_angles - 1) - 1.0)
    secant = 1.0 / jnp.cos(angle_rad)
    height = jnp.arange(rows, dtype=jnp.float32) - (rows - 1) / 2.0
    offsets = jnp.arange(2 * band_extent + 1, dtype=jnp.float32) - band_extent
    shifts = height[None, :] * jnp.tan(angle_rad)[:, None] - drift_vals.astype(jnp.float32)[:, None]
    weight_factors = secant[:, None, None] * jnp.maximum(
        0.0, 1.0 - jnp.abs(shifts[:, :, None] - offsets[None, None, :])
    )
    return (weight_factors, jnp.cos(angle_rad) / rows)


def secant_sum(total_angles):
    angle_rad = TILT_MAX * (
        2.0 * jnp.arange(total_angles, dtype=jnp.float32) / (total_angles - 1) - 1.0
    )
    return jnp.sum(1.0 / jnp.cos(angle_rad))


def local_geometry(angle_ids, drift, total_angles, rows_all, band_extent):
    matches = angle_ids[:, None] == jnp.arange(total_angles, dtype=jnp.int32)[None, :]
    local_drift = jnp.sum(jnp.where(matches, drift[None, :], 0), axis=1)
    return geometry(angle_ids, local_drift, total_angles, rows_all, band_extent)


def apply_correction(
    row_band_strip, measurement_part, weight_factors, residual_scale, global_scale, band_extent
):
    col_count = row_band_strip.shape[2]
    span = 2 * band_extent + 1
    padded = jnp.pad(row_band_strip, ((0, 0), (0, 0), (band_extent, band_extent)))
    shifted = jnp.stack(
        [padded[:, :, shift_id : shift_id + col_count] for shift_id in range(span)], axis=2
    )
    forward_projected = jnp.einsum(
        "ark,zrku->azu", weight_factors, shifted, precision=lax.Precision.HIGHEST
    )
    residual_error = residual_scale[:, None, None] * (measurement_part - forward_projected)
    spread = jnp.einsum(
        "ark,azu->kzru", weight_factors, residual_error, precision=lax.Precision.HIGHEST
    )
    spread = jnp.pad(spread, ((0, 0), (0, 0), (0, 0), (band_extent, band_extent)))
    pieces = [
        spread[shift_id, :, :, 2 * band_extent - shift_id : 2 * band_extent - shift_id + col_count]
        for shift_id in range(span)
    ]
    return global_scale * reduce(lambda left, right: left + right, pieces)


def divergence(extended, z_first, r_first, zcount, rcount):
    plane_count, height, col_count = extended.shape
    z_index = z_first + jnp.arange(plane_count, dtype=jnp.int32)[:, None, None]
    row_index = r_first + jnp.arange(height, dtype=jnp.int32)[None, :, None]
    col_index = jnp.arange(col_count, dtype=jnp.int32)[None, None, :]
    diff_z = jnp.concatenate([extended[1:] - extended[:-1], jnp.zeros_like(extended[:1])], axis=0)
    diff_z = jnp.where((z_index >= 0) & (z_index < zcount - 1), diff_z, 0.0)
    diff_r = jnp.concatenate(
        [extended[:, 1:] - extended[:, :-1], jnp.zeros_like(extended[:, :1])], axis=1
    )
    diff_r = jnp.where((row_index >= 0) & (row_index < rcount - 1), diff_r, 0.0)
    diff_c = jnp.concatenate(
        [extended[:, :, 1:] - extended[:, :, :-1], jnp.zeros_like(extended[:, :, :1])], axis=2
    )
    diff_c = jnp.where(col_index < col_count - 1, diff_c, 0.0)
    magnitude = jnp.sqrt(
        diff_z * diff_z + diff_r * diff_r + diff_c * diff_c + SMOOTH_EPS * SMOOTH_EPS
    )
    unit_z = diff_z / magnitude
    unit_r = diff_r / magnitude
    unit_c = diff_c / magnitude
    back_c = unit_c - jnp.concatenate([jnp.zeros_like(unit_c[:, :, :1]), unit_c[:, :, :-1]], axis=2)
    return (
        unit_z[1:-1, 1:-1]
        - unit_z[:-2, 1:-1]
        + (unit_r[1:-1, 1:-1] - unit_r[1:-1, :-2])
        + back_c[1:-1, 1:-1]
    )


def on_device(measured, drift, start_volume):
    wide_count = lax.axis_size("wide")
    groups = lax.axis_size("grp")
    slab_count, rows_tile, col_count = start_volume.shape
    rows_all = rows_tile * groups
    band_extent = rows_all // 2 + DMAX + 2
    per_device = measured.shape[0]
    total_angles = per_device * wide_count * groups
    global_scale = 1.0 / secant_sum(total_angles)
    z_first = lax.axis_index("wide") * slab_count - 1
    zcount = slab_count * wide_count
    local_measurement = lax.all_to_all(measured, "wide", split_axis=1, concat_axis=0, tiled=True)
    bin_position = jnp.arange(local_measurement.shape[0], dtype=jnp.int32)
    angle_ids = (
        bin_position // per_device * groups + lax.axis_index("grp")
    ) * per_device + bin_position % per_device
    weight_factors, residual_scale = local_geometry(
        angle_ids, drift, total_angles, rows_all, band_extent
    )
    own_tile = start_volume
    r_first = lax.axis_index("grp") * rows_tile - 1
    for sweep in range(ITERS):
        row_band_strip = lax.all_gather(own_tile, "grp", axis=1, tiled=True)
        volume_update = apply_correction(
            row_band_strip,
            local_measurement,
            weight_factors,
            residual_scale,
            global_scale,
            band_extent,
        )
        own_tile = own_tile + lax.psum_scatter(
            volume_update, "grp", scatter_dimension=1, tiled=True
        )
        extended = with_halo(own_tile, (("wide", 0), ("grp", 1)), 1)
        own_tile = own_tile + TV_STEP * divergence(extended, z_first, r_first, zcount, rows_all)
    return own_tile


LANES = 128
SUB = 8
HALO = 64


def tan_and_secant(total_angles):
    angle = TILT_MAX * (2.0 * np.arange(total_angles) / (total_angles - 1) - 1.0)
    return np.tan(angle), 1.0 / np.cos(angle)


def coords():
    wide, y = lax.axis_index("wide"), lax.axis_index("grp")
    return wide // 4, wide // 2 % 2, wide % 2, y


def move(value, target):
    pairs = []
    for z in range(4):
        for x in range(2):
            for c in range(2):
                for y in range(2):
                    tz, tx, tc, ty = target(z, x, c, y)
                    pairs.append((((z * 2 + x) * 2 + c) * 2 + y, ((tz * 2 + tx) * 2 + tc) * 2 + ty))
    return lax.ppermute(value, ("wide", "grp"), pairs)


def beside(z, x, c, y):
    if (z, x) in ((0, 0), (3, 1)):
        return z, x, 1 - c, y
    return (z + 1, 0, c, y) if x else (z - 1, 1, c, y)


def split_rows(value):
    high = value.astype(jnp.bfloat16).astype(jnp.float32)
    return jnp.concatenate([high, value - high], axis=0)


def left_terms(value):
    high = value.astype(jnp.bfloat16).astype(jnp.float32)
    return jnp.concatenate([high, high, value - high], axis=1)


def split_terms(value):
    high = value.astype(jnp.bfloat16)
    low = (value - high.astype(jnp.float32)).astype(jnp.bfloat16)
    return jnp.concatenate([high, low], axis=0)


def right_terms(value):
    high = value.astype(jnp.bfloat16)
    low = (value - high.astype(jnp.float32)).astype(jnp.bfloat16)
    return jnp.concatenate([high, low, high], axis=0)


def lane_iota(shape):
    return lax.broadcasted_iota(jnp.int32, shape, len(shape) - 1)


def row_iota(shape):
    return lax.broadcasted_iota(jnp.int32, shape, len(shape) - 2)


STEP = 3


def view_weights(views, rows, band, scale, tan_ref, drift_ref):
    z, x, c, y = coords()
    first_view = (((z * 2 + x) * 2 + c) * 2 + y) * views
    parts = 2 * band // STEP + 1
    shape = (parts * rows, STEP * views)
    lane, row = lane_iota(shape), row_iota(shape)
    view_of = lane_iota((1, STEP * views)) % views
    tan_lane = jnp.zeros((1, STEP * views), jnp.float32)
    drift_lane = tan_lane
    for a in range(views):
        tan_lane = jnp.where(view_of == a, tan_ref[first_view + a], tan_lane)
        drift_lane = jnp.where(view_of == a, drift_ref[first_view + a].astype(jnp.float32), drift_lane)
    shift = ((row % rows).astype(jnp.float32) - (rows - 1) / 2.0) * tan_lane - drift_lane
    offset = ((row // rows) * STEP + lane // views - band).astype(jnp.float32)
    weights = (scale / rows) * jnp.maximum(0.0, 1.0 - jnp.abs(shift - offset))
    return left_terms(weights).astype(jnp.bfloat16)


def back_project(views, slices, rows, band, weights, load_strip, out_ref, terms):
    out_cols = out_ref.shape[2]
    width = terms.shape[2]
    parts = 2 * band // STEP + 1

    def prepare(s, buf):
        strip = load_strip(s)
        high = strip.astype(jnp.bfloat16)
        low = (strip - high.astype(jnp.float32)).astype(jnp.bfloat16)
        for j in range(STEP):
            moved = pltpu.roll(high, j, 1) if j else high
            buf[j * views : (j + 1) * views] = moved
            buf[(STEP + j) * views : (STEP + j + 1) * views] = pltpu.roll(low, j, 1) if j else low
            buf[(2 * STEP + j) * views : (2 * STEP + j + 1) * views] = moved

    prepare(0, terms.at[0])
    for s in range(slices):
        if s + 1 < slices:
            prepare(s + 1, terms.at[(s + 1) % 2])
        spread = jnp.dot(weights, terms[s % 2], preferred_element_type=jnp.float32)
        total = None
        for i in range(parts):
            piece = pltpu.roll(spread[i * rows : (i + 1) * rows], width - HALO - band + STEP * i, 1)
            total = piece if total is None else total + piece
        out_ref[s] = total[:, :out_cols]


def strip_loader(buf, half, views, tiles):
    pitch = (tiles + 2) * SUB

    def load(s):
        first = half * SUB + s % SUB
        return jnp.concatenate(
            [buf[s // SUB, pl.ds(first + t * SUB, views, stride=pitch), :] for t in range(tiles + 1)], axis=1
        )

    return load


def volume_window(vol_ref, half, half_cols, vbuf):
    part, cols = vol_ref.shape[1:]
    vbuf[:, 0:LANES] = jnp.zeros((part, LANES), jnp.float32)
    vbuf[:, LANES : LANES + cols] = vol_ref[0]
    vbuf[:, LANES + cols :] = jnp.zeros((part, LANES), jnp.float32)
    width = half_cols + 2 * LANES
    window = vbuf[:, pl.ds(pl.multiple_of(half * half_cols, LANES), width)]
    return pltpu.roll(window, width - HALO, 1)[:, : half_cols + LANES]


def sibling_kernel(views, slices, rows, band, scale, tan_hbm, drift_hbm, meas_hbm, vol_hbm, out_ref, own_buf,
                   weights_ref, tan_ref, drift_ref, vol_ref, buf, terms, vbuf, table_sem, sem):
    _, _, c, _ = coords()
    tiles = out_ref.shape[2] // LANES
    groups = slices // SUB

    def fetch(half, target, g, semaphore):
        return pltpu.make_async_copy(
            meas_hbm.at[:, g, pl.ds(half * (tiles - 2), tiles)], target.at[g, :, 1 : tiles + 1], semaphore
        )

    tables = [
        pltpu.make_async_copy(tan_hbm, tan_ref, table_sem.at[0]),
        pltpu.make_async_copy(drift_hbm, drift_ref, table_sem.at[1]),
    ]
    vol_copy = pltpu.make_async_copy(vol_hbm, vol_ref, table_sem.at[2])
    first = [fetch(1 - c, buf, g, sem.at[0, g]) for g in range(groups)]
    later = [fetch(c, own_buf, g, sem.at[1, g]) for g in range(groups)]
    for copy in tables + first + [vol_copy] + later:
        copy.start()
    zero = jnp.zeros((views, SUB, LANES), jnp.float32)
    for g in range(groups):
        for target in (buf, own_buf):
            target[g, :, 0] = zero
            target[g, :, tiles + 1] = zero
    for copy in tables:
        copy.wait()
    weights = view_weights(views, rows, band, scale, tan_ref, drift_ref)
    weights_ref[...] = weights.astype(jnp.float32)
    load = strip_loader(buf.reshape(groups, views * (tiles + 2) * SUB, LANES), 1 - c, views, tiles)

    def load_strip(s):
        if s % SUB == 0:
            first[s // SUB].wait()
        return load(s)

    back_project(views, slices, rows, band, weights, load_strip, out_ref, terms)
    half_cols = out_ref.shape[2] - LANES
    part = vol_ref.shape[1]
    vol_copy.wait()
    out_ref[slices, 0:part] = volume_window(vol_ref, 1 - c, half_cols, vbuf)
    out_ref[slices, part:] = jnp.zeros((rows - part, half_cols + LANES), jnp.float32)
    for copy in later:
        copy.wait()


def own_kernel(views, slices, rows, band, buf, weights_ref, out_ref, terms):
    _, _, c, _ = coords()
    tiles = out_ref.shape[2] // LANES
    load = strip_loader(buf.reshape(slices // SUB, views * (tiles + 2) * SUB, LANES), c, views, tiles)
    back_project(views, slices, rows, band, weights_ref[...].astype(jnp.bfloat16), load, out_ref, terms)


def plane_pack_kernel(own_ref, got_ref, vol_ref, mine, to_x, to_y, to_xy, acc, both, vbuf):
    slices, rows, half_width = own_ref.shape
    width = mine.shape[2]
    part = vol_ref.shape[1]
    z, x, c, y = coords()
    acc[...] = own_ref[...] + got_ref[0:slices]
    here = volume_window(vol_ref, c, half_width - LANES, vbuf)
    there = got_ref[slices, 0:part]
    both[0:part] = jnp.where(c == 0, here, there)
    both[part:] = jnp.where(c == 0, there, here)
    for out, px, py in ((mine, x, y), (to_x, 1 - x, y), (to_y, x, 1 - y), (to_xy, 1 - x, 1 - y)):
        begin = pl.multiple_of(py * (width - LANES), LANES)
        for pz in range(slices // 4):
            out[2 * pz : 2 * pz + 2] = acc[pl.ds(4 * pz + 2 * px, 2), :, pl.ds(begin, width)]
        if out.shape[0] > slices // 2:
            out[slices // 2] = both[:, pl.ds(begin, width)]


def depth_pack_kernel(mine, got_xy, got_x, got_y, own_pair, to_1, to_2, to_3, vol_pair, acc):
    count, rows, _ = acc.shape
    part = rows // 2
    z, x, c, y = coords()
    acc[...] = (mine[0:count] + got_x[...]) + (got_y[0:count] + got_xy[...])
    for out, pz in (
        (own_pair, z),
        (to_1, jnp.where(z % 2 == 0, z + 1, z - 1)),
        (to_2, jnp.where(z < 2, z + 2, z - 2)),
        (to_3, 3 - z),
    ):
        out[...] = acc[pl.ds(2 * pz, 2)]
    here, there = mine[count], got_y[count]
    upper = jnp.where(y == 0, here, there)
    lower = jnp.where(y == 0, there, here)
    for i in range(2):
        vol_pair[i] = jnp.concatenate([upper[i * part : (i + 1) * part], lower[i * part : (i + 1) * part]], axis=0)


def gram_kernel(rows, band, scale, tan_ref, sec_ref, drift_ref, after_ref, conv_ref, low_ref, high_ref):
    views = tan_ref.shape[1]
    span = 2 * band + 1
    shape = (span * rows, views)
    row = row_iota(shape)
    shift = ((row % rows).astype(jnp.float32) - (rows - 1) / 2.0) * tan_ref[...] - drift_ref[...].astype(jnp.float32)
    hat = jnp.maximum(0.0, 1.0 - jnp.abs(shift - (row // rows - band).astype(jnp.float32)))
    gram = lax.dot_general(
        hat * ((scale / rows) * sec_ref[...]),
        hat,
        (((1,), (1,)), ((), ())),
        precision=lax.Precision.HIGHEST,
        preferred_element_type=jnp.float32,
    )
    edge = band * rows
    low_ref[...] = left_terms(gram[edge + rows :, edge + rows :])
    high_ref[...] = left_terms(gram[:edge, :edge])
    width = conv_ref.shape[1] // 2 * 3
    padded = jnp.concatenate([gram, jnp.zeros((span * rows, width - span * rows), jnp.float32)], axis=1)
    total = jnp.zeros((rows, width), jnp.float32)
    for k in range(span):
        total = total + pltpu.roll(padded[k * rows : (k + 1) * rows], rows * (2 * band - k), 1)
    lanes = width // 3
    stacked = jnp.concatenate([total[:, i * lanes : (i + 1) * lanes] for i in range(3)], axis=0)
    stacked = split_rows(stacked)
    conv_ref[...] = jnp.concatenate([stacked, stacked], axis=1)


def normal(volumes, conv, low_ref, high_ref, out, band, is_low, is_high):
    rows, width = volumes[0].shape
    count = len(volumes)
    step = conv.shape[1] // 2 // rows
    parts = conv.shape[0] // 2 // rows
    for s in range(count):
        moved = jnp.concatenate(
            [pltpu.roll(volumes[s], (2 * band - j) % width, 1) for j in range(step)], axis=0
        )
        spread = jnp.dot(conv, split_terms(moved), preferred_element_type=jnp.float32)
        spread = spread[: parts * rows] + spread[parts * rows :]
        total = spread[0:rows]
        for i in range(1, parts):
            total = total + pltpu.roll(spread[i * rows : (i + 1) * rows], width - step * i, 1)
        out[s] = total

    lane = lane_iota((rows, LANES))

    @pl.when(is_low)
    def _():
        tiles = [v[:, :LANES] for v in volumes]
        moved = jnp.concatenate(
            [jnp.concatenate([pltpu.roll(t, LANES - k, 1) for k in range(1, band + 1)], axis=0) for t in tiles], axis=1
        )
        spread = jnp.dot(low_ref[...].astype(jnp.bfloat16), right_terms(moved), preferred_element_type=jnp.float32)
        for s in range(count):
            total = jnp.zeros((rows, LANES), jnp.float32)
            for k in range(1, band + 1):
                piece = spread[(k - 1) * rows : k * rows, s * LANES : (s + 1) * LANES]
                piece = jnp.where((lane >= HALO - band) & (lane < HALO), piece, 0.0)
                total = total + pltpu.roll(piece, k, 1)
            out[s, :, 0:LANES] = out[s, :, 0:LANES] - total

    @pl.when(is_high)
    def _():
        tiles = [v[:, width - LANES :] for v in volumes]
        moved = jnp.concatenate(
            [jnp.concatenate([pltpu.roll(t, k, 1) for k in range(band, 0, -1)], axis=0) for t in tiles], axis=1
        )
        spread = jnp.dot(high_ref[...].astype(jnp.bfloat16), right_terms(moved), preferred_element_type=jnp.float32)
        for s in range(count):
            total = jnp.zeros((rows, LANES), jnp.float32)
            for k in range(band, 0, -1):
                piece = spread[(band - k) * rows : (band - k + 1) * rows, s * LANES : (s + 1) * LANES]
                piece = jnp.where((lane >= LANES - HALO) & (lane < LANES - HALO + band), piece, 0.0)
                total = total + pltpu.roll(piece, LANES - k, 1)
            out[s, :, width - LANES :] = out[s, :, width - LANES :] - total


def block_place(width, total_cols):
    z, x, c, y = coords()
    block = width - 2 * HALO
    index = c * 2 + y
    return index * block - HALO, index == 0, index == total_cols // block - 1


def first_normal_kernel(band, total_cols, vol_pair, conv_ref, low_ref, high_ref, out, work):
    _, is_low, is_high = block_place(vol_pair.shape[2], total_cols)
    volumes = [vol_pair[i] for i in range(2)]
    normal(volumes, conv_ref[...].astype(jnp.bfloat16), low_ref, high_ref, work, band, is_low, is_high)
    for i in range(2):
        out[i] = volumes[i] - work[i]


def half_pair_kernel(first_ref, own_pair, got_1, got_3, got_2, mine, to_x, to_diag, corr):
    _, x, _, _ = coords()
    corr[...] = (own_pair[...] + got_1[...]) + (got_2[...] + got_3[...])
    half = first_ref[...] + corr[...]
    mine[0:2] = half
    mine[2:4] = corr[...]
    to_x[0:2] = half
    to_x[2] = corr[1 - x]
    to_diag[0:2] = half
    to_diag[2] = corr[x]


def variation_step(half, z_of, first_col, depth, total_cols):
    rows, width = half[0].shape
    col = first_col + lane_iota((rows, width))
    row = row_iota((rows, width))
    inside = (col >= 0) & (col < total_cols - 1)
    units = []
    for w in range(len(half) - 1):
        v = half[w]
        keep = (z_of(w) >= 0) & (z_of(w) < depth - 1)
        dz = jnp.where(keep, half[w + 1] - v, 0.0)
        dr = jnp.where(row < rows - 1, pltpu.roll(v, rows - 1, 0) - v, 0.0)
        dc = jnp.where(inside, pltpu.roll(v, width - 1, 1) - v, 0.0)
        inverse = 1.0 / jnp.sqrt(dz * dz + dr * dr + dc * dc + SMOOTH_EPS * SMOOTH_EPS)
        units.append((dz * inverse, dr * inverse, dc * inverse))
    result = []
    for w in range(1, len(half) - 1):
        uz, ur, uc = units[w]
        div = (uz - units[w - 1][0]) + (ur - pltpu.roll(ur, 1, 0)) + (uc - pltpu.roll(uc, 1, 1))
        result.append(jnp.where((col >= 0) & (col < total_cols), half[w] + TV_STEP * div, 0.0))
    return result


def finish_kernel(
    band, depth, total_cols, mine, got_diag, got_x, conv_ref, low_ref, high_ref, keep_ref, send_ref, work, done
):
    width = mine.shape[2]
    first_col, is_low, is_high = block_place(width, total_cols)
    z, x, c, _ = coords()
    before = [jnp.where(x == 0, got_diag[i], got_x[i]) for i in range(3)]
    after = [jnp.where(x == 0, got_x[i], got_diag[i]) for i in range(3)]
    half = [before[0], before[1], mine[0], mine[1], after[0], after[1]]
    corr = [before[2], mine[2], mine[3], after[2]]
    slice_0 = 4 * z + 2 * x
    volumes = variation_step(half, lambda w: slice_0 - 2 + w, first_col, depth, total_cols)
    normal(volumes, conv_ref[...].astype(jnp.bfloat16), low_ref, high_ref, work, band, is_low, is_high)
    half = [volumes[s] + corr[s] - work[s] for s in range(4)]
    volumes = variation_step(half, lambda w: slice_0 - 1 + w, first_col, depth, total_cols)
    for s in range(2):
        done[s] = pltpu.roll(volumes[s], width - HALO, 1)[:, : width - LANES]
    keep_ref[...] = done[c]
    send_ref[...] = done[1 - c]


def result_pack_kernel(own_ref, got_ref, to_y):
    _, _, c, y = coords()
    part = to_y.shape[1]
    own, got = own_ref[...], got_ref[...]
    to_y[c] = jnp.where(y == 0, own[part:], own[:part])
    to_y[1 - c] = jnp.where(y == 0, got[part:], got[:part])


def result_kernel(own_ref, got_ref, got_y, out):
    _, _, c, y = coords()
    _, part, block = got_y.shape
    own, got = own_ref[...], got_ref[...]
    here = jnp.where(y == 0, own[:part], own[part:])
    there = jnp.where(y == 0, got[:part], got[part:])
    for value, h, q in ((here, c, y), (there, 1 - c, y), (got_y[0], 0, 1 - y), (got_y[1], 1, 1 - y)):
        out[0, :, pl.ds(pl.multiple_of((2 * h + q) * block, LANES), block)] = value


def f32(*shape):
    return jax.ShapeDtypeStruct(shape, jnp.float32)


VMEM_SPEC = pl.BlockSpec(memory_space=pltpu.VMEM)
SMEM_SPEC = pl.BlockSpec(memory_space=pltpu.SMEM)
ANY_SPEC = pl.BlockSpec(memory_space=pl.ANY)
HBM_SPEC = pl.BlockSpec(memory_space=pltpu.HBM)
PARAMS = pltpu.CompilerParams(vmem_limit_bytes=40 * 1024 * 1024)


def in_hbm(value):
    return pltpu.with_memory_space_constraint(value, pltpu.HBM)


def kernel_call(body, outs, in_specs, scratch, name, flops=0, size=0):
    many = isinstance(outs, (list, tuple))
    return pl.pallas_call(
        body,
        out_shape=outs,
        in_specs=in_specs,
        out_specs=[VMEM_SPEC] * len(outs) if many else VMEM_SPEC,
        scratch_shapes=scratch,
        compiler_params=PARAMS,
        name=name,
        cost_estimate=pl.CostEstimate(flops=flops, bytes_accessed=size, transcendentals=0),
    )


def summed_plan(measured, drift, start_volume):
    views, slices, cols = measured.shape
    part = start_volume.shape[1]
    rows = 2 * part
    band = rows // 2 + DMAX + 2
    total_angles = drift.shape[0]
    half_cols = cols // 2
    half_width = half_cols + LANES
    width = cols // 4 + 2 * HALO
    tangent, secant = tan_and_secant(total_angles)
    scale = float(1.0 / np.sum(secant))
    tangent, secant = tangent.astype(np.float32), secant.astype(np.float32)

    tiles = half_width // LANES
    groups = slices // SUB
    window = (groups, views, tiles + 2, SUB, LANES)
    tiled = measured.reshape(views, groups, SUB, cols // LANES, LANES).transpose(0, 1, 3, 2, 4)
    table = ((2 * band // STEP + 1) * rows, 3 * STEP * views)
    terms = pltpu.VMEM((2, 3 * STEP * views, half_width + LANES), jnp.bfloat16)
    vbuf = pltpu.VMEM((part, cols + 2 * LANES), jnp.float32)
    sibling, own_buf, weights = kernel_call(
        functools.partial(sibling_kernel, views, slices, rows, band, scale),
        [f32(slices + 1, rows, half_width), f32(*window), f32(*table)],
        [HBM_SPEC] * 4,
        [
            pltpu.SMEM((total_angles,), jnp.float32),
            pltpu.SMEM((total_angles,), jnp.int32),
            pltpu.VMEM((1, part, cols), jnp.float32),
            pltpu.VMEM(window, jnp.float32),
            terms,
            vbuf,
            pltpu.SemaphoreType.DMA((3,)),
            pltpu.SemaphoreType.DMA((2, groups)),
        ],
        "back_project_sibling",
        flops=2 * 10**9,
        size=2**21,
    )(in_hbm(jnp.asarray(tangent)), in_hbm(drift), in_hbm(tiled), in_hbm(start_volume))
    got = move(sibling, lambda z, x, c, y: (z, x, 1 - c, y))
    own = kernel_call(
        functools.partial(own_kernel, views, slices, rows, band),
        f32(slices, rows, half_width),
        [VMEM_SPEC] * 2,
        [terms],
        "back_project_own",
        flops=2 * 10**9,
        size=2**21,
    )(own_buf, weights)

    count = slices // 2
    mine, to_x, to_y, to_xy = kernel_call(
        plane_pack_kernel,
        [f32(count + 1, rows, width), f32(count, rows, width), f32(count + 1, rows, width), f32(count, rows, width)],
        [VMEM_SPEC] * 3,
        [pltpu.VMEM((slices, rows, half_width), jnp.float32), pltpu.VMEM((rows, half_width), jnp.float32), vbuf],
        "plane_pack",
    )(own, got, start_volume)
    got_xy = move(to_xy, lambda z, x, c, y: (z, 1 - x, c, 1 - y))
    got_x = move(to_x, lambda z, x, c, y: (z, 1 - x, c, y))
    got_y = move(to_y, lambda z, x, c, y: (z, x, c, 1 - y))

    edge = band * rows
    conv, low, high = kernel_call(
        functools.partial(gram_kernel, rows, band, scale),
        [f32(6 * rows, 2 * LANES), f32(edge, 3 * edge), f32(edge, 3 * edge)],
        [VMEM_SPEC] * 3 + [ANY_SPEC],
        [],
        "gram",
        flops=10**9,
    )(tangent[None], secant[None], drift[None], mine)

    pair = f32(2, rows, width)
    own_pair, to_1, to_2, to_3, vol_pair = kernel_call(
        depth_pack_kernel,
        [pair] * 5,
        [VMEM_SPEC] * 4,
        [pltpu.VMEM((count, rows, width), jnp.float32)],
        "depth_pack",
    )(mine, got_xy, got_x, got_y)
    got_2 = move(to_2, lambda z, x, c, y: (z ^ 2, x, c, y))
    got_1 = move(to_1, lambda z, x, c, y: (z ^ 1, x, c, y))
    got_3 = move(to_3, lambda z, x, c, y: (z ^ 3, x, c, y))

    first = kernel_call(
        functools.partial(first_normal_kernel, band, cols),
        pair,
        [VMEM_SPEC] * 4,
        [pltpu.VMEM((2, rows, width), jnp.float32)],
        "first_normal",
        flops=10**9,
    )(vol_pair, conv, low, high)

    three = f32(3, rows, width)
    mine, to_x, to_diag = kernel_call(
        half_pair_kernel,
        [f32(4, rows, width), three, three],
        [VMEM_SPEC] * 5,
        [pltpu.VMEM((2, rows, width), jnp.float32)],
        "half_pair",
    )(first, own_pair, got_1, got_3, got_2)
    got_diag = move(to_diag, beside)
    got_x = move(to_x, lambda z, x, c, y: (z, 1 - x, c, y))

    block = width - 2 * HALO
    quarter = f32(rows, block)
    keep, send = kernel_call(
        functools.partial(finish_kernel, band, slices, cols),
        [quarter, quarter],
        [VMEM_SPEC] * 6,
        [pltpu.VMEM((4, rows, width), jnp.float32), pltpu.VMEM((2, rows, block), jnp.float32)],
        "finish",
    )(mine, got_diag, got_x, conv, low, high)
    swapped = move(send, lambda z, x, c, y: (z, x, 1 - c, y))
    to_y = kernel_call(result_pack_kernel, f32(2, part, block), [VMEM_SPEC] * 2, [], "result_pack")(keep, swapped)
    got_y = move(to_y, lambda z, x, c, y: (z, x, c, 1 - y))
    return kernel_call(result_kernel, f32(1, part, cols), [VMEM_SPEC] * 3, [], "result")(keep, swapped, got_y)


def summed_plan_fits(mesh, measured, start_volume):
    rows = start_volume.shape[1]
    cols = measured.shape[2]
    return (
        ITERS == 2
        and dict(mesh.shape) == {"wide": 16, "grp": 2}
        and measured.shape[1] == start_volume.shape[0] == 16
        and rows == SUB
        and cols % (16 * LANES) == 0
        and measured.shape[0] % 256 == 0
    )


def solution(mesh):
    in_specs = (P(("wide", "grp"), None, None), P(), P("wide", "grp", None))
    out_specs = P("wide", "grp", None)

    def run(measured, drift, start_volume):
        plan = summed_plan if summed_plan_fits(mesh, measured, start_volume) else on_device
        return jax.shard_map(plan, mesh=mesh, in_specs=in_specs, out_specs=out_specs, check_vma=False)(
            measured, drift, start_volume
        )

    return run
```

```python
import functools
from functools import reduce
import math

import jax
import jax.numpy as jnp
import numpy as np
from jax import lax
from jax.experimental import pallas as pl
from jax.experimental.pallas import tpu as pltpu
from jax.sharding import PartitionSpec as P

ITERS = 2
DMAX = 4


TILT_MAX = math.pi / 4
SMOOTH_EPS = 0.05
TV_STEP = 0.1


def with_halo(block, sides, width):
    for axis, dim in sides:
        count = lax.axis_size(axis)
        forward = [(i, i + 1) for i in range(count - 1)]
        backward = [(target, source) for source, target in forward]
        low = lax.ppermute(
            lax.slice_in_dim(block, block.shape[dim] - width, None, axis=dim), axis, forward
        )
        high = lax.ppermute(lax.slice_in_dim(block, 0, width, axis=dim), axis, backward)
        block = jnp.concatenate([low, block, high], axis=dim)
    return block


def geometry(angle_ids, drift_vals, total_angles, rows, band_extent):
    angle_rad = TILT_MAX * (2.0 * angle_ids.astype(jnp.float32) / (total_angles - 1) - 1.0)
    secant = 1.0 / jnp.cos(angle_rad)
    height = jnp.arange(rows, dtype=jnp.float32) - (rows - 1) / 2.0
    offsets = jnp.arange(2 * band_extent + 1, dtype=jnp.float32) - band_extent
    shifts = height[None, :] * jnp.tan(angle_rad)[:, None] - drift_vals.astype(jnp.float32)[:, None]
    weight_factors = secant[:, None, None] * jnp.maximum(
        0.0, 1.0 - jnp.abs(shifts[:, :, None] - offsets[None, None, :])
    )
    return (weight_factors, jnp.cos(angle_rad) / rows)


def secant_sum(total_angles):
    angle_rad = TILT_MAX * (
        2.0 * jnp.arange(total_angles, dtype=jnp.float32) / (total_angles - 1) - 1.0
    )
    return jnp.sum(1.0 / jnp.cos(angle_rad))


def local_geometry(angle_ids, drift, total_angles, rows_all, band_extent):
    matches = angle_ids[:, None] == jnp.arange(total_angles, dtype=jnp.int32)[None, :]
    local_drift = jnp.sum(jnp.where(matches, drift[None, :], 0), axis=1)
    return geometry(angle_ids, local_drift, total_angles, rows_all, band_extent)


def apply_correction(
    row_band_strip, measurement_part, weight_factors, residual_scale, global_scale, band_extent
):
    col_count = row_band_strip.shape[2]
    span = 2 * band_extent + 1
    padded = jnp.pad(row_band_strip, ((0, 0), (0, 0), (band_extent, band_extent)))
    shifted = jnp.stack(
        [padded[:, :, shift_id : shift_id + col_count] for shift_id in range(span)], axis=2
    )
    forward_projected = jnp.einsum(
        "ark,zrku->azu", weight_factors, shifted, precision=lax.Precision.HIGHEST
    )
    residual_error = residual_scale[:, None, None] * (measurement_part - forward_projected)
    spread = jnp.einsum(
        "ark,azu->kzru", weight_factors, residual_error, precision=lax.Precision.HIGHEST
    )
    spread = jnp.pad(spread, ((0, 0), (0, 0), (0, 0), (band_extent, band_extent)))
    pieces = [
        spread[shift_id, :, :, 2 * band_extent - shift_id : 2 * band_extent - shift_id + col_count]
        for shift_id in range(span)
    ]
    return global_scale * reduce(lambda left, right: left + right, pieces)


def divergence(extended, z_first, r_first, zcount, rcount):
    plane_count, height, col_count = extended.shape
    z_index = z_first + jnp.arange(plane_count, dtype=jnp.int32)[:, None, None]
    row_index = r_first + jnp.arange(height, dtype=jnp.int32)[None, :, None]
    col_index = jnp.arange(col_count, dtype=jnp.int32)[None, None, :]
    diff_z = jnp.concatenate([extended[1:] - extended[:-1], jnp.zeros_like(extended[:1])], axis=0)
    diff_z = jnp.where((z_index >= 0) & (z_index < zcount - 1), diff_z, 0.0)
    diff_r = jnp.concatenate(
        [extended[:, 1:] - extended[:, :-1], jnp.zeros_like(extended[:, :1])], axis=1
    )
    diff_r = jnp.where((row_index >= 0) & (row_index < rcount - 1), diff_r, 0.0)
    diff_c = jnp.concatenate(
        [extended[:, :, 1:] - extended[:, :, :-1], jnp.zeros_like(extended[:, :, :1])], axis=2
    )
    diff_c = jnp.where(col_index < col_count - 1, diff_c, 0.0)
    magnitude = jnp.sqrt(
        diff_z * diff_z + diff_r * diff_r + diff_c * diff_c + SMOOTH_EPS * SMOOTH_EPS
    )
    unit_z = diff_z / magnitude
    unit_r = diff_r / magnitude
    unit_c = diff_c / magnitude
    back_c = unit_c - jnp.concatenate([jnp.zeros_like(unit_c[:, :, :1]), unit_c[:, :, :-1]], axis=2)
    return (
        unit_z[1:-1, 1:-1]
        - unit_z[:-2, 1:-1]
        + (unit_r[1:-1, 1:-1] - unit_r[1:-1, :-2])
        + back_c[1:-1, 1:-1]
    )


def on_device(measured, drift, start_volume):
    wide_count = lax.axis_size("wide")
    groups = lax.axis_size("grp")
    slab_count, rows_tile, col_count = start_volume.shape
    rows_all = rows_tile * groups
    band_extent = rows_all // 2 + DMAX + 2
    per_device = measured.shape[0]
    total_angles = per_device * wide_count * groups
    global_scale = 1.0 / secant_sum(total_angles)
    z_first = lax.axis_index("wide") * slab_count - 1
    zcount = slab_count * wide_count
    local_measurement = lax.all_to_all(measured, "wide", split_axis=1, concat_axis=0, tiled=True)
    bin_position = jnp.arange(local_measurement.shape[0], dtype=jnp.int32)
    angle_ids = (
        bin_position // per_device * groups + lax.axis_index("grp")
    ) * per_device + bin_position % per_device
    weight_factors, residual_scale = local_geometry(
        angle_ids, drift, total_angles, rows_all, band_extent
    )
    own_tile = start_volume
    r_first = lax.axis_index("grp") * rows_tile - 1
    for sweep in range(ITERS):
        row_band_strip = lax.all_gather(own_tile, "grp", axis=1, tiled=True)
        volume_update = apply_correction(
            row_band_strip,
            local_measurement,
            weight_factors,
            residual_scale,
            global_scale,
            band_extent,
        )
        own_tile = own_tile + lax.psum_scatter(
            volume_update, "grp", scatter_dimension=1, tiled=True
        )
        extended = with_halo(own_tile, (("wide", 0), ("grp", 1)), 1)
        own_tile = own_tile + TV_STEP * divergence(extended, z_first, r_first, zcount, rows_all)
    return own_tile


LANES = 128
SUB = 8
HALO = 64


def tan_and_secant(total_angles):
    angle = TILT_MAX * (2.0 * np.arange(total_angles) / (total_angles - 1) - 1.0)
    return np.tan(angle), 1.0 / np.cos(angle)


def coords():
    wide, y = lax.axis_index("wide"), lax.axis_index("grp")
    return wide // 4, wide // 2 % 2, wide % 2, y


def move(value, target):
    pairs = []
    for z in range(4):
        for x in range(2):
            for c in range(2):
                for y in range(2):
                    tz, tx, tc, ty = target(z, x, c, y)
                    pairs.append((((z * 2 + x) * 2 + c) * 2 + y, ((tz * 2 + tx) * 2 + tc) * 2 + ty))
    return lax.ppermute(value, ("wide", "grp"), pairs)


def beside(z, x, c, y):
    if (z, x) in ((0, 0), (3, 1)):
        return z, x, 1 - c, y
    return (z + 1, 0, c, y) if x else (z - 1, 1, c, y)


def split_rows(value):
    high = value.astype(jnp.bfloat16).astype(jnp.float32)
    return jnp.concatenate([high, value - high], axis=0)


def left_terms(value):
    high = value.astype(jnp.bfloat16).astype(jnp.float32)
    return jnp.concatenate([high, high, value - high], axis=1)


def split_terms(value):
    high = value.astype(jnp.bfloat16)
    low = (value - high.astype(jnp.float32)).astype(jnp.bfloat16)
    return jnp.concatenate([high, low], axis=0)


def right_terms(value):
    high = value.astype(jnp.bfloat16)
    low = (value - high.astype(jnp.float32)).astype(jnp.bfloat16)
    return jnp.concatenate([high, low, high], axis=0)


def lane_iota(shape):
    return lax.broadcasted_iota(jnp.int32, shape, len(shape) - 1)


def row_iota(shape):
    return lax.broadcasted_iota(jnp.int32, shape, len(shape) - 2)


STEP = 3


def view_weights(views, rows, band, scale, tan_ref, drift_ref):
    z, x, c, y = coords()
    first_view = (((z * 2 + x) * 2 + c) * 2 + y) * views
    parts = 2 * band // STEP + 1
    shape = (parts * rows, STEP * views)
    lane, row = lane_iota(shape), row_iota(shape)
    view_of = lane_iota((1, STEP * views)) % views
    tan_lane = jnp.zeros((1, STEP * views), jnp.float32)
    drift_lane = tan_lane
    for a in range(views):
        tan_lane = jnp.where(view_of == a, tan_ref[first_view + a], tan_lane)
        drift_lane = jnp.where(view_of == a, drift_ref[first_view + a].astype(jnp.float32), drift_lane)
    shift = ((row % rows).astype(jnp.float32) - (rows - 1) / 2.0) * tan_lane - drift_lane
    offset = ((row // rows) * STEP + lane // views - band).astype(jnp.float32)
    weights = (scale / rows) * jnp.maximum(0.0, 1.0 - jnp.abs(shift - offset))
    return left_terms(weights).astype(jnp.bfloat16)


def back_project(views, rows, band, weights, load_strip, out_ref, terms):
    count, _, width = terms.shape
    out_cols = out_ref.shape[2]
    parts = 2 * band // STEP + 1
    for n in range(count):
        strip = load_strip(n)
        high = strip.astype(jnp.bfloat16)
        low = (strip - high.astype(jnp.float32)).astype(jnp.bfloat16)
        for j in range(STEP):
            moved = pltpu.roll(high, j, 1) if j else high
            terms[n, j * views : (j + 1) * views] = moved
            terms[n, (STEP + j) * views : (STEP + j + 1) * views] = pltpu.roll(low, j, 1) if j else low
            terms[n, (2 * STEP + j) * views : (2 * STEP + j + 1) * views] = moved
    for n in range(count):
        spread = jnp.dot(weights, terms[n], preferred_element_type=jnp.float32)
        total = None
        for i in range(parts):
            piece = pltpu.roll(spread[i * rows : (i + 1) * rows], width - HALO - band + STEP * i, 1)
            total = piece if total is None else total + piece
        out_ref[n] = total[:, :out_cols]


def strip_loader(buf, half, parity, views, tiles):
    pitch = (tiles + 2) * SUB

    def load(n):
        first = half * SUB + 4 * (n // 2 % 2) + 2 * parity + n % 2
        return jnp.concatenate(
            [buf[n // 4, pl.ds(first + t * SUB, views, stride=pitch), :] for t in range(tiles + 1)], axis=1
        )

    return load


def volume_window(vol_ref, half, half_cols, vbuf):
    part, cols = vol_ref.shape[1:]
    vbuf[:, 0:LANES] = jnp.zeros((part, LANES), jnp.float32)
    vbuf[:, LANES : LANES + cols] = vol_ref[0]
    vbuf[:, LANES + cols :] = jnp.zeros((part, LANES), jnp.float32)
    width = half_cols + 2 * LANES
    window = vbuf[:, pl.ds(pl.multiple_of(half * half_cols, LANES), width)]
    return pltpu.roll(window, width - HALO, 1)[:, : half_cols + LANES]


def fetch_kernel(views, rows, band, scale, tan_hbm, drift_hbm, meas_hbm, vol_hbm, out_ref, sibling_buf, own_buf,
                 weights_ref, vol_ref, tan_ref, drift_ref, terms, table_sem, sem):
    _, x, c, _ = coords()
    tiles = out_ref.shape[2] // LANES
    groups = sibling_buf.shape[0]

    def fetch(half, target, g, semaphore):
        return pltpu.make_async_copy(
            meas_hbm.at[:, g, pl.ds(half * (tiles - 2), tiles)], target.at[g, :, 1 : tiles + 1], semaphore
        )

    tables = [
        pltpu.make_async_copy(tan_hbm, tan_ref, table_sem.at[0]),
        pltpu.make_async_copy(drift_hbm, drift_ref, table_sem.at[1]),
    ]
    vol_copy = pltpu.make_async_copy(vol_hbm, vol_ref, table_sem.at[2])
    first = [fetch(1 - c, sibling_buf, g, sem.at[0, g]) for g in range(groups)]
    later = [fetch(c, own_buf, g, sem.at[1, g]) for g in range(groups)]
    for copy in tables + first + [vol_copy] + later:
        copy.start()
    zero = jnp.zeros((views, SUB, LANES), jnp.float32)
    for g in range(groups):
        for target in (sibling_buf, own_buf):
            target[g, :, 0] = zero
            target[g, :, tiles + 1] = zero
    for copy in tables:
        copy.wait()
    weights = view_weights(views, rows, band, scale, tan_ref, drift_ref)
    weights_ref[...] = weights.astype(jnp.float32)
    load = strip_loader(flat_rows(sibling_buf), 1 - c, 1 - x, views, tiles)

    def load_strip(n):
        if n % 4 == 0:
            first[n // 4].wait()
        return load(n)

    back_project(views, rows, band, weights, load_strip, out_ref, terms)
    vol_copy.wait()
    for copy in later:
        copy.wait()


def flat_rows(buf):
    groups, views, tiles, sub, lanes = buf.shape
    return buf.reshape(groups, views * tiles * sub, lanes)


def sibling_kernel(views, rows, band, buf, weights_ref, vol_ref, out_ref, terms, vbuf):
    _, x, c, _ = coords()
    tiles = out_ref.shape[2] // LANES
    load = strip_loader(flat_rows(buf), 1 - c, x, views, tiles)
    back_project(views, rows, band, weights_ref[...].astype(jnp.bfloat16), load, out_ref, terms)
    count = terms.shape[0]
    half_cols = out_ref.shape[2] - LANES
    part = vol_ref.shape[1]
    out_ref[count, 0:part] = volume_window(vol_ref, 1 - c, half_cols, vbuf)
    out_ref[count, part:] = jnp.zeros((rows - part, half_cols + LANES), jnp.float32)


def own_kernel(kept, views, rows, band, buf, weights_ref, after_ref, out_ref, terms):
    _, x, c, _ = coords()
    tiles = out_ref.shape[2] // LANES
    load = strip_loader(flat_rows(buf), c, x if kept else 1 - x, views, tiles)
    back_project(views, rows, band, weights_ref[...].astype(jnp.bfloat16), load, out_ref, terms)


def pass_pack_kernel(own_ref, got_ref, to_x, to_xy, acc):
    width = to_x.shape[2]
    _, _, _, y = coords()
    acc[...] = own_ref[...] + got_ref[...]
    for out, py in ((to_x, y), (to_xy, 1 - y)):
        out[...] = acc[:, :, pl.ds(pl.multiple_of(py * (width - LANES), LANES), width)]


def keep_pack_kernel(own_ref, got_ref, vol_ref, mine, to_y, acc, vbuf):
    count, rows, half_width = own_ref.shape
    width = mine.shape[2]
    part = vol_ref.shape[1]
    _, _, c, y = coords()
    acc[0:count] = own_ref[...] + got_ref[0:count]
    here = volume_window(vol_ref, c, half_width - LANES, vbuf)
    there = got_ref[count, 0:part]
    acc[count, 0:part] = jnp.where(c == 0, here, there)
    acc[count, part:] = jnp.where(c == 0, there, here)
    for out, py in ((mine, y), (to_y, 1 - y)):
        out[...] = acc[:, :, pl.ds(pl.multiple_of(py * (width - LANES), LANES), width)]


def depth_pack_kernel(mine, got_xy, got_x, got_y, own_pair, to_1, to_2, to_3, vol_pair, acc):
    count, rows, _ = acc.shape
    part = rows // 2
    z, x, c, y = coords()
    acc[...] = (mine[0:count] + got_x[...]) + (got_y[0:count] + got_xy[...])
    for out, pz in (
        (own_pair, z),
        (to_1, jnp.where(z % 2 == 0, z + 1, z - 1)),
        (to_2, jnp.where(z < 2, z + 2, z - 2)),
        (to_3, 3 - z),
    ):
        out[...] = acc[pl.ds(2 * pz, 2)]
    here, there = mine[count], got_y[count]
    upper = jnp.where(y == 0, here, there)
    lower = jnp.where(y == 0, there, here)
    for i in range(2):
        vol_pair[i] = jnp.concatenate([upper[i * part : (i + 1) * part], lower[i * part : (i + 1) * part]], axis=0)


def gram_kernel(rows, band, scale, tan_ref, sec_ref, drift_ref, after_ref, conv_ref, low_ref, high_ref):
    views = tan_ref.shape[1]
    span = 2 * band + 1
    shape = (span * rows, views)
    row = row_iota(shape)
    shift = ((row % rows).astype(jnp.float32) - (rows - 1) / 2.0) * tan_ref[...] - drift_ref[...].astype(jnp.float32)
    hat = jnp.maximum(0.0, 1.0 - jnp.abs(shift - (row // rows - band).astype(jnp.float32)))
    gram = lax.dot_general(
        hat * ((scale / rows) * sec_ref[...]),
        hat,
        (((1,), (1,)), ((), ())),
        precision=lax.Precision.HIGHEST,
        preferred_element_type=jnp.float32,
    )
    edge = band * rows
    low_ref[...] = left_terms(gram[edge + rows :, edge + rows :])
    high_ref[...] = left_terms(gram[:edge, :edge])
    width = conv_ref.shape[1] // 2 * 3
    padded = jnp.concatenate([gram, jnp.zeros((span * rows, width - span * rows), jnp.float32)], axis=1)
    total = jnp.zeros((rows, width), jnp.float32)
    for k in range(span):
        total = total + pltpu.roll(padded[k * rows : (k + 1) * rows], rows * (2 * band - k), 1)
    lanes = width // 3
    stacked = jnp.concatenate([total[:, i * lanes : (i + 1) * lanes] for i in range(3)], axis=0)
    stacked = split_rows(stacked)
    conv_ref[...] = jnp.concatenate([stacked, stacked], axis=1)


def normal(volumes, conv, low_ref, high_ref, out, band, is_low, is_high):
    rows, width = volumes[0].shape
    count = len(volumes)
    step = conv.shape[1] // 2 // rows
    parts = conv.shape[0] // 2 // rows
    for s in range(count):
        moved = jnp.concatenate(
            [pltpu.roll(volumes[s], (2 * band - j) % width, 1) for j in range(step)], axis=0
        )
        spread = jnp.dot(conv, split_terms(moved), preferred_element_type=jnp.float32)
        spread = spread[: parts * rows] + spread[parts * rows :]
        total = spread[0:rows]
        for i in range(1, parts):
            total = total + pltpu.roll(spread[i * rows : (i + 1) * rows], width - step * i, 1)
        out[s] = total

    lane = lane_iota((rows, LANES))

    @pl.when(is_low)
    def _():
        tiles = [v[:, :LANES] for v in volumes]
        moved = jnp.concatenate(
            [jnp.concatenate([pltpu.roll(t, LANES - k, 1) for k in range(1, band + 1)], axis=0) for t in tiles], axis=1
        )
        spread = jnp.dot(low_ref[...].astype(jnp.bfloat16), right_terms(moved), preferred_element_type=jnp.float32)
        for s in range(count):
            total = jnp.zeros((rows, LANES), jnp.float32)
            for k in range(1, band + 1):
                piece = spread[(k - 1) * rows : k * rows, s * LANES : (s + 1) * LANES]
                piece = jnp.where((lane >= HALO - band) & (lane < HALO), piece, 0.0)
                total = total + pltpu.roll(piece, k, 1)
            out[s, :, 0:LANES] = out[s, :, 0:LANES] - total

    @pl.when(is_high)
    def _():
        tiles = [v[:, width - LANES :] for v in volumes]
        moved = jnp.concatenate(
            [jnp.concatenate([pltpu.roll(t, k, 1) for k in range(band, 0, -1)], axis=0) for t in tiles], axis=1
        )
        spread = jnp.dot(high_ref[...].astype(jnp.bfloat16), right_terms(moved), preferred_element_type=jnp.float32)
        for s in range(count):
            total = jnp.zeros((rows, LANES), jnp.float32)
            for k in range(band, 0, -1):
                piece = spread[(band - k) * rows : (band - k + 1) * rows, s * LANES : (s + 1) * LANES]
                piece = jnp.where((lane >= LANES - HALO) & (lane < LANES - HALO + band), piece, 0.0)
                total = total + pltpu.roll(piece, LANES - k, 1)
            out[s, :, width - LANES :] = out[s, :, width - LANES :] - total


def block_place(width, total_cols):
    z, x, c, y = coords()
    block = width - 2 * HALO
    index = c * 2 + y
    return index * block - HALO, index == 0, index == total_cols // block - 1


def first_normal_kernel(band, total_cols, vol_pair, conv_ref, low_ref, high_ref, out, work):
    _, is_low, is_high = block_place(vol_pair.shape[2], total_cols)
    volumes = [vol_pair[i] for i in range(2)]
    normal(volumes, conv_ref[...].astype(jnp.bfloat16), low_ref, high_ref, work, band, is_low, is_high)
    for i in range(2):
        out[i] = volumes[i] - work[i]


def half_pair_kernel(first_ref, own_pair, got_1, got_3, got_2, mine, to_x, to_diag, corr):
    _, x, _, _ = coords()
    corr[...] = (own_pair[...] + got_1[...]) + (got_2[...] + got_3[...])
    half = first_ref[...] + corr[...]
    mine[0:2] = half
    mine[2:4] = corr[...]
    to_x[0:2] = half
    to_x[2] = corr[1 - x]
    to_diag[0:2] = half
    to_diag[2] = corr[x]


def variation_step(half, z_of, first_col, depth, total_cols):
    rows, width = half[0].shape
    col = first_col + lane_iota((rows, width))
    row = row_iota((rows, width))
    inside = (col >= 0) & (col < total_cols - 1)
    units = []
    for w in range(len(half) - 1):
        v = half[w]
        keep = (z_of(w) >= 0) & (z_of(w) < depth - 1)
        dz = jnp.where(keep, half[w + 1] - v, 0.0)
        dr = jnp.where(row < rows - 1, pltpu.roll(v, rows - 1, 0) - v, 0.0)
        dc = jnp.where(inside, pltpu.roll(v, width - 1, 1) - v, 0.0)
        inverse = 1.0 / jnp.sqrt(dz * dz + dr * dr + dc * dc + SMOOTH_EPS * SMOOTH_EPS)
        units.append((dz * inverse, dr * inverse, dc * inverse))
    result = []
    for w in range(1, len(half) - 1):
        uz, ur, uc = units[w]
        div = (uz - units[w - 1][0]) + (ur - pltpu.roll(ur, 1, 0)) + (uc - pltpu.roll(uc, 1, 1))
        result.append(jnp.where((col >= 0) & (col < total_cols), half[w] + TV_STEP * div, 0.0))
    return result


def finish_kernel(
    band, depth, total_cols, mine, got_diag, got_x, conv_ref, low_ref, high_ref, keep_ref, send_ref, work, done
):
    width = mine.shape[2]
    first_col, is_low, is_high = block_place(width, total_cols)
    z, x, c, _ = coords()
    before = [jnp.where(x == 0, got_diag[i], got_x[i]) for i in range(3)]
    after = [jnp.where(x == 0, got_x[i], got_diag[i]) for i in range(3)]
    half = [before[0], before[1], mine[0], mine[1], after[0], after[1]]
    corr = [before[2], mine[2], mine[3], after[2]]
    slice_0 = 4 * z + 2 * x
    volumes = variation_step(half, lambda w: slice_0 - 2 + w, first_col, depth, total_cols)
    normal(volumes, conv_ref[...].astype(jnp.bfloat16), low_ref, high_ref, work, band, is_low, is_high)
    half = [volumes[s] + corr[s] - work[s] for s in range(4)]
    volumes = variation_step(half, lambda w: slice_0 - 1 + w, first_col, depth, total_cols)
    for s in range(2):
        done[s] = pltpu.roll(volumes[s], width - HALO, 1)[:, : width - LANES]
    keep_ref[...] = done[c]
    send_ref[...] = done[1 - c]


def result_pack_kernel(own_ref, got_ref, to_y):
    _, _, c, y = coords()
    part = to_y.shape[1]
    own, got = own_ref[...], got_ref[...]
    to_y[c] = jnp.where(y == 0, own[part:], own[:part])
    to_y[1 - c] = jnp.where(y == 0, got[part:], got[:part])


def result_kernel(own_ref, got_ref, got_y, out):
    _, _, c, y = coords()
    _, part, block = got_y.shape
    own, got = own_ref[...], got_ref[...]
    here = jnp.where(y == 0, own[:part], own[part:])
    there = jnp.where(y == 0, got[:part], got[part:])
    for value, h, q in ((here, c, y), (there, 1 - c, y), (got_y[0], 0, 1 - y), (got_y[1], 1, 1 - y)):
        out[0, :, pl.ds(pl.multiple_of((2 * h + q) * block, LANES), block)] = value


def f32(*shape):
    return jax.ShapeDtypeStruct(shape, jnp.float32)


VMEM_SPEC = pl.BlockSpec(memory_space=pltpu.VMEM)
SMEM_SPEC = pl.BlockSpec(memory_space=pltpu.SMEM)
ANY_SPEC = pl.BlockSpec(memory_space=pl.ANY)
HBM_SPEC = pl.BlockSpec(memory_space=pltpu.HBM)
PARAMS = pltpu.CompilerParams(vmem_limit_bytes=40 * 1024 * 1024)


def in_hbm(value):
    return pltpu.with_memory_space_constraint(value, pltpu.HBM)


def kernel_call(body, outs, in_specs, scratch, name, flops=0, size=0):
    many = isinstance(outs, (list, tuple))
    return pl.pallas_call(
        body,
        out_shape=outs,
        in_specs=in_specs,
        out_specs=[VMEM_SPEC] * len(outs) if many else VMEM_SPEC,
        scratch_shapes=scratch,
        compiler_params=PARAMS,
        name=name,
        cost_estimate=pl.CostEstimate(flops=flops, bytes_accessed=size, transcendentals=0),
    )


def summed_plan(measured, drift, start_volume):
    views, slices, cols = measured.shape
    part = start_volume.shape[1]
    rows = 2 * part
    band = rows // 2 + DMAX + 2
    total_angles = drift.shape[0]
    half_cols = cols // 2
    half_width = half_cols + LANES
    width = cols // 4 + 2 * HALO
    tangent, secant = tan_and_secant(total_angles)
    scale = float(1.0 / np.sum(secant))
    tangent, secant = tangent.astype(np.float32), secant.astype(np.float32)

    tiles = half_width // LANES
    groups = slices // SUB
    window = (groups, views, tiles + 2, SUB, LANES)
    tiled = measured.reshape(views, groups, SUB, cols // LANES, LANES).transpose(0, 1, 3, 2, 4)
    table = ((2 * band // STEP + 1) * rows, 3 * STEP * views)
    count = slices // 2
    terms = pltpu.VMEM((count, 3 * STEP * views, half_width + LANES), jnp.bfloat16)
    vbuf = pltpu.VMEM((part, cols + 2 * LANES), jnp.float32)
    half_of = f32(count, rows, half_width)
    half_and = f32(count + 1, rows, half_width)
    across = lambda z, x, c, y: (z, x, 1 - c, y)

    pass_sibling, sibling_buf, own_buf, weights, volume = kernel_call(
        functools.partial(fetch_kernel, views, rows, band, scale),
        [half_of, f32(*window), f32(*window), f32(*table), f32(1, part, cols)],
        [HBM_SPEC] * 4,
        [
            pltpu.SMEM((total_angles,), jnp.float32),
            pltpu.SMEM((total_angles,), jnp.int32),
            terms,
            pltpu.SemaphoreType.DMA((3,)),
            pltpu.SemaphoreType.DMA((2, groups)),
        ],
        "pass_sibling",
        flops=10**9,
    )(in_hbm(jnp.asarray(tangent)), in_hbm(drift), in_hbm(tiled), in_hbm(start_volume))
    pass_got = move(pass_sibling, across)
    keep_sibling = kernel_call(
        functools.partial(sibling_kernel, views, rows, band),
        half_and,
        [VMEM_SPEC] * 3,
        [terms, vbuf],
        "keep_sibling",
        flops=10**9,
    )(sibling_buf, weights, volume)
    keep_got = move(keep_sibling, across)

    def own(kept, after):
        return kernel_call(
            functools.partial(own_kernel, kept, views, rows, band),
            half_of,
            [VMEM_SPEC] * 2 + [ANY_SPEC],
            [terms],
            "keep_own" if kept else "pass_own",
            flops=10**9,
        )(own_buf, weights, after)

    message, longer = f32(count, rows, width), f32(count + 1, rows, width)
    to_x, to_xy = kernel_call(
        pass_pack_kernel, [message] * 2, [VMEM_SPEC] * 2, [pltpu.VMEM(half_of.shape, jnp.float32)], "pass_pack"
    )(own(False, keep_sibling), pass_got)
    got_xy = move(to_xy, lambda z, x, c, y: (z, 1 - x, c, 1 - y))
    got_x = move(to_x, lambda z, x, c, y: (z, 1 - x, c, y))
    mine, to_y = kernel_call(
        keep_pack_kernel,
        [longer] * 2,
        [VMEM_SPEC] * 3,
        [pltpu.VMEM(half_and.shape, jnp.float32), vbuf],
        "keep_pack",
    )(own(True, to_xy), keep_got, volume)
    got_y = move(to_y, lambda z, x, c, y: (z, x, c, 1 - y))

    edge = band * rows
    conv, low, high = kernel_call(
        functools.partial(gram_kernel, rows, band, scale),
        [f32(6 * rows, 2 * LANES), f32(edge, 3 * edge), f32(edge, 3 * edge)],
        [VMEM_SPEC] * 3 + [ANY_SPEC],
        [],
        "gram",
    )(tangent[None], secant[None], drift[None], mine)

    pair = f32(2, rows, width)
    own_pair, to_1, to_2, to_3, vol_pair = kernel_call(
        depth_pack_kernel,
        [pair] * 5,
        [VMEM_SPEC] * 4,
        [pltpu.VMEM((count, rows, width), jnp.float32)],
        "depth_pack",
    )(mine, got_xy, got_x, got_y)
    got_2 = move(to_2, lambda z, x, c, y: (z ^ 2, x, c, y))
    got_1 = move(to_1, lambda z, x, c, y: (z ^ 1, x, c, y))
    got_3 = move(to_3, lambda z, x, c, y: (z ^ 3, x, c, y))

    first = kernel_call(
        functools.partial(first_normal_kernel, band, cols),
        pair,
        [VMEM_SPEC] * 4,
        [pltpu.VMEM((2, rows, width), jnp.float32)],
        "first_normal",
        flops=10**9,
    )(vol_pair, conv, low, high)

    three = f32(3, rows, width)
    mine, to_x, to_diag = kernel_call(
        half_pair_kernel,
        [f32(4, rows, width), three, three],
        [VMEM_SPEC] * 5,
        [pltpu.VMEM((2, rows, width), jnp.float32)],
        "half_pair",
    )(first, own_pair, got_1, got_3, got_2)
    got_diag = move(to_diag, beside)
    got_x = move(to_x, lambda z, x, c, y: (z, 1 - x, c, y))

    block = width - 2 * HALO
    quarter = f32(rows, block)
    keep, send = kernel_call(
        functools.partial(finish_kernel, band, slices, cols),
        [quarter, quarter],
        [VMEM_SPEC] * 6,
        [pltpu.VMEM((4, rows, width), jnp.float32), pltpu.VMEM((2, rows, block), jnp.float32)],
        "finish",
    )(mine, got_diag, got_x, conv, low, high)
    swapped = move(send, lambda z, x, c, y: (z, x, 1 - c, y))
    to_y = kernel_call(result_pack_kernel, f32(2, part, block), [VMEM_SPEC] * 2, [], "result_pack")(keep, swapped)
    got_y = move(to_y, lambda z, x, c, y: (z, x, c, 1 - y))
    return kernel_call(result_kernel, f32(1, part, cols), [VMEM_SPEC] * 3, [], "result")(keep, swapped, got_y)


def summed_plan_fits(mesh, measured, start_volume):
    rows = start_volume.shape[1]
    cols = measured.shape[2]
    return (
        ITERS == 2
        and dict(mesh.shape) == {"wide": 16, "grp": 2}
        and measured.shape[1] == start_volume.shape[0] == 16
        and rows == SUB
        and cols % (16 * LANES) == 0
        and measured.shape[0] % 256 == 0
    )


def solution(mesh):
    in_specs = (P(("wide", "grp"), None, None), P(), P("wide", "grp", None))
    out_specs = P("wide", "grp", None)

    def run(measured, drift, start_volume):
        plan = summed_plan if summed_plan_fits(mesh, measured, start_volume) else on_device
        return jax.shard_map(plan, mesh=mesh, in_specs=in_specs, out_specs=out_specs, check_vma=False)(
            measured, drift, start_volume
        )

    return run
```

```python
import functools
from functools import reduce
import math

import jax
import jax.numpy as jnp
import numpy as np
from jax import lax
from jax.experimental import pallas as pl
from jax.experimental.pallas import tpu as pltpu
from jax.sharding import PartitionSpec as P

ITERS = 2
DMAX = 4


TILT_MAX = math.pi / 4
SMOOTH_EPS = 0.05
TV_STEP = 0.1


def with_halo(block, sides, width):
    for axis, dim in sides:
        count = lax.axis_size(axis)
        forward = [(i, i + 1) for i in range(count - 1)]
        backward = [(target, source) for source, target in forward]
        low = lax.ppermute(
            lax.slice_in_dim(block, block.shape[dim] - width, None, axis=dim), axis, forward
        )
        high = lax.ppermute(lax.slice_in_dim(block, 0, width, axis=dim), axis, backward)
        block = jnp.concatenate([low, block, high], axis=dim)
    return block


def geometry(angle_ids, drift_vals, total_angles, rows, band_extent):
    angle_rad = TILT_MAX * (2.0 * angle_ids.astype(jnp.float32) / (total_angles - 1) - 1.0)
    secant = 1.0 / jnp.cos(angle_rad)
    height = jnp.arange(rows, dtype=jnp.float32) - (rows - 1) / 2.0
    offsets = jnp.arange(2 * band_extent + 1, dtype=jnp.float32) - band_extent
    shifts = height[None, :] * jnp.tan(angle_rad)[:, None] - drift_vals.astype(jnp.float32)[:, None]
    weight_factors = secant[:, None, None] * jnp.maximum(
        0.0, 1.0 - jnp.abs(shifts[:, :, None] - offsets[None, None, :])
    )
    return (weight_factors, jnp.cos(angle_rad) / rows)


def secant_sum(total_angles):
    angle_rad = TILT_MAX * (
        2.0 * jnp.arange(total_angles, dtype=jnp.float32) / (total_angles - 1) - 1.0
    )
    return jnp.sum(1.0 / jnp.cos(angle_rad))


def local_geometry(angle_ids, drift, total_angles, rows_all, band_extent):
    matches = angle_ids[:, None] == jnp.arange(total_angles, dtype=jnp.int32)[None, :]
    local_drift = jnp.sum(jnp.where(matches, drift[None, :], 0), axis=1)
    return geometry(angle_ids, local_drift, total_angles, rows_all, band_extent)


def apply_correction(
    row_band_strip, measurement_part, weight_factors, residual_scale, global_scale, band_extent
):
    col_count = row_band_strip.shape[2]
    span = 2 * band_extent + 1
    padded = jnp.pad(row_band_strip, ((0, 0), (0, 0), (band_extent, band_extent)))
    shifted = jnp.stack(
        [padded[:, :, shift_id : shift_id + col_count] for shift_id in range(span)], axis=2
    )
    forward_projected = jnp.einsum(
        "ark,zrku->azu", weight_factors, shifted, precision=lax.Precision.HIGHEST
    )
    residual_error = residual_scale[:, None, None] * (measurement_part - forward_projected)
    spread = jnp.einsum(
        "ark,azu->kzru", weight_factors, residual_error, precision=lax.Precision.HIGHEST
    )
    spread = jnp.pad(spread, ((0, 0), (0, 0), (0, 0), (band_extent, band_extent)))
    pieces = [
        spread[shift_id, :, :, 2 * band_extent - shift_id : 2 * band_extent - shift_id + col_count]
        for shift_id in range(span)
    ]
    return global_scale * reduce(lambda left, right: left + right, pieces)


def divergence(extended, z_first, r_first, zcount, rcount):
    plane_count, height, col_count = extended.shape
    z_index = z_first + jnp.arange(plane_count, dtype=jnp.int32)[:, None, None]
    row_index = r_first + jnp.arange(height, dtype=jnp.int32)[None, :, None]
    col_index = jnp.arange(col_count, dtype=jnp.int32)[None, None, :]
    diff_z = jnp.concatenate([extended[1:] - extended[:-1], jnp.zeros_like(extended[:1])], axis=0)
    diff_z = jnp.where((z_index >= 0) & (z_index < zcount - 1), diff_z, 0.0)
    diff_r = jnp.concatenate(
        [extended[:, 1:] - extended[:, :-1], jnp.zeros_like(extended[:, :1])], axis=1
    )
    diff_r = jnp.where((row_index >= 0) & (row_index < rcount - 1), diff_r, 0.0)
    diff_c = jnp.concatenate(
        [extended[:, :, 1:] - extended[:, :, :-1], jnp.zeros_like(extended[:, :, :1])], axis=2
    )
    diff_c = jnp.where(col_index < col_count - 1, diff_c, 0.0)
    magnitude = jnp.sqrt(
        diff_z * diff_z + diff_r * diff_r + diff_c * diff_c + SMOOTH_EPS * SMOOTH_EPS
    )
    unit_z = diff_z / magnitude
    unit_r = diff_r / magnitude
    unit_c = diff_c / magnitude
    back_c = unit_c - jnp.concatenate([jnp.zeros_like(unit_c[:, :, :1]), unit_c[:, :, :-1]], axis=2)
    return (
        unit_z[1:-1, 1:-1]
        - unit_z[:-2, 1:-1]
        + (unit_r[1:-1, 1:-1] - unit_r[1:-1, :-2])
        + back_c[1:-1, 1:-1]
    )


def on_device(measured, drift, start_volume):
    wide_count = lax.axis_size("wide")
    groups = lax.axis_size("grp")
    slab_count, rows_tile, col_count = start_volume.shape
    rows_all = rows_tile * groups
    band_extent = rows_all // 2 + DMAX + 2
    per_device = measured.shape[0]
    total_angles = per_device * wide_count * groups
    global_scale = 1.0 / secant_sum(total_angles)
    z_first = lax.axis_index("wide") * slab_count - 1
    zcount = slab_count * wide_count
    local_measurement = lax.all_to_all(measured, "wide", split_axis=1, concat_axis=0, tiled=True)
    bin_position = jnp.arange(local_measurement.shape[0], dtype=jnp.int32)
    angle_ids = (
        bin_position // per_device * groups + lax.axis_index("grp")
    ) * per_device + bin_position % per_device
    weight_factors, residual_scale = local_geometry(
        angle_ids, drift, total_angles, rows_all, band_extent
    )
    own_tile = start_volume
    r_first = lax.axis_index("grp") * rows_tile - 1
    for sweep in range(ITERS):
        row_band_strip = lax.all_gather(own_tile, "grp", axis=1, tiled=True)
        volume_update = apply_correction(
            row_band_strip,
            local_measurement,
            weight_factors,
            residual_scale,
            global_scale,
            band_extent,
        )
        own_tile = own_tile + lax.psum_scatter(
            volume_update, "grp", scatter_dimension=1, tiled=True
        )
        extended = with_halo(own_tile, (("wide", 0), ("grp", 1)), 1)
        own_tile = own_tile + TV_STEP * divergence(extended, z_first, r_first, zcount, rows_all)
    return own_tile


LANES = 128
SUB = 8
HALO = 64


def tan_and_secant(total_angles):
    angle = TILT_MAX * (2.0 * np.arange(total_angles) / (total_angles - 1) - 1.0)
    return np.tan(angle), 1.0 / np.cos(angle)


def coords():
    wide, y = lax.axis_index("wide"), lax.axis_index("grp")
    return wide // 4, wide // 2 % 2, wide % 2, y


def move(value, target):
    pairs = []
    for z in range(4):
        for x in range(2):
            for c in range(2):
                for y in range(2):
                    tz, tx, tc, ty = target(z, x, c, y)
                    pairs.append((((z * 2 + x) * 2 + c) * 2 + y, ((tz * 2 + tx) * 2 + tc) * 2 + ty))
    return lax.ppermute(value, ("wide", "grp"), pairs)


def beside(z, x, c, y):
    if (z, x) in ((0, 0), (3, 1)):
        return z, x, 1 - c, y
    return (z + 1, 0, c, y) if x else (z - 1, 1, c, y)


def split_rows(value):
    high = value.astype(jnp.bfloat16).astype(jnp.float32)
    return jnp.concatenate([high, value - high], axis=0)


def left_terms(value):
    high = value.astype(jnp.bfloat16).astype(jnp.float32)
    return jnp.concatenate([high, high, value - high], axis=1)


def split_terms(value):
    high = value.astype(jnp.bfloat16)
    low = (value - high.astype(jnp.float32)).astype(jnp.bfloat16)
    return jnp.concatenate([high, low], axis=0)


def right_terms(value):
    high = value.astype(jnp.bfloat16)
    low = (value - high.astype(jnp.float32)).astype(jnp.bfloat16)
    return jnp.concatenate([high, low, high], axis=0)


def lane_iota(shape):
    return lax.broadcasted_iota(jnp.int32, shape, len(shape) - 1)


def row_iota(shape):
    return lax.broadcasted_iota(jnp.int32, shape, len(shape) - 2)


STEP = 3


def view_weights(views, rows, band, scale, tan_ref, drift_ref):
    z, x, c, y = coords()
    first_view = (((z * 2 + x) * 2 + c) * 2 + y) * views
    parts = 2 * band // STEP + 1
    shape = (parts * rows, STEP * views)
    lane, row = lane_iota(shape), row_iota(shape)
    view_of = lane_iota((1, STEP * views)) % views
    tan_lane = jnp.zeros((1, STEP * views), jnp.float32)
    drift_lane = tan_lane
    for a in range(views):
        tan_lane = jnp.where(view_of == a, tan_ref[first_view + a], tan_lane)
        drift_lane = jnp.where(view_of == a, drift_ref[first_view + a].astype(jnp.float32), drift_lane)
    shift = ((row % rows).astype(jnp.float32) - (rows - 1) / 2.0) * tan_lane - drift_lane
    offset = ((row // rows) * STEP + lane // views - band).astype(jnp.float32)
    weights = (scale / rows) * jnp.maximum(0.0, 1.0 - jnp.abs(shift - offset))
    return left_terms(weights).astype(jnp.bfloat16)


def back_project(views, rows, band, weights, load_strip, out_ref, terms):
    count, _, width = terms.shape
    out_cols = out_ref.shape[2]
    parts = 2 * band // STEP + 1
    for n in range(count):
        strip = load_strip(n)
        high = strip.astype(jnp.bfloat16)
        low = (strip - high.astype(jnp.float32)).astype(jnp.bfloat16)
        for j in range(STEP):
            moved = pltpu.roll(high, j, 1) if j else high
            terms[n, j * views : (j + 1) * views] = moved
            terms[n, (STEP + j) * views : (STEP + j + 1) * views] = pltpu.roll(low, j, 1) if j else low
            terms[n, (2 * STEP + j) * views : (2 * STEP + j + 1) * views] = moved
    for n in range(count):
        spread = jnp.dot(weights, terms[n], preferred_element_type=jnp.float32)
        total = None
        for i in range(parts):
            piece = pltpu.roll(spread[i * rows : (i + 1) * rows], width - HALO - band + STEP * i, 1)
            total = piece if total is None else total + piece
        out_ref[n] = total[:, :out_cols]


def strip_loader(buf, half, parity, views, tiles):
    pitch = (tiles + 2) * SUB

    def load(n):
        first = half * SUB + 4 * (n // 2 % 2) + 2 * parity + n % 2
        return jnp.concatenate(
            [buf[n // 4, pl.ds(first + t * SUB, views, stride=pitch), :] for t in range(tiles + 1)], axis=1
        )

    return load


def volume_window(vol_ref, half, half_cols, vbuf):
    part, cols = vol_ref.shape[1:]
    vbuf[:, 0:LANES] = jnp.zeros((part, LANES), jnp.float32)
    vbuf[:, LANES : LANES + cols] = vol_ref[0]
    vbuf[:, LANES + cols :] = jnp.zeros((part, LANES), jnp.float32)
    width = half_cols + 2 * LANES
    window = vbuf[:, pl.ds(pl.multiple_of(half * half_cols, LANES), width)]
    return pltpu.roll(window, width - HALO, 1)[:, : half_cols + LANES]


def fetch_kernel(views, rows, band, scale, tan_hbm, drift_hbm, meas_hbm, vol_hbm, out_ref, sibling_buf, own_buf,
                 weights_ref, vol_ref, tan_ref, drift_ref, terms, table_sem, sem):
    _, x, c, _ = coords()
    tiles = out_ref.shape[2] // LANES
    groups = sibling_buf.shape[0]

    def fetch(half, target, g, semaphore):
        return pltpu.make_async_copy(
            meas_hbm.at[:, g, pl.ds(half * (tiles - 2), tiles)], target.at[g, :, 1 : tiles + 1], semaphore
        )

    tables = [
        pltpu.make_async_copy(tan_hbm, tan_ref, table_sem.at[0]),
        pltpu.make_async_copy(drift_hbm, drift_ref, table_sem.at[1]),
    ]
    vol_copy = pltpu.make_async_copy(vol_hbm, vol_ref, table_sem.at[2])
    first = [fetch(1 - c, sibling_buf, g, sem.at[0, g]) for g in range(groups)]
    later = [fetch(c, own_buf, g, sem.at[1, g]) for g in range(groups)]
    for copy in tables + first + [vol_copy] + later:
        copy.start()
    zero = jnp.zeros((views, SUB, LANES), jnp.float32)
    for g in range(groups):
        for target in (sibling_buf, own_buf):
            target[g, :, 0] = zero
            target[g, :, tiles + 1] = zero
    for copy in tables:
        copy.wait()
    weights = view_weights(views, rows, band, scale, tan_ref, drift_ref)
    weights_ref[...] = weights.astype(jnp.float32)
    load = strip_loader(flat_rows(sibling_buf), 1 - c, 1 - x, views, tiles)

    def load_strip(n):
        if n % 4 == 0:
            first[n // 4].wait()
        return load(n)

    back_project(views, rows, band, weights, load_strip, out_ref, terms)
    vol_copy.wait()
    for copy in later:
        copy.wait()


def flat_rows(buf):
    groups, views, tiles, sub, lanes = buf.shape
    return buf.reshape(groups, views * tiles * sub, lanes)


def sibling_kernel(views, rows, band, buf, weights_ref, vol_ref, out_ref, terms, vbuf):
    _, x, c, _ = coords()
    tiles = out_ref.shape[2] // LANES
    load = strip_loader(flat_rows(buf), 1 - c, x, views, tiles)
    back_project(views, rows, band, weights_ref[...].astype(jnp.bfloat16), load, out_ref, terms)
    count = terms.shape[0]
    half_cols = out_ref.shape[2] - LANES
    part = vol_ref.shape[1]
    out_ref[count, 0:part] = volume_window(vol_ref, 1 - c, half_cols, vbuf)
    out_ref[count, part:] = jnp.zeros((rows - part, half_cols + LANES), jnp.float32)


def own_kernel(kept, views, rows, band, buf, weights_ref, after_ref, out_ref, terms):
    _, x, c, _ = coords()
    tiles = out_ref.shape[2] // LANES
    load = strip_loader(flat_rows(buf), c, x if kept else 1 - x, views, tiles)
    back_project(views, rows, band, weights_ref[...].astype(jnp.bfloat16), load, out_ref, terms)


def pass_pack_kernel(own_ref, got_ref, to_xy, acc):
    width = to_xy.shape[2]
    _, _, _, y = coords()
    acc[...] = own_ref[...] + got_ref[...]
    to_xy[...] = acc[:, :, pl.ds(pl.multiple_of((1 - y) * (width - LANES), LANES), width)]


def keep_pack_kernel(pass_ref, pass_got, own_ref, got_ref, vol_ref, mine, to_x, to_y, vol_mine, vol_to_y, acc, both, vbuf):
    count, rows, half_width = own_ref.shape
    width = mine.shape[2]
    part = vol_ref.shape[1]
    _, _, c, y = coords()
    acc[...] = own_ref[...] + got_ref[0:count]
    here = volume_window(vol_ref, c, half_width - LANES, vbuf)
    there = got_ref[count, 0:part]
    both[0:part] = jnp.where(c == 0, here, there)
    both[part:] = jnp.where(c == 0, there, here)
    window = pl.ds(pl.multiple_of(y * (width - LANES), LANES), width)
    to_x[...] = pass_ref[:, :, window] + pass_got[:, :, window]
    for out, vol, py in ((mine, vol_mine, y), (to_y, vol_to_y, 1 - y)):
        begin = pl.multiple_of(py * (width - LANES), LANES)
        out[...] = acc[:, :, pl.ds(begin, width)]
        vol[...] = both[:, pl.ds(begin, width)]


def depth_pack_kernel(mine, got_xy, got_x, got_y, own_pair, to_1, to_2, to_3, acc):
    z, _, _, _ = coords()
    acc[...] = (mine[...] + got_x[...]) + (got_y[...] + got_xy[...])
    for out, pz in (
        (own_pair, z),
        (to_1, jnp.where(z % 2 == 0, z + 1, z - 1)),
        (to_2, jnp.where(z < 2, z + 2, z - 2)),
        (to_3, 3 - z),
    ):
        out[...] = acc[pl.ds(2 * pz, 2)]


def gram_kernel(rows, band, scale, tan_ref, sec_ref, drift_ref, after_ref, conv_ref, low_ref, high_ref):
    views = tan_ref.shape[1]
    span = 2 * band + 1
    shape = (span * rows, views)
    row = row_iota(shape)
    shift = ((row % rows).astype(jnp.float32) - (rows - 1) / 2.0) * tan_ref[...] - drift_ref[...].astype(jnp.float32)
    hat = jnp.maximum(0.0, 1.0 - jnp.abs(shift - (row // rows - band).astype(jnp.float32)))
    gram = lax.dot_general(
        hat * ((scale / rows) * sec_ref[...]),
        hat,
        (((1,), (1,)), ((), ())),
        precision=lax.Precision.HIGHEST,
        preferred_element_type=jnp.float32,
    )
    edge = band * rows
    low_ref[...] = left_terms(gram[edge + rows :, edge + rows :])
    high_ref[...] = left_terms(gram[:edge, :edge])
    width = conv_ref.shape[1] // 2 * 3
    padded = jnp.concatenate([gram, jnp.zeros((span * rows, width - span * rows), jnp.float32)], axis=1)
    total = jnp.zeros((rows, width), jnp.float32)
    for k in range(span):
        total = total + pltpu.roll(padded[k * rows : (k + 1) * rows], rows * (2 * band - k), 1)
    lanes = width // 3
    stacked = jnp.concatenate([total[:, i * lanes : (i + 1) * lanes] for i in range(3)], axis=0)
    stacked = split_rows(stacked)
    conv_ref[...] = jnp.concatenate([stacked, stacked], axis=1)


def normal(volumes, conv, low_ref, high_ref, out, band, is_low, is_high):
    rows, width = volumes[0].shape
    count = len(volumes)
    step = conv.shape[1] // 2 // rows
    parts = conv.shape[0] // 2 // rows
    for s in range(count):
        moved = jnp.concatenate(
            [pltpu.roll(volumes[s], (2 * band - j) % width, 1) for j in range(step)], axis=0
        )
        spread = jnp.dot(conv, split_terms(moved), preferred_element_type=jnp.float32)
        spread = spread[: parts * rows] + spread[parts * rows :]
        total = spread[0:rows]
        for i in range(1, parts):
            total = total + pltpu.roll(spread[i * rows : (i + 1) * rows], width - step * i, 1)
        out[s] = total

    lane = lane_iota((rows, LANES))

    @pl.when(is_low)
    def _():
        tiles = [v[:, :LANES] for v in volumes]
        moved = jnp.concatenate(
            [jnp.concatenate([pltpu.roll(t, LANES - k, 1) for k in range(1, band + 1)], axis=0) for t in tiles], axis=1
        )
        spread = jnp.dot(low_ref[...].astype(jnp.bfloat16), right_terms(moved), preferred_element_type=jnp.float32)
        for s in range(count):
            total = jnp.zeros((rows, LANES), jnp.float32)
            for k in range(1, band + 1):
                piece = spread[(k - 1) * rows : k * rows, s * LANES : (s + 1) * LANES]
                piece = jnp.where((lane >= HALO - band) & (lane < HALO), piece, 0.0)
                total = total + pltpu.roll(piece, k, 1)
            out[s, :, 0:LANES] = out[s, :, 0:LANES] - total

    @pl.when(is_high)
    def _():
        tiles = [v[:, width - LANES :] for v in volumes]
        moved = jnp.concatenate(
            [jnp.concatenate([pltpu.roll(t, k, 1) for k in range(band, 0, -1)], axis=0) for t in tiles], axis=1
        )
        spread = jnp.dot(high_ref[...].astype(jnp.bfloat16), right_terms(moved), preferred_element_type=jnp.float32)
        for s in range(count):
            total = jnp.zeros((rows, LANES), jnp.float32)
            for k in range(band, 0, -1):
                piece = spread[(band - k) * rows : (band - k + 1) * rows, s * LANES : (s + 1) * LANES]
                piece = jnp.where((lane >= LANES - HALO) & (lane < LANES - HALO + band), piece, 0.0)
                total = total + pltpu.roll(piece, LANES - k, 1)
            out[s, :, width - LANES :] = out[s, :, width - LANES :] - total


def block_place(width, total_cols):
    z, x, c, y = coords()
    block = width - 2 * HALO
    index = c * 2 + y
    return index * block - HALO, index == 0, index == total_cols // block - 1


def first_normal_kernel(band, total_cols, vol_mine, vol_got, conv_ref, low_ref, high_ref, out, work):
    _, is_low, is_high = block_place(vol_mine.shape[1], total_cols)
    _, _, _, y = coords()
    part = vol_mine.shape[0] // 2
    here, there = vol_mine[...], vol_got[...]
    upper = jnp.where(y == 0, here, there)
    lower = jnp.where(y == 0, there, here)
    volumes = [
        jnp.concatenate([upper[i * part : (i + 1) * part], lower[i * part : (i + 1) * part]], axis=0) for i in range(2)
    ]
    normal(volumes, conv_ref[...].astype(jnp.bfloat16), low_ref, high_ref, work, band, is_low, is_high)
    for i in range(2):
        out[i] = volumes[i] - work[i]


def half_pair_kernel(first_ref, own_pair, got_1, got_3, got_2, mine, to_x, to_diag, corr):
    _, x, _, _ = coords()
    corr[...] = (own_pair[...] + got_1[...]) + (got_2[...] + got_3[...])
    half = first_ref[...] + corr[...]
    mine[0:2] = half
    mine[2:4] = corr[...]
    to_x[0:2] = half
    to_x[2] = corr[1 - x]
    to_diag[0:2] = half
    to_diag[2] = corr[x]


def variation_step(half, z_of, first_col, depth, total_cols):
    rows, width = half[0].shape
    col = first_col + lane_iota((rows, width))
    row = row_iota((rows, width))
    inside = (col >= 0) & (col < total_cols - 1)
    units = []
    for w in range(len(half) - 1):
        v = half[w]
        keep = (z_of(w) >= 0) & (z_of(w) < depth - 1)
        dz = jnp.where(keep, half[w + 1] - v, 0.0)
        dr = jnp.where(row < rows - 1, pltpu.roll(v, rows - 1, 0) - v, 0.0)
        dc = jnp.where(inside, pltpu.roll(v, width - 1, 1) - v, 0.0)
        inverse = 1.0 / jnp.sqrt(dz * dz + dr * dr + dc * dc + SMOOTH_EPS * SMOOTH_EPS)
        units.append((dz * inverse, dr * inverse, dc * inverse))
    result = []
    for w in range(1, len(half) - 1):
        uz, ur, uc = units[w]
        div = (uz - units[w - 1][0]) + (ur - pltpu.roll(ur, 1, 0)) + (uc - pltpu.roll(uc, 1, 1))
        result.append(jnp.where((col >= 0) & (col < total_cols), half[w] + TV_STEP * div, 0.0))
    return result


def finish_kernel(
    band, depth, total_cols, mine, got_diag, got_x, conv_ref, low_ref, high_ref, keep_ref, send_ref, work, done
):
    width = mine.shape[2]
    first_col, is_low, is_high = block_place(width, total_cols)
    z, x, c, _ = coords()
    before = [jnp.where(x == 0, got_diag[i], got_x[i]) for i in range(3)]
    after = [jnp.where(x == 0, got_x[i], got_diag[i]) for i in range(3)]
    half = [before[0], before[1], mine[0], mine[1], after[0], after[1]]
    corr = [before[2], mine[2], mine[3], after[2]]
    slice_0 = 4 * z + 2 * x
    volumes = variation_step(half, lambda w: slice_0 - 2 + w, first_col, depth, total_cols)
    normal(volumes, conv_ref[...].astype(jnp.bfloat16), low_ref, high_ref, work, band, is_low, is_high)
    half = [volumes[s] + corr[s] - work[s] for s in range(4)]
    volumes = variation_step(half, lambda w: slice_0 - 1 + w, first_col, depth, total_cols)
    for s in range(2):
        done[s] = pltpu.roll(volumes[s], width - HALO, 1)[:, : width - LANES]
    keep_ref[...] = done[c]
    send_ref[...] = done[1 - c]


def result_pack_kernel(own_ref, got_ref, to_y):
    _, _, c, y = coords()
    part = to_y.shape[1]
    own, got = own_ref[...], got_ref[...]
    to_y[c] = jnp.where(y == 0, own[part:], own[:part])
    to_y[1 - c] = jnp.where(y == 0, got[part:], got[:part])


def result_kernel(own_ref, got_ref, got_y, out):
    _, _, c, y = coords()
    _, part, block = got_y.shape
    own, got = own_ref[...], got_ref[...]
    here = jnp.where(y == 0, own[:part], own[part:])
    there = jnp.where(y == 0, got[:part], got[part:])
    for value, h, q in ((here, c, y), (there, 1 - c, y), (got_y[0], 0, 1 - y), (got_y[1], 1, 1 - y)):
        out[0, :, pl.ds(pl.multiple_of((2 * h + q) * block, LANES), block)] = value


def f32(*shape):
    return jax.ShapeDtypeStruct(shape, jnp.float32)


VMEM_SPEC = pl.BlockSpec(memory_space=pltpu.VMEM)
SMEM_SPEC = pl.BlockSpec(memory_space=pltpu.SMEM)
ANY_SPEC = pl.BlockSpec(memory_space=pl.ANY)
HBM_SPEC = pl.BlockSpec(memory_space=pltpu.HBM)
PARAMS = pltpu.CompilerParams(vmem_limit_bytes=40 * 1024 * 1024)


def in_hbm(value):
    return pltpu.with_memory_space_constraint(value, pltpu.HBM)


def kernel_call(body, outs, in_specs, scratch, name, flops=0, size=0):
    many = isinstance(outs, (list, tuple))
    return pl.pallas_call(
        body,
        out_shape=outs,
        in_specs=in_specs,
        out_specs=[VMEM_SPEC] * len(outs) if many else VMEM_SPEC,
        scratch_shapes=scratch,
        compiler_params=PARAMS,
        name=name,
        cost_estimate=pl.CostEstimate(flops=flops, bytes_accessed=size, transcendentals=0),
    )


def summed_plan(measured, drift, start_volume):
    views, slices, cols = measured.shape
    part = start_volume.shape[1]
    rows = 2 * part
    band = rows // 2 + DMAX + 2
    total_angles = drift.shape[0]
    half_cols = cols // 2
    half_width = half_cols + LANES
    width = cols // 4 + 2 * HALO
    tangent, secant = tan_and_secant(total_angles)
    scale = float(1.0 / np.sum(secant))
    tangent, secant = tangent.astype(np.float32), secant.astype(np.float32)

    tiles = half_width // LANES
    groups = slices // SUB
    window = (groups, views, tiles + 2, SUB, LANES)
    tiled = measured.reshape(views, groups, SUB, cols // LANES, LANES).transpose(0, 1, 3, 2, 4)
    table = ((2 * band // STEP + 1) * rows, 3 * STEP * views)
    count = slices // 2
    terms = pltpu.VMEM((count, 3 * STEP * views, half_width + LANES), jnp.bfloat16)
    vbuf = pltpu.VMEM((part, cols + 2 * LANES), jnp.float32)
    half_of = f32(count, rows, half_width)
    half_and = f32(count + 1, rows, half_width)
    across = lambda z, x, c, y: (z, x, 1 - c, y)

    pass_sibling, sibling_buf, own_buf, weights, volume = kernel_call(
        functools.partial(fetch_kernel, views, rows, band, scale),
        [half_of, f32(*window), f32(*window), f32(*table), f32(1, part, cols)],
        [HBM_SPEC] * 4,
        [
            pltpu.SMEM((total_angles,), jnp.float32),
            pltpu.SMEM((total_angles,), jnp.int32),
            terms,
            pltpu.SemaphoreType.DMA((3,)),
            pltpu.SemaphoreType.DMA((2, groups)),
        ],
        "pass_sibling",
        flops=10**9,
    )(in_hbm(jnp.asarray(tangent)), in_hbm(drift), in_hbm(tiled), in_hbm(start_volume))
    pass_got = move(pass_sibling, across)
    keep_sibling = kernel_call(
        functools.partial(sibling_kernel, views, rows, band),
        half_and,
        [VMEM_SPEC] * 3,
        [terms, vbuf],
        "keep_sibling",
        flops=10**9,
    )(sibling_buf, weights, volume)
    keep_got = move(keep_sibling, across)

    def own(kept, after):
        return kernel_call(
            functools.partial(own_kernel, kept, views, rows, band),
            half_of,
            [VMEM_SPEC] * 2 + [ANY_SPEC],
            [terms],
            "keep_own" if kept else "pass_own",
            flops=10**9,
        )(own_buf, weights, after)

    message = f32(count, rows, width)
    pass_own = own(False, keep_sibling)
    to_xy = kernel_call(pass_pack_kernel, message, [VMEM_SPEC] * 2, [pltpu.VMEM(half_of.shape, jnp.float32)], "pass_pack")(
        pass_own, pass_got
    )
    got_xy = move(to_xy, lambda z, x, c, y: (z, 1 - x, c, 1 - y))
    mine, to_x, to_y, vol_mine, vol_to_y = kernel_call(
        keep_pack_kernel,
        [message] * 3 + [f32(rows, width)] * 2,
        [VMEM_SPEC] * 5,
        [pltpu.VMEM(half_of.shape, jnp.float32), pltpu.VMEM((rows, half_width), jnp.float32), vbuf],
        "keep_pack",
    )(pass_own, pass_got, own(True, to_xy), keep_got, volume)
    got_x = move(to_x, lambda z, x, c, y: (z, 1 - x, c, y))
    got_y = move(to_y, lambda z, x, c, y: (z, x, c, 1 - y))
    vol_got = move(vol_to_y, lambda z, x, c, y: (z, x, c, 1 - y))

    edge = band * rows
    conv, low, high = kernel_call(
        functools.partial(gram_kernel, rows, band, scale),
        [f32(6 * rows, 2 * LANES), f32(edge, 3 * edge), f32(edge, 3 * edge)],
        [VMEM_SPEC] * 3 + [ANY_SPEC],
        [],
        "gram",
    )(tangent[None], secant[None], drift[None], mine)

    pair = f32(2, rows, width)
    own_pair, to_1, to_2, to_3 = kernel_call(
        depth_pack_kernel,
        [pair] * 4,
        [VMEM_SPEC] * 4,
        [pltpu.VMEM((count, rows, width), jnp.float32)],
        "depth_pack",
    )(mine, got_xy, got_x, got_y)
    got_2 = move(to_2, lambda z, x, c, y: (z ^ 2, x, c, y))
    got_1 = move(to_1, lambda z, x, c, y: (z ^ 1, x, c, y))
    got_3 = move(to_3, lambda z, x, c, y: (z ^ 3, x, c, y))

    first = kernel_call(
        functools.partial(first_normal_kernel, band, cols),
        pair,
        [VMEM_SPEC] * 5,
        [pltpu.VMEM((2, rows, width), jnp.float32)],
        "first_normal",
        flops=10**9,
    )(vol_mine, vol_got, conv, low, high)

    three = f32(3, rows, width)
    mine, to_x, to_diag = kernel_call(
        half_pair_kernel,
        [f32(4, rows, width), three, three],
        [VMEM_SPEC] * 5,
        [pltpu.VMEM((2, rows, width), jnp.float32)],
        "half_pair",
    )(first, own_pair, got_1, got_3, got_2)
    got_diag = move(to_diag, beside)
    got_x = move(to_x, lambda z, x, c, y: (z, 1 - x, c, y))

    block = width - 2 * HALO
    quarter = f32(rows, block)
    keep, send = kernel_call(
        functools.partial(finish_kernel, band, slices, cols),
        [quarter, quarter],
        [VMEM_SPEC] * 6,
        [pltpu.VMEM((4, rows, width), jnp.float32), pltpu.VMEM((2, rows, block), jnp.float32)],
        "finish",
    )(mine, got_diag, got_x, conv, low, high)
    swapped = move(send, lambda z, x, c, y: (z, x, 1 - c, y))
    to_y = kernel_call(result_pack_kernel, f32(2, part, block), [VMEM_SPEC] * 2, [], "result_pack")(keep, swapped)
    got_y = move(to_y, lambda z, x, c, y: (z, x, c, 1 - y))
    return kernel_call(result_kernel, f32(1, part, cols), [VMEM_SPEC] * 3, [], "result")(keep, swapped, got_y)


def summed_plan_fits(mesh, measured, start_volume):
    rows = start_volume.shape[1]
    cols = measured.shape[2]
    return (
        ITERS == 2
        and dict(mesh.shape) == {"wide": 16, "grp": 2}
        and measured.shape[1] == start_volume.shape[0] == 16
        and rows == SUB
        and cols % (16 * LANES) == 0
        and measured.shape[0] % 256 == 0
    )


def solution(mesh):
    in_specs = (P(("wide", "grp"), None, None), P(), P("wide", "grp", None))
    out_specs = P("wide", "grp", None)

    def run(measured, drift, start_volume):
        plan = summed_plan if summed_plan_fits(mesh, measured, start_volume) else on_device
        return jax.shard_map(plan, mesh=mesh, in_specs=in_specs, out_specs=out_specs, check_vma=False)(
            measured, drift, start_volume
        )

    return run
```

```python
import functools
from functools import reduce
import math

import jax
import jax.numpy as jnp
import numpy as np
from jax import lax
from jax.experimental import pallas as pl
from jax.experimental.pallas import tpu as pltpu
from jax.sharding import PartitionSpec as P

ITERS = 2
DMAX = 4


TILT_MAX = math.pi / 4
SMOOTH_EPS = 0.05
TV_STEP = 0.1


def with_halo(block, sides, width):
    for axis, dim in sides:
        count = lax.axis_size(axis)
        forward = [(i, i + 1) for i in range(count - 1)]
        backward = [(target, source) for source, target in forward]
        low = lax.ppermute(
            lax.slice_in_dim(block, block.shape[dim] - width, None, axis=dim), axis, forward
        )
        high = lax.ppermute(lax.slice_in_dim(block, 0, width, axis=dim), axis, backward)
        block = jnp.concatenate([low, block, high], axis=dim)
    return block


def geometry(angle_ids, drift_vals, total_angles, rows, band_extent):
    angle_rad = TILT_MAX * (2.0 * angle_ids.astype(jnp.float32) / (total_angles - 1) - 1.0)
    secant = 1.0 / jnp.cos(angle_rad)
    height = jnp.arange(rows, dtype=jnp.float32) - (rows - 1) / 2.0
    offsets = jnp.arange(2 * band_extent + 1, dtype=jnp.float32) - band_extent
    shifts = height[None, :] * jnp.tan(angle_rad)[:, None] - drift_vals.astype(jnp.float32)[:, None]
    weight_factors = secant[:, None, None] * jnp.maximum(
        0.0, 1.0 - jnp.abs(shifts[:, :, None] - offsets[None, None, :])
    )
    return (weight_factors, jnp.cos(angle_rad) / rows)


def secant_sum(total_angles):
    angle_rad = TILT_MAX * (
        2.0 * jnp.arange(total_angles, dtype=jnp.float32) / (total_angles - 1) - 1.0
    )
    return jnp.sum(1.0 / jnp.cos(angle_rad))


def local_geometry(angle_ids, drift, total_angles, rows_all, band_extent):
    matches = angle_ids[:, None] == jnp.arange(total_angles, dtype=jnp.int32)[None, :]
    local_drift = jnp.sum(jnp.where(matches, drift[None, :], 0), axis=1)
    return geometry(angle_ids, local_drift, total_angles, rows_all, band_extent)


def apply_correction(
    row_band_strip, measurement_part, weight_factors, residual_scale, global_scale, band_extent
):
    col_count = row_band_strip.shape[2]
    span = 2 * band_extent + 1
    padded = jnp.pad(row_band_strip, ((0, 0), (0, 0), (band_extent, band_extent)))
    shifted = jnp.stack(
        [padded[:, :, shift_id : shift_id + col_count] for shift_id in range(span)], axis=2
    )
    forward_projected = jnp.einsum(
        "ark,zrku->azu", weight_factors, shifted, precision=lax.Precision.HIGHEST
    )
    residual_error = residual_scale[:, None, None] * (measurement_part - forward_projected)
    spread = jnp.einsum(
        "ark,azu->kzru", weight_factors, residual_error, precision=lax.Precision.HIGHEST
    )
    spread = jnp.pad(spread, ((0, 0), (0, 0), (0, 0), (band_extent, band_extent)))
    pieces = [
        spread[shift_id, :, :, 2 * band_extent - shift_id : 2 * band_extent - shift_id + col_count]
        for shift_id in range(span)
    ]
    return global_scale * reduce(lambda left, right: left + right, pieces)


def divergence(extended, z_first, r_first, zcount, rcount):
    plane_count, height, col_count = extended.shape
    z_index = z_first + jnp.arange(plane_count, dtype=jnp.int32)[:, None, None]
    row_index = r_first + jnp.arange(height, dtype=jnp.int32)[None, :, None]
    col_index = jnp.arange(col_count, dtype=jnp.int32)[None, None, :]
    diff_z = jnp.concatenate([extended[1:] - extended[:-1], jnp.zeros_like(extended[:1])], axis=0)
    diff_z = jnp.where((z_index >= 0) & (z_index < zcount - 1), diff_z, 0.0)
    diff_r = jnp.concatenate(
        [extended[:, 1:] - extended[:, :-1], jnp.zeros_like(extended[:, :1])], axis=1
    )
    diff_r = jnp.where((row_index >= 0) & (row_index < rcount - 1), diff_r, 0.0)
    diff_c = jnp.concatenate(
        [extended[:, :, 1:] - extended[:, :, :-1], jnp.zeros_like(extended[:, :, :1])], axis=2
    )
    diff_c = jnp.where(col_index < col_count - 1, diff_c, 0.0)
    magnitude = jnp.sqrt(
        diff_z * diff_z + diff_r * diff_r + diff_c * diff_c + SMOOTH_EPS * SMOOTH_EPS
    )
    unit_z = diff_z / magnitude
    unit_r = diff_r / magnitude
    unit_c = diff_c / magnitude
    back_c = unit_c - jnp.concatenate([jnp.zeros_like(unit_c[:, :, :1]), unit_c[:, :, :-1]], axis=2)
    return (
        unit_z[1:-1, 1:-1]
        - unit_z[:-2, 1:-1]
        + (unit_r[1:-1, 1:-1] - unit_r[1:-1, :-2])
        + back_c[1:-1, 1:-1]
    )


def on_device(measured, drift, start_volume):
    wide_count = lax.axis_size("wide")
    groups = lax.axis_size("grp")
    slab_count, rows_tile, col_count = start_volume.shape
    rows_all = rows_tile * groups
    band_extent = rows_all // 2 + DMAX + 2
    per_device = measured.shape[0]
    total_angles = per_device * wide_count * groups
    global_scale = 1.0 / secant_sum(total_angles)
    z_first = lax.axis_index("wide") * slab_count - 1
    zcount = slab_count * wide_count
    local_measurement = lax.all_to_all(measured, "wide", split_axis=1, concat_axis=0, tiled=True)
    bin_position = jnp.arange(local_measurement.shape[0], dtype=jnp.int32)
    angle_ids = (
        bin_position // per_device * groups + lax.axis_index("grp")
    ) * per_device + bin_position % per_device
    weight_factors, residual_scale = local_geometry(
        angle_ids, drift, total_angles, rows_all, band_extent
    )
    own_tile = start_volume
    r_first = lax.axis_index("grp") * rows_tile - 1
    for sweep in range(ITERS):
        row_band_strip = lax.all_gather(own_tile, "grp", axis=1, tiled=True)
        volume_update = apply_correction(
            row_band_strip,
            local_measurement,
            weight_factors,
            residual_scale,
            global_scale,
            band_extent,
        )
        own_tile = own_tile + lax.psum_scatter(
            volume_update, "grp", scatter_dimension=1, tiled=True
        )
        extended = with_halo(own_tile, (("wide", 0), ("grp", 1)), 1)
        own_tile = own_tile + TV_STEP * divergence(extended, z_first, r_first, zcount, rows_all)
    return own_tile


LANES = 128
SUB = 8
HALO = 64


def tan_and_secant(total_angles):
    angle = TILT_MAX * (2.0 * np.arange(total_angles) / (total_angles - 1) - 1.0)
    return np.tan(angle), 1.0 / np.cos(angle)


def coords():
    wide, y = lax.axis_index("wide"), lax.axis_index("grp")
    return wide // 4, wide // 2 % 2, wide % 2, y


def move(value, target):
    pairs = []
    for z in range(4):
        for x in range(2):
            for c in range(2):
                for y in range(2):
                    tz, tx, tc, ty = target(z, x, c, y)
                    pairs.append((((z * 2 + x) * 2 + c) * 2 + y, ((tz * 2 + tx) * 2 + tc) * 2 + ty))
    return lax.ppermute(value, ("wide", "grp"), pairs)


def beside(z, x, c, y):
    if (z, x) in ((0, 0), (3, 1)):
        return z, x, 1 - c, y
    return (z + 1, 0, c, y) if x else (z - 1, 1, c, y)


def split_rows(value):
    high = value.astype(jnp.bfloat16).astype(jnp.float32)
    return jnp.concatenate([high, value - high], axis=0)


def left_terms(value):
    high = value.astype(jnp.bfloat16).astype(jnp.float32)
    return jnp.concatenate([high, high, value - high], axis=1)


def split_terms(value):
    high = value.astype(jnp.bfloat16)
    low = (value - high.astype(jnp.float32)).astype(jnp.bfloat16)
    return jnp.concatenate([high, low], axis=0)


def right_terms(value):
    high = value.astype(jnp.bfloat16)
    low = (value - high.astype(jnp.float32)).astype(jnp.bfloat16)
    return jnp.concatenate([high, low, high], axis=0)


def lane_iota(shape):
    return lax.broadcasted_iota(jnp.int32, shape, len(shape) - 1)


def row_iota(shape):
    return lax.broadcasted_iota(jnp.int32, shape, len(shape) - 2)


STEP = 3


def view_weights(views, rows, band, scale, tan_ref, drift_ref):
    z, x, c, y = coords()
    first_view = (((z * 2 + x) * 2 + c) * 2 + y) * views
    parts = 2 * band // STEP + 1
    shape = (parts * rows, STEP * views)
    lane, row = lane_iota(shape), row_iota(shape)
    view_of = lane_iota((1, STEP * views)) % views
    tan_lane = jnp.zeros((1, STEP * views), jnp.float32)
    drift_lane = tan_lane
    for a in range(views):
        tan_lane = jnp.where(view_of == a, tan_ref[first_view + a], tan_lane)
        drift_lane = jnp.where(view_of == a, drift_ref[first_view + a].astype(jnp.float32), drift_lane)
    shift = ((row % rows).astype(jnp.float32) - (rows - 1) / 2.0) * tan_lane - drift_lane
    offset = ((row // rows) * STEP + lane // views - band).astype(jnp.float32)
    weights = (scale / rows) * jnp.maximum(0.0, 1.0 - jnp.abs(shift - offset))
    return left_terms(weights).astype(jnp.bfloat16)


def back_project(views, rows, band, weights, load_strip, out_ref, terms):
    count, _, width = terms.shape
    out_cols = out_ref.shape[2]
    parts = 2 * band // STEP + 1
    for n in range(count):
        strip = load_strip(n)
        high = strip.astype(jnp.bfloat16)
        low = (strip - high.astype(jnp.float32)).astype(jnp.bfloat16)
        for j in range(STEP):
            moved = pltpu.roll(high, j, 1) if j else high
            terms[n, j * views : (j + 1) * views] = moved
            terms[n, (STEP + j) * views : (STEP + j + 1) * views] = pltpu.roll(low, j, 1) if j else low
            terms[n, (2 * STEP + j) * views : (2 * STEP + j + 1) * views] = moved
    for n in range(count):
        spread = jnp.dot(weights, terms[n], preferred_element_type=jnp.float32)
        total = None
        for i in range(parts):
            piece = pltpu.roll(spread[i * rows : (i + 1) * rows], width - HALO - band + STEP * i, 1)
            total = piece if total is None else total + piece
        out_ref[n] = total[:, :out_cols]


def depth_partner(z, bits):
    return {0: z, 1: z + 1 - 2 * (z % 2), 2: (z + 2) % 4, 3: 3 - z}[bits]


def slice_place(half, kept, n):
    z, x, _, _ = coords()
    parity = x if kept else 1 - x
    four = depth_partner(z, (1, 0)[n // 4] if kept else (2, 3)[n // 4])
    group = jnp.where(half == 0, n // 4, four // 2)
    place = jnp.where(half == 0, 4 * (n // 2 % 2) + 2 * parity + n % 2, 4 * (four % 2) + n % 4)
    return group, place


def strip_loader(buf, half, kept, views, tiles):
    pitch = (tiles + 2) * SUB

    def load(n):
        group, place = slice_place(half, kept, n)
        first = half * SUB + place
        return jnp.concatenate(
            [buf[group, pl.ds(first + t * SUB, views, stride=pitch), :] for t in range(tiles + 1)], axis=1
        )

    return load


def volume_window(vol_ref, half, half_cols, vbuf):
    part, cols = vol_ref.shape[1:]
    vbuf[:, 0:LANES] = jnp.zeros((part, LANES), jnp.float32)
    vbuf[:, LANES : LANES + cols] = vol_ref[0]
    vbuf[:, LANES + cols :] = jnp.zeros((part, LANES), jnp.float32)
    width = half_cols + 2 * LANES
    window = vbuf[:, pl.ds(pl.multiple_of(half * half_cols, LANES), width)]
    return pltpu.roll(window, width - HALO, 1)[:, : half_cols + LANES]


def fetch_kernel(views, rows, band, scale, tan_hbm, drift_hbm, meas_hbm, vol_hbm, out_ref, sibling_buf, own_buf,
                 weights_ref, vol_ref, tan_ref, drift_ref, terms, table_sem, sem):
    _, _, c, _ = coords()
    tiles = out_ref.shape[2] // LANES
    groups = sibling_buf.shape[0]

    def fetch(half, target, g, semaphore):
        return pltpu.make_async_copy(
            meas_hbm.at[:, g, pl.ds(half * (tiles - 2), tiles)], target.at[g, :, 1 : tiles + 1], semaphore
        )

    tables = [
        pltpu.make_async_copy(tan_hbm, tan_ref, table_sem.at[0]),
        pltpu.make_async_copy(drift_hbm, drift_ref, table_sem.at[1]),
    ]
    vol_copy = pltpu.make_async_copy(vol_hbm, vol_ref, table_sem.at[2])
    first = [fetch(1 - c, sibling_buf, g, sem.at[0, g]) for g in range(groups)]
    later = [fetch(c, own_buf, g, sem.at[1, g]) for g in range(groups)]
    for copy in tables + first + [vol_copy] + later:
        copy.start()
    zero = jnp.zeros((views, SUB, LANES), jnp.float32)
    for g in range(groups):
        for target in (sibling_buf, own_buf):
            target[g, :, 0] = zero
            target[g, :, tiles + 1] = zero
    for copy in tables:
        copy.wait()
    weights = view_weights(views, rows, band, scale, tan_ref, drift_ref)
    weights_ref[...] = weights.astype(jnp.float32)
    load = strip_loader(flat_rows(sibling_buf), 1 - c, False, views, tiles)

    for copy in first:
        copy.wait()
    back_project(views, rows, band, weights, load, out_ref, terms)
    vol_copy.wait()
    for copy in later:
        copy.wait()


def flat_rows(buf):
    groups, views, tiles, sub, lanes = buf.shape
    return buf.reshape(groups, views * tiles * sub, lanes)


def sibling_kernel(views, rows, band, buf, weights_ref, vol_ref, out_ref, terms, vbuf):
    _, _, c, _ = coords()
    tiles = out_ref.shape[2] // LANES
    load = strip_loader(flat_rows(buf), 1 - c, True, views, tiles)
    back_project(views, rows, band, weights_ref[...].astype(jnp.bfloat16), load, out_ref, terms)
    count = terms.shape[0]
    half_cols = out_ref.shape[2] - LANES
    part = vol_ref.shape[1]
    out_ref[count, 0:part] = volume_window(vol_ref, 1 - c, half_cols, vbuf)
    out_ref[count, part:] = jnp.zeros((rows - part, half_cols + LANES), jnp.float32)


def own_kernel(kept, views, rows, band, buf, weights_ref, after_ref, out_ref, terms):
    _, _, c, _ = coords()
    tiles = out_ref.shape[2] // LANES
    load = strip_loader(flat_rows(buf), c, kept, views, tiles)
    back_project(views, rows, band, weights_ref[...].astype(jnp.bfloat16), load, out_ref, terms)


def put_quarter(out, acc, py, tiles):
    for n in range(acc.shape[0]):
        for t in range(tiles):
            out[n * tiles + t] = acc[n, :, pl.ds(pl.multiple_of(((tiles - 1) * py + t) * LANES, LANES), LANES)]


def put_four(out, acc, first):
    tiles = acc.shape[2] // LANES
    for n in range(4):
        for t in range(tiles):
            out[n * tiles + t] = acc[first + n, :, t * LANES : (t + 1) * LANES]
    for t in range(4 * tiles, out.shape[0]):
        out[t] = jnp.zeros(out.shape[1:], jnp.float32)


def pass_pack_kernel(own_ref, got_ref, send, acc):
    _, _, c, y = coords()
    acc[...] = own_ref[...] + got_ref[...]

    @pl.when(c == 0)
    def _():
        put_quarter(send, acc, 1 - y, send.shape[0] // acc.shape[0])

    @pl.when(c == 1)
    def _():
        put_four(send, acc, 0)


def keep_pack_kernel(pass_ref, pass_got, own_ref, got_ref, vol_ref, mine, send_2, send_3, vol_mine, vol_to_y,
                     passed, acc, both, vbuf):
    count, rows, half_width = own_ref.shape
    tiles = mine.shape[0] // count
    part = vol_ref.shape[1]
    _, _, c, y = coords()
    passed[...] = pass_ref[...] + pass_got[...]
    acc[...] = own_ref[...] + got_ref[0:count]

    @pl.when(c == 0)
    def _():
        put_quarter(send_2, passed, y, tiles)
        put_quarter(send_3, acc, 1 - y, tiles)
        put_quarter(mine, acc, y, tiles)

    @pl.when(c == 1)
    def _():
        put_four(send_2, passed, 4)
        put_four(send_3, acc, 0)
        put_four(mine, acc, 4)

    here = volume_window(vol_ref, c, half_width - LANES, vbuf)
    there = got_ref[count, 0:part]
    both[0:part] = jnp.where(c == 0, here, there)
    both[part:] = jnp.where(c == 0, there, here)
    width = tiles * LANES
    for vol, py in ((vol_mine, y), (vol_to_y, 1 - y)):
        vol[...] = both[:, pl.ds(pl.multiple_of(py * (width - LANES), LANES), width)]


def middle_pack_kernel(mine, got_1, got_2, got_3, own_pair, send_1, send_2, send_3, acc):
    z, x, c, y = coords()
    tiles = own_pair.shape[2] // LANES
    half_tiles = 2 * tiles - 1
    acc[...] = (mine[...] + got_1[...]) + (got_2[...] + got_3[...])

    def put(out, first, pitch):
        for i in range(2):
            for t in range(tiles):
                out[i, :, t * LANES : (t + 1) * LANES] = acc[first + i * pitch + t]

    for out, bits, px, py in ((own_pair, 0, x, y), (send_1, 1, 1 - x, 1 - y), (send_2, 3, 1 - x, y), (send_3, 2, x, 1 - y)):
        depth_first = 2 * tiles * depth_partner(z, bits)
        plane_first = 2 * half_tiles * px + (tiles - 1) * py
        put(out, jnp.where(c == 0, depth_first, plane_first), jnp.where(c == 0, tiles, half_tiles))


def gram_kernel(rows, band, scale, tan_ref, sec_ref, drift_ref, after_ref, conv_ref, low_ref, high_ref):
    views = tan_ref.shape[1]
    span = 2 * band + 1
    shape = (span * rows, views)
    row = row_iota(shape)
    shift = ((row % rows).astype(jnp.float32) - (rows - 1) / 2.0) * tan_ref[...] - drift_ref[...].astype(jnp.float32)
    hat = jnp.maximum(0.0, 1.0 - jnp.abs(shift - (row // rows - band).astype(jnp.float32)))
    gram = lax.dot_general(
        hat * ((scale / rows) * sec_ref[...]),
        hat,
        (((1,), (1,)), ((), ())),
        precision=lax.Precision.HIGHEST,
        preferred_element_type=jnp.float32,
    )
    edge = band * rows
    low_ref[...] = left_terms(gram[edge + rows :, edge + rows :])
    high_ref[...] = left_terms(gram[:edge, :edge])
    width = conv_ref.shape[1] // 2 * 3
    padded = jnp.concatenate([gram, jnp.zeros((span * rows, width - span * rows), jnp.float32)], axis=1)
    total = jnp.zeros((rows, width), jnp.float32)
    for k in range(span):
        total = total + pltpu.roll(padded[k * rows : (k + 1) * rows], rows * (2 * band - k), 1)
    lanes = width // 3
    stacked = jnp.concatenate([total[:, i * lanes : (i + 1) * lanes] for i in range(3)], axis=0)
    stacked = split_rows(stacked)
    conv_ref[...] = jnp.concatenate([stacked, stacked], axis=1)


def normal(volumes, conv, low_ref, high_ref, out, band, is_low, is_high):
    rows, width = volumes[0].shape
    count = len(volumes)
    step = conv.shape[1] // 2 // rows
    parts = conv.shape[0] // 2 // rows
    for s in range(count):
        moved = jnp.concatenate(
            [pltpu.roll(volumes[s], (2 * band - j) % width, 1) for j in range(step)], axis=0
        )
        spread = jnp.dot(conv, split_terms(moved), preferred_element_type=jnp.float32)
        spread = spread[: parts * rows] + spread[parts * rows :]
        total = spread[0:rows]
        for i in range(1, parts):
            total = total + pltpu.roll(spread[i * rows : (i + 1) * rows], width - step * i, 1)
        out[s] = total

    lane = lane_iota((rows, LANES))

    @pl.when(is_low)
    def _():
        tiles = [v[:, :LANES] for v in volumes]
        moved = jnp.concatenate(
            [jnp.concatenate([pltpu.roll(t, LANES - k, 1) for k in range(1, band + 1)], axis=0) for t in tiles], axis=1
        )
        spread = jnp.dot(low_ref[...].astype(jnp.bfloat16), right_terms(moved), preferred_element_type=jnp.float32)
        for s in range(count):
            total = jnp.zeros((rows, LANES), jnp.float32)
            for k in range(1, band + 1):
                piece = spread[(k - 1) * rows : k * rows, s * LANES : (s + 1) * LANES]
                piece = jnp.where((lane >= HALO - band) & (lane < HALO), piece, 0.0)
                total = total + pltpu.roll(piece, k, 1)
            out[s, :, 0:LANES] = out[s, :, 0:LANES] - total

    @pl.when(is_high)
    def _():
        tiles = [v[:, width - LANES :] for v in volumes]
        moved = jnp.concatenate(
            [jnp.concatenate([pltpu.roll(t, k, 1) for k in range(band, 0, -1)], axis=0) for t in tiles], axis=1
        )
        spread = jnp.dot(high_ref[...].astype(jnp.bfloat16), right_terms(moved), preferred_element_type=jnp.float32)
        for s in range(count):
            total = jnp.zeros((rows, LANES), jnp.float32)
            for k in range(band, 0, -1):
                piece = spread[(band - k) * rows : (band - k + 1) * rows, s * LANES : (s + 1) * LANES]
                piece = jnp.where((lane >= LANES - HALO) & (lane < LANES - HALO + band), piece, 0.0)
                total = total + pltpu.roll(piece, LANES - k, 1)
            out[s, :, width - LANES :] = out[s, :, width - LANES :] - total


def block_place(width, total_cols):
    z, x, c, y = coords()
    block = width - 2 * HALO
    index = c * 2 + y
    return index * block - HALO, index == 0, index == total_cols // block - 1


def first_normal_kernel(band, total_cols, vol_mine, vol_got, conv_ref, low_ref, high_ref, out, work):
    _, is_low, is_high = block_place(vol_mine.shape[1], total_cols)
    _, _, _, y = coords()
    part = vol_mine.shape[0] // 2
    here, there = vol_mine[...], vol_got[...]
    upper = jnp.where(y == 0, here, there)
    lower = jnp.where(y == 0, there, here)
    volumes = [
        jnp.concatenate([upper[i * part : (i + 1) * part], lower[i * part : (i + 1) * part]], axis=0) for i in range(2)
    ]
    normal(volumes, conv_ref[...].astype(jnp.bfloat16), low_ref, high_ref, work, band, is_low, is_high)
    for i in range(2):
        out[i] = volumes[i] - work[i]


def half_pair_kernel(first_ref, own_pair, got_1, got_2, got_3, mine, to_x, to_diag, corr):
    _, x, _, _ = coords()
    corr[...] = (own_pair[...] + got_1[...]) + (got_2[...] + got_3[...])
    half = first_ref[...] + corr[...]
    mine[0:2] = half
    mine[2:4] = corr[...]
    to_x[0:2] = half
    to_x[2] = corr[1 - x]
    to_diag[0:2] = half
    to_diag[2] = corr[x]


def variation_step(half, z_of, first_col, depth, total_cols):
    rows, width = half[0].shape
    col = first_col + lane_iota((rows, width))
    row = row_iota((rows, width))
    inside = (col >= 0) & (col < total_cols - 1)
    units = []
    for w in range(len(half) - 1):
        v = half[w]
        keep = (z_of(w) >= 0) & (z_of(w) < depth - 1)
        dz = jnp.where(keep, half[w + 1] - v, 0.0)
        dr = jnp.where(row < rows - 1, pltpu.roll(v, rows - 1, 0) - v, 0.0)
        dc = jnp.where(inside, pltpu.roll(v, width - 1, 1) - v, 0.0)
        inverse = 1.0 / jnp.sqrt(dz * dz + dr * dr + dc * dc + SMOOTH_EPS * SMOOTH_EPS)
        units.append((dz * inverse, dr * inverse, dc * inverse))
    result = []
    for w in range(1, len(half) - 1):
        uz, ur, uc = units[w]
        div = (uz - units[w - 1][0]) + (ur - pltpu.roll(ur, 1, 0)) + (uc - pltpu.roll(uc, 1, 1))
        result.append(jnp.where((col >= 0) & (col < total_cols), half[w] + TV_STEP * div, 0.0))
    return result


def finish_kernel(
    band, depth, total_cols, mine, got_diag, got_x, conv_ref, low_ref, high_ref, keep_ref, send_ref, work, done
):
    width = mine.shape[2]
    first_col, is_low, is_high = block_place(width, total_cols)
    z, x, c, _ = coords()
    before = [jnp.where(x == 0, got_diag[i], got_x[i]) for i in range(3)]
    after = [jnp.where(x == 0, got_x[i], got_diag[i]) for i in range(3)]
    half = [before[0], before[1], mine[0], mine[1], after[0], after[1]]
    corr = [before[2], mine[2], mine[3], after[2]]
    slice_0 = 4 * z + 2 * x
    volumes = variation_step(half, lambda w: slice_0 - 2 + w, first_col, depth, total_cols)
    normal(volumes, conv_ref[...].astype(jnp.bfloat16), low_ref, high_ref, work, band, is_low, is_high)
    half = [volumes[s] + corr[s] - work[s] for s in range(4)]
    volumes = variation_step(half, lambda w: slice_0 - 1 + w, first_col, depth, total_cols)
    for s in range(2):
        done[s] = pltpu.roll(volumes[s], width - HALO, 1)[:, : width - LANES]
    keep_ref[...] = done[c]
    send_ref[...] = done[1 - c]


def result_pack_kernel(own_ref, got_ref, to_y):
    _, _, c, y = coords()
    part = to_y.shape[1]
    own, got = own_ref[...], got_ref[...]
    to_y[c] = jnp.where(y == 0, own[part:], own[:part])
    to_y[1 - c] = jnp.where(y == 0, got[part:], got[:part])


def result_kernel(own_ref, got_ref, got_y, out):
    _, _, c, y = coords()
    _, part, block = got_y.shape
    own, got = own_ref[...], got_ref[...]
    here = jnp.where(y == 0, own[:part], own[part:])
    there = jnp.where(y == 0, got[:part], got[part:])
    for value, h, q in ((here, c, y), (there, 1 - c, y), (got_y[0], 0, 1 - y), (got_y[1], 1, 1 - y)):
        out[0, :, pl.ds(pl.multiple_of((2 * h + q) * block, LANES), block)] = value


def f32(*shape):
    return jax.ShapeDtypeStruct(shape, jnp.float32)


VMEM_SPEC = pl.BlockSpec(memory_space=pltpu.VMEM)
SMEM_SPEC = pl.BlockSpec(memory_space=pltpu.SMEM)
ANY_SPEC = pl.BlockSpec(memory_space=pl.ANY)
HBM_SPEC = pl.BlockSpec(memory_space=pltpu.HBM)
PARAMS = pltpu.CompilerParams(vmem_limit_bytes=40 * 1024 * 1024)


def in_hbm(value):
    return pltpu.with_memory_space_constraint(value, pltpu.HBM)


def kernel_call(body, outs, in_specs, scratch, name, flops=0, size=0):
    many = isinstance(outs, (list, tuple))
    return pl.pallas_call(
        body,
        out_shape=outs,
        in_specs=in_specs,
        out_specs=[VMEM_SPEC] * len(outs) if many else VMEM_SPEC,
        scratch_shapes=scratch,
        compiler_params=PARAMS,
        name=name,
        cost_estimate=pl.CostEstimate(flops=flops, bytes_accessed=size, transcendentals=0),
    )


def summed_plan(measured, drift, start_volume):
    views, slices, cols = measured.shape
    part = start_volume.shape[1]
    rows = 2 * part
    band = rows // 2 + DMAX + 2
    total_angles = drift.shape[0]
    half_cols = cols // 2
    half_width = half_cols + LANES
    width = cols // 4 + 2 * HALO
    tangent, secant = tan_and_secant(total_angles)
    scale = float(1.0 / np.sum(secant))
    tangent, secant = tangent.astype(np.float32), secant.astype(np.float32)

    tiles = half_width // LANES
    groups = slices // SUB
    window = (groups, views, tiles + 2, SUB, LANES)
    tiled = measured.reshape(views, groups, SUB, cols // LANES, LANES).transpose(0, 1, 3, 2, 4)
    table = ((2 * band // STEP + 1) * rows, 3 * STEP * views)
    count = slices // 2
    terms = pltpu.VMEM((count, 3 * STEP * views, half_width + LANES), jnp.bfloat16)
    vbuf = pltpu.VMEM((part, cols + 2 * LANES), jnp.float32)
    half_of = f32(count, rows, half_width)
    half_and = f32(count + 1, rows, half_width)
    across = lambda z, x, c, y: (z, x, 1 - c, y)

    pass_sibling, sibling_buf, own_buf, weights, volume = kernel_call(
        functools.partial(fetch_kernel, views, rows, band, scale),
        [half_of, f32(*window), f32(*window), f32(*table), f32(1, part, cols)],
        [HBM_SPEC] * 4,
        [
            pltpu.SMEM((total_angles,), jnp.float32),
            pltpu.SMEM((total_angles,), jnp.int32),
            terms,
            pltpu.SemaphoreType.DMA((3,)),
            pltpu.SemaphoreType.DMA((2, groups)),
        ],
        "pass_sibling",
        flops=10**9,
    )(in_hbm(jnp.asarray(tangent)), in_hbm(drift), in_hbm(tiled), in_hbm(start_volume))
    pass_got = move(pass_sibling, across)
    keep_sibling = kernel_call(
        functools.partial(sibling_kernel, views, rows, band),
        half_and,
        [VMEM_SPEC] * 3,
        [terms, vbuf],
        "keep_sibling",
        flops=10**9,
    )(sibling_buf, weights, volume)
    keep_got = move(keep_sibling, across)

    def own(kept, after):
        return kernel_call(
            functools.partial(own_kernel, kept, views, rows, band),
            half_of,
            [VMEM_SPEC] * 2 + [ANY_SPEC],
            [terms],
            "keep_own" if kept else "pass_own",
            flops=10**9,
        )(own_buf, weights, after)

    message = f32(count * width // LANES, rows, LANES)
    pass_own = own(False, keep_sibling)
    send_1 = kernel_call(pass_pack_kernel, message, [VMEM_SPEC] * 2, [pltpu.VMEM(half_of.shape, jnp.float32)], "pass_pack")(
        pass_own, pass_got
    )
    got_1 = move(send_1, lambda z, x, c, y: (z ^ 2, x, c, y) if c else (z, 1 - x, c, 1 - y))
    mine, send_2, send_3, vol_mine, vol_to_y = kernel_call(
        keep_pack_kernel,
        [message] * 3 + [f32(rows, width)] * 2,
        [VMEM_SPEC] * 5,
        [pltpu.VMEM(half_of.shape, jnp.float32)] * 2 + [pltpu.VMEM((rows, half_width), jnp.float32), vbuf],
        "keep_pack",
    )(pass_own, pass_got, own(True, send_1), keep_got, volume)
    got_2 = move(send_2, lambda z, x, c, y: (z ^ 3, x, c, y) if c else (z, 1 - x, c, y))
    got_3 = move(send_3, lambda z, x, c, y: (z ^ 1, x, c, y) if c else (z, x, c, 1 - y))
    vol_got = move(vol_to_y, lambda z, x, c, y: (z, x, c, 1 - y))

    edge = band * rows
    conv, low, high = kernel_call(
        functools.partial(gram_kernel, rows, band, scale),
        [f32(6 * rows, 2 * LANES), f32(edge, 3 * edge), f32(edge, 3 * edge)],
        [VMEM_SPEC] * 3 + [ANY_SPEC],
        [],
        "gram",
    )(tangent[None], secant[None], drift[None], mine)

    pair = f32(2, rows, width)
    own_pair, send_1, send_2, send_3 = kernel_call(
        middle_pack_kernel,
        [pair] * 4,
        [VMEM_SPEC] * 4,
        [pltpu.VMEM(message.shape, jnp.float32)],
        "middle_pack",
    )(mine, got_1, got_2, got_3)
    got_1 = move(send_1, lambda z, x, c, y: (z, 1 - x, c, 1 - y) if c else (z ^ 1, x, c, y))
    got_2 = move(send_2, lambda z, x, c, y: (z, 1 - x, c, y) if c else (z ^ 3, x, c, y))
    got_3 = move(send_3, lambda z, x, c, y: (z, x, c, 1 - y) if c else (z ^ 2, x, c, y))

    first = kernel_call(
        functools.partial(first_normal_kernel, band, cols),
        pair,
        [VMEM_SPEC] * 5,
        [pltpu.VMEM((2, rows, width), jnp.float32)],
        "first_normal",
        flops=10**9,
    )(vol_mine, vol_got, conv, low, high)

    three = f32(3, rows, width)
    mine, to_x, to_diag = kernel_call(
        half_pair_kernel,
        [f32(4, rows, width), three, three],
        [VMEM_SPEC] * 5,
        [pltpu.VMEM((2, rows, width), jnp.float32)],
        "half_pair",
    )(first, own_pair, got_1, got_2, got_3)
    got_diag = move(to_diag, beside)
    got_x = move(to_x, lambda z, x, c, y: (z, 1 - x, c, y))

    block = width - 2 * HALO
    quarter = f32(rows, block)
    keep, send = kernel_call(
        functools.partial(finish_kernel, band, slices, cols),
        [quarter, quarter],
        [VMEM_SPEC] * 6,
        [pltpu.VMEM((4, rows, width), jnp.float32), pltpu.VMEM((2, rows, block), jnp.float32)],
        "finish",
    )(mine, got_diag, got_x, conv, low, high)
    swapped = move(send, lambda z, x, c, y: (z, x, 1 - c, y))
    to_y = kernel_call(result_pack_kernel, f32(2, part, block), [VMEM_SPEC] * 2, [], "result_pack")(keep, swapped)
    got_y = move(to_y, lambda z, x, c, y: (z, x, c, 1 - y))
    return kernel_call(result_kernel, f32(1, part, cols), [VMEM_SPEC] * 3, [], "result")(keep, swapped, got_y)


def summed_plan_fits(mesh, measured, start_volume):
    rows = start_volume.shape[1]
    cols = measured.shape[2]
    return (
        ITERS == 2
        and dict(mesh.shape) == {"wide": 16, "grp": 2}
        and measured.shape[1] == start_volume.shape[0] == 16
        and rows == SUB
        and cols % (16 * LANES) == 0
        and measured.shape[0] % 256 == 0
    )


def solution(mesh):
    in_specs = (P(("wide", "grp"), None, None), P(), P("wide", "grp", None))
    out_specs = P("wide", "grp", None)

    def run(measured, drift, start_volume):
        plan = summed_plan if summed_plan_fits(mesh, measured, start_volume) else on_device
        return jax.shard_map(plan, mesh=mesh, in_specs=in_specs, out_specs=out_specs, check_vma=False)(
            measured, drift, start_volume
        )

    return run
```

```python
import functools
from functools import reduce
import math

import jax
import jax.numpy as jnp
import numpy as np
from jax import lax
from jax.experimental import pallas as pl
from jax.experimental.pallas import tpu as pltpu
from jax.sharding import PartitionSpec as P

ITERS = 2
DMAX = 4


TILT_MAX = math.pi / 4
SMOOTH_EPS = 0.05
TV_STEP = 0.1


def with_halo(block, sides, width):
    for axis, dim in sides:
        count = lax.axis_size(axis)
        forward = [(i, i + 1) for i in range(count - 1)]
        backward = [(target, source) for source, target in forward]
        low = lax.ppermute(
            lax.slice_in_dim(block, block.shape[dim] - width, None, axis=dim), axis, forward
        )
        high = lax.ppermute(lax.slice_in_dim(block, 0, width, axis=dim), axis, backward)
        block = jnp.concatenate([low, block, high], axis=dim)
    return block


def geometry(angle_ids, drift_vals, total_angles, rows, band_extent):
    angle_rad = TILT_MAX * (2.0 * angle_ids.astype(jnp.float32) / (total_angles - 1) - 1.0)
    secant = 1.0 / jnp.cos(angle_rad)
    height = jnp.arange(rows, dtype=jnp.float32) - (rows - 1) / 2.0
    offsets = jnp.arange(2 * band_extent + 1, dtype=jnp.float32) - band_extent
    shifts = height[None, :] * jnp.tan(angle_rad)[:, None] - drift_vals.astype(jnp.float32)[:, None]
    weight_factors = secant[:, None, None] * jnp.maximum(
        0.0, 1.0 - jnp.abs(shifts[:, :, None] - offsets[None, None, :])
    )
    return (weight_factors, jnp.cos(angle_rad) / rows)


def secant_sum(total_angles):
    angle_rad = TILT_MAX * (
        2.0 * jnp.arange(total_angles, dtype=jnp.float32) / (total_angles - 1) - 1.0
    )
    return jnp.sum(1.0 / jnp.cos(angle_rad))


def local_geometry(angle_ids, drift, total_angles, rows_all, band_extent):
    matches = angle_ids[:, None] == jnp.arange(total_angles, dtype=jnp.int32)[None, :]
    local_drift = jnp.sum(jnp.where(matches, drift[None, :], 0), axis=1)
    return geometry(angle_ids, local_drift, total_angles, rows_all, band_extent)


def apply_correction(
    row_band_strip, measurement_part, weight_factors, residual_scale, global_scale, band_extent
):
    col_count = row_band_strip.shape[2]
    span = 2 * band_extent + 1
    padded = jnp.pad(row_band_strip, ((0, 0), (0, 0), (band_extent, band_extent)))
    shifted = jnp.stack(
        [padded[:, :, shift_id : shift_id + col_count] for shift_id in range(span)], axis=2
    )
    forward_projected = jnp.einsum(
        "ark,zrku->azu", weight_factors, shifted, precision=lax.Precision.HIGHEST
    )
    residual_error = residual_scale[:, None, None] * (measurement_part - forward_projected)
    spread = jnp.einsum(
        "ark,azu->kzru", weight_factors, residual_error, precision=lax.Precision.HIGHEST
    )
    spread = jnp.pad(spread, ((0, 0), (0, 0), (0, 0), (band_extent, band_extent)))
    pieces = [
        spread[shift_id, :, :, 2 * band_extent - shift_id : 2 * band_extent - shift_id + col_count]
        for shift_id in range(span)
    ]
    return global_scale * reduce(lambda left, right: left + right, pieces)


def divergence(extended, z_first, r_first, zcount, rcount):
    plane_count, height, col_count = extended.shape
    z_index = z_first + jnp.arange(plane_count, dtype=jnp.int32)[:, None, None]
    row_index = r_first + jnp.arange(height, dtype=jnp.int32)[None, :, None]
    col_index = jnp.arange(col_count, dtype=jnp.int32)[None, None, :]
    diff_z = jnp.concatenate([extended[1:] - extended[:-1], jnp.zeros_like(extended[:1])], axis=0)
    diff_z = jnp.where((z_index >= 0) & (z_index < zcount - 1), diff_z, 0.0)
    diff_r = jnp.concatenate(
        [extended[:, 1:] - extended[:, :-1], jnp.zeros_like(extended[:, :1])], axis=1
    )
    diff_r = jnp.where((row_index >= 0) & (row_index < rcount - 1), diff_r, 0.0)
    diff_c = jnp.concatenate(
        [extended[:, :, 1:] - extended[:, :, :-1], jnp.zeros_like(extended[:, :, :1])], axis=2
    )
    diff_c = jnp.where(col_index < col_count - 1, diff_c, 0.0)
    magnitude = jnp.sqrt(
        diff_z * diff_z + diff_r * diff_r + diff_c * diff_c + SMOOTH_EPS * SMOOTH_EPS
    )
    unit_z = diff_z / magnitude
    unit_r = diff_r / magnitude
    unit_c = diff_c / magnitude
    back_c = unit_c - jnp.concatenate([jnp.zeros_like(unit_c[:, :, :1]), unit_c[:, :, :-1]], axis=2)
    return (
        unit_z[1:-1, 1:-1]
        - unit_z[:-2, 1:-1]
        + (unit_r[1:-1, 1:-1] - unit_r[1:-1, :-2])
        + back_c[1:-1, 1:-1]
    )


def on_device(measured, drift, start_volume):
    wide_count = lax.axis_size("wide")
    groups = lax.axis_size("grp")
    slab_count, rows_tile, col_count = start_volume.shape
    rows_all = rows_tile * groups
    band_extent = rows_all // 2 + DMAX + 2
    per_device = measured.shape[0]
    total_angles = per_device * wide_count * groups
    global_scale = 1.0 / secant_sum(total_angles)
    z_first = lax.axis_index("wide") * slab_count - 1
    zcount = slab_count * wide_count
    local_measurement = lax.all_to_all(measured, "wide", split_axis=1, concat_axis=0, tiled=True)
    bin_position = jnp.arange(local_measurement.shape[0], dtype=jnp.int32)
    angle_ids = (
        bin_position // per_device * groups + lax.axis_index("grp")
    ) * per_device + bin_position % per_device
    weight_factors, residual_scale = local_geometry(
        angle_ids, drift, total_angles, rows_all, band_extent
    )
    own_tile = start_volume
    r_first = lax.axis_index("grp") * rows_tile - 1
    for sweep in range(ITERS):
        row_band_strip = lax.all_gather(own_tile, "grp", axis=1, tiled=True)
        volume_update = apply_correction(
            row_band_strip,
            local_measurement,
            weight_factors,
            residual_scale,
            global_scale,
            band_extent,
        )
        own_tile = own_tile + lax.psum_scatter(
            volume_update, "grp", scatter_dimension=1, tiled=True
        )
        extended = with_halo(own_tile, (("wide", 0), ("grp", 1)), 1)
        own_tile = own_tile + TV_STEP * divergence(extended, z_first, r_first, zcount, rows_all)
    return own_tile


LANES = 128
SUB = 8
HALO = 64


def tan_and_secant(total_angles):
    angle = TILT_MAX * (2.0 * np.arange(total_angles) / (total_angles - 1) - 1.0)
    return np.tan(angle), 1.0 / np.cos(angle)


def coords():
    wide, y = lax.axis_index("wide"), lax.axis_index("grp")
    return wide // 4, wide // 2 % 2, wide % 2, y


def move(value, target):
    pairs = []
    for z in range(4):
        for x in range(2):
            for c in range(2):
                for y in range(2):
                    tz, tx, tc, ty = target(z, x, c, y)
                    pairs.append((((z * 2 + x) * 2 + c) * 2 + y, ((tz * 2 + tx) * 2 + tc) * 2 + ty))
    return lax.ppermute(value, ("wide", "grp"), pairs)


def beside(z, x, c, y):
    if (z, x) in ((0, 0), (3, 1)):
        return z, x, 1 - c, y
    return (z + 1, 0, c, y) if x else (z - 1, 1, c, y)


def split_rows(value):
    high = value.astype(jnp.bfloat16).astype(jnp.float32)
    return jnp.concatenate([high, value - high], axis=0)


def left_terms(value):
    high = value.astype(jnp.bfloat16).astype(jnp.float32)
    return jnp.concatenate([high, high, value - high], axis=1)


def split_terms(value):
    high = value.astype(jnp.bfloat16)
    low = (value - high.astype(jnp.float32)).astype(jnp.bfloat16)
    return jnp.concatenate([high, low], axis=0)


def right_terms(value):
    high = value.astype(jnp.bfloat16)
    low = (value - high.astype(jnp.float32)).astype(jnp.bfloat16)
    return jnp.concatenate([high, low, high], axis=0)


def lane_iota(shape):
    return lax.broadcasted_iota(jnp.int32, shape, len(shape) - 1)


def row_iota(shape):
    return lax.broadcasted_iota(jnp.int32, shape, len(shape) - 2)


STEP = 3


def view_weights(views, rows, band, scale, tan_ref, drift_ref):
    z, x, c, y = coords()
    first_view = (((z * 2 + x) * 2 + c) * 2 + y) * views
    parts = 2 * band // STEP + 1
    shape = (parts * rows, STEP * views)
    lane, row = lane_iota(shape), row_iota(shape)
    view_of = lane_iota((1, STEP * views)) % views
    tan_lane = jnp.zeros((1, STEP * views), jnp.float32)
    drift_lane = tan_lane
    for a in range(views):
        tan_lane = jnp.where(view_of == a, tan_ref[first_view + a], tan_lane)
        drift_lane = jnp.where(view_of == a, drift_ref[first_view + a].astype(jnp.float32), drift_lane)
    shift = ((row % rows).astype(jnp.float32) - (rows - 1) / 2.0) * tan_lane - drift_lane
    offset = ((row // rows) * STEP + lane // views - band).astype(jnp.float32)
    weights = (scale / rows) * jnp.maximum(0.0, 1.0 - jnp.abs(shift - offset))
    return left_terms(weights).astype(jnp.bfloat16)


def back_project(views, rows, band, weights, load_strip, out_ref, terms):
    count, _, width = terms.shape
    out_cols = out_ref.shape[2]
    parts = 2 * band // STEP + 1
    for n in range(count):
        strip = load_strip(n)
        high = strip.astype(jnp.bfloat16)
        low = (strip - high.astype(jnp.float32)).astype(jnp.bfloat16)
        for j in range(STEP):
            moved = pltpu.roll(high, j, 1) if j else high
            terms[n, j * views : (j + 1) * views] = moved
            terms[n, (STEP + j) * views : (STEP + j + 1) * views] = pltpu.roll(low, j, 1) if j else low
            terms[n, (2 * STEP + j) * views : (2 * STEP + j + 1) * views] = moved
    for n in range(count):
        spread = jnp.dot(weights, terms[n], preferred_element_type=jnp.float32)
        total = None
        for i in range(parts):
            piece = pltpu.roll(spread[i * rows : (i + 1) * rows], width - HALO - band + STEP * i, 1)
            total = piece if total is None else total + piece
        out_ref[n] = total[:, :out_cols]


def depth_partner(z, bits):
    return {0: z, 1: z + 1 - 2 * (z % 2), 2: (z + 2) % 4, 3: 3 - z}[bits]


def slice_place(half, kept, n):
    z, x, _, _ = coords()
    parity = x if kept else 1 - x
    four = depth_partner(z, (1, 0)[n // 4] if kept else (2, 3)[n // 4])
    group = jnp.where(half == 0, n // 4, four // 2)
    place = jnp.where(half == 0, 4 * (n // 2 % 2) + 2 * parity + n % 2, 4 * (four % 2) + n % 4)
    return group, place


def strip_loader(buf, half, kept, views, tiles):
    pitch = (tiles + 2) * SUB

    def load(n):
        group, place = slice_place(half, kept, n)
        first = half * SUB + place
        return jnp.concatenate(
            [buf[group, pl.ds(first + t * SUB, views, stride=pitch), :] for t in range(tiles + 1)], axis=1
        )

    return load


def volume_window(vol_ref, half, half_cols, vbuf):
    part, cols = vol_ref.shape[1:]
    vbuf[:, 0:LANES] = jnp.zeros((part, LANES), jnp.float32)
    vbuf[:, LANES : LANES + cols] = vol_ref[0]
    vbuf[:, LANES + cols :] = jnp.zeros((part, LANES), jnp.float32)
    width = half_cols + 2 * LANES
    window = vbuf[:, pl.ds(pl.multiple_of(half * half_cols, LANES), width)]
    return pltpu.roll(window, width - HALO, 1)[:, : half_cols + LANES]


def fetch_kernel(views, rows, band, scale, tan_hbm, drift_hbm, meas_hbm, vol_hbm, out_ref, sibling_buf, own_buf,
                 weights_ref, vol_ref, tan_ref, drift_ref, terms, table_sem, sem):
    _, _, c, _ = coords()
    tiles = out_ref.shape[2] // LANES
    groups = sibling_buf.shape[0]

    def fetch(half, target, g, semaphore):
        return pltpu.make_async_copy(
            meas_hbm.at[:, g, pl.ds(half * (tiles - 2), tiles)], target.at[g, :, 1 : tiles + 1], semaphore
        )

    tables = [
        pltpu.make_async_copy(tan_hbm, tan_ref, table_sem.at[0]),
        pltpu.make_async_copy(drift_hbm, drift_ref, table_sem.at[1]),
    ]
    vol_copy = pltpu.make_async_copy(vol_hbm, vol_ref, table_sem.at[2])
    first = [fetch(1 - c, sibling_buf, g, sem.at[0, g]) for g in range(groups)]
    later = [fetch(c, own_buf, g, sem.at[1, g]) for g in range(groups)]
    for copy in tables + first + [vol_copy] + later:
        copy.start()
    zero = jnp.zeros((views, SUB, LANES), jnp.float32)
    for g in range(groups):
        for target in (sibling_buf, own_buf):
            target[g, :, 0] = zero
            target[g, :, tiles + 1] = zero
    for copy in tables:
        copy.wait()
    weights = view_weights(views, rows, band, scale, tan_ref, drift_ref)
    weights_ref[...] = weights.astype(jnp.float32)
    load = strip_loader(flat_rows(sibling_buf), 1 - c, False, views, tiles)

    for copy in first:
        copy.wait()
    back_project(views, rows, band, weights, load, out_ref, terms)
    vol_copy.wait()
    for copy in later:
        copy.wait()


def flat_rows(buf):
    groups, views, tiles, sub, lanes = buf.shape
    return buf.reshape(groups, views * tiles * sub, lanes)


def sibling_kernel(views, rows, band, buf, weights_ref, vol_ref, out_ref, terms, vbuf):
    _, _, c, _ = coords()
    tiles = out_ref.shape[2] // LANES
    load = strip_loader(flat_rows(buf), 1 - c, True, views, tiles)
    back_project(views, rows, band, weights_ref[...].astype(jnp.bfloat16), load, out_ref, terms)
    count = terms.shape[0]
    half_cols = out_ref.shape[2] - LANES
    part = vol_ref.shape[1]
    out_ref[count, 0:part] = volume_window(vol_ref, 1 - c, half_cols, vbuf)
    out_ref[count, part:] = jnp.zeros((rows - part, half_cols + LANES), jnp.float32)


def own_kernel(kept, views, rows, band, buf, weights_ref, after_ref, out_ref, terms):
    _, _, c, _ = coords()
    tiles = out_ref.shape[2] // LANES
    load = strip_loader(flat_rows(buf), c, kept, views, tiles)
    back_project(views, rows, band, weights_ref[...].astype(jnp.bfloat16), load, out_ref, terms)


def put_quarter(out, acc, py, tiles):
    for n in range(acc.shape[0]):
        for t in range(tiles):
            out[n * tiles + t] = acc[n, :, pl.ds(pl.multiple_of(((tiles - 1) * py + t) * LANES, LANES), LANES)]


def put_four(out, acc, first):
    tiles = acc.shape[2] // LANES
    for n in range(4):
        for t in range(tiles):
            out[n * tiles + t] = acc[first + n, :, t * LANES : (t + 1) * LANES]
    for t in range(4 * tiles, out.shape[0]):
        out[t] = jnp.zeros(out.shape[1:], jnp.float32)


def pass_pack_kernel(own_ref, got_ref, send, acc):
    _, _, c, y = coords()
    acc[...] = own_ref[...] + got_ref[...]

    @pl.when(c == 0)
    def _():
        put_quarter(send, acc, 1 - y, send.shape[0] // acc.shape[0])

    @pl.when(c == 1)
    def _():
        put_four(send, acc, 0)


def keep_pack_kernel(pass_ref, pass_got, own_ref, got_ref, vol_ref, mine, send_2, send_3, vol_mine, vol_to_y,
                     passed, acc, both, vbuf):
    count, rows, half_width = own_ref.shape
    tiles = mine.shape[0] // count
    part = vol_ref.shape[1]
    _, _, c, y = coords()
    passed[...] = pass_ref[...] + pass_got[...]
    acc[...] = own_ref[...] + got_ref[0:count]

    @pl.when(c == 0)
    def _():
        put_quarter(send_2, passed, y, tiles)
        put_quarter(send_3, acc, 1 - y, tiles)
        put_quarter(mine, acc, y, tiles)

    @pl.when(c == 1)
    def _():
        put_four(send_2, passed, 4)
        put_four(send_3, acc, 0)
        put_four(mine, acc, 4)

    here = volume_window(vol_ref, c, half_width - LANES, vbuf)
    there = got_ref[count, 0:part]
    both[0:part] = jnp.where(c == 0, here, there)
    both[part:] = jnp.where(c == 0, there, here)
    width = tiles * LANES
    for vol, py in ((vol_mine, y), (vol_to_y, 1 - y)):
        vol[...] = both[:, pl.ds(pl.multiple_of(py * (width - LANES), LANES), width)]


def middle_pack_kernel(mine, got_1, got_2, got_3, own_pair, send_1, send_2, send_3, acc):
    z, x, c, y = coords()
    tiles = own_pair.shape[2] // LANES
    half_tiles = 2 * tiles - 1
    acc[...] = (mine[...] + got_1[...]) + (got_2[...] + got_3[...])

    def put(out, first, pitch):
        for i in range(2):
            for t in range(tiles):
                out[i, :, t * LANES : (t + 1) * LANES] = acc[first + i * pitch + t]

    for out, bits, px, py in ((own_pair, 0, x, y), (send_1, 3, 1 - x, 1 - y), (send_2, 2, 1 - x, y), (send_3, 1, x, 1 - y)):
        depth_first = 2 * tiles * depth_partner(z, bits)
        plane_first = 2 * half_tiles * px + (tiles - 1) * py
        put(out, jnp.where(c == 0, depth_first, plane_first), jnp.where(c == 0, tiles, half_tiles))


def gram_kernel(rows, band, scale, tan_ref, sec_ref, drift_ref, after_ref, conv_ref, low_ref, high_ref):
    views = tan_ref.shape[1]
    span = 2 * band + 1
    shape = (span * rows, views)
    row = row_iota(shape)
    shift = ((row % rows).astype(jnp.float32) - (rows - 1) / 2.0) * tan_ref[...] - drift_ref[...].astype(jnp.float32)
    hat = jnp.maximum(0.0, 1.0 - jnp.abs(shift - (row // rows - band).astype(jnp.float32)))
    gram = lax.dot_general(
        hat * ((scale / rows) * sec_ref[...]),
        hat,
        (((1,), (1,)), ((), ())),
        precision=lax.Precision.HIGHEST,
        preferred_element_type=jnp.float32,
    )
    edge = band * rows
    low_ref[...] = left_terms(gram[edge + rows :, edge + rows :])
    high_ref[...] = left_terms(gram[:edge, :edge])
    width = conv_ref.shape[1] // 2 * 3
    padded = jnp.concatenate([gram, jnp.zeros((span * rows, width - span * rows), jnp.float32)], axis=1)
    total = jnp.zeros((rows, width), jnp.float32)
    for k in range(span):
        total = total + pltpu.roll(padded[k * rows : (k + 1) * rows], rows * (2 * band - k), 1)
    lanes = width // 3
    stacked = jnp.concatenate([total[:, i * lanes : (i + 1) * lanes] for i in range(3)], axis=0)
    stacked = split_rows(stacked)
    conv_ref[...] = jnp.concatenate([stacked, stacked], axis=1)


def normal(volumes, conv, low_ref, high_ref, out, band, is_low, is_high):
    rows, width = volumes[0].shape
    count = len(volumes)
    step = conv.shape[1] // 2 // rows
    parts = conv.shape[0] // 2 // rows
    for s in range(count):
        moved = jnp.concatenate(
            [pltpu.roll(volumes[s], (2 * band - j) % width, 1) for j in range(step)], axis=0
        )
        spread = jnp.dot(conv, split_terms(moved), preferred_element_type=jnp.float32)
        spread = spread[: parts * rows] + spread[parts * rows :]
        total = spread[0:rows]
        for i in range(1, parts):
            total = total + pltpu.roll(spread[i * rows : (i + 1) * rows], width - step * i, 1)
        out[s] = total

    lane = lane_iota((rows, LANES))

    @pl.when(is_low)
    def _():
        tiles = [v[:, :LANES] for v in volumes]
        moved = jnp.concatenate(
            [jnp.concatenate([pltpu.roll(t, LANES - k, 1) for k in range(1, band + 1)], axis=0) for t in tiles], axis=1
        )
        spread = jnp.dot(low_ref[...].astype(jnp.bfloat16), right_terms(moved), preferred_element_type=jnp.float32)
        for s in range(count):
            total = jnp.zeros((rows, LANES), jnp.float32)
            for k in range(1, band + 1):
                piece = spread[(k - 1) * rows : k * rows, s * LANES : (s + 1) * LANES]
                piece = jnp.where((lane >= HALO - band) & (lane < HALO), piece, 0.0)
                total = total + pltpu.roll(piece, k, 1)
            out[s, :, 0:LANES] = out[s, :, 0:LANES] - total

    @pl.when(is_high)
    def _():
        tiles = [v[:, width - LANES :] for v in volumes]
        moved = jnp.concatenate(
            [jnp.concatenate([pltpu.roll(t, k, 1) for k in range(band, 0, -1)], axis=0) for t in tiles], axis=1
        )
        spread = jnp.dot(high_ref[...].astype(jnp.bfloat16), right_terms(moved), preferred_element_type=jnp.float32)
        for s in range(count):
            total = jnp.zeros((rows, LANES), jnp.float32)
            for k in range(band, 0, -1):
                piece = spread[(band - k) * rows : (band - k + 1) * rows, s * LANES : (s + 1) * LANES]
                piece = jnp.where((lane >= LANES - HALO) & (lane < LANES - HALO + band), piece, 0.0)
                total = total + pltpu.roll(piece, LANES - k, 1)
            out[s, :, width - LANES :] = out[s, :, width - LANES :] - total


def block_place(width, total_cols):
    z, x, c, y = coords()
    block = width - 2 * HALO
    index = c * 2 + y
    return index * block - HALO, index == 0, index == total_cols // block - 1


def first_normal_kernel(band, total_cols, vol_mine, vol_got, conv_ref, low_ref, high_ref, out, work):
    _, is_low, is_high = block_place(vol_mine.shape[1], total_cols)
    _, _, _, y = coords()
    part = vol_mine.shape[0] // 2
    here, there = vol_mine[...], vol_got[...]
    upper = jnp.where(y == 0, here, there)
    lower = jnp.where(y == 0, there, here)
    volumes = [
        jnp.concatenate([upper[i * part : (i + 1) * part], lower[i * part : (i + 1) * part]], axis=0) for i in range(2)
    ]
    normal(volumes, conv_ref[...].astype(jnp.bfloat16), low_ref, high_ref, work, band, is_low, is_high)
    for i in range(2):
        out[i] = volumes[i] - work[i]


def half_pair_kernel(first_ref, own_pair, got_1, got_2, got_3, mine, to_x, to_diag, corr):
    _, x, _, _ = coords()
    corr[...] = (own_pair[...] + got_1[...]) + (got_2[...] + got_3[...])
    half = first_ref[...] + corr[...]
    mine[0:2] = half
    mine[2:4] = corr[...]
    to_x[0:2] = half
    to_x[2] = corr[1 - x]
    to_diag[0:2] = half
    to_diag[2] = corr[x]


def variation_step(half, z_of, first_col, depth, total_cols):
    rows, width = half[0].shape
    col = first_col + lane_iota((rows, width))
    row = row_iota((rows, width))
    inside = (col >= 0) & (col < total_cols - 1)
    units = []
    for w in range(len(half) - 1):
        v = half[w]
        keep = (z_of(w) >= 0) & (z_of(w) < depth - 1)
        dz = jnp.where(keep, half[w + 1] - v, 0.0)
        dr = jnp.where(row < rows - 1, pltpu.roll(v, rows - 1, 0) - v, 0.0)
        dc = jnp.where(inside, pltpu.roll(v, width - 1, 1) - v, 0.0)
        inverse = 1.0 / jnp.sqrt(dz * dz + dr * dr + dc * dc + SMOOTH_EPS * SMOOTH_EPS)
        units.append((dz * inverse, dr * inverse, dc * inverse))
    result = []
    for w in range(1, len(half) - 1):
        uz, ur, uc = units[w]
        div = (uz - units[w - 1][0]) + (ur - pltpu.roll(ur, 1, 0)) + (uc - pltpu.roll(uc, 1, 1))
        result.append(jnp.where((col >= 0) & (col < total_cols), half[w] + TV_STEP * div, 0.0))
    return result


def finish_kernel(
    band, depth, total_cols, mine, got_diag, got_x, conv_ref, low_ref, high_ref, keep_ref, send_ref, work, done
):
    width = mine.shape[2]
    first_col, is_low, is_high = block_place(width, total_cols)
    z, x, c, _ = coords()
    before = [jnp.where(x == 0, got_diag[i], got_x[i]) for i in range(3)]
    after = [jnp.where(x == 0, got_x[i], got_diag[i]) for i in range(3)]
    half = [before[0], before[1], mine[0], mine[1], after[0], after[1]]
    corr = [before[2], mine[2], mine[3], after[2]]
    slice_0 = 4 * z + 2 * x
    volumes = variation_step(half, lambda w: slice_0 - 2 + w, first_col, depth, total_cols)
    normal(volumes, conv_ref[...].astype(jnp.bfloat16), low_ref, high_ref, work, band, is_low, is_high)
    half = [volumes[s] + corr[s] - work[s] for s in range(4)]
    volumes = variation_step(half, lambda w: slice_0 - 1 + w, first_col, depth, total_cols)
    for s in range(2):
        done[s] = pltpu.roll(volumes[s], width - HALO, 1)[:, : width - LANES]
    keep_ref[...] = done[c]
    send_ref[...] = done[1 - c]


def result_pack_kernel(own_ref, got_ref, to_y):
    _, _, c, y = coords()
    part = to_y.shape[1]
    own, got = own_ref[...], got_ref[...]
    to_y[c] = jnp.where(y == 0, own[part:], own[:part])
    to_y[1 - c] = jnp.where(y == 0, got[part:], got[:part])


def result_kernel(own_ref, got_ref, got_y, out):
    _, _, c, y = coords()
    _, part, block = got_y.shape
    own, got = own_ref[...], got_ref[...]
    here = jnp.where(y == 0, own[:part], own[part:])
    there = jnp.where(y == 0, got[:part], got[part:])
    for value, h, q in ((here, c, y), (there, 1 - c, y), (got_y[0], 0, 1 - y), (got_y[1], 1, 1 - y)):
        out[0, :, pl.ds(pl.multiple_of((2 * h + q) * block, LANES), block)] = value


def f32(*shape):
    return jax.ShapeDtypeStruct(shape, jnp.float32)


VMEM_SPEC = pl.BlockSpec(memory_space=pltpu.VMEM)
SMEM_SPEC = pl.BlockSpec(memory_space=pltpu.SMEM)
ANY_SPEC = pl.BlockSpec(memory_space=pl.ANY)
HBM_SPEC = pl.BlockSpec(memory_space=pltpu.HBM)
PARAMS = pltpu.CompilerParams(vmem_limit_bytes=40 * 1024 * 1024)


def in_hbm(value):
    return pltpu.with_memory_space_constraint(value, pltpu.HBM)


def kernel_call(body, outs, in_specs, scratch, name, flops=0, size=0):
    many = isinstance(outs, (list, tuple))
    return pl.pallas_call(
        body,
        out_shape=outs,
        in_specs=in_specs,
        out_specs=[VMEM_SPEC] * len(outs) if many else VMEM_SPEC,
        scratch_shapes=scratch,
        compiler_params=PARAMS,
        name=name,
        cost_estimate=pl.CostEstimate(flops=flops, bytes_accessed=size, transcendentals=0),
    )


def summed_plan(measured, drift, start_volume):
    views, slices, cols = measured.shape
    part = start_volume.shape[1]
    rows = 2 * part
    band = rows // 2 + DMAX + 2
    total_angles = drift.shape[0]
    half_cols = cols // 2
    half_width = half_cols + LANES
    width = cols // 4 + 2 * HALO
    tangent, secant = tan_and_secant(total_angles)
    scale = float(1.0 / np.sum(secant))
    tangent, secant = tangent.astype(np.float32), secant.astype(np.float32)

    tiles = half_width // LANES
    groups = slices // SUB
    window = (groups, views, tiles + 2, SUB, LANES)
    tiled = measured.reshape(views, groups, SUB, cols // LANES, LANES).transpose(0, 1, 3, 2, 4)
    table = ((2 * band // STEP + 1) * rows, 3 * STEP * views)
    count = slices // 2
    terms = pltpu.VMEM((count, 3 * STEP * views, half_width + LANES), jnp.bfloat16)
    vbuf = pltpu.VMEM((part, cols + 2 * LANES), jnp.float32)
    half_of = f32(count, rows, half_width)
    half_and = f32(count + 1, rows, half_width)
    across = lambda z, x, c, y: (z, x, 1 - c, y)

    pass_sibling, sibling_buf, own_buf, weights, volume = kernel_call(
        functools.partial(fetch_kernel, views, rows, band, scale),
        [half_of, f32(*window), f32(*window), f32(*table), f32(1, part, cols)],
        [HBM_SPEC] * 4,
        [
            pltpu.SMEM((total_angles,), jnp.float32),
            pltpu.SMEM((total_angles,), jnp.int32),
            terms,
            pltpu.SemaphoreType.DMA((3,)),
            pltpu.SemaphoreType.DMA((2, groups)),
        ],
        "pass_sibling",
        flops=10**9,
    )(in_hbm(jnp.asarray(tangent)), in_hbm(drift), in_hbm(tiled), in_hbm(start_volume))
    pass_got = move(pass_sibling, across)
    keep_sibling = kernel_call(
        functools.partial(sibling_kernel, views, rows, band),
        half_and,
        [VMEM_SPEC] * 3,
        [terms, vbuf],
        "keep_sibling",
        flops=10**9,
    )(sibling_buf, weights, volume)
    keep_got = move(keep_sibling, across)

    def own(kept, after):
        return kernel_call(
            functools.partial(own_kernel, kept, views, rows, band),
            half_of,
            [VMEM_SPEC] * 2 + [ANY_SPEC],
            [terms],
            "keep_own" if kept else "pass_own",
            flops=10**9,
        )(own_buf, weights, after)

    message = f32(count * width // LANES, rows, LANES)
    pass_own = own(False, keep_sibling)
    send_1 = kernel_call(pass_pack_kernel, message, [VMEM_SPEC] * 2, [pltpu.VMEM(half_of.shape, jnp.float32)], "pass_pack")(
        pass_own, pass_got
    )
    got_1 = move(send_1, lambda z, x, c, y: (z ^ 2, x, c, y) if c else (z, 1 - x, c, 1 - y))
    mine, send_2, send_3, vol_mine, vol_to_y = kernel_call(
        keep_pack_kernel,
        [message] * 3 + [f32(rows, width)] * 2,
        [VMEM_SPEC] * 5,
        [pltpu.VMEM(half_of.shape, jnp.float32)] * 2 + [pltpu.VMEM((rows, half_width), jnp.float32), vbuf],
        "keep_pack",
    )(pass_own, pass_got, own(True, send_1), keep_got, volume)
    got_2 = move(send_2, lambda z, x, c, y: (z ^ 3, x, c, y) if c else (z, 1 - x, c, y))
    got_3 = move(send_3, lambda z, x, c, y: (z ^ 1, x, c, y) if c else (z, x, c, 1 - y))
    vol_got = move(vol_to_y, lambda z, x, c, y: (z, x, c, 1 - y))

    edge = band * rows
    conv, low, high = kernel_call(
        functools.partial(gram_kernel, rows, band, scale),
        [f32(6 * rows, 2 * LANES), f32(edge, 3 * edge), f32(edge, 3 * edge)],
        [VMEM_SPEC] * 3 + [ANY_SPEC],
        [],
        "gram",
    )(tangent[None], secant[None], drift[None], mine)

    pair = f32(2, rows, width)
    own_pair, send_1, send_2, send_3 = kernel_call(
        middle_pack_kernel,
        [pair] * 4,
        [VMEM_SPEC] * 4,
        [pltpu.VMEM(message.shape, jnp.float32)],
        "middle_pack",
    )(mine, got_1, got_2, got_3)
    got_1 = move(send_1, lambda z, x, c, y: (z, 1 - x, c, 1 - y) if c else (z ^ 3, x, c, y))
    got_2 = move(send_2, lambda z, x, c, y: (z, 1 - x, c, y) if c else (z ^ 2, x, c, y))
    got_3 = move(send_3, lambda z, x, c, y: (z, x, c, 1 - y) if c else (z ^ 1, x, c, y))

    first = kernel_call(
        functools.partial(first_normal_kernel, band, cols),
        pair,
        [VMEM_SPEC] * 5,
        [pltpu.VMEM((2, rows, width), jnp.float32)],
        "first_normal",
        flops=10**9,
    )(vol_mine, vol_got, conv, low, high)

    three = f32(3, rows, width)
    mine, to_x, to_diag = kernel_call(
        half_pair_kernel,
        [f32(4, rows, width), three, three],
        [VMEM_SPEC] * 5,
        [pltpu.VMEM((2, rows, width), jnp.float32)],
        "half_pair",
    )(first, own_pair, got_1, got_2, got_3)
    got_diag = move(to_diag, beside)
    got_x = move(to_x, lambda z, x, c, y: (z, 1 - x, c, y))

    block = width - 2 * HALO
    quarter = f32(rows, block)
    keep, send = kernel_call(
        functools.partial(finish_kernel, band, slices, cols),
        [quarter, quarter],
        [VMEM_SPEC] * 6,
        [pltpu.VMEM((4, rows, width), jnp.float32), pltpu.VMEM((2, rows, block), jnp.float32)],
        "finish",
    )(mine, got_diag, got_x, conv, low, high)
    swapped = move(send, lambda z, x, c, y: (z, x, 1 - c, y))
    to_y = kernel_call(result_pack_kernel, f32(2, part, block), [VMEM_SPEC] * 2, [], "result_pack")(keep, swapped)
    got_y = move(to_y, lambda z, x, c, y: (z, x, c, 1 - y))
    return kernel_call(result_kernel, f32(1, part, cols), [VMEM_SPEC] * 3, [], "result")(keep, swapped, got_y)


def summed_plan_fits(mesh, measured, start_volume):
    rows = start_volume.shape[1]
    cols = measured.shape[2]
    return (
        ITERS == 2
        and dict(mesh.shape) == {"wide": 16, "grp": 2}
        and measured.shape[1] == start_volume.shape[0] == 16
        and rows == SUB
        and cols % (16 * LANES) == 0
        and measured.shape[0] % 256 == 0
    )


def solution(mesh):
    in_specs = (P(("wide", "grp"), None, None), P(), P("wide", "grp", None))
    out_specs = P("wide", "grp", None)

    def run(measured, drift, start_volume):
        plan = summed_plan if summed_plan_fits(mesh, measured, start_volume) else on_device
        return jax.shard_map(plan, mesh=mesh, in_specs=in_specs, out_specs=out_specs, check_vma=False)(
            measured, drift, start_volume
        )

    return run
```

```python
import functools
from functools import reduce
import math

import jax
import jax.numpy as jnp
import numpy as np
from jax import lax
from jax.experimental import pallas as pl
from jax.experimental.pallas import tpu as pltpu
from jax.sharding import PartitionSpec as P

ITERS = 2
DMAX = 4


TILT_MAX = math.pi / 4
SMOOTH_EPS = 0.05
TV_STEP = 0.1


def with_halo(block, sides, width):
    for axis, dim in sides:
        count = lax.axis_size(axis)
        forward = [(i, i + 1) for i in range(count - 1)]
        backward = [(target, source) for source, target in forward]
        low = lax.ppermute(
            lax.slice_in_dim(block, block.shape[dim] - width, None, axis=dim), axis, forward
        )
        high = lax.ppermute(lax.slice_in_dim(block, 0, width, axis=dim), axis, backward)
        block = jnp.concatenate([low, block, high], axis=dim)
    return block


def geometry(angle_ids, drift_vals, total_angles, rows, band_extent):
    angle_rad = TILT_MAX * (2.0 * angle_ids.astype(jnp.float32) / (total_angles - 1) - 1.0)
    secant = 1.0 / jnp.cos(angle_rad)
    height = jnp.arange(rows, dtype=jnp.float32) - (rows - 1) / 2.0
    offsets = jnp.arange(2 * band_extent + 1, dtype=jnp.float32) - band_extent
    shifts = height[None, :] * jnp.tan(angle_rad)[:, None] - drift_vals.astype(jnp.float32)[:, None]
    weight_factors = secant[:, None, None] * jnp.maximum(
        0.0, 1.0 - jnp.abs(shifts[:, :, None] - offsets[None, None, :])
    )
    return (weight_factors, jnp.cos(angle_rad) / rows)


def secant_sum(total_angles):
    angle_rad = TILT_MAX * (
        2.0 * jnp.arange(total_angles, dtype=jnp.float32) / (total_angles - 1) - 1.0
    )
    return jnp.sum(1.0 / jnp.cos(angle_rad))


def local_geometry(angle_ids, drift, total_angles, rows_all, band_extent):
    matches = angle_ids[:, None] == jnp.arange(total_angles, dtype=jnp.int32)[None, :]
    local_drift = jnp.sum(jnp.where(matches, drift[None, :], 0), axis=1)
    return geometry(angle_ids, local_drift, total_angles, rows_all, band_extent)


def apply_correction(
    row_band_strip, measurement_part, weight_factors, residual_scale, global_scale, band_extent
):
    col_count = row_band_strip.shape[2]
    span = 2 * band_extent + 1
    padded = jnp.pad(row_band_strip, ((0, 0), (0, 0), (band_extent, band_extent)))
    shifted = jnp.stack(
        [padded[:, :, shift_id : shift_id + col_count] for shift_id in range(span)], axis=2
    )
    forward_projected = jnp.einsum(
        "ark,zrku->azu", weight_factors, shifted, precision=lax.Precision.HIGHEST
    )
    residual_error = residual_scale[:, None, None] * (measurement_part - forward_projected)
    spread = jnp.einsum(
        "ark,azu->kzru", weight_factors, residual_error, precision=lax.Precision.HIGHEST
    )
    spread = jnp.pad(spread, ((0, 0), (0, 0), (0, 0), (band_extent, band_extent)))
    pieces = [
        spread[shift_id, :, :, 2 * band_extent - shift_id : 2 * band_extent - shift_id + col_count]
        for shift_id in range(span)
    ]
    return global_scale * reduce(lambda left, right: left + right, pieces)


def divergence(extended, z_first, r_first, zcount, rcount):
    plane_count, height, col_count = extended.shape
    z_index = z_first + jnp.arange(plane_count, dtype=jnp.int32)[:, None, None]
    row_index = r_first + jnp.arange(height, dtype=jnp.int32)[None, :, None]
    col_index = jnp.arange(col_count, dtype=jnp.int32)[None, None, :]
    diff_z = jnp.concatenate([extended[1:] - extended[:-1], jnp.zeros_like(extended[:1])], axis=0)
    diff_z = jnp.where((z_index >= 0) & (z_index < zcount - 1), diff_z, 0.0)
    diff_r = jnp.concatenate(
        [extended[:, 1:] - extended[:, :-1], jnp.zeros_like(extended[:, :1])], axis=1
    )
    diff_r = jnp.where((row_index >= 0) & (row_index < rcount - 1), diff_r, 0.0)
    diff_c = jnp.concatenate(
        [extended[:, :, 1:] - extended[:, :, :-1], jnp.zeros_like(extended[:, :, :1])], axis=2
    )
    diff_c = jnp.where(col_index < col_count - 1, diff_c, 0.0)
    magnitude = jnp.sqrt(
        diff_z * diff_z + diff_r * diff_r + diff_c * diff_c + SMOOTH_EPS * SMOOTH_EPS
    )
    unit_z = diff_z / magnitude
    unit_r = diff_r / magnitude
    unit_c = diff_c / magnitude
    back_c = unit_c - jnp.concatenate([jnp.zeros_like(unit_c[:, :, :1]), unit_c[:, :, :-1]], axis=2)
    return (
        unit_z[1:-1, 1:-1]
        - unit_z[:-2, 1:-1]
        + (unit_r[1:-1, 1:-1] - unit_r[1:-1, :-2])
        + back_c[1:-1, 1:-1]
    )


def on_device(measured, drift, start_volume):
    wide_count = lax.axis_size("wide")
    groups = lax.axis_size("grp")
    slab_count, rows_tile, col_count = start_volume.shape
    rows_all = rows_tile * groups
    band_extent = rows_all // 2 + DMAX + 2
    per_device = measured.shape[0]
    total_angles = per_device * wide_count * groups
    global_scale = 1.0 / secant_sum(total_angles)
    z_first = lax.axis_index("wide") * slab_count - 1
    zcount = slab_count * wide_count
    local_measurement = lax.all_to_all(measured, "wide", split_axis=1, concat_axis=0, tiled=True)
    bin_position = jnp.arange(local_measurement.shape[0], dtype=jnp.int32)
    angle_ids = (
        bin_position // per_device * groups + lax.axis_index("grp")
    ) * per_device + bin_position % per_device
    weight_factors, residual_scale = local_geometry(
        angle_ids, drift, total_angles, rows_all, band_extent
    )
    own_tile = start_volume
    r_first = lax.axis_index("grp") * rows_tile - 1
    for sweep in range(ITERS):
        row_band_strip = lax.all_gather(own_tile, "grp", axis=1, tiled=True)
        volume_update = apply_correction(
            row_band_strip,
            local_measurement,
            weight_factors,
            residual_scale,
            global_scale,
            band_extent,
        )
        own_tile = own_tile + lax.psum_scatter(
            volume_update, "grp", scatter_dimension=1, tiled=True
        )
        extended = with_halo(own_tile, (("wide", 0), ("grp", 1)), 1)
        own_tile = own_tile + TV_STEP * divergence(extended, z_first, r_first, zcount, rows_all)
    return own_tile


LANES = 128
SUB = 8
HALO = 64


def tan_and_secant(total_angles):
    angle = TILT_MAX * (2.0 * np.arange(total_angles) / (total_angles - 1) - 1.0)
    return np.tan(angle), 1.0 / np.cos(angle)


def coords():
    wide, y = lax.axis_index("wide"), lax.axis_index("grp")
    return wide // 4, wide // 2 % 2, wide % 2, y


def move(value, target):
    pairs = []
    for z in range(4):
        for x in range(2):
            for c in range(2):
                for y in range(2):
                    tz, tx, tc, ty = target(z, x, c, y)
                    pairs.append((((z * 2 + x) * 2 + c) * 2 + y, ((tz * 2 + tx) * 2 + tc) * 2 + ty))
    return lax.ppermute(value, ("wide", "grp"), pairs)


def beside(z, x, c, y):
    if (z, x) in ((0, 0), (3, 1)):
        return z, x, 1 - c, y
    return (z + 1, 0, c, y) if x else (z - 1, 1, c, y)


def split_rows(value):
    high = value.astype(jnp.bfloat16).astype(jnp.float32)
    return jnp.concatenate([high, value - high], axis=0)


def left_terms(value):
    high = value.astype(jnp.bfloat16).astype(jnp.float32)
    return jnp.concatenate([high, high, value - high], axis=1)


def split_terms(value):
    high = value.astype(jnp.bfloat16)
    low = (value - high.astype(jnp.float32)).astype(jnp.bfloat16)
    return jnp.concatenate([high, low], axis=0)


def right_terms(value):
    high = value.astype(jnp.bfloat16)
    low = (value - high.astype(jnp.float32)).astype(jnp.bfloat16)
    return jnp.concatenate([high, low, high], axis=0)


def lane_iota(shape):
    return lax.broadcasted_iota(jnp.int32, shape, len(shape) - 1)


def row_iota(shape):
    return lax.broadcasted_iota(jnp.int32, shape, len(shape) - 2)


STEP = 3


def view_weights(views, rows, band, scale, tan_ref, drift_ref):
    z, x, c, y = coords()
    first_view = (((z * 2 + x) * 2 + c) * 2 + y) * views
    parts = 2 * band // STEP + 1
    shape = (parts * rows, STEP * views)
    lane, row = lane_iota(shape), row_iota(shape)
    view_of = lane_iota((1, STEP * views)) % views
    tan_lane = jnp.zeros((1, STEP * views), jnp.float32)
    drift_lane = tan_lane
    for a in range(views):
        tan_lane = jnp.where(view_of == a, tan_ref[first_view + a], tan_lane)
        drift_lane = jnp.where(view_of == a, drift_ref[first_view + a].astype(jnp.float32), drift_lane)
    shift = ((row % rows).astype(jnp.float32) - (rows - 1) / 2.0) * tan_lane - drift_lane
    offset = ((row // rows) * STEP + lane // views - band).astype(jnp.float32)
    weights = (scale / rows) * jnp.maximum(0.0, 1.0 - jnp.abs(shift - offset))
    return left_terms(weights).astype(jnp.bfloat16)


def back_project(views, rows, band, weights, load_strip, out_ref, terms):
    count, _, width = terms.shape
    out_cols = out_ref.shape[2]
    parts = 2 * band // STEP + 1
    for n in range(count):
        strip = load_strip(n)
        high = strip.astype(jnp.bfloat16)
        low = (strip - high.astype(jnp.float32)).astype(jnp.bfloat16)
        for j in range(STEP):
            moved = pltpu.roll(high, j, 1) if j else high
            terms[n, j * views : (j + 1) * views] = moved
            terms[n, (STEP + j) * views : (STEP + j + 1) * views] = pltpu.roll(low, j, 1) if j else low
            terms[n, (2 * STEP + j) * views : (2 * STEP + j + 1) * views] = moved
    for n in range(count):
        spread = jnp.dot(weights, terms[n], preferred_element_type=jnp.float32)
        total = None
        for i in range(parts):
            piece = pltpu.roll(spread[i * rows : (i + 1) * rows], width - HALO - band + STEP * i, 1)
            total = piece if total is None else total + piece
        out_ref[n] = total[:, :out_cols]


def depth_partner(z, bits):
    return {0: z, 1: z + 1 - 2 * (z % 2), 2: (z + 2) % 4, 3: 3 - z}[bits]


def slice_place(half, kept, n):
    z, x, _, _ = coords()
    parity = x if kept else 1 - x
    four = depth_partner(z, (1, 0)[n // 4] if kept else (2, 3)[n // 4])
    group = jnp.where(half == 0, n // 4, four // 2)
    place = jnp.where(half == 0, 4 * (n // 2 % 2) + 2 * parity + n % 2, 4 * (four % 2) + n % 4)
    return group, place


def strip_loader(buf, half, kept, views, tiles):
    pitch = (tiles + 2) * SUB

    def load(n):
        group, place = slice_place(half, kept, n)
        first = half * SUB + place
        return jnp.concatenate(
            [buf[group, pl.ds(first + t * SUB, views, stride=pitch), :] for t in range(tiles + 1)], axis=1
        )

    return load


def volume_window(vol_ref, half, half_cols, vbuf):
    part, cols = vol_ref.shape[1:]
    vbuf[:, 0:LANES] = jnp.zeros((part, LANES), jnp.float32)
    vbuf[:, LANES : LANES + cols] = vol_ref[0]
    vbuf[:, LANES + cols :] = jnp.zeros((part, LANES), jnp.float32)
    width = half_cols + 2 * LANES
    window = vbuf[:, pl.ds(pl.multiple_of(half * half_cols, LANES), width)]
    return pltpu.roll(window, width - HALO, 1)[:, : half_cols + LANES]


def fetch_kernel(views, rows, band, scale, tan_hbm, drift_hbm, meas_hbm, vol_hbm, out_ref, sibling_buf, own_buf,
                 weights_ref, vol_ref, tan_ref, drift_ref, terms, table_sem, sem):
    z, _, c, _ = coords()
    tiles = out_ref.shape[2] // LANES
    groups = sibling_buf.shape[0]

    def fetch(half, target, g, semaphore):
        return pltpu.make_async_copy(
            meas_hbm.at[:, g, pl.ds(half * (tiles - 2), tiles)], target.at[g, :, 1 : tiles + 1], semaphore
        )

    tables = [
        pltpu.make_async_copy(tan_hbm, tan_ref, table_sem.at[0]),
        pltpu.make_async_copy(drift_hbm, drift_ref, table_sem.at[1]),
    ]
    vol_copy = pltpu.make_async_copy(vol_hbm, vol_ref, table_sem.at[2])
    soon = jnp.where(c == 0, 1 - z // 2, 0)
    first = [fetch(1 - c, sibling_buf, g, sem.at[0, g]) for g in (soon, 1 - soon)]
    later = [fetch(c, own_buf, g, sem.at[1, g]) for g in range(groups)]
    for copy in tables + first + [vol_copy] + later:
        copy.start()
    zero = jnp.zeros((views, SUB, LANES), jnp.float32)
    for g in range(groups):
        for target in (sibling_buf, own_buf):
            target[g, :, 0] = zero
            target[g, :, tiles + 1] = zero
    for copy in tables:
        copy.wait()
    weights = view_weights(views, rows, band, scale, tan_ref, drift_ref)
    weights_ref[...] = weights.astype(jnp.float32)
    load = strip_loader(flat_rows(sibling_buf), 1 - c, False, views, tiles)

    def load_strip(n):
        if n % 4 == 0:
            first[n // 4].wait()
        return load(n)

    back_project(views, rows, band, weights, load_strip, out_ref, terms)
    vol_copy.wait()
    for copy in later:
        copy.wait()


def flat_rows(buf):
    groups, views, tiles, sub, lanes = buf.shape
    return buf.reshape(groups, views * tiles * sub, lanes)


def sibling_kernel(views, rows, band, buf, weights_ref, vol_ref, out_ref, terms, vbuf):
    _, _, c, _ = coords()
    tiles = out_ref.shape[2] // LANES
    load = strip_loader(flat_rows(buf), 1 - c, True, views, tiles)
    back_project(views, rows, band, weights_ref[...].astype(jnp.bfloat16), load, out_ref, terms)
    count = terms.shape[0]
    half_cols = out_ref.shape[2] - LANES
    part = vol_ref.shape[1]
    out_ref[count, 0:part] = volume_window(vol_ref, 1 - c, half_cols, vbuf)
    out_ref[count, part:] = jnp.zeros((rows - part, half_cols + LANES), jnp.float32)


def own_kernel(kept, views, rows, band, buf, weights_ref, after_ref, out_ref, terms):
    _, _, c, _ = coords()
    tiles = out_ref.shape[2] // LANES
    load = strip_loader(flat_rows(buf), c, kept, views, tiles)
    back_project(views, rows, band, weights_ref[...].astype(jnp.bfloat16), load, out_ref, terms)


def put_quarter(out, acc, py, tiles):
    for n in range(acc.shape[0]):
        for t in range(tiles):
            out[n * tiles + t] = acc[n, :, pl.ds(pl.multiple_of(((tiles - 1) * py + t) * LANES, LANES), LANES)]


def put_four(out, acc, first):
    tiles = acc.shape[2] // LANES
    for n in range(4):
        for t in range(tiles):
            out[n * tiles + t] = acc[first + n, :, t * LANES : (t + 1) * LANES]
    for t in range(4 * tiles, out.shape[0]):
        out[t] = jnp.zeros(out.shape[1:], jnp.float32)


def pass_pack_kernel(own_ref, got_ref, send, acc):
    _, _, c, y = coords()
    acc[...] = own_ref[...] + got_ref[...]

    @pl.when(c == 0)
    def _():
        put_quarter(send, acc, 1 - y, send.shape[0] // acc.shape[0])

    @pl.when(c == 1)
    def _():
        put_four(send, acc, 0)


def keep_pack_kernel(pass_ref, pass_got, own_ref, got_ref, vol_ref, mine, send_2, send_3, vol_mine, vol_to_y,
                     passed, acc, both, vbuf):
    count, rows, half_width = own_ref.shape
    tiles = mine.shape[0] // count
    part = vol_ref.shape[1]
    _, _, c, y = coords()
    passed[...] = pass_ref[...] + pass_got[...]
    acc[...] = own_ref[...] + got_ref[0:count]

    @pl.when(c == 0)
    def _():
        put_quarter(send_2, passed, y, tiles)
        put_quarter(send_3, acc, 1 - y, tiles)
        put_quarter(mine, acc, y, tiles)

    @pl.when(c == 1)
    def _():
        put_four(send_2, passed, 4)
        put_four(send_3, acc, 0)
        put_four(mine, acc, 4)

    here = volume_window(vol_ref, c, half_width - LANES, vbuf)
    there = got_ref[count, 0:part]
    both[0:part] = jnp.where(c == 0, here, there)
    both[part:] = jnp.where(c == 0, there, here)
    width = tiles * LANES
    for vol, py in ((vol_mine, y), (vol_to_y, 1 - y)):
        vol[...] = both[:, pl.ds(pl.multiple_of(py * (width - LANES), LANES), width)]


def middle_pack_kernel(mine, got_1, got_2, got_3, own_pair, send_1, send_2, send_3, acc):
    z, x, c, y = coords()
    tiles = own_pair.shape[2] // LANES
    half_tiles = 2 * tiles - 1
    acc[...] = (mine[...] + got_1[...]) + (got_2[...] + got_3[...])

    def put(out, first, pitch):
        for i in range(2):
            for t in range(tiles):
                out[i, :, t * LANES : (t + 1) * LANES] = acc[first + i * pitch + t]

    for out, bits, px, py in ((own_pair, 0, x, y), (send_1, 3, 1 - x, 1 - y), (send_2, 2, 1 - x, y), (send_3, 1, x, 1 - y)):
        depth_first = 2 * tiles * depth_partner(z, bits)
        plane_first = 2 * half_tiles * px + (tiles - 1) * py
        put(out, jnp.where(c == 0, depth_first, plane_first), jnp.where(c == 0, tiles, half_tiles))


def gram_kernel(rows, band, scale, tan_ref, sec_ref, drift_ref, after_ref, conv_ref, low_ref, high_ref):
    views = tan_ref.shape[1]
    span = 2 * band + 1
    shape = (span * rows, views)
    row = row_iota(shape)
    shift = ((row % rows).astype(jnp.float32) - (rows - 1) / 2.0) * tan_ref[...] - drift_ref[...].astype(jnp.float32)
    hat = jnp.maximum(0.0, 1.0 - jnp.abs(shift - (row // rows - band).astype(jnp.float32)))
    gram = lax.dot_general(
        hat * ((scale / rows) * sec_ref[...]),
        hat,
        (((1,), (1,)), ((), ())),
        precision=lax.Precision.HIGHEST,
        preferred_element_type=jnp.float32,
    )
    edge = band * rows
    low_ref[...] = left_terms(gram[edge + rows :, edge + rows :])
    high_ref[...] = left_terms(gram[:edge, :edge])
    width = conv_ref.shape[1] // 2 * 3
    padded = jnp.concatenate([gram, jnp.zeros((span * rows, width - span * rows), jnp.float32)], axis=1)
    total = jnp.zeros((rows, width), jnp.float32)
    for k in range(span):
        total = total + pltpu.roll(padded[k * rows : (k + 1) * rows], rows * (2 * band - k), 1)
    lanes = width // 3
    stacked = jnp.concatenate([total[:, i * lanes : (i + 1) * lanes] for i in range(3)], axis=0)
    stacked = split_rows(stacked)
    conv_ref[...] = jnp.concatenate([stacked, stacked], axis=1)


def normal(volumes, conv, low_ref, high_ref, band, is_low, is_high):
    rows, width = volumes[0].shape
    step = conv.shape[1] // 2 // rows
    parts = conv.shape[0] // 2 // rows
    beyond = beyond_ends(volumes, low_ref, high_ref, band, is_low, is_high)
    zero = jnp.zeros((rows, width - 2 * LANES), jnp.float32)
    result = []
    for volume, piece in zip(volumes, beyond):
        moved = jnp.concatenate([pltpu.roll(volume, (2 * band - j) % width, 1) for j in range(step)], axis=0)
        spread = jnp.dot(conv, split_terms(moved), preferred_element_type=jnp.float32)
        spread = spread[: parts * rows] + spread[parts * rows :]
        total = spread[0:rows]
        for i in range(1, parts):
            total = total + pltpu.roll(spread[i * rows : (i + 1) * rows], width - step * i, 1)
        ends = [jnp.where(is_low, piece, 0.0), zero, jnp.where(is_high, piece, 0.0)]
        result.append(total - jnp.concatenate(ends, axis=1))
    return result


def beyond_ends(volumes, low_ref, high_ref, band, is_low, is_high):
    rows, width = volumes[0].shape
    pitch = LANES // len(volumes)
    lane = lane_iota((rows, LANES))
    packed = jnp.zeros((rows, LANES), jnp.float32)
    for s, volume in enumerate(volumes):
        tile = jnp.where(is_low, volume[:, :LANES], volume[:, width - LANES :])
        inside = (lane >= s * pitch) & (lane < s * pitch + 2 * band)
        packed = jnp.where(inside, pltpu.roll(tile, (s * pitch - (HALO - band)) % LANES, 1), packed)
    offsets = [jnp.where(is_low, i + 1, LANES + i - band) for i in range(band)]
    moved = jnp.concatenate([pltpu.roll(packed, LANES - k, 1) for k in offsets], axis=0)
    matrix = jnp.where(is_low, low_ref[...], high_ref[...]).astype(jnp.bfloat16)
    spread = jnp.dot(matrix, right_terms(moved), preferred_element_type=jnp.float32)
    place = lane % pitch - jnp.where(is_low, 0, band)
    total = jnp.zeros((rows, LANES), jnp.float32)
    for i, k in enumerate(offsets):
        piece = jnp.where((place >= 0) & (place < band), spread[i * rows : (i + 1) * rows], 0.0)
        total = total + pltpu.roll(piece, k, 1)
    near = (lane >= HALO - band) & (lane < HALO + band)
    return [
        jnp.where(near, pltpu.roll(total, (HALO - band - s * pitch) % LANES, 1), 0.0) for s in range(len(volumes))
    ]


def block_place(width, total_cols):
    z, x, c, y = coords()
    block = width - 2 * HALO
    index = c * 2 + y
    return index * block - HALO, index == 0, index == total_cols // block - 1


def first_normal_kernel(band, total_cols, vol_mine, vol_got, conv_ref, low_ref, high_ref, out):
    _, is_low, is_high = block_place(vol_mine.shape[1], total_cols)
    _, _, _, y = coords()
    part = vol_mine.shape[0] // 2
    here, there = vol_mine[...], vol_got[...]
    upper = jnp.where(y == 0, here, there)
    lower = jnp.where(y == 0, there, here)
    volumes = [
        jnp.concatenate([upper[i * part : (i + 1) * part], lower[i * part : (i + 1) * part]], axis=0) for i in range(2)
    ]
    back = normal(volumes, conv_ref[...].astype(jnp.bfloat16), low_ref, high_ref, band, is_low, is_high)
    for i in range(2):
        out[i] = volumes[i] - back[i]


def half_pair_kernel(first_ref, own_pair, got_1, got_2, got_3, mine, to_x, to_diag, corr):
    _, x, _, _ = coords()
    corr[...] = (own_pair[...] + got_1[...]) + (got_2[...] + got_3[...])
    half = first_ref[...] + corr[...]
    mine[0:2] = half
    mine[2:4] = corr[...]
    to_x[0:2] = half
    to_x[2] = corr[1 - x]
    to_diag[0:2] = half
    to_diag[2] = corr[x]


def variation_step(half, z_of, first_col, depth, total_cols):
    rows, width = half[0].shape
    col = first_col + lane_iota((rows, width))
    row = row_iota((rows, width))
    inside = (col >= 0) & (col < total_cols - 1)
    units = []
    for w in range(len(half) - 1):
        v = half[w]
        keep = (z_of(w) >= 0) & (z_of(w) < depth - 1)
        dz = jnp.where(keep, half[w + 1] - v, 0.0)
        dr = jnp.where(row < rows - 1, pltpu.roll(v, rows - 1, 0) - v, 0.0)
        dc = jnp.where(inside, pltpu.roll(v, width - 1, 1) - v, 0.0)
        inverse = lax.rsqrt(dz * dz + dr * dr + dc * dc + SMOOTH_EPS * SMOOTH_EPS)
        units.append((dz * inverse, dr * inverse, dc * inverse))
    result = []
    for w in range(1, len(half) - 1):
        uz, ur, uc = units[w]
        div = (uz - units[w - 1][0]) + (ur - pltpu.roll(ur, 1, 0)) + (uc - pltpu.roll(uc, 1, 1))
        result.append(jnp.where((col >= 0) & (col < total_cols), half[w] + TV_STEP * div, 0.0))
    return result


def finish_kernel(
    band, depth, total_cols, mine, got_diag, got_x, conv_ref, low_ref, high_ref, keep_ref, send_ref, done
):
    width = mine.shape[2]
    first_col, is_low, is_high = block_place(width, total_cols)
    z, x, c, _ = coords()
    before = [jnp.where(x == 0, got_diag[i], got_x[i]) for i in range(3)]
    after = [jnp.where(x == 0, got_x[i], got_diag[i]) for i in range(3)]
    half = [before[0], before[1], mine[0], mine[1], after[0], after[1]]
    corr = [before[2], mine[2], mine[3], after[2]]
    slice_0 = 4 * z + 2 * x
    volumes = variation_step(half, lambda w: slice_0 - 2 + w, first_col, depth, total_cols)
    back = normal(volumes, conv_ref[...].astype(jnp.bfloat16), low_ref, high_ref, band, is_low, is_high)
    half = [volumes[s] + corr[s] - back[s] for s in range(4)]
    volumes = variation_step(half, lambda w: slice_0 - 1 + w, first_col, depth, total_cols)
    for s in range(2):
        done[s] = pltpu.roll(volumes[s], width - HALO, 1)[:, : width - LANES]
    keep_ref[...] = done[c]
    send_ref[...] = done[1 - c]


def result_pack_kernel(own_ref, got_ref, to_y):
    _, _, c, y = coords()
    part = to_y.shape[1]
    own, got = own_ref[...], got_ref[...]
    to_y[c] = jnp.where(y == 0, own[part:], own[:part])
    to_y[1 - c] = jnp.where(y == 0, got[part:], got[:part])


def result_kernel(own_ref, got_ref, got_y, out):
    _, _, c, y = coords()
    _, part, block = got_y.shape
    own, got = own_ref[...], got_ref[...]
    here = jnp.where(y == 0, own[:part], own[part:])
    there = jnp.where(y == 0, got[:part], got[part:])
    for value, h, q in ((here, c, y), (there, 1 - c, y), (got_y[0], 0, 1 - y), (got_y[1], 1, 1 - y)):
        out[0, :, pl.ds(pl.multiple_of((2 * h + q) * block, LANES), block)] = value


def f32(*shape):
    return jax.ShapeDtypeStruct(shape, jnp.float32)


VMEM_SPEC = pl.BlockSpec(memory_space=pltpu.VMEM)
SMEM_SPEC = pl.BlockSpec(memory_space=pltpu.SMEM)
ANY_SPEC = pl.BlockSpec(memory_space=pl.ANY)
HBM_SPEC = pl.BlockSpec(memory_space=pltpu.HBM)
PARAMS = pltpu.CompilerParams(vmem_limit_bytes=40 * 1024 * 1024)


def in_hbm(value):
    return pltpu.with_memory_space_constraint(value, pltpu.HBM)


def kernel_call(body, outs, in_specs, scratch, name, flops=0, size=0):
    many = isinstance(outs, (list, tuple))
    return pl.pallas_call(
        body,
        out_shape=outs,
        in_specs=in_specs,
        out_specs=[VMEM_SPEC] * len(outs) if many else VMEM_SPEC,
        scratch_shapes=scratch,
        compiler_params=PARAMS,
        name=name,
        cost_estimate=pl.CostEstimate(flops=flops, bytes_accessed=size, transcendentals=0),
    )


def summed_plan(measured, drift, start_volume):
    views, slices, cols = measured.shape
    part = start_volume.shape[1]
    rows = 2 * part
    band = rows // 2 + DMAX + 2
    total_angles = drift.shape[0]
    half_cols = cols // 2
    half_width = half_cols + LANES
    width = cols // 4 + 2 * HALO
    tangent, secant = tan_and_secant(total_angles)
    scale = float(1.0 / np.sum(secant))
    tangent, secant = tangent.astype(np.float32), secant.astype(np.float32)

    tiles = half_width // LANES
    groups = slices // SUB
    window = (groups, views, tiles + 2, SUB, LANES)
    tiled = measured.reshape(views, groups, SUB, cols // LANES, LANES).transpose(0, 1, 3, 2, 4)
    table = ((2 * band // STEP + 1) * rows, 3 * STEP * views)
    count = slices // 2
    terms = pltpu.VMEM((count, 3 * STEP * views, half_width + LANES), jnp.bfloat16)
    vbuf = pltpu.VMEM((part, cols + 2 * LANES), jnp.float32)
    half_of = f32(count, rows, half_width)
    half_and = f32(count + 1, rows, half_width)
    across = lambda z, x, c, y: (z, x, 1 - c, y)

    pass_sibling, sibling_buf, own_buf, weights, volume = kernel_call(
        functools.partial(fetch_kernel, views, rows, band, scale),
        [half_of, f32(*window), f32(*window), f32(*table), f32(1, part, cols)],
        [HBM_SPEC] * 4,
        [
            pltpu.SMEM((total_angles,), jnp.float32),
            pltpu.SMEM((total_angles,), jnp.int32),
            terms,
            pltpu.SemaphoreType.DMA((3,)),
            pltpu.SemaphoreType.DMA((2, groups)),
        ],
        "pass_sibling",
        flops=10**9,
    )(in_hbm(jnp.asarray(tangent)), in_hbm(drift), in_hbm(tiled), in_hbm(start_volume))
    pass_got = move(pass_sibling, across)
    keep_sibling = kernel_call(
        functools.partial(sibling_kernel, views, rows, band),
        half_and,
        [VMEM_SPEC] * 3,
        [terms, vbuf],
        "keep_sibling",
        flops=10**9,
    )(sibling_buf, weights, volume)
    keep_got = move(keep_sibling, across)

    def own(kept, after):
        return kernel_call(
            functools.partial(own_kernel, kept, views, rows, band),
            half_of,
            [VMEM_SPEC] * 2 + [ANY_SPEC],
            [terms],
            "keep_own" if kept else "pass_own",
            flops=10**9,
        )(own_buf, weights, after)

    message = f32(count * width // LANES, rows, LANES)
    pass_own = own(False, keep_sibling)
    send_1 = kernel_call(pass_pack_kernel, message, [VMEM_SPEC] * 2, [pltpu.VMEM(half_of.shape, jnp.float32)], "pass_pack")(
        pass_own, pass_got
    )
    got_1 = move(send_1, lambda z, x, c, y: (z ^ 2, x, c, y) if c else (z, 1 - x, c, 1 - y))
    mine, send_2, send_3, vol_mine, vol_to_y = kernel_call(
        keep_pack_kernel,
        [message] * 3 + [f32(rows, width)] * 2,
        [VMEM_SPEC] * 5,
        [pltpu.VMEM(half_of.shape, jnp.float32)] * 2 + [pltpu.VMEM((rows, half_width), jnp.float32), vbuf],
        "keep_pack",
    )(pass_own, pass_got, own(True, send_1), keep_got, volume)
    got_2 = move(send_2, lambda z, x, c, y: (z ^ 3, x, c, y) if c else (z, 1 - x, c, y))
    got_3 = move(send_3, lambda z, x, c, y: (z ^ 1, x, c, y) if c else (z, x, c, 1 - y))
    vol_got = move(vol_to_y, lambda z, x, c, y: (z, x, c, 1 - y))

    edge = band * rows
    conv, low, high = kernel_call(
        functools.partial(gram_kernel, rows, band, scale),
        [f32(6 * rows, 2 * LANES), f32(edge, 3 * edge), f32(edge, 3 * edge)],
        [VMEM_SPEC] * 3 + [ANY_SPEC],
        [],
        "gram",
    )(tangent[None], secant[None], drift[None], mine)

    pair = f32(2, rows, width)
    own_pair, send_1, send_2, send_3 = kernel_call(
        middle_pack_kernel,
        [pair] * 4,
        [VMEM_SPEC] * 4,
        [pltpu.VMEM(message.shape, jnp.float32)],
        "middle_pack",
    )(mine, got_1, got_2, got_3)
    got_1 = move(send_1, lambda z, x, c, y: (z, 1 - x, c, 1 - y) if c else (z ^ 3, x, c, y))
    got_2 = move(send_2, lambda z, x, c, y: (z, 1 - x, c, y) if c else (z ^ 2, x, c, y))
    got_3 = move(send_3, lambda z, x, c, y: (z, x, c, 1 - y) if c else (z ^ 1, x, c, y))

    first = kernel_call(
        functools.partial(first_normal_kernel, band, cols),
        pair,
        [VMEM_SPEC] * 5,
        [],
        "first_normal",
        flops=10**9,
    )(vol_mine, vol_got, conv, low, high)

    three = f32(3, rows, width)
    mine, to_x, to_diag = kernel_call(
        half_pair_kernel,
        [f32(4, rows, width), three, three],
        [VMEM_SPEC] * 5,
        [pltpu.VMEM((2, rows, width), jnp.float32)],
        "half_pair",
    )(first, own_pair, got_1, got_2, got_3)
    got_diag = move(to_diag, beside)
    got_x = move(to_x, lambda z, x, c, y: (z, 1 - x, c, y))

    block = width - 2 * HALO
    quarter = f32(rows, block)
    keep, send = kernel_call(
        functools.partial(finish_kernel, band, slices, cols),
        [quarter, quarter],
        [VMEM_SPEC] * 6,
        [pltpu.VMEM((2, rows, block), jnp.float32)],
        "finish",
    )(mine, got_diag, got_x, conv, low, high)
    swapped = move(send, lambda z, x, c, y: (z, x, 1 - c, y))
    to_y = kernel_call(result_pack_kernel, f32(2, part, block), [VMEM_SPEC] * 2, [], "result_pack")(keep, swapped)
    got_y = move(to_y, lambda z, x, c, y: (z, x, c, 1 - y))
    return kernel_call(result_kernel, f32(1, part, cols), [VMEM_SPEC] * 3, [], "result")(keep, swapped, got_y)


def summed_plan_fits(mesh, measured, start_volume):
    rows = start_volume.shape[1]
    cols = measured.shape[2]
    return (
        ITERS == 2
        and dict(mesh.shape) == {"wide": 16, "grp": 2}
        and measured.shape[1] == start_volume.shape[0] == 16
        and rows == SUB
        and cols % (16 * LANES) == 0
        and measured.shape[0] % 256 == 0
    )


def solution(mesh):
    in_specs = (P(("wide", "grp"), None, None), P(), P("wide", "grp", None))
    out_specs = P("wide", "grp", None)

    def run(measured, drift, start_volume):
        plan = summed_plan if summed_plan_fits(mesh, measured, start_volume) else on_device
        return jax.shard_map(plan, mesh=mesh, in_specs=in_specs, out_specs=out_specs, check_vma=False)(
            measured, drift, start_volume
        )

    return run
```

```python
import functools
from functools import reduce
import math

import jax
import jax.numpy as jnp
import numpy as np
from jax import lax
from jax.experimental import pallas as pl
from jax.experimental.pallas import tpu as pltpu
from jax.sharding import PartitionSpec as P

ITERS = 2
DMAX = 4


TILT_MAX = math.pi / 4
SMOOTH_EPS = 0.05
TV_STEP = 0.1


def with_halo(block, sides, width):
    for axis, dim in sides:
        count = lax.axis_size(axis)
        forward = [(i, i + 1) for i in range(count - 1)]
        backward = [(target, source) for source, target in forward]
        low = lax.ppermute(
            lax.slice_in_dim(block, block.shape[dim] - width, None, axis=dim), axis, forward
        )
        high = lax.ppermute(lax.slice_in_dim(block, 0, width, axis=dim), axis, backward)
        block = jnp.concatenate([low, block, high], axis=dim)
    return block


def geometry(angle_ids, drift_vals, total_angles, rows, band_extent):
    angle_rad = TILT_MAX * (2.0 * angle_ids.astype(jnp.float32) / (total_angles - 1) - 1.0)
    secant = 1.0 / jnp.cos(angle_rad)
    height = jnp.arange(rows, dtype=jnp.float32) - (rows - 1) / 2.0
    offsets = jnp.arange(2 * band_extent + 1, dtype=jnp.float32) - band_extent
    shifts = height[None, :] * jnp.tan(angle_rad)[:, None] - drift_vals.astype(jnp.float32)[:, None]
    weight_factors = secant[:, None, None] * jnp.maximum(
        0.0, 1.0 - jnp.abs(shifts[:, :, None] - offsets[None, None, :])
    )
    return (weight_factors, jnp.cos(angle_rad) / rows)


def secant_sum(total_angles):
    angle_rad = TILT_MAX * (
        2.0 * jnp.arange(total_angles, dtype=jnp.float32) / (total_angles - 1) - 1.0
    )
    return jnp.sum(1.0 / jnp.cos(angle_rad))


def local_geometry(angle_ids, drift, total_angles, rows_all, band_extent):
    matches = angle_ids[:, None] == jnp.arange(total_angles, dtype=jnp.int32)[None, :]
    local_drift = jnp.sum(jnp.where(matches, drift[None, :], 0), axis=1)
    return geometry(angle_ids, local_drift, total_angles, rows_all, band_extent)


def apply_correction(
    row_band_strip, measurement_part, weight_factors, residual_scale, global_scale, band_extent
):
    col_count = row_band_strip.shape[2]
    span = 2 * band_extent + 1
    padded = jnp.pad(row_band_strip, ((0, 0), (0, 0), (band_extent, band_extent)))
    shifted = jnp.stack(
        [padded[:, :, shift_id : shift_id + col_count] for shift_id in range(span)], axis=2
    )
    forward_projected = jnp.einsum(
        "ark,zrku->azu", weight_factors, shifted, precision=lax.Precision.HIGHEST
    )
    residual_error = residual_scale[:, None, None] * (measurement_part - forward_projected)
    spread = jnp.einsum(
        "ark,azu->kzru", weight_factors, residual_error, precision=lax.Precision.HIGHEST
    )
    spread = jnp.pad(spread, ((0, 0), (0, 0), (0, 0), (band_extent, band_extent)))
    pieces = [
        spread[shift_id, :, :, 2 * band_extent - shift_id : 2 * band_extent - shift_id + col_count]
        for shift_id in range(span)
    ]
    return global_scale * reduce(lambda left, right: left + right, pieces)


def divergence(extended, z_first, r_first, zcount, rcount):
    plane_count, height, col_count = extended.shape
    z_index = z_first + jnp.arange(plane_count, dtype=jnp.int32)[:, None, None]
    row_index = r_first + jnp.arange(height, dtype=jnp.int32)[None, :, None]
    col_index = jnp.arange(col_count, dtype=jnp.int32)[None, None, :]
    diff_z = jnp.concatenate([extended[1:] - extended[:-1], jnp.zeros_like(extended[:1])], axis=0)
    diff_z = jnp.where((z_index >= 0) & (z_index < zcount - 1), diff_z, 0.0)
    diff_r = jnp.concatenate(
        [extended[:, 1:] - extended[:, :-1], jnp.zeros_like(extended[:, :1])], axis=1
    )
    diff_r = jnp.where((row_index >= 0) & (row_index < rcount - 1), diff_r, 0.0)
    diff_c = jnp.concatenate(
        [extended[:, :, 1:] - extended[:, :, :-1], jnp.zeros_like(extended[:, :, :1])], axis=2
    )
    diff_c = jnp.where(col_index < col_count - 1, diff_c, 0.0)
    magnitude = jnp.sqrt(
        diff_z * diff_z + diff_r * diff_r + diff_c * diff_c + SMOOTH_EPS * SMOOTH_EPS
    )
    unit_z = diff_z / magnitude
    unit_r = diff_r / magnitude
    unit_c = diff_c / magnitude
    back_c = unit_c - jnp.concatenate([jnp.zeros_like(unit_c[:, :, :1]), unit_c[:, :, :-1]], axis=2)
    return (
        unit_z[1:-1, 1:-1]
        - unit_z[:-2, 1:-1]
        + (unit_r[1:-1, 1:-1] - unit_r[1:-1, :-2])
        + back_c[1:-1, 1:-1]
    )


def on_device(measured, drift, start_volume):
    wide_count = lax.axis_size("wide")
    groups = lax.axis_size("grp")
    slab_count, rows_tile, col_count = start_volume.shape
    rows_all = rows_tile * groups
    band_extent = rows_all // 2 + DMAX + 2
    per_device = measured.shape[0]
    total_angles = per_device * wide_count * groups
    global_scale = 1.0 / secant_sum(total_angles)
    z_first = lax.axis_index("wide") * slab_count - 1
    zcount = slab_count * wide_count
    local_measurement = lax.all_to_all(measured, "wide", split_axis=1, concat_axis=0, tiled=True)
    bin_position = jnp.arange(local_measurement.shape[0], dtype=jnp.int32)
    angle_ids = (
        bin_position // per_device * groups + lax.axis_index("grp")
    ) * per_device + bin_position % per_device
    weight_factors, residual_scale = local_geometry(
        angle_ids, drift, total_angles, rows_all, band_extent
    )
    own_tile = start_volume
    r_first = lax.axis_index("grp") * rows_tile - 1
    for sweep in range(ITERS):
        row_band_strip = lax.all_gather(own_tile, "grp", axis=1, tiled=True)
        volume_update = apply_correction(
            row_band_strip,
            local_measurement,
            weight_factors,
            residual_scale,
            global_scale,
            band_extent,
        )
        own_tile = own_tile + lax.psum_scatter(
            volume_update, "grp", scatter_dimension=1, tiled=True
        )
        extended = with_halo(own_tile, (("wide", 0), ("grp", 1)), 1)
        own_tile = own_tile + TV_STEP * divergence(extended, z_first, r_first, zcount, rows_all)
    return own_tile


LANES = 128
SUB = 8
HALO = 64


def tan_and_secant(total_angles):
    angle = TILT_MAX * (2.0 * np.arange(total_angles) / (total_angles - 1) - 1.0)
    return np.tan(angle), 1.0 / np.cos(angle)


def coords():
    wide, y = lax.axis_index("wide"), lax.axis_index("grp")
    return wide // 4, wide // 2 % 2, wide % 2, y


def move(value, target):
    pairs = []
    for z in range(4):
        for x in range(2):
            for c in range(2):
                for y in range(2):
                    tz, tx, tc, ty = target(z, x, c, y)
                    pairs.append((((z * 2 + x) * 2 + c) * 2 + y, ((tz * 2 + tx) * 2 + tc) * 2 + ty))
    return lax.ppermute(value, ("wide", "grp"), pairs)


def beside(z, x, c, y):
    if (z, x) in ((0, 0), (3, 1)):
        return z, x, 1 - c, y
    return (z + 1, 0, c, y) if x else (z - 1, 1, c, y)


def split_rows(value):
    high = value.astype(jnp.bfloat16).astype(jnp.float32)
    return jnp.concatenate([high, value - high], axis=0)


def left_terms(value):
    high = value.astype(jnp.bfloat16).astype(jnp.float32)
    return jnp.concatenate([high, high, value - high], axis=1)


def split_terms(value):
    high = value.astype(jnp.bfloat16)
    low = (value - high.astype(jnp.float32)).astype(jnp.bfloat16)
    return jnp.concatenate([high, low], axis=0)


def right_terms(value):
    high = value.astype(jnp.bfloat16)
    low = (value - high.astype(jnp.float32)).astype(jnp.bfloat16)
    return jnp.concatenate([high, low, high], axis=0)


def lane_iota(shape):
    return lax.broadcasted_iota(jnp.int32, shape, len(shape) - 1)


def row_iota(shape):
    return lax.broadcasted_iota(jnp.int32, shape, len(shape) - 2)


STEP = 3


def view_weights(views, rows, band, scale, tan_ref, drift_ref):
    z, x, c, y = coords()
    first_view = (((z * 2 + x) * 2 + c) * 2 + y) * views
    parts = 2 * band // STEP + 1
    shape = (parts * rows, STEP * views)
    lane, row = lane_iota(shape), row_iota(shape)
    view_of = lane_iota((1, STEP * views)) % views
    tan_lane = jnp.zeros((1, STEP * views), jnp.float32)
    drift_lane = tan_lane
    for a in range(views):
        tan_lane = jnp.where(view_of == a, tan_ref[first_view + a], tan_lane)
        drift_lane = jnp.where(view_of == a, drift_ref[first_view + a].astype(jnp.float32), drift_lane)
    shift = ((row % rows).astype(jnp.float32) - (rows - 1) / 2.0) * tan_lane - drift_lane
    offset = ((row // rows) * STEP + lane // views - band).astype(jnp.float32)
    weights = (scale / rows) * jnp.maximum(0.0, 1.0 - jnp.abs(shift - offset))
    return left_terms(weights).astype(jnp.bfloat16)


def back_project(views, rows, band, weights, load_strip, begin, out_ref, terms):
    count, _, width = terms.shape[0] // 2, *terms.shape[1:]
    out_cols = out_ref.shape[2]
    parts = 2 * band // STEP + 1
    for n in range(count):
        strip = load_strip(n)
        high = strip.astype(jnp.bfloat16)
        low = (strip - high.astype(jnp.float32)).astype(jnp.bfloat16)
        for j in range(STEP):
            moved = pltpu.roll(high, j, 1) if j else high
            terms[begin + n, j * views : (j + 1) * views] = moved
            terms[begin + n, (STEP + j) * views : (STEP + j + 1) * views] = pltpu.roll(low, j, 1) if j else low
            terms[begin + n, (2 * STEP + j) * views : (2 * STEP + j + 1) * views] = moved
    for n in range(count):
        spread = jnp.dot(weights, terms[begin + n], preferred_element_type=jnp.float32)
        total = None
        for i in range(parts):
            piece = pltpu.roll(spread[i * rows : (i + 1) * rows], width - HALO - band + STEP * i, 1)
            total = piece if total is None else total + piece
        out_ref[begin + n] = total[:, :out_cols]


def depth_partner(z, bits):
    return {0: z, 1: z + 1 - 2 * (z % 2), 2: (z + 2) % 4, 3: 3 - z}[bits]


def slice_place(half, kept, n):
    z, x, _, _ = coords()
    parity = x if kept else 1 - x
    four = depth_partner(z, (1, 0)[n // 4] if kept else (2, 3)[n // 4])
    group = jnp.where(half == 0, n // 4, four // 2)
    place = jnp.where(half == 0, 4 * (n // 2 % 2) + 2 * parity + n % 2, 4 * (four % 2) + n % 4)
    return group, place


def strip_loader(buf, half, kept, views, tiles):
    pitch = (tiles + 2) * SUB

    def load(n):
        group, place = slice_place(half, kept, n)
        first = half * SUB + place
        return jnp.concatenate(
            [buf[group, pl.ds(first + t * SUB, views, stride=pitch), :] for t in range(tiles + 1)], axis=1
        )

    return load


def volume_window(vol_ref, half, half_cols, vbuf):
    part, cols = vol_ref.shape[1:]
    vbuf[:, 0:LANES] = jnp.zeros((part, LANES), jnp.float32)
    vbuf[:, LANES : LANES + cols] = vol_ref[0]
    vbuf[:, LANES + cols :] = jnp.zeros((part, LANES), jnp.float32)
    width = half_cols + 2 * LANES
    window = vbuf[:, pl.ds(pl.multiple_of(half * half_cols, LANES), width)]
    return pltpu.roll(window, width - HALO, 1)[:, : half_cols + LANES]


def fetch_kernel(views, rows, band, scale, tan_hbm, drift_hbm, meas_hbm, vol_hbm, out_ref, own_buf, weights_ref, vol_ref,
                 tan_ref, drift_ref, sibling_buf, terms, vbuf, table_sem, sem):
    z, _, c, _ = coords()
    tiles = out_ref.shape[2] // LANES
    groups = sibling_buf.shape[0]

    def fetch(half, target, g, semaphore):
        return pltpu.make_async_copy(
            meas_hbm.at[:, g, pl.ds(half * (tiles - 2), tiles)], target.at[g, :, 1 : tiles + 1], semaphore
        )

    tables = [
        pltpu.make_async_copy(tan_hbm, tan_ref, table_sem.at[0]),
        pltpu.make_async_copy(drift_hbm, drift_ref, table_sem.at[1]),
    ]
    vol_copy = pltpu.make_async_copy(vol_hbm, vol_ref, table_sem.at[2])
    soon = jnp.where(c == 0, 1 - z // 2, 0)
    first = [fetch(1 - c, sibling_buf, g, sem.at[0, g]) for g in (soon, 1 - soon)]
    later = [fetch(c, own_buf, g, sem.at[1, g]) for g in range(groups)]
    for copy in tables + first + [vol_copy] + later:
        copy.start()
    zero = jnp.zeros((views, SUB, LANES), jnp.float32)
    for g in range(groups):
        for target in (sibling_buf, own_buf):
            target[g, :, 0] = zero
            target[g, :, tiles + 1] = zero
    for copy in tables:
        copy.wait()
    weights = view_weights(views, rows, band, scale, tan_ref, drift_ref)
    weights_ref[...] = weights.astype(jnp.float32)
    load, load_kept = (strip_loader(flat_rows(sibling_buf), 1 - c, kept, views, tiles) for kept in (False, True))

    def load_strip(n):
        if n % 4 == 0:
            first[n // 4].wait()
        return load(n)

    count = terms.shape[0] // 2
    back_project(views, rows, band, weights, load_strip, 0, out_ref, terms)
    back_project(views, rows, band, weights, load_kept, count, out_ref, terms)
    vol_copy.wait()
    half_cols = out_ref.shape[2] - LANES
    part = vol_ref.shape[1]
    out_ref[2 * count, 0:part] = volume_window(vol_ref, 1 - c, half_cols, vbuf)
    out_ref[2 * count, part:] = jnp.zeros((rows - part, half_cols + LANES), jnp.float32)
    for copy in later:
        copy.wait()


def flat_rows(buf):
    groups, views, tiles, sub, lanes = buf.shape
    return buf.reshape(groups, views * tiles * sub, lanes)


def own_kernel(views, rows, band, buf, weights_ref, out_ref, terms):
    _, _, c, _ = coords()
    tiles = out_ref.shape[2] // LANES
    weights = weights_ref[...].astype(jnp.bfloat16)
    for kept in (False, True):
        load = strip_loader(flat_rows(buf), c, kept, views, tiles)
        back_project(views, rows, band, weights, load, terms.shape[0] // 2 if kept else 0, out_ref, terms)


def put_quarter(out, acc, py, tiles):
    for n in range(acc.shape[0]):
        for t in range(tiles):
            out[n * tiles + t] = acc[n, :, pl.ds(pl.multiple_of(((tiles - 1) * py + t) * LANES, LANES), LANES)]


def put_four(out, acc, first):
    tiles = acc.shape[2] // LANES
    for n in range(4):
        for t in range(tiles):
            out[n * tiles + t] = acc[first + n, :, t * LANES : (t + 1) * LANES]
    for t in range(4 * tiles, out.shape[0]):
        out[t] = jnp.zeros(out.shape[1:], jnp.float32)


def plane_pack_kernel(own_ref, got_ref, vol_ref, mine, send_1, send_2, send_3, vol_mine, vol_to_y,
                     passed, acc, both, vbuf):
    count, _, half_width = passed.shape
    tiles = mine.shape[0] // count
    part = vol_ref.shape[1]
    _, _, c, y = coords()
    passed[...] = own_ref[0:count] + got_ref[0:count]
    acc[...] = own_ref[count:] + got_ref[count : 2 * count]

    @pl.when(c == 0)
    def _():
        put_quarter(send_1, passed, 1 - y, tiles)
        put_quarter(send_2, passed, y, tiles)
        put_quarter(send_3, acc, 1 - y, tiles)
        put_quarter(mine, acc, y, tiles)

    @pl.when(c == 1)
    def _():
        put_four(send_1, passed, 0)
        put_four(send_2, passed, 4)
        put_four(send_3, acc, 0)
        put_four(mine, acc, 4)

    here = volume_window(vol_ref, c, half_width - LANES, vbuf)
    there = got_ref[2 * count, 0:part]
    both[0:part] = jnp.where(c == 0, here, there)
    both[part:] = jnp.where(c == 0, there, here)
    width = tiles * LANES
    for vol, py in ((vol_mine, y), (vol_to_y, 1 - y)):
        vol[...] = both[:, pl.ds(pl.multiple_of(py * (width - LANES), LANES), width)]


def middle_pack_kernel(mine, got_1, got_2, got_3, own_pair, send_1, send_2, send_3, acc):
    z, x, c, y = coords()
    tiles = own_pair.shape[2] // LANES
    half_tiles = 2 * tiles - 1
    acc[...] = (mine[...] + got_1[...]) + (got_2[...] + got_3[...])

    def put(out, first, pitch):
        for i in range(2):
            for t in range(tiles):
                out[i, :, t * LANES : (t + 1) * LANES] = acc[first + i * pitch + t]

    for out, bits, px, py in ((own_pair, 0, x, y), (send_1, 3, 1 - x, 1 - y), (send_2, 2, 1 - x, y), (send_3, 1, x, 1 - y)):
        depth_first = 2 * tiles * depth_partner(z, bits)
        plane_first = 2 * half_tiles * px + (tiles - 1) * py
        put(out, jnp.where(c == 0, depth_first, plane_first), jnp.where(c == 0, tiles, half_tiles))


def gram_kernel(rows, band, scale, tan_ref, sec_ref, drift_ref, after_ref, conv_ref, low_ref, high_ref):
    views = tan_ref.shape[1]
    span = 2 * band + 1
    shape = (span * rows, views)
    row = row_iota(shape)
    shift = ((row % rows).astype(jnp.float32) - (rows - 1) / 2.0) * tan_ref[...] - drift_ref[...].astype(jnp.float32)
    hat = jnp.maximum(0.0, 1.0 - jnp.abs(shift - (row // rows - band).astype(jnp.float32)))
    gram = lax.dot_general(
        hat * ((scale / rows) * sec_ref[...]),
        hat,
        (((1,), (1,)), ((), ())),
        precision=lax.Precision.HIGHEST,
        preferred_element_type=jnp.float32,
    )
    edge = band * rows
    low_ref[...] = left_terms(gram[edge + rows :, edge + rows :])
    high_ref[...] = left_terms(gram[:edge, :edge])
    width = conv_ref.shape[1] // 2 * 3
    padded = jnp.concatenate([gram, jnp.zeros((span * rows, width - span * rows), jnp.float32)], axis=1)
    total = jnp.zeros((rows, width), jnp.float32)
    for k in range(span):
        total = total + pltpu.roll(padded[k * rows : (k + 1) * rows], rows * (2 * band - k), 1)
    lanes = width // 3
    stacked = jnp.concatenate([total[:, i * lanes : (i + 1) * lanes] for i in range(3)], axis=0)
    stacked = split_rows(stacked)
    conv_ref[...] = jnp.concatenate([stacked, stacked], axis=1)


def normal(volumes, conv, low_ref, high_ref, band, is_low, is_high):
    rows, width = volumes[0].shape
    step = conv.shape[1] // 2 // rows
    parts = conv.shape[0] // 2 // rows
    beyond = beyond_ends(volumes, low_ref, high_ref, band, is_low, is_high)
    zero = jnp.zeros((rows, width - 2 * LANES), jnp.float32)
    result = []
    for volume, piece in zip(volumes, beyond):
        moved = jnp.concatenate([pltpu.roll(volume, (2 * band - j) % width, 1) for j in range(step)], axis=0)
        spread = jnp.dot(conv, split_terms(moved), preferred_element_type=jnp.float32)
        spread = spread[: parts * rows] + spread[parts * rows :]
        total = spread[0:rows]
        for i in range(1, parts):
            total = total + pltpu.roll(spread[i * rows : (i + 1) * rows], width - step * i, 1)
        ends = [jnp.where(is_low, piece, 0.0), zero, jnp.where(is_high, piece, 0.0)]
        result.append(total - jnp.concatenate(ends, axis=1))
    return result


def beyond_ends(volumes, low_ref, high_ref, band, is_low, is_high):
    rows, width = volumes[0].shape
    pitch = LANES // len(volumes)
    lane = lane_iota((rows, LANES))
    packed = jnp.zeros((rows, LANES), jnp.float32)
    for s, volume in enumerate(volumes):
        tile = jnp.where(is_low, volume[:, :LANES], volume[:, width - LANES :])
        inside = (lane >= s * pitch) & (lane < s * pitch + 2 * band)
        packed = jnp.where(inside, pltpu.roll(tile, (s * pitch - (HALO - band)) % LANES, 1), packed)
    offsets = [jnp.where(is_low, i + 1, LANES + i - band) for i in range(band)]
    moved = jnp.concatenate([pltpu.roll(packed, LANES - k, 1) for k in offsets], axis=0)
    matrix = jnp.where(is_low, low_ref[...], high_ref[...]).astype(jnp.bfloat16)
    spread = jnp.dot(matrix, right_terms(moved), preferred_element_type=jnp.float32)
    place = lane % pitch - jnp.where(is_low, 0, band)
    total = jnp.zeros((rows, LANES), jnp.float32)
    for i, k in enumerate(offsets):
        piece = jnp.where((place >= 0) & (place < band), spread[i * rows : (i + 1) * rows], 0.0)
        total = total + pltpu.roll(piece, k, 1)
    near = (lane >= HALO - band) & (lane < HALO + band)
    return [
        jnp.where(near, pltpu.roll(total, (HALO - band - s * pitch) % LANES, 1), 0.0) for s in range(len(volumes))
    ]


def block_place(width, total_cols):
    z, x, c, y = coords()
    block = width - 2 * HALO
    index = c * 2 + y
    return index * block - HALO, index == 0, index == total_cols // block - 1


def first_normal_kernel(band, total_cols, vol_mine, vol_got, conv_ref, low_ref, high_ref, out):
    _, is_low, is_high = block_place(vol_mine.shape[1], total_cols)
    _, _, _, y = coords()
    part = vol_mine.shape[0] // 2
    here, there = vol_mine[...], vol_got[...]
    upper = jnp.where(y == 0, here, there)
    lower = jnp.where(y == 0, there, here)
    volumes = [
        jnp.concatenate([upper[i * part : (i + 1) * part], lower[i * part : (i + 1) * part]], axis=0) for i in range(2)
    ]
    back = normal(volumes, conv_ref[...].astype(jnp.bfloat16), low_ref, high_ref, band, is_low, is_high)
    for i in range(2):
        out[i] = volumes[i] - back[i]


def half_pair_kernel(first_ref, own_pair, got_1, got_2, got_3, mine, to_x, to_diag, corr):
    _, x, _, _ = coords()
    corr[...] = (own_pair[...] + got_1[...]) + (got_2[...] + got_3[...])
    half = first_ref[...] + corr[...]
    mine[0:2] = half
    mine[2:4] = corr[...]
    to_x[0:2] = half
    to_x[2] = corr[1 - x]
    to_diag[0:2] = half
    to_diag[2] = corr[x]


def variation_step(half, z_of, first_col, depth, total_cols):
    rows, width = half[0].shape
    col = first_col + lane_iota((rows, width))
    row = row_iota((rows, width))
    inside = (col >= 0) & (col < total_cols - 1)
    units = []
    for w in range(len(half) - 1):
        v = half[w]
        keep = (z_of(w) >= 0) & (z_of(w) < depth - 1)
        dz = jnp.where(keep, half[w + 1] - v, 0.0)
        dr = jnp.where(row < rows - 1, pltpu.roll(v, rows - 1, 0) - v, 0.0)
        dc = jnp.where(inside, pltpu.roll(v, width - 1, 1) - v, 0.0)
        inverse = lax.rsqrt(dz * dz + dr * dr + dc * dc + SMOOTH_EPS * SMOOTH_EPS)
        units.append((dz * inverse, dr * inverse, dc * inverse))
    result = []
    for w in range(1, len(half) - 1):
        uz, ur, uc = units[w]
        div = (uz - units[w - 1][0]) + (ur - pltpu.roll(ur, 1, 0)) + (uc - pltpu.roll(uc, 1, 1))
        result.append(jnp.where((col >= 0) & (col < total_cols), half[w] + TV_STEP * div, 0.0))
    return result


def finish_kernel(
    band, depth, total_cols, mine, got_diag, got_x, conv_ref, low_ref, high_ref, keep_ref, send_ref, done
):
    width = mine.shape[2]
    first_col, is_low, is_high = block_place(width, total_cols)
    z, x, c, _ = coords()
    before = [jnp.where(x == 0, got_diag[i], got_x[i]) for i in range(3)]
    after = [jnp.where(x == 0, got_x[i], got_diag[i]) for i in range(3)]
    half = [before[0], before[1], mine[0], mine[1], after[0], after[1]]
    corr = [before[2], mine[2], mine[3], after[2]]
    slice_0 = 4 * z + 2 * x
    volumes = variation_step(half, lambda w: slice_0 - 2 + w, first_col, depth, total_cols)
    back = normal(volumes, conv_ref[...].astype(jnp.bfloat16), low_ref, high_ref, band, is_low, is_high)
    half = [volumes[s] + corr[s] - back[s] for s in range(4)]
    volumes = variation_step(half, lambda w: slice_0 - 1 + w, first_col, depth, total_cols)
    for s in range(2):
        done[s] = pltpu.roll(volumes[s], width - HALO, 1)[:, : width - LANES]
    keep_ref[...] = done[c]
    send_ref[...] = done[1 - c]


def result_pack_kernel(own_ref, got_ref, to_y):
    _, _, c, y = coords()
    part = to_y.shape[1]
    own, got = own_ref[...], got_ref[...]
    to_y[c] = jnp.where(y == 0, own[part:], own[:part])
    to_y[1 - c] = jnp.where(y == 0, got[part:], got[:part])


def result_kernel(own_ref, got_ref, got_y, out):
    _, _, c, y = coords()
    _, part, block = got_y.shape
    own, got = own_ref[...], got_ref[...]
    here = jnp.where(y == 0, own[:part], own[part:])
    there = jnp.where(y == 0, got[:part], got[part:])
    for value, h, q in ((here, c, y), (there, 1 - c, y), (got_y[0], 0, 1 - y), (got_y[1], 1, 1 - y)):
        out[0, :, pl.ds(pl.multiple_of((2 * h + q) * block, LANES), block)] = value


def f32(*shape):
    return jax.ShapeDtypeStruct(shape, jnp.float32)


VMEM_SPEC = pl.BlockSpec(memory_space=pltpu.VMEM)
SMEM_SPEC = pl.BlockSpec(memory_space=pltpu.SMEM)
ANY_SPEC = pl.BlockSpec(memory_space=pl.ANY)
HBM_SPEC = pl.BlockSpec(memory_space=pltpu.HBM)
PARAMS = pltpu.CompilerParams(vmem_limit_bytes=40 * 1024 * 1024)


def in_hbm(value):
    return pltpu.with_memory_space_constraint(value, pltpu.HBM)


def kernel_call(body, outs, in_specs, scratch, name, flops=0, size=0):
    many = isinstance(outs, (list, tuple))
    return pl.pallas_call(
        body,
        out_shape=outs,
        in_specs=in_specs,
        out_specs=[VMEM_SPEC] * len(outs) if many else VMEM_SPEC,
        scratch_shapes=scratch,
        compiler_params=PARAMS,
        name=name,
        cost_estimate=pl.CostEstimate(flops=flops, bytes_accessed=size, transcendentals=0),
    )


def summed_plan(measured, drift, start_volume):
    views, slices, cols = measured.shape
    part = start_volume.shape[1]
    rows = 2 * part
    band = rows // 2 + DMAX + 2
    total_angles = drift.shape[0]
    half_cols = cols // 2
    half_width = half_cols + LANES
    width = cols // 4 + 2 * HALO
    tangent, secant = tan_and_secant(total_angles)
    scale = float(1.0 / np.sum(secant))
    tangent, secant = tangent.astype(np.float32), secant.astype(np.float32)

    tiles = half_width // LANES
    groups = slices // SUB
    window = (groups, views, tiles + 2, SUB, LANES)
    tiled = measured.reshape(views, groups, SUB, cols // LANES, LANES).transpose(0, 1, 3, 2, 4)
    table = ((2 * band // STEP + 1) * rows, 3 * STEP * views)
    count = slices // 2
    terms = pltpu.VMEM((slices, 3 * STEP * views, half_width + LANES), jnp.bfloat16)
    vbuf = pltpu.VMEM((part, cols + 2 * LANES), jnp.float32)
    half_of = f32(count, rows, half_width)
    sibling, own_buf, weights, volume = kernel_call(
        functools.partial(fetch_kernel, views, rows, band, scale),
        [f32(slices + 1, rows, half_width), f32(*window), f32(*table), f32(1, part, cols)],
        [HBM_SPEC] * 4,
        [
            pltpu.SMEM((total_angles,), jnp.float32),
            pltpu.SMEM((total_angles,), jnp.int32),
            pltpu.VMEM(window, jnp.float32),
            terms,
            vbuf,
            pltpu.SemaphoreType.DMA((3,)),
            pltpu.SemaphoreType.DMA((2, groups)),
        ],
        "other_share",
        flops=10**9,
    )(in_hbm(jnp.asarray(tangent)), in_hbm(drift), in_hbm(tiled), in_hbm(start_volume))
    got = move(sibling, lambda z, x, c, y: (z, x, 1 - c, y))
    own = kernel_call(
        functools.partial(own_kernel, views, rows, band),
        f32(slices, rows, half_width),
        [VMEM_SPEC] * 2,
        [terms],
        "own_share",
        flops=10**9,
    )(own_buf, weights)

    message = f32(count * width // LANES, rows, LANES)
    mine, send_1, send_2, send_3, vol_mine, vol_to_y = kernel_call(
        plane_pack_kernel,
        [message] * 4 + [f32(rows, width)] * 2,
        [VMEM_SPEC] * 3,
        [pltpu.VMEM(half_of.shape, jnp.float32)] * 2 + [pltpu.VMEM((rows, half_width), jnp.float32), vbuf],
        "plane_pack",
    )(own, got, volume)
    got_1 = move(send_1, lambda z, x, c, y: (z ^ 2, x, c, y) if c else (z, 1 - x, c, 1 - y))
    got_2 = move(send_2, lambda z, x, c, y: (z ^ 3, x, c, y) if c else (z, 1 - x, c, y))
    got_3 = move(send_3, lambda z, x, c, y: (z ^ 1, x, c, y) if c else (z, x, c, 1 - y))
    vol_got = move(vol_to_y, lambda z, x, c, y: (z, x, c, 1 - y))

    edge = band * rows
    conv, low, high = kernel_call(
        functools.partial(gram_kernel, rows, band, scale),
        [f32(6 * rows, 2 * LANES), f32(edge, 3 * edge), f32(edge, 3 * edge)],
        [VMEM_SPEC] * 3 + [ANY_SPEC],
        [],
        "gram",
    )(tangent[None], secant[None], drift[None], mine)

    pair = f32(2, rows, width)
    own_pair, send_1, send_2, send_3 = kernel_call(
        middle_pack_kernel,
        [pair] * 4,
        [VMEM_SPEC] * 4,
        [pltpu.VMEM(message.shape, jnp.float32)],
        "middle_pack",
    )(mine, got_1, got_2, got_3)
    got_1 = move(send_1, lambda z, x, c, y: (z, 1 - x, c, 1 - y) if c else (z ^ 3, x, c, y))
    got_2 = move(send_2, lambda z, x, c, y: (z, 1 - x, c, y) if c else (z ^ 2, x, c, y))
    got_3 = move(send_3, lambda z, x, c, y: (z, x, c, 1 - y) if c else (z ^ 1, x, c, y))

    first = kernel_call(
        functools.partial(first_normal_kernel, band, cols),
        pair,
        [VMEM_SPEC] * 5,
        [],
        "first_normal",
        flops=10**9,
    )(vol_mine, vol_got, conv, low, high)

    three = f32(3, rows, width)
    mine, to_x, to_diag = kernel_call(
        half_pair_kernel,
        [f32(4, rows, width), three, three],
        [VMEM_SPEC] * 5,
        [pltpu.VMEM((2, rows, width), jnp.float32)],
        "half_pair",
    )(first, own_pair, got_1, got_2, got_3)
    got_diag = move(to_diag, beside)
    got_x = move(to_x, lambda z, x, c, y: (z, 1 - x, c, y))

    block = width - 2 * HALO
    quarter = f32(rows, block)
    keep, send = kernel_call(
        functools.partial(finish_kernel, band, slices, cols),
        [quarter, quarter],
        [VMEM_SPEC] * 6,
        [pltpu.VMEM((2, rows, block), jnp.float32)],
        "finish",
    )(mine, got_diag, got_x, conv, low, high)
    swapped = move(send, lambda z, x, c, y: (z, x, 1 - c, y))
    to_y = kernel_call(result_pack_kernel, f32(2, part, block), [VMEM_SPEC] * 2, [], "result_pack")(keep, swapped)
    got_y = move(to_y, lambda z, x, c, y: (z, x, c, 1 - y))
    return kernel_call(result_kernel, f32(1, part, cols), [VMEM_SPEC] * 3, [], "result")(keep, swapped, got_y)


def summed_plan_fits(mesh, measured, start_volume):
    rows = start_volume.shape[1]
    cols = measured.shape[2]
    return (
        ITERS == 2
        and dict(mesh.shape) == {"wide": 16, "grp": 2}
        and measured.shape[1] == start_volume.shape[0] == 16
        and rows == SUB
        and cols % (16 * LANES) == 0
        and measured.shape[0] % 256 == 0
    )


def solution(mesh):
    in_specs = (P(("wide", "grp"), None, None), P(), P("wide", "grp", None))
    out_specs = P("wide", "grp", None)

    def run(measured, drift, start_volume):
        plan = summed_plan if summed_plan_fits(mesh, measured, start_volume) else on_device
        return jax.shard_map(plan, mesh=mesh, in_specs=in_specs, out_specs=out_specs, check_vma=False)(
            measured, drift, start_volume
        )

    return run
```

```python
import functools
from functools import reduce
import math

import jax
import jax.numpy as jnp
import numpy as np
from jax import lax
from jax.experimental import pallas as pl
from jax.experimental.pallas import tpu as pltpu
from jax.sharding import PartitionSpec as P

ITERS = 2
DMAX = 4


TILT_MAX = math.pi / 4
SMOOTH_EPS = 0.05
TV_STEP = 0.1


def with_halo(block, sides, width):
    for axis, dim in sides:
        count = lax.axis_size(axis)
        forward = [(i, i + 1) for i in range(count - 1)]
        backward = [(target, source) for source, target in forward]
        low = lax.ppermute(
            lax.slice_in_dim(block, block.shape[dim] - width, None, axis=dim), axis, forward
        )
        high = lax.ppermute(lax.slice_in_dim(block, 0, width, axis=dim), axis, backward)
        block = jnp.concatenate([low, block, high], axis=dim)
    return block


def geometry(angle_ids, drift_vals, total_angles, rows, band_extent):
    angle_rad = TILT_MAX * (2.0 * angle_ids.astype(jnp.float32) / (total_angles - 1) - 1.0)
    secant = 1.0 / jnp.cos(angle_rad)
    height = jnp.arange(rows, dtype=jnp.float32) - (rows - 1) / 2.0
    offsets = jnp.arange(2 * band_extent + 1, dtype=jnp.float32) - band_extent
    shifts = height[None, :] * jnp.tan(angle_rad)[:, None] - drift_vals.astype(jnp.float32)[:, None]
    weight_factors = secant[:, None, None] * jnp.maximum(
        0.0, 1.0 - jnp.abs(shifts[:, :, None] - offsets[None, None, :])
    )
    return (weight_factors, jnp.cos(angle_rad) / rows)


def secant_sum(total_angles):
    angle_rad = TILT_MAX * (
        2.0 * jnp.arange(total_angles, dtype=jnp.float32) / (total_angles - 1) - 1.0
    )
    return jnp.sum(1.0 / jnp.cos(angle_rad))


def local_geometry(angle_ids, drift, total_angles, rows_all, band_extent):
    matches = angle_ids[:, None] == jnp.arange(total_angles, dtype=jnp.int32)[None, :]
    local_drift = jnp.sum(jnp.where(matches, drift[None, :], 0), axis=1)
    return geometry(angle_ids, local_drift, total_angles, rows_all, band_extent)


def apply_correction(
    row_band_strip, measurement_part, weight_factors, residual_scale, global_scale, band_extent
):
    col_count = row_band_strip.shape[2]
    span = 2 * band_extent + 1
    padded = jnp.pad(row_band_strip, ((0, 0), (0, 0), (band_extent, band_extent)))
    shifted = jnp.stack(
        [padded[:, :, shift_id : shift_id + col_count] for shift_id in range(span)], axis=2
    )
    forward_projected = jnp.einsum(
        "ark,zrku->azu", weight_factors, shifted, precision=lax.Precision.HIGHEST
    )
    residual_error = residual_scale[:, None, None] * (measurement_part - forward_projected)
    spread = jnp.einsum(
        "ark,azu->kzru", weight_factors, residual_error, precision=lax.Precision.HIGHEST
    )
    spread = jnp.pad(spread, ((0, 0), (0, 0), (0, 0), (band_extent, band_extent)))
    pieces = [
        spread[shift_id, :, :, 2 * band_extent - shift_id : 2 * band_extent - shift_id + col_count]
        for shift_id in range(span)
    ]
    return global_scale * reduce(lambda left, right: left + right, pieces)


def divergence(extended, z_first, r_first, zcount, rcount):
    plane_count, height, col_count = extended.shape
    z_index = z_first + jnp.arange(plane_count, dtype=jnp.int32)[:, None, None]
    row_index = r_first + jnp.arange(height, dtype=jnp.int32)[None, :, None]
    col_index = jnp.arange(col_count, dtype=jnp.int32)[None, None, :]
    diff_z = jnp.concatenate([extended[1:] - extended[:-1], jnp.zeros_like(extended[:1])], axis=0)
    diff_z = jnp.where((z_index >= 0) & (z_index < zcount - 1), diff_z, 0.0)
    diff_r = jnp.concatenate(
        [extended[:, 1:] - extended[:, :-1], jnp.zeros_like(extended[:, :1])], axis=1
    )
    diff_r = jnp.where((row_index >= 0) & (row_index < rcount - 1), diff_r, 0.0)
    diff_c = jnp.concatenate(
        [extended[:, :, 1:] - extended[:, :, :-1], jnp.zeros_like(extended[:, :, :1])], axis=2
    )
    diff_c = jnp.where(col_index < col_count - 1, diff_c, 0.0)
    magnitude = jnp.sqrt(
        diff_z * diff_z + diff_r * diff_r + diff_c * diff_c + SMOOTH_EPS * SMOOTH_EPS
    )
    unit_z = diff_z / magnitude
    unit_r = diff_r / magnitude
    unit_c = diff_c / magnitude
    back_c = unit_c - jnp.concatenate([jnp.zeros_like(unit_c[:, :, :1]), unit_c[:, :, :-1]], axis=2)
    return (
        unit_z[1:-1, 1:-1]
        - unit_z[:-2, 1:-1]
        + (unit_r[1:-1, 1:-1] - unit_r[1:-1, :-2])
        + back_c[1:-1, 1:-1]
    )


def on_device(measured, drift, start_volume):
    wide_count = lax.axis_size("wide")
    groups = lax.axis_size("grp")
    slab_count, rows_tile, col_count = start_volume.shape
    rows_all = rows_tile * groups
    band_extent = rows_all // 2 + DMAX + 2
    per_device = measured.shape[0]
    total_angles = per_device * wide_count * groups
    global_scale = 1.0 / secant_sum(total_angles)
    z_first = lax.axis_index("wide") * slab_count - 1
    zcount = slab_count * wide_count
    local_measurement = lax.all_to_all(measured, "wide", split_axis=1, concat_axis=0, tiled=True)
    bin_position = jnp.arange(local_measurement.shape[0], dtype=jnp.int32)
    angle_ids = (
        bin_position // per_device * groups + lax.axis_index("grp")
    ) * per_device + bin_position % per_device
    weight_factors, residual_scale = local_geometry(
        angle_ids, drift, total_angles, rows_all, band_extent
    )
    own_tile = start_volume
    r_first = lax.axis_index("grp") * rows_tile - 1
    for sweep in range(ITERS):
        row_band_strip = lax.all_gather(own_tile, "grp", axis=1, tiled=True)
        volume_update = apply_correction(
            row_band_strip,
            local_measurement,
            weight_factors,
            residual_scale,
            global_scale,
            band_extent,
        )
        own_tile = own_tile + lax.psum_scatter(
            volume_update, "grp", scatter_dimension=1, tiled=True
        )
        extended = with_halo(own_tile, (("wide", 0), ("grp", 1)), 1)
        own_tile = own_tile + TV_STEP * divergence(extended, z_first, r_first, zcount, rows_all)
    return own_tile


LANES = 128
SUB = 8
HALO = 64


def tan_and_secant(total_angles):
    angle = TILT_MAX * (2.0 * np.arange(total_angles) / (total_angles - 1) - 1.0)
    return np.tan(angle), 1.0 / np.cos(angle)


def coords():
    wide, y = lax.axis_index("wide"), lax.axis_index("grp")
    return wide // 4, wide // 2 % 2, wide % 2, y


def move(value, target):
    pairs = []
    for z in range(4):
        for x in range(2):
            for c in range(2):
                for y in range(2):
                    tz, tx, tc, ty = target(z, x, c, y)
                    pairs.append((((z * 2 + x) * 2 + c) * 2 + y, ((tz * 2 + tx) * 2 + tc) * 2 + ty))
    return lax.ppermute(value, ("wide", "grp"), pairs)


def beside(z, x, c, y):
    if (z, x) in ((0, 0), (3, 1)):
        return z, x, 1 - c, y
    return (z + 1, 0, c, y) if x else (z - 1, 1, c, y)


def split_rows(value):
    high = value.astype(jnp.bfloat16).astype(jnp.float32)
    return jnp.concatenate([high, value - high], axis=0)


def left_terms(value):
    high = value.astype(jnp.bfloat16).astype(jnp.float32)
    return jnp.concatenate([high, high, value - high], axis=1)


def split_terms(value):
    high = value.astype(jnp.bfloat16)
    low = (value - high.astype(jnp.float32)).astype(jnp.bfloat16)
    return jnp.concatenate([high, low], axis=0)


def right_terms(value):
    high = value.astype(jnp.bfloat16)
    low = (value - high.astype(jnp.float32)).astype(jnp.bfloat16)
    return jnp.concatenate([high, low, high], axis=0)


def lane_iota(shape):
    return lax.broadcasted_iota(jnp.int32, shape, len(shape) - 1)


def row_iota(shape):
    return lax.broadcasted_iota(jnp.int32, shape, len(shape) - 2)


STEP = 3


def view_weights(views, rows, band, scale, tan_ref, drift_ref):
    z, x, c, y = coords()
    first_view = (((z * 2 + x) * 2 + c) * 2 + y) * views
    parts = 2 * band // STEP + 1
    shape = (parts * rows, STEP * views)
    lane, row = lane_iota(shape), row_iota(shape)
    view_of = lane_iota((1, STEP * views)) % views
    tan_lane = jnp.zeros((1, STEP * views), jnp.float32)
    drift_lane = tan_lane
    for a in range(views):
        tan_lane = jnp.where(view_of == a, tan_ref[first_view + a], tan_lane)
        drift_lane = jnp.where(view_of == a, drift_ref[first_view + a].astype(jnp.float32), drift_lane)
    shift = ((row % rows).astype(jnp.float32) - (rows - 1) / 2.0) * tan_lane - drift_lane
    offset = ((row // rows) * STEP + lane // views - band).astype(jnp.float32)
    weights = (scale / rows) * jnp.maximum(0.0, 1.0 - jnp.abs(shift - offset))
    return left_terms(weights).astype(jnp.bfloat16)


def back_project(views, rows, band, weights, load_strip, begin, out_ref, terms):
    count, _, width = terms.shape[0] // 2, *terms.shape[1:]
    out_cols = out_ref.shape[2]
    parts = 2 * band // STEP + 1
    for n in range(count):
        strip = load_strip(n)
        high = strip.astype(jnp.bfloat16)
        low = (strip - high.astype(jnp.float32)).astype(jnp.bfloat16)
        for j in range(STEP):
            moved = pltpu.roll(high, j, 1) if j else high
            terms[begin + n, j * views : (j + 1) * views] = moved
            terms[begin + n, (STEP + j) * views : (STEP + j + 1) * views] = pltpu.roll(low, j, 1) if j else low
            terms[begin + n, (2 * STEP + j) * views : (2 * STEP + j + 1) * views] = moved
    for n in range(count):
        spread = jnp.dot(weights, terms[begin + n], preferred_element_type=jnp.float32)
        total = None
        for i in range(parts):
            piece = pltpu.roll(spread[i * rows : (i + 1) * rows], width - HALO - band + STEP * i, 1)
            total = piece if total is None else total + piece
        out_ref[begin + n] = total[:, :out_cols]


def depth_partner(z, bits):
    return {0: z, 1: z + 1 - 2 * (z % 2), 2: (z + 2) % 4, 3: 3 - z}[bits]


def slice_place(half, kept, n):
    z, x, _, _ = coords()
    parity = x if kept else 1 - x
    four = depth_partner(z, (1, 0)[n // 4] if kept else (2, 3)[n // 4])
    group = jnp.where(half == 0, n // 4, four // 2)
    place = jnp.where(half == 0, 4 * (n // 2 % 2) + 2 * parity + n % 2, 4 * (four % 2) + n % 4)
    return group, place


def strip_loader(buf, half, kept, views, tiles):
    pitch = (tiles + 2) * SUB

    def load(n):
        group, place = slice_place(half, kept, n)
        first = half * SUB + place
        return jnp.concatenate(
            [buf[group, pl.ds(first + t * SUB, views, stride=pitch), :] for t in range(tiles + 1)], axis=1
        )

    return load


def volume_window(vol_ref, half, half_cols, vbuf):
    part, cols = vol_ref.shape[1:]
    vbuf[:, 0:LANES] = jnp.zeros((part, LANES), jnp.float32)
    vbuf[:, LANES : LANES + cols] = vol_ref[0]
    vbuf[:, LANES + cols :] = jnp.zeros((part, LANES), jnp.float32)
    width = half_cols + 2 * LANES
    window = vbuf[:, pl.ds(pl.multiple_of(half * half_cols, LANES), width)]
    return pltpu.roll(window, width - HALO, 1)[:, : half_cols + LANES]


def fetch_kernel(views, rows, band, scale, tan_hbm, drift_hbm, meas_hbm, vol_hbm, out_ref, own_buf, weights_ref, vol_ref,
                 tan_ref, drift_ref, sibling_buf, terms, vbuf, table_sem, sem):
    z, _, c, _ = coords()
    tiles = out_ref.shape[2] // LANES
    groups = sibling_buf.shape[0]

    def fetch(half, target, g, semaphore):
        return pltpu.make_async_copy(
            meas_hbm.at[:, g, pl.ds(half * (tiles - 2), tiles)], target.at[g, 0:views, 1 : tiles + 1], semaphore
        )

    tables = [
        pltpu.make_async_copy(tan_hbm, tan_ref, table_sem.at[0]),
        pltpu.make_async_copy(drift_hbm, drift_ref, table_sem.at[1]),
    ]
    vol_copy = pltpu.make_async_copy(vol_hbm, vol_ref, table_sem.at[2])
    soon = jnp.where(c == 0, 1 - z // 2, 0)
    first = [fetch(1 - c, sibling_buf, g, sem.at[0, g]) for g in (soon, 1 - soon)]
    later = [fetch(c, own_buf, g, sem.at[1, g]) for g in range(groups)]
    for copy in first[:1] + tables + first[1:] + [vol_copy] + later:
        copy.start()
    zero = jnp.zeros((views, SUB, LANES), jnp.float32)
    for g in range(groups):
        for target in (sibling_buf, own_buf):
            target[g, 0:views, 0] = zero
            target[g, 0:views, tiles + 1] = zero
    for copy in tables:
        copy.wait()
    weights = view_weights(views, rows, band, scale, tan_ref, drift_ref)
    weights_ref[...] = weights.astype(jnp.float32)
    load, load_kept = (strip_loader(flat_rows(sibling_buf), 1 - c, kept, views, tiles) for kept in (False, True))

    def load_strip(n):
        if n % 4 == 0:
            first[n // 4].wait()
        return load(n)

    count = terms.shape[0] // 2
    back_project(views, rows, band, weights, load_strip, 0, out_ref, terms)
    back_project(views, rows, band, weights, load_kept, count, out_ref, terms)
    vol_copy.wait()
    half_cols = out_ref.shape[2] - LANES
    part = vol_ref.shape[1]
    out_ref[2 * count, 0:part] = volume_window(vol_ref, 1 - c, half_cols, vbuf)
    out_ref[2 * count, part:] = jnp.zeros((rows - part, half_cols + LANES), jnp.float32)
    for copy in later:
        copy.wait()


def flat_rows(buf):
    groups, views, tiles, sub, lanes = buf.shape
    return buf.reshape(groups, views * tiles * sub, lanes)


def own_kernel(views, rows, band, buf, weights_ref, out_ref, terms):
    _, _, c, _ = coords()
    tiles = out_ref.shape[2] // LANES
    weights = weights_ref[...].astype(jnp.bfloat16)
    for kept in (False, True):
        load = strip_loader(flat_rows(buf), c, kept, views, tiles)
        back_project(views, rows, band, weights, load, terms.shape[0] // 2 if kept else 0, out_ref, terms)


def put_quarter(out, acc, py, tiles):
    for n in range(acc.shape[0]):
        for t in range(tiles):
            out[n * tiles + t] = acc[n, :, pl.ds(pl.multiple_of(((tiles - 1) * py + t) * LANES, LANES), LANES)]


def put_four(out, acc, first):
    tiles = acc.shape[2] // LANES
    for n in range(4):
        for t in range(tiles):
            out[n * tiles + t] = acc[first + n, :, t * LANES : (t + 1) * LANES]
    for t in range(4 * tiles, out.shape[0]):
        out[t] = jnp.zeros(out.shape[1:], jnp.float32)


def plane_pack_kernel(own_ref, got_ref, mine, send_1, send_2, send_3, passed, acc):
    count, _, half_width = passed.shape
    tiles = mine.shape[0] // count
    _, _, c, y = coords()
    passed[...] = own_ref[0:count] + got_ref[0:count]
    acc[...] = own_ref[count:] + got_ref[count : 2 * count]

    @pl.when(c == 0)
    def _():
        put_quarter(send_1, passed, 1 - y, tiles)
        put_quarter(send_2, acc, 1 - y, tiles)
        put_quarter(send_3, passed, y, tiles)
        put_quarter(mine, acc, y, tiles)

    @pl.when(c == 1)
    def _():
        put_four(send_1, passed, 0)
        put_four(send_2, passed, 4)
        put_four(send_3, acc, 0)
        put_four(mine, acc, 4)


def volume_pack_kernel(own_ref, got_ref, vol_ref, vol_mine, vol_to_y, both, vbuf):
    count, rows, half_width = own_ref.shape
    part = vol_ref.shape[1]
    _, _, c, y = coords()
    here = volume_window(vol_ref, c, half_width - LANES, vbuf)
    there = got_ref[count, 0:part]
    both[0:part] = jnp.where(c == 0, here, there)
    both[part:] = jnp.where(c == 0, there, here)
    width = vol_mine.shape[1]
    for vol, py in ((vol_mine, y), (vol_to_y, 1 - y)):
        vol[...] = both[:, pl.ds(pl.multiple_of(py * (width - LANES), LANES), width)]


def middle_pack_kernel(mine, got_1, got_2, got_3, own_pair, send_1, send_2, send_3, acc):
    z, x, c, y = coords()
    tiles = own_pair.shape[2] // LANES
    half_tiles = 2 * tiles - 1
    acc[...] = (mine[...] + got_1[...]) + (got_2[...] + got_3[...])

    def put(out, first, pitch):
        for i in range(2):
            for t in range(tiles):
                out[i, :, t * LANES : (t + 1) * LANES] = acc[first + i * pitch + t]

    for out, bits, px, py in ((own_pair, 0, x, y), (send_1, 3, 1 - x, 1 - y), (send_2, 2, 1 - x, y), (send_3, 1, x, 1 - y)):
        depth_first = 2 * tiles * depth_partner(z, bits)
        plane_first = 2 * half_tiles * px + (tiles - 1) * py
        put(out, jnp.where(c == 0, depth_first, plane_first), jnp.where(c == 0, tiles, half_tiles))


def gram_kernel(rows, band, scale, tan_ref, sec_ref, drift_ref, after_ref, conv_ref, low_ref, high_ref):
    views = tan_ref.shape[1]
    span = 2 * band + 1
    shape = (span * rows, views)
    row = row_iota(shape)
    shift = ((row % rows).astype(jnp.float32) - (rows - 1) / 2.0) * tan_ref[...] - drift_ref[...].astype(jnp.float32)
    hat = jnp.maximum(0.0, 1.0 - jnp.abs(shift - (row // rows - band).astype(jnp.float32)))
    gram = lax.dot_general(
        hat * ((scale / rows) * sec_ref[...]),
        hat,
        (((1,), (1,)), ((), ())),
        precision=lax.Precision.HIGHEST,
        preferred_element_type=jnp.float32,
    )
    edge = band * rows
    low_ref[...] = left_terms(gram[edge + rows :, edge + rows :])
    high_ref[...] = left_terms(gram[:edge, :edge])
    width = conv_ref.shape[1] // 2 * 3
    padded = jnp.concatenate([gram, jnp.zeros((span * rows, width - span * rows), jnp.float32)], axis=1)
    total = jnp.zeros((rows, width), jnp.float32)
    for k in range(span):
        total = total + pltpu.roll(padded[k * rows : (k + 1) * rows], rows * (2 * band - k), 1)
    lanes = width // 3
    stacked = jnp.concatenate([total[:, i * lanes : (i + 1) * lanes] for i in range(3)], axis=0)
    stacked = split_rows(stacked)
    conv_ref[...] = jnp.concatenate([stacked, stacked], axis=1)


def normal(volumes, conv, low_ref, high_ref, band, is_low, is_high):
    rows, width = volumes[0].shape
    step = conv.shape[1] // 2 // rows
    parts = conv.shape[0] // 2 // rows
    beyond = beyond_ends(volumes, low_ref, high_ref, band, is_low, is_high)
    zero = jnp.zeros((rows, width - 2 * LANES), jnp.float32)
    result = []
    for volume, piece in zip(volumes, beyond):
        moved = jnp.concatenate([pltpu.roll(volume, (2 * band - j) % width, 1) for j in range(step)], axis=0)
        spread = jnp.dot(conv, split_terms(moved), preferred_element_type=jnp.float32)
        spread = spread[: parts * rows] + spread[parts * rows :]
        total = spread[0:rows]
        for i in range(1, parts):
            total = total + pltpu.roll(spread[i * rows : (i + 1) * rows], width - step * i, 1)
        ends = [jnp.where(is_low, piece, 0.0), zero, jnp.where(is_high, piece, 0.0)]
        result.append(total - jnp.concatenate(ends, axis=1))
    return result


def beyond_ends(volumes, low_ref, high_ref, band, is_low, is_high):
    rows, width = volumes[0].shape
    pitch = LANES // len(volumes)
    lane = lane_iota((rows, LANES))
    packed = jnp.zeros((rows, LANES), jnp.float32)
    for s, volume in enumerate(volumes):
        tile = jnp.where(is_low, volume[:, :LANES], volume[:, width - LANES :])
        inside = (lane >= s * pitch) & (lane < s * pitch + 2 * band)
        packed = jnp.where(inside, pltpu.roll(tile, (s * pitch - (HALO - band)) % LANES, 1), packed)
    offsets = [jnp.where(is_low, i + 1, LANES + i - band) for i in range(band)]
    moved = jnp.concatenate([pltpu.roll(packed, LANES - k, 1) for k in offsets], axis=0)
    matrix = jnp.where(is_low, low_ref[...], high_ref[...]).astype(jnp.bfloat16)
    spread = jnp.dot(matrix, right_terms(moved), preferred_element_type=jnp.float32)
    place = lane % pitch - jnp.where(is_low, 0, band)
    total = jnp.zeros((rows, LANES), jnp.float32)
    for i, k in enumerate(offsets):
        piece = jnp.where((place >= 0) & (place < band), spread[i * rows : (i + 1) * rows], 0.0)
        total = total + pltpu.roll(piece, k, 1)
    near = (lane >= HALO - band) & (lane < HALO + band)
    return [
        jnp.where(near, pltpu.roll(total, (HALO - band - s * pitch) % LANES, 1), 0.0) for s in range(len(volumes))
    ]


def block_place(width, total_cols):
    z, x, c, y = coords()
    block = width - 2 * HALO
    index = c * 2 + y
    return index * block - HALO, index == 0, index == total_cols // block - 1


def first_normal_kernel(band, total_cols, vol_mine, vol_got, conv_ref, low_ref, high_ref, out):
    _, is_low, is_high = block_place(vol_mine.shape[1], total_cols)
    _, _, _, y = coords()
    part = vol_mine.shape[0] // 2
    here, there = vol_mine[...], vol_got[...]
    upper = jnp.where(y == 0, here, there)
    lower = jnp.where(y == 0, there, here)
    volumes = [
        jnp.concatenate([upper[i * part : (i + 1) * part], lower[i * part : (i + 1) * part]], axis=0) for i in range(2)
    ]
    back = normal(volumes, conv_ref[...].astype(jnp.bfloat16), low_ref, high_ref, band, is_low, is_high)
    for i in range(2):
        out[i] = volumes[i] - back[i]


def half_pair_kernel(first_ref, own_pair, got_1, got_2, got_3, mine, to_x, to_diag, corr):
    _, x, _, _ = coords()
    corr[...] = (own_pair[...] + got_1[...]) + (got_2[...] + got_3[...])
    half = first_ref[...] + corr[...]
    mine[0:2] = half
    mine[2:4] = corr[...]
    to_x[0:2] = half
    to_x[2] = corr[1 - x]
    to_diag[0:2] = half
    to_diag[2] = corr[x]


def variation_step(half, z_of, first_col, depth, total_cols):
    rows, width = half[0].shape
    col = first_col + lane_iota((rows, width))
    row = row_iota((rows, width))
    inside = (col >= 0) & (col < total_cols - 1)
    units = []
    for w in range(len(half) - 1):
        v = half[w]
        keep = (z_of(w) >= 0) & (z_of(w) < depth - 1)
        dz = jnp.where(keep, half[w + 1] - v, 0.0)
        dr = jnp.where(row < rows - 1, pltpu.roll(v, rows - 1, 0) - v, 0.0)
        dc = jnp.where(inside, pltpu.roll(v, width - 1, 1) - v, 0.0)
        inverse = lax.rsqrt(dz * dz + dr * dr + dc * dc + SMOOTH_EPS * SMOOTH_EPS)
        units.append((dz * inverse, dr * inverse, dc * inverse))
    result = []
    for w in range(1, len(half) - 1):
        uz, ur, uc = units[w]
        div = (uz - units[w - 1][0]) + (ur - pltpu.roll(ur, 1, 0)) + (uc - pltpu.roll(uc, 1, 1))
        result.append(jnp.where((col >= 0) & (col < total_cols), half[w] + TV_STEP * div, 0.0))
    return result


def finish_kernel(
    band, depth, total_cols, mine, got_diag, got_x, conv_ref, low_ref, high_ref, keep_ref, send_ref, done
):
    width = mine.shape[2]
    first_col, is_low, is_high = block_place(width, total_cols)
    z, x, c, _ = coords()
    before = [jnp.where(x == 0, got_diag[i], got_x[i]) for i in range(3)]
    after = [jnp.where(x == 0, got_x[i], got_diag[i]) for i in range(3)]
    half = [before[0], before[1], mine[0], mine[1], after[0], after[1]]
    corr = [before[2], mine[2], mine[3], after[2]]
    slice_0 = 4 * z + 2 * x
    volumes = variation_step(half, lambda w: slice_0 - 2 + w, first_col, depth, total_cols)
    back = normal(volumes, conv_ref[...].astype(jnp.bfloat16), low_ref, high_ref, band, is_low, is_high)
    half = [volumes[s] + corr[s] - back[s] for s in range(4)]
    volumes = variation_step(half, lambda w: slice_0 - 1 + w, first_col, depth, total_cols)
    for s in range(2):
        done[s] = pltpu.roll(volumes[s], width - HALO, 1)[:, : width - LANES]
    keep_ref[...] = done[c]
    send_ref[...] = done[1 - c]


def result_pack_kernel(own_ref, got_ref, to_y):
    _, _, c, y = coords()
    part = to_y.shape[1]
    own, got = own_ref[...], got_ref[...]
    to_y[c] = jnp.where(y == 0, own[part:], own[:part])
    to_y[1 - c] = jnp.where(y == 0, got[part:], got[:part])


def result_kernel(own_ref, got_ref, got_y, out):
    _, _, c, y = coords()
    _, part, block = got_y.shape
    own, got = own_ref[...], got_ref[...]
    here = jnp.where(y == 0, own[:part], own[part:])
    there = jnp.where(y == 0, got[:part], got[part:])
    for value, h, q in ((here, c, y), (there, 1 - c, y), (got_y[0], 0, 1 - y), (got_y[1], 1, 1 - y)):
        out[0, :, pl.ds(pl.multiple_of((2 * h + q) * block, LANES), block)] = value


def f32(*shape):
    return jax.ShapeDtypeStruct(shape, jnp.float32)


VMEM_SPEC = pl.BlockSpec(memory_space=pltpu.VMEM)
SMEM_SPEC = pl.BlockSpec(memory_space=pltpu.SMEM)
ANY_SPEC = pl.BlockSpec(memory_space=pl.ANY)
HBM_SPEC = pl.BlockSpec(memory_space=pltpu.HBM)
PARAMS = pltpu.CompilerParams(vmem_limit_bytes=40 * 1024 * 1024)


def in_hbm(value):
    return pltpu.with_memory_space_constraint(value, pltpu.HBM)


def kernel_call(body, outs, in_specs, scratch, name, flops=0, size=0):
    many = isinstance(outs, (list, tuple))
    return pl.pallas_call(
        body,
        out_shape=outs,
        in_specs=in_specs,
        out_specs=[VMEM_SPEC] * len(outs) if many else VMEM_SPEC,
        scratch_shapes=scratch,
        compiler_params=PARAMS,
        name=name,
        cost_estimate=pl.CostEstimate(flops=flops, bytes_accessed=size, transcendentals=0),
    )


def summed_plan(measured, drift, start_volume):
    views, slices, cols = measured.shape
    part = start_volume.shape[1]
    rows = 2 * part
    band = rows // 2 + DMAX + 2
    total_angles = drift.shape[0]
    half_cols = cols // 2
    half_width = half_cols + LANES
    width = cols // 4 + 2 * HALO
    tangent, secant = tan_and_secant(total_angles)
    scale = float(1.0 / np.sum(secant))
    tangent, secant = tangent.astype(np.float32), secant.astype(np.float32)

    tiles = half_width // LANES
    groups = slices // SUB
    window = (groups, views + 1, tiles + 2, SUB, LANES)
    tiled = measured.reshape(views, groups, SUB, cols // LANES, LANES).transpose(0, 1, 3, 2, 4)
    table = ((2 * band // STEP + 1) * rows, 3 * STEP * views)
    count = slices // 2
    terms = pltpu.VMEM((slices, 3 * STEP * views, half_width + LANES), jnp.bfloat16)
    vbuf = pltpu.VMEM((part, cols + 2 * LANES), jnp.float32)
    half_of = f32(count, rows, half_width)
    sibling, own_buf, weights, volume = kernel_call(
        functools.partial(fetch_kernel, views, rows, band, scale),
        [f32(slices + 1, rows, half_width), f32(*window), f32(*table), f32(1, part, cols)],
        [HBM_SPEC] * 4,
        [
            pltpu.SMEM((total_angles,), jnp.float32),
            pltpu.SMEM((total_angles,), jnp.int32),
            pltpu.VMEM(window, jnp.float32),
            terms,
            vbuf,
            pltpu.SemaphoreType.DMA((3,)),
            pltpu.SemaphoreType.DMA((2, groups)),
        ],
        "other_share",
        flops=10**9,
    )(in_hbm(jnp.asarray(tangent)), in_hbm(drift), in_hbm(tiled), in_hbm(start_volume))
    got = move(sibling, lambda z, x, c, y: (z, x, 1 - c, y))
    own = kernel_call(
        functools.partial(own_kernel, views, rows, band),
        f32(slices, rows, half_width),
        [VMEM_SPEC] * 2,
        [terms],
        "own_share",
        flops=10**9,
    )(own_buf, weights)

    message = f32(count * width // LANES, rows, LANES)
    mine, send_1, send_2, send_3 = kernel_call(
        plane_pack_kernel,
        [message] * 4,
        [VMEM_SPEC] * 2,
        [pltpu.VMEM(half_of.shape, jnp.float32)] * 2,
        "plane_pack",
    )(own, got)
    vol_mine, vol_to_y = kernel_call(
        volume_pack_kernel,
        [f32(rows, width)] * 2,
        [ANY_SPEC, VMEM_SPEC, VMEM_SPEC],
        [pltpu.VMEM((rows, half_width), jnp.float32), vbuf],
        "volume_pack",
    )(own, got, volume)
    got_1 = move(send_1, lambda z, x, c, y: (z ^ 2, x, c, y) if c else (z, 1 - x, c, 1 - y))
    got_2 = move(send_2, lambda z, x, c, y: (z ^ 3, x, c, y) if c else (z, x, c, 1 - y))
    got_3 = move(send_3, lambda z, x, c, y: (z ^ 1, x, c, y) if c else (z, 1 - x, c, y))
    vol_got = move(vol_to_y, lambda z, x, c, y: (z, x, c, 1 - y))

    edge = band * rows
    conv, low, high = kernel_call(
        functools.partial(gram_kernel, rows, band, scale),
        [f32(6 * rows, 2 * LANES), f32(edge, 3 * edge), f32(edge, 3 * edge)],
        [VMEM_SPEC] * 3 + [ANY_SPEC],
        [],
        "gram",
    )(tangent[None], secant[None], drift[None], mine)

    pair = f32(2, rows, width)
    own_pair, send_1, send_2, send_3 = kernel_call(
        middle_pack_kernel,
        [pair] * 4,
        [VMEM_SPEC] * 4,
        [pltpu.VMEM(message.shape, jnp.float32)],
        "middle_pack",
    )(mine, got_1, got_2, got_3)
    got_1 = move(send_1, lambda z, x, c, y: (z, 1 - x, c, 1 - y) if c else (z ^ 3, x, c, y))
    got_2 = move(send_2, lambda z, x, c, y: (z, 1 - x, c, y) if c else (z ^ 2, x, c, y))
    got_3 = move(send_3, lambda z, x, c, y: (z, x, c, 1 - y) if c else (z ^ 1, x, c, y))

    first = kernel_call(
        functools.partial(first_normal_kernel, band, cols),
        pair,
        [VMEM_SPEC] * 5,
        [],
        "first_normal",
        flops=10**9,
    )(vol_mine, vol_got, conv, low, high)

    three = f32(3, rows, width)
    mine, to_x, to_diag = kernel_call(
        half_pair_kernel,
        [f32(4, rows, width), three, three],
        [VMEM_SPEC] * 5,
        [pltpu.VMEM((2, rows, width), jnp.float32)],
        "half_pair",
    )(first, own_pair, got_1, got_2, got_3)
    got_diag = move(to_diag, beside)
    got_x = move(to_x, lambda z, x, c, y: (z, 1 - x, c, y))

    block = width - 2 * HALO
    quarter = f32(rows, block)
    keep, send = kernel_call(
        functools.partial(finish_kernel, band, slices, cols),
        [quarter, quarter],
        [VMEM_SPEC] * 6,
        [pltpu.VMEM((2, rows, block), jnp.float32)],
        "finish",
    )(mine, got_diag, got_x, conv, low, high)
    swapped = move(send, lambda z, x, c, y: (z, x, 1 - c, y))
    to_y = kernel_call(result_pack_kernel, f32(2, part, block), [VMEM_SPEC] * 2, [], "result_pack")(keep, swapped)
    got_y = move(to_y, lambda z, x, c, y: (z, x, c, 1 - y))
    return kernel_call(result_kernel, f32(1, part, cols), [VMEM_SPEC] * 3, [], "result")(keep, swapped, got_y)


def summed_plan_fits(mesh, measured, start_volume):
    rows = start_volume.shape[1]
    cols = measured.shape[2]
    return (
        ITERS == 2
        and dict(mesh.shape) == {"wide": 16, "grp": 2}
        and measured.shape[1] == start_volume.shape[0] == 16
        and rows == SUB
        and cols % (16 * LANES) == 0
        and measured.shape[0] % 256 == 0
    )


def solution(mesh):
    in_specs = (P(("wide", "grp"), None, None), P(), P("wide", "grp", None))
    out_specs = P("wide", "grp", None)

    def run(measured, drift, start_volume):
        plan = summed_plan if summed_plan_fits(mesh, measured, start_volume) else on_device
        return jax.shard_map(plan, mesh=mesh, in_specs=in_specs, out_specs=out_specs, check_vma=False)(
            measured, drift, start_volume
        )

    return run
```

```python
import functools
from functools import reduce
import math

import jax
import jax.numpy as jnp
import numpy as np
from jax import lax
from jax.experimental import pallas as pl
from jax.experimental.pallas import tpu as pltpu
from jax.sharding import PartitionSpec as P

ITERS = 2
DMAX = 4


TILT_MAX = math.pi / 4
SMOOTH_EPS = 0.05
TV_STEP = 0.1


def with_halo(block, sides, width):
    for axis, dim in sides:
        count = lax.axis_size(axis)
        forward = [(i, i + 1) for i in range(count - 1)]
        backward = [(target, source) for source, target in forward]
        low = lax.ppermute(
            lax.slice_in_dim(block, block.shape[dim] - width, None, axis=dim), axis, forward
        )
        high = lax.ppermute(lax.slice_in_dim(block, 0, width, axis=dim), axis, backward)
        block = jnp.concatenate([low, block, high], axis=dim)
    return block


def geometry(angle_ids, drift_vals, total_angles, rows, band_extent):
    angle_rad = TILT_MAX * (2.0 * angle_ids.astype(jnp.float32) / (total_angles - 1) - 1.0)
    secant = 1.0 / jnp.cos(angle_rad)
    height = jnp.arange(rows, dtype=jnp.float32) - (rows - 1) / 2.0
    offsets = jnp.arange(2 * band_extent + 1, dtype=jnp.float32) - band_extent
    shifts = height[None, :] * jnp.tan(angle_rad)[:, None] - drift_vals.astype(jnp.float32)[:, None]
    weight_factors = secant[:, None, None] * jnp.maximum(
        0.0, 1.0 - jnp.abs(shifts[:, :, None] - offsets[None, None, :])
    )
    return (weight_factors, jnp.cos(angle_rad) / rows)


def secant_sum(total_angles):
    angle_rad = TILT_MAX * (
        2.0 * jnp.arange(total_angles, dtype=jnp.float32) / (total_angles - 1) - 1.0
    )
    return jnp.sum(1.0 / jnp.cos(angle_rad))


def local_geometry(angle_ids, drift, total_angles, rows_all, band_extent):
    matches = angle_ids[:, None] == jnp.arange(total_angles, dtype=jnp.int32)[None, :]
    local_drift = jnp.sum(jnp.where(matches, drift[None, :], 0), axis=1)
    return geometry(angle_ids, local_drift, total_angles, rows_all, band_extent)


def apply_correction(
    row_band_strip, measurement_part, weight_factors, residual_scale, global_scale, band_extent
):
    col_count = row_band_strip.shape[2]
    span = 2 * band_extent + 1
    padded = jnp.pad(row_band_strip, ((0, 0), (0, 0), (band_extent, band_extent)))
    shifted = jnp.stack(
        [padded[:, :, shift_id : shift_id + col_count] for shift_id in range(span)], axis=2
    )
    forward_projected = jnp.einsum(
        "ark,zrku->azu", weight_factors, shifted, precision=lax.Precision.HIGHEST
    )
    residual_error = residual_scale[:, None, None] * (measurement_part - forward_projected)
    spread = jnp.einsum(
        "ark,azu->kzru", weight_factors, residual_error, precision=lax.Precision.HIGHEST
    )
    spread = jnp.pad(spread, ((0, 0), (0, 0), (0, 0), (band_extent, band_extent)))
    pieces = [
        spread[shift_id, :, :, 2 * band_extent - shift_id : 2 * band_extent - shift_id + col_count]
        for shift_id in range(span)
    ]
    return global_scale * reduce(lambda left, right: left + right, pieces)


def divergence(extended, z_first, r_first, zcount, rcount):
    plane_count, height, col_count = extended.shape
    z_index = z_first + jnp.arange(plane_count, dtype=jnp.int32)[:, None, None]
    row_index = r_first + jnp.arange(height, dtype=jnp.int32)[None, :, None]
    col_index = jnp.arange(col_count, dtype=jnp.int32)[None, None, :]
    diff_z = jnp.concatenate([extended[1:] - extended[:-1], jnp.zeros_like(extended[:1])], axis=0)
    diff_z = jnp.where((z_index >= 0) & (z_index < zcount - 1), diff_z, 0.0)
    diff_r = jnp.concatenate(
        [extended[:, 1:] - extended[:, :-1], jnp.zeros_like(extended[:, :1])], axis=1
    )
    diff_r = jnp.where((row_index >= 0) & (row_index < rcount - 1), diff_r, 0.0)
    diff_c = jnp.concatenate(
        [extended[:, :, 1:] - extended[:, :, :-1], jnp.zeros_like(extended[:, :, :1])], axis=2
    )
    diff_c = jnp.where(col_index < col_count - 1, diff_c, 0.0)
    magnitude = jnp.sqrt(
        diff_z * diff_z + diff_r * diff_r + diff_c * diff_c + SMOOTH_EPS * SMOOTH_EPS
    )
    unit_z = diff_z / magnitude
    unit_r = diff_r / magnitude
    unit_c = diff_c / magnitude
    back_c = unit_c - jnp.concatenate([jnp.zeros_like(unit_c[:, :, :1]), unit_c[:, :, :-1]], axis=2)
    return (
        unit_z[1:-1, 1:-1]
        - unit_z[:-2, 1:-1]
        + (unit_r[1:-1, 1:-1] - unit_r[1:-1, :-2])
        + back_c[1:-1, 1:-1]
    )


def on_device(measured, drift, start_volume):
    wide_count = lax.axis_size("wide")
    groups = lax.axis_size("grp")
    slab_count, rows_tile, col_count = start_volume.shape
    rows_all = rows_tile * groups
    band_extent = rows_all // 2 + DMAX + 2
    per_device = measured.shape[0]
    total_angles = per_device * wide_count * groups
    global_scale = 1.0 / secant_sum(total_angles)
    z_first = lax.axis_index("wide") * slab_count - 1
    zcount = slab_count * wide_count
    local_measurement = lax.all_to_all(measured, "wide", split_axis=1, concat_axis=0, tiled=True)
    bin_position = jnp.arange(local_measurement.shape[0], dtype=jnp.int32)
    angle_ids = (
        bin_position // per_device * groups + lax.axis_index("grp")
    ) * per_device + bin_position % per_device
    weight_factors, residual_scale = local_geometry(
        angle_ids, drift, total_angles, rows_all, band_extent
    )
    own_tile = start_volume
    r_first = lax.axis_index("grp") * rows_tile - 1
    for sweep in range(ITERS):
        row_band_strip = lax.all_gather(own_tile, "grp", axis=1, tiled=True)
        volume_update = apply_correction(
            row_band_strip,
            local_measurement,
            weight_factors,
            residual_scale,
            global_scale,
            band_extent,
        )
        own_tile = own_tile + lax.psum_scatter(
            volume_update, "grp", scatter_dimension=1, tiled=True
        )
        extended = with_halo(own_tile, (("wide", 0), ("grp", 1)), 1)
        own_tile = own_tile + TV_STEP * divergence(extended, z_first, r_first, zcount, rows_all)
    return own_tile


LANES = 128
SUB = 8
HALO = 64


def tan_and_secant(total_angles):
    angle = TILT_MAX * (2.0 * np.arange(total_angles) / (total_angles - 1) - 1.0)
    return np.tan(angle), 1.0 / np.cos(angle)


def coords():
    wide, y = lax.axis_index("wide"), lax.axis_index("grp")
    return wide // 4, wide // 2 % 2, wide % 2, y


def move(value, target):
    pairs = []
    for z in range(4):
        for x in range(2):
            for c in range(2):
                for y in range(2):
                    tz, tx, tc, ty = target(z, x, c, y)
                    pairs.append((((z * 2 + x) * 2 + c) * 2 + y, ((tz * 2 + tx) * 2 + tc) * 2 + ty))
    return lax.ppermute(value, ("wide", "grp"), pairs)


def beside(z, x, c, y):
    if (z, x) in ((0, 0), (3, 1)):
        return z, x, 1 - c, y
    return (z + 1, 0, c, y) if x else (z - 1, 1, c, y)


def split_rows(value):
    high = value.astype(jnp.bfloat16).astype(jnp.float32)
    return jnp.concatenate([high, value - high], axis=0)


def left_terms(value):
    high = value.astype(jnp.bfloat16).astype(jnp.float32)
    return jnp.concatenate([high, high, value - high], axis=1)


def split_terms(value):
    high = value.astype(jnp.bfloat16)
    low = (value - high.astype(jnp.float32)).astype(jnp.bfloat16)
    return jnp.concatenate([high, low], axis=0)


def right_terms(value):
    high = value.astype(jnp.bfloat16)
    low = (value - high.astype(jnp.float32)).astype(jnp.bfloat16)
    return jnp.concatenate([high, low, high], axis=0)


def lane_iota(shape):
    return lax.broadcasted_iota(jnp.int32, shape, len(shape) - 1)


def row_iota(shape):
    return lax.broadcasted_iota(jnp.int32, shape, len(shape) - 2)


STEP = 3


def view_weights(views, rows, band, scale, tan_ref, drift_ref):
    z, x, c, y = coords()
    first_view = (((z * 2 + x) * 2 + c) * 2 + y) * views
    parts = 2 * band // STEP + 1
    shape = (parts * rows, STEP * views)
    lane, row = lane_iota(shape), row_iota(shape)
    view_of = lane_iota((1, STEP * views)) % views
    tan_lane = jnp.zeros((1, STEP * views), jnp.float32)
    drift_lane = tan_lane
    for a in range(views):
        tan_lane = jnp.where(view_of == a, tan_ref[first_view + a], tan_lane)
        drift_lane = jnp.where(view_of == a, drift_ref[first_view + a].astype(jnp.float32), drift_lane)
    shift = ((row % rows).astype(jnp.float32) - (rows - 1) / 2.0) * tan_lane - drift_lane
    offset = ((row // rows) * STEP + lane // views - band).astype(jnp.float32)
    weights = (scale / rows) * jnp.maximum(0.0, 1.0 - jnp.abs(shift - offset))
    return left_terms(weights).astype(jnp.bfloat16)


def back_project(views, rows, band, weights, load_strip, begin, out_ref, terms):
    count, _, width = terms.shape[0] // 2, *terms.shape[1:]
    out_cols = out_ref.shape[2]
    parts = 2 * band // STEP + 1
    for n in range(count):
        strip = load_strip(n)
        high = strip.astype(jnp.bfloat16)
        low = (strip - high.astype(jnp.float32)).astype(jnp.bfloat16)
        for j in range(STEP):
            moved = pltpu.roll(high, j, 1) if j else high
            terms[begin + n, j * views : (j + 1) * views] = moved
            terms[begin + n, (STEP + j) * views : (STEP + j + 1) * views] = pltpu.roll(low, j, 1) if j else low
            terms[begin + n, (2 * STEP + j) * views : (2 * STEP + j + 1) * views] = moved
    for n in range(count):
        spread = jnp.dot(weights, terms[begin + n], preferred_element_type=jnp.float32)
        total = None
        for i in range(parts):
            piece = pltpu.roll(spread[i * rows : (i + 1) * rows], width - HALO - band + STEP * i, 1)
            total = piece if total is None else total + piece
        out_ref[begin + n] = total[:, :out_cols]


def depth_partner(z, bits):
    return {0: z, 1: z + 1 - 2 * (z % 2), 2: (z + 2) % 4, 3: 3 - z}[bits]


def slice_place(half, kept, n):
    z, x, _, _ = coords()
    parity = x if kept else 1 - x
    four = depth_partner(z, (1, 0)[n // 4] if kept else (2, 3)[n // 4])
    group = jnp.where(half == 0, n // 4, four // 2)
    place = jnp.where(half == 0, 4 * (n // 2 % 2) + 2 * parity + n % 2, 4 * (four % 2) + n % 4)
    return group, place


def strip_loader(buf, half, kept, views, tiles):
    pitch = (tiles + 2) * SUB

    def load(n):
        group, place = slice_place(half, kept, n)
        first = half * SUB + place
        return jnp.concatenate(
            [buf[group, pl.ds(first + t * SUB, views, stride=pitch), :] for t in range(tiles + 1)], axis=1
        )

    return load


def volume_window(vol_ref, half, half_cols, vbuf):
    part, cols = vol_ref.shape[1:]
    vbuf[:, 0:LANES] = jnp.zeros((part, LANES), jnp.float32)
    vbuf[:, LANES : LANES + cols] = vol_ref[0]
    vbuf[:, LANES + cols :] = jnp.zeros((part, LANES), jnp.float32)
    width = half_cols + 2 * LANES
    window = vbuf[:, pl.ds(pl.multiple_of(half * half_cols, LANES), width)]
    return pltpu.roll(window, width - HALO, 1)[:, : half_cols + LANES]


def fetch_kernel(views, rows, band, scale, tan_hbm, drift_hbm, meas_hbm, vol_hbm, out_ref, own_buf, weights_ref, vol_ref,
                 tan_ref, drift_ref, sibling_buf, terms, vbuf, table_sem, sem):
    z, _, c, _ = coords()
    tiles = out_ref.shape[2] // LANES
    groups = sibling_buf.shape[0]

    def fetch(half, target, g, semaphore):
        return pltpu.make_async_copy(
            meas_hbm.at[:, g, pl.ds(half * (tiles - 2), tiles)], target.at[g, 0:views, 1 : tiles + 1], semaphore
        )

    tables = [
        pltpu.make_async_copy(tan_hbm, tan_ref, table_sem.at[0]),
        pltpu.make_async_copy(drift_hbm, drift_ref, table_sem.at[1]),
    ]
    vol_copy = pltpu.make_async_copy(vol_hbm, vol_ref, table_sem.at[2])
    soon = jnp.where(c == 0, 1 - z // 2, 0)
    first = [fetch(1 - c, sibling_buf, g, sem.at[0, g]) for g in (soon, 1 - soon)]
    later = [fetch(c, own_buf, g, sem.at[1, g]) for g in range(groups)]
    for copy in first[:1] + tables + first[1:] + [vol_copy] + later:
        copy.start()
    zero = jnp.zeros((views, SUB, LANES), jnp.float32)
    for g in range(groups):
        for target in (sibling_buf, own_buf):
            target[g, 0:views, 0] = zero
            target[g, 0:views, tiles + 1] = zero
    for copy in tables:
        copy.wait()
    weights = view_weights(views, rows, band, scale, tan_ref, drift_ref)
    weights_ref[...] = weights.astype(jnp.float32)
    load, load_kept = (strip_loader(flat_rows(sibling_buf), 1 - c, kept, views, tiles) for kept in (False, True))

    def load_strip(n):
        if n % 4 == 0:
            first[n // 4].wait()
        return load(n)

    count = terms.shape[0] // 2
    back_project(views, rows, band, weights, load_strip, 0, out_ref, terms)
    back_project(views, rows, band, weights, load_kept, count, out_ref, terms)
    vol_copy.wait()
    half_cols = out_ref.shape[2] - LANES
    part = vol_ref.shape[1]
    out_ref[2 * count, 0:part] = volume_window(vol_ref, 1 - c, half_cols, vbuf)
    out_ref[2 * count, part:] = jnp.zeros((rows - part, half_cols + LANES), jnp.float32)
    for copy in later:
        copy.wait()


def flat_rows(buf):
    groups, views, tiles, sub, lanes = buf.shape
    return buf.reshape(groups, views * tiles * sub, lanes)


def own_kernel(views, rows, band, buf, weights_ref, out_ref, terms):
    _, _, c, _ = coords()
    tiles = out_ref.shape[2] // LANES
    weights = weights_ref[...].astype(jnp.bfloat16)
    for kept in (False, True):
        load = strip_loader(flat_rows(buf), c, kept, views, tiles)
        back_project(views, rows, band, weights, load, terms.shape[0] // 2 if kept else 0, out_ref, terms)


def put_quarter(out, acc, py, tiles):
    for n in range(acc.shape[0]):
        for t in range(tiles):
            out[n * tiles + t] = acc[n, :, pl.ds(pl.multiple_of(((tiles - 1) * py + t) * LANES, LANES), LANES)]


def put_four(out, acc, first):
    tiles = acc.shape[2] // LANES
    for n in range(4):
        for t in range(tiles):
            out[n * tiles + t] = acc[first + n, :, t * LANES : (t + 1) * LANES]
    for t in range(4 * tiles, out.shape[0]):
        out[t] = jnp.zeros(out.shape[1:], jnp.float32)


def plane_pack_kernel(own_ref, got_ref, mine, send_1, send_2, send_3, passed, acc):
    count, _, half_width = passed.shape
    tiles = mine.shape[0] // count
    _, _, c, y = coords()
    passed[...] = own_ref[0:count] + got_ref[0:count]
    acc[...] = own_ref[count:] + got_ref[count : 2 * count]

    @pl.when(c == 0)
    def _():
        put_quarter(send_1, passed, 1 - y, tiles)
        put_quarter(send_2, acc, 1 - y, tiles)
        put_quarter(send_3, passed, y, tiles)
        put_quarter(mine, acc, y, tiles)

    @pl.when(c == 1)
    def _():
        put_four(send_1, passed, 0)
        put_four(send_2, passed, 4)
        put_four(send_3, acc, 0)
        put_four(mine, acc, 4)


def volume_pack_kernel(own_ref, got_ref, vol_ref, vol_mine, vol_to_y, both, vbuf):
    count, rows, half_width = own_ref.shape
    part = vol_ref.shape[1]
    _, _, c, y = coords()
    here = volume_window(vol_ref, c, half_width - LANES, vbuf)
    there = got_ref[count, 0:part]
    both[0:part] = jnp.where(c == 0, here, there)
    both[part:] = jnp.where(c == 0, there, here)
    width = vol_mine.shape[1]
    for vol, py in ((vol_mine, y), (vol_to_y, 1 - y)):
        vol[...] = both[:, pl.ds(pl.multiple_of(py * (width - LANES), LANES), width)]


def middle_pack_kernel(mine, got_1, got_2, got_3, own_pair, send_1, send_2, send_3, acc):
    z, x, c, y = coords()
    tiles = own_pair.shape[2] // LANES
    half_tiles = 2 * tiles - 1
    acc[...] = (mine[...] + got_1[...]) + (got_2[...] + got_3[...])

    def put(out, first, pitch):
        for i in range(2):
            for t in range(tiles):
                out[i, :, t * LANES : (t + 1) * LANES] = acc[first + i * pitch + t]

    for out, bits, px, py in ((own_pair, 0, x, y), (send_1, 3, 1 - x, 1 - y), (send_2, 2, 1 - x, y), (send_3, 1, x, 1 - y)):
        depth_first = 2 * tiles * depth_partner(z, bits)
        plane_first = 2 * half_tiles * px + (tiles - 1) * py
        put(out, jnp.where(c == 0, depth_first, plane_first), jnp.where(c == 0, tiles, half_tiles))


def gram_kernel(rows, band, scale, tan_ref, sec_ref, drift_ref, after_ref, conv_ref, low_ref, high_ref):
    views = tan_ref.shape[1]
    span = 2 * band + 1
    shape = (span * rows, views)
    row = row_iota(shape)
    shift = ((row % rows).astype(jnp.float32) - (rows - 1) / 2.0) * tan_ref[...] - drift_ref[...].astype(jnp.float32)
    hat = jnp.maximum(0.0, 1.0 - jnp.abs(shift - (row // rows - band).astype(jnp.float32)))
    gram = lax.dot_general(
        hat * ((scale / rows) * sec_ref[...]),
        hat,
        (((1,), (1,)), ((), ())),
        precision=lax.Precision.HIGHEST,
        preferred_element_type=jnp.float32,
    )
    edge = band * rows
    low_ref[...] = left_terms(gram[edge + rows :, edge + rows :])
    high_ref[...] = left_terms(gram[:edge, :edge])
    lanes = conv_ref.shape[1] // 3
    parts = conv_ref.shape[0] // rows
    width = lanes * parts
    padded = jnp.concatenate([gram, jnp.zeros((span * rows, width - span * rows), jnp.float32)], axis=1)
    total = jnp.zeros((rows, width), jnp.float32)
    for k in range(span):
        total = total + pltpu.roll(padded[k * rows : (k + 1) * rows], rows * (2 * band - k), 1)
    conv_ref[...] = left_terms(jnp.concatenate([total[:, i * lanes : (i + 1) * lanes] for i in range(parts)], axis=0))


def normal(volumes, conv, low_ref, high_ref, band, is_low, is_high):
    rows, width = volumes[0].shape
    step = conv.shape[1] // 3 // rows
    parts = conv.shape[0] // rows
    beyond = beyond_ends(volumes, low_ref, high_ref, band, is_low, is_high)
    zero = jnp.zeros((rows, width - 2 * LANES), jnp.float32)
    result = []
    for volume, piece in zip(volumes, beyond):
        moved = jnp.concatenate([pltpu.roll(volume, (2 * band - j) % width, 1) for j in range(step)], axis=0)
        spread = jnp.dot(conv, right_terms(moved), preferred_element_type=jnp.float32)
        total = spread[0:rows]
        for i in range(1, parts):
            total = total + pltpu.roll(spread[i * rows : (i + 1) * rows], width - step * i, 1)
        ends = [jnp.where(is_low, piece, 0.0), zero, jnp.where(is_high, piece, 0.0)]
        result.append(total - jnp.concatenate(ends, axis=1))
    return result


def beyond_ends(volumes, low_ref, high_ref, band, is_low, is_high):
    rows, width = volumes[0].shape
    pitch = LANES // len(volumes)
    lane = lane_iota((rows, LANES))
    tiles = [jnp.where(is_low, volume[:, :LANES], volume[:, width - LANES :]) for volume in volumes]
    offsets = [jnp.where(is_low, i + 1, i - band) for i in range(band)]
    moved = []
    for k in offsets:
        packed = jnp.zeros((rows, LANES), jnp.float32)
        for s, tile in enumerate(tiles):
            piece = pltpu.roll(tile, (s * pitch - (HALO - band) - k) % LANES, 1)
            packed = jnp.where((lane >= s * pitch) & (lane < (s + 1) * pitch), piece, packed)
        moved.append(packed)
    matrix = jnp.where(is_low, low_ref[...], high_ref[...]).astype(jnp.bfloat16)
    spread = jnp.dot(matrix, right_terms(jnp.concatenate(moved, axis=0)), preferred_element_type=jnp.float32)
    place = lane % pitch - jnp.where(is_low, 0, band)
    kept = [jnp.where((place >= 0) & (place < band), spread[i * rows : (i + 1) * rows], 0.0) for i in range(band)]
    near = (lane >= HALO - band) & (lane < HALO + band)
    result = []
    for s in range(len(volumes)):
        back = [pltpu.roll(kept[i], (HALO - band - s * pitch + k) % LANES, 1) for i, k in enumerate(offsets)]
        while len(back) > 1:
            back = [sum(back[i + 1 : i + 2], back[i]) for i in range(0, len(back), 2)]
        result.append(jnp.where(near, back[0], 0.0))
    return result


def block_place(width, total_cols):
    z, x, c, y = coords()
    block = width - 2 * HALO
    index = c * 2 + y
    return index * block - HALO, index == 0, index == total_cols // block - 1


def first_normal_kernel(band, total_cols, vol_mine, vol_got, conv_ref, low_ref, high_ref, out):
    _, is_low, is_high = block_place(vol_mine.shape[1], total_cols)
    _, _, _, y = coords()
    part = vol_mine.shape[0] // 2
    here, there = vol_mine[...], vol_got[...]
    upper = jnp.where(y == 0, here, there)
    lower = jnp.where(y == 0, there, here)
    volumes = [
        jnp.concatenate([upper[i * part : (i + 1) * part], lower[i * part : (i + 1) * part]], axis=0) for i in range(2)
    ]
    back = normal(volumes, conv_ref[...].astype(jnp.bfloat16), low_ref, high_ref, band, is_low, is_high)
    for i in range(2):
        out[i] = volumes[i] - back[i]


def half_pair_kernel(first_ref, own_pair, got_1, got_2, got_3, mine, to_x, to_diag, corr):
    _, x, _, _ = coords()
    corr[...] = (own_pair[...] + got_1[...]) + (got_2[...] + got_3[...])
    half = first_ref[...] + corr[...]
    mine[0:2] = half
    mine[2:4] = corr[...]
    to_x[0:2] = half
    to_x[2] = corr[1 - x]
    to_diag[0:2] = half
    to_diag[2] = corr[x]


def variation_step(half, z_of, first_col, depth, total_cols):
    rows, width = half[0].shape
    col = first_col + lane_iota((rows, width))
    row = row_iota((rows, width))
    inside = (col >= 0) & (col < total_cols - 1)
    units = []
    for w in range(len(half) - 1):
        v = half[w]
        keep = (z_of(w) >= 0) & (z_of(w) < depth - 1)
        dz = jnp.where(keep, half[w + 1] - v, 0.0)
        dr = jnp.where(row < rows - 1, pltpu.roll(v, rows - 1, 0) - v, 0.0)
        dc = jnp.where(inside, pltpu.roll(v, width - 1, 1) - v, 0.0)
        inverse = lax.rsqrt(dz * dz + dr * dr + dc * dc + SMOOTH_EPS * SMOOTH_EPS)
        units.append((dz * inverse, dr * inverse, dc * inverse))
    result = []
    for w in range(1, len(half) - 1):
        uz, ur, uc = units[w]
        div = (uz - units[w - 1][0]) + (ur - pltpu.roll(ur, 1, 0)) + (uc - pltpu.roll(uc, 1, 1))
        result.append(jnp.where((col >= 0) & (col < total_cols), half[w] + TV_STEP * div, 0.0))
    return result


def finish_kernel(
    band, depth, total_cols, mine, got_diag, got_x, conv_ref, low_ref, high_ref, keep_ref, send_ref, done
):
    width = mine.shape[2]
    first_col, is_low, is_high = block_place(width, total_cols)
    z, x, c, _ = coords()
    before = [jnp.where(x == 0, got_diag[i], got_x[i]) for i in range(3)]
    after = [jnp.where(x == 0, got_x[i], got_diag[i]) for i in range(3)]
    half = [before[0], before[1], mine[0], mine[1], after[0], after[1]]
    corr = [before[2], mine[2], mine[3], after[2]]
    slice_0 = 4 * z + 2 * x
    volumes = variation_step(half, lambda w: slice_0 - 2 + w, first_col, depth, total_cols)
    back = normal(volumes, conv_ref[...].astype(jnp.bfloat16), low_ref, high_ref, band, is_low, is_high)
    half = [volumes[s] + corr[s] - back[s] for s in range(4)]
    volumes = variation_step(half, lambda w: slice_0 - 1 + w, first_col, depth, total_cols)
    for s in range(2):
        done[s] = pltpu.roll(volumes[s], width - HALO, 1)[:, : width - LANES]
    keep_ref[...] = done[c]
    send_ref[...] = done[1 - c]


def result_pack_kernel(own_ref, got_ref, to_y):
    _, _, c, y = coords()
    part = to_y.shape[1]
    own, got = own_ref[...], got_ref[...]
    to_y[c] = jnp.where(y == 0, own[part:], own[:part])
    to_y[1 - c] = jnp.where(y == 0, got[part:], got[:part])


def result_kernel(own_ref, got_ref, got_y, out):
    _, _, c, y = coords()
    _, part, block = got_y.shape
    own, got = own_ref[...], got_ref[...]
    here = jnp.where(y == 0, own[:part], own[part:])
    there = jnp.where(y == 0, got[:part], got[part:])
    for value, h, q in ((here, c, y), (there, 1 - c, y), (got_y[0], 0, 1 - y), (got_y[1], 1, 1 - y)):
        out[0, :, pl.ds(pl.multiple_of((2 * h + q) * block, LANES), block)] = value


def f32(*shape):
    return jax.ShapeDtypeStruct(shape, jnp.float32)


VMEM_SPEC = pl.BlockSpec(memory_space=pltpu.VMEM)
SMEM_SPEC = pl.BlockSpec(memory_space=pltpu.SMEM)
ANY_SPEC = pl.BlockSpec(memory_space=pl.ANY)
HBM_SPEC = pl.BlockSpec(memory_space=pltpu.HBM)
PARAMS = pltpu.CompilerParams(vmem_limit_bytes=40 * 1024 * 1024)


def in_hbm(value):
    return pltpu.with_memory_space_constraint(value, pltpu.HBM)


def kernel_call(body, outs, in_specs, scratch, name, flops=0, size=0):
    many = isinstance(outs, (list, tuple))
    return pl.pallas_call(
        body,
        out_shape=outs,
        in_specs=in_specs,
        out_specs=[VMEM_SPEC] * len(outs) if many else VMEM_SPEC,
        scratch_shapes=scratch,
        compiler_params=PARAMS,
        name=name,
        cost_estimate=pl.CostEstimate(flops=flops, bytes_accessed=size, transcendentals=0),
    )


def summed_plan(measured, drift, start_volume):
    views, slices, cols = measured.shape
    part = start_volume.shape[1]
    rows = 2 * part
    band = rows // 2 + DMAX + 2
    total_angles = drift.shape[0]
    half_cols = cols // 2
    half_width = half_cols + LANES
    width = cols // 4 + 2 * HALO
    tangent, secant = tan_and_secant(total_angles)
    scale = float(1.0 / np.sum(secant))
    tangent, secant = tangent.astype(np.float32), secant.astype(np.float32)

    tiles = half_width // LANES
    groups = slices // SUB
    window = (groups, views + 1, tiles + 2, SUB, LANES)
    tiled = measured.reshape(views, groups, SUB, cols // LANES, LANES).transpose(0, 1, 3, 2, 4)
    table = ((2 * band // STEP + 1) * rows, 3 * STEP * views)
    count = slices // 2
    terms = pltpu.VMEM((slices, 3 * STEP * views, half_width + LANES), jnp.bfloat16)
    vbuf = pltpu.VMEM((part, cols + 2 * LANES), jnp.float32)
    half_of = f32(count, rows, half_width)
    sibling, own_buf, weights, volume = kernel_call(
        functools.partial(fetch_kernel, views, rows, band, scale),
        [f32(slices + 1, rows, half_width), f32(*window), f32(*table), f32(1, part, cols)],
        [HBM_SPEC] * 4,
        [
            pltpu.SMEM((total_angles,), jnp.float32),
            pltpu.SMEM((total_angles,), jnp.int32),
            pltpu.VMEM(window, jnp.float32),
            terms,
            vbuf,
            pltpu.SemaphoreType.DMA((3,)),
            pltpu.SemaphoreType.DMA((2, groups)),
        ],
        "other_share",
        flops=10**9,
    )(in_hbm(jnp.asarray(tangent)), in_hbm(drift), in_hbm(tiled), in_hbm(start_volume))
    got = move(sibling, lambda z, x, c, y: (z, x, 1 - c, y))
    own = kernel_call(
        functools.partial(own_kernel, views, rows, band),
        f32(slices, rows, half_width),
        [VMEM_SPEC] * 2,
        [terms],
        "own_share",
        flops=10**9,
    )(own_buf, weights)

    message = f32(count * width // LANES, rows, LANES)
    mine, send_1, send_2, send_3 = kernel_call(
        plane_pack_kernel,
        [message] * 4,
        [VMEM_SPEC] * 2,
        [pltpu.VMEM(half_of.shape, jnp.float32)] * 2,
        "plane_pack",
    )(own, got)
    vol_mine, vol_to_y = kernel_call(
        volume_pack_kernel,
        [f32(rows, width)] * 2,
        [ANY_SPEC, VMEM_SPEC, VMEM_SPEC],
        [pltpu.VMEM((rows, half_width), jnp.float32), vbuf],
        "volume_pack",
    )(own, got, volume)
    got_1 = move(send_1, lambda z, x, c, y: (z ^ 2, x, c, y) if c else (z, 1 - x, c, 1 - y))
    got_2 = move(send_2, lambda z, x, c, y: (z ^ 3, x, c, y) if c else (z, x, c, 1 - y))
    got_3 = move(send_3, lambda z, x, c, y: (z ^ 1, x, c, y) if c else (z, 1 - x, c, y))
    vol_got = move(vol_to_y, lambda z, x, c, y: (z, x, c, 1 - y))

    edge = band * rows
    conv, low, high = kernel_call(
        functools.partial(gram_kernel, rows, band, scale),
        [f32(6 * rows, 24 * rows), f32(edge, 3 * edge), f32(edge, 3 * edge)],
        [VMEM_SPEC] * 3 + [ANY_SPEC],
        [],
        "gram",
    )(tangent[None], secant[None], drift[None], mine)

    pair = f32(2, rows, width)
    own_pair, send_1, send_2, send_3 = kernel_call(
        middle_pack_kernel,
        [pair] * 4,
        [VMEM_SPEC] * 4,
        [pltpu.VMEM(message.shape, jnp.float32)],
        "middle_pack",
    )(mine, got_1, got_2, got_3)
    got_1 = move(send_1, lambda z, x, c, y: (z, 1 - x, c, 1 - y) if c else (z ^ 3, x, c, y))
    got_2 = move(send_2, lambda z, x, c, y: (z, 1 - x, c, y) if c else (z ^ 2, x, c, y))
    got_3 = move(send_3, lambda z, x, c, y: (z, x, c, 1 - y) if c else (z ^ 1, x, c, y))

    first = kernel_call(
        functools.partial(first_normal_kernel, band, cols),
        pair,
        [VMEM_SPEC] * 5,
        [],
        "first_normal",
        flops=10**9,
    )(vol_mine, vol_got, conv, low, high)

    three = f32(3, rows, width)
    mine, to_x, to_diag = kernel_call(
        half_pair_kernel,
        [f32(4, rows, width), three, three],
        [VMEM_SPEC] * 5,
        [pltpu.VMEM((2, rows, width), jnp.float32)],
        "half_pair",
    )(first, own_pair, got_1, got_2, got_3)
    got_diag = move(to_diag, beside)
    got_x = move(to_x, lambda z, x, c, y: (z, 1 - x, c, y))

    block = width - 2 * HALO
    quarter = f32(rows, block)
    keep, send = kernel_call(
        functools.partial(finish_kernel, band, slices, cols),
        [quarter, quarter],
        [VMEM_SPEC] * 6,
        [pltpu.VMEM((2, rows, block), jnp.float32)],
        "finish",
    )(mine, got_diag, got_x, conv, low, high)
    swapped = move(send, lambda z, x, c, y: (z, x, 1 - c, y))
    to_y = kernel_call(result_pack_kernel, f32(2, part, block), [VMEM_SPEC] * 2, [], "result_pack")(keep, swapped)
    got_y = move(to_y, lambda z, x, c, y: (z, x, c, 1 - y))
    return kernel_call(result_kernel, f32(1, part, cols), [VMEM_SPEC] * 3, [], "result")(keep, swapped, got_y)


def summed_plan_fits(mesh, measured, start_volume):
    rows = start_volume.shape[1]
    cols = measured.shape[2]
    return (
        ITERS == 2
        and dict(mesh.shape) == {"wide": 16, "grp": 2}
        and measured.shape[1] == start_volume.shape[0] == 16
        and rows == SUB
        and cols % (16 * LANES) == 0
        and measured.shape[0] % 256 == 0
    )


def solution(mesh):
    in_specs = (P(("wide", "grp"), None, None), P(), P("wide", "grp", None))
    out_specs = P("wide", "grp", None)

    def run(measured, drift, start_volume):
        plan = summed_plan if summed_plan_fits(mesh, measured, start_volume) else on_device
        return jax.shard_map(plan, mesh=mesh, in_specs=in_specs, out_specs=out_specs, check_vma=False)(
            measured, drift, start_volume
        )

    return run
```

```python
import functools
from functools import reduce
import math

import jax
import jax.numpy as jnp
import numpy as np
from jax import lax
from jax.experimental import pallas as pl
from jax.experimental.pallas import tpu as pltpu
from jax.sharding import PartitionSpec as P

ITERS = 2
DMAX = 4


TILT_MAX = math.pi / 4
SMOOTH_EPS = 0.05
TV_STEP = 0.1


def with_halo(block, sides, width):
    for axis, dim in sides:
        count = lax.axis_size(axis)
        forward = [(i, i + 1) for i in range(count - 1)]
        backward = [(target, source) for source, target in forward]
        low = lax.ppermute(
            lax.slice_in_dim(block, block.shape[dim] - width, None, axis=dim), axis, forward
        )
        high = lax.ppermute(lax.slice_in_dim(block, 0, width, axis=dim), axis, backward)
        block = jnp.concatenate([low, block, high], axis=dim)
    return block


def geometry(angle_ids, drift_vals, total_angles, rows, band_extent):
    angle_rad = TILT_MAX * (2.0 * angle_ids.astype(jnp.float32) / (total_angles - 1) - 1.0)
    secant = 1.0 / jnp.cos(angle_rad)
    height = jnp.arange(rows, dtype=jnp.float32) - (rows - 1) / 2.0
    offsets = jnp.arange(2 * band_extent + 1, dtype=jnp.float32) - band_extent
    shifts = height[None, :] * jnp.tan(angle_rad)[:, None] - drift_vals.astype(jnp.float32)[:, None]
    weight_factors = secant[:, None, None] * jnp.maximum(
        0.0, 1.0 - jnp.abs(shifts[:, :, None] - offsets[None, None, :])
    )
    return (weight_factors, jnp.cos(angle_rad) / rows)


def secant_sum(total_angles):
    angle_rad = TILT_MAX * (
        2.0 * jnp.arange(total_angles, dtype=jnp.float32) / (total_angles - 1) - 1.0
    )
    return jnp.sum(1.0 / jnp.cos(angle_rad))


def local_geometry(angle_ids, drift, total_angles, rows_all, band_extent):
    matches = angle_ids[:, None] == jnp.arange(total_angles, dtype=jnp.int32)[None, :]
    local_drift = jnp.sum(jnp.where(matches, drift[None, :], 0), axis=1)
    return geometry(angle_ids, local_drift, total_angles, rows_all, band_extent)


def apply_correction(
    row_band_strip, measurement_part, weight_factors, residual_scale, global_scale, band_extent
):
    col_count = row_band_strip.shape[2]
    span = 2 * band_extent + 1
    padded = jnp.pad(row_band_strip, ((0, 0), (0, 0), (band_extent, band_extent)))
    shifted = jnp.stack(
        [padded[:, :, shift_id : shift_id + col_count] for shift_id in range(span)], axis=2
    )
    forward_projected = jnp.einsum(
        "ark,zrku->azu", weight_factors, shifted, precision=lax.Precision.HIGHEST
    )
    residual_error = residual_scale[:, None, None] * (measurement_part - forward_projected)
    spread = jnp.einsum(
        "ark,azu->kzru", weight_factors, residual_error, precision=lax.Precision.HIGHEST
    )
    spread = jnp.pad(spread, ((0, 0), (0, 0), (0, 0), (band_extent, band_extent)))
    pieces = [
        spread[shift_id, :, :, 2 * band_extent - shift_id : 2 * band_extent - shift_id + col_count]
        for shift_id in range(span)
    ]
    return global_scale * reduce(lambda left, right: left + right, pieces)


def divergence(extended, z_first, r_first, zcount, rcount):
    plane_count, height, col_count = extended.shape
    z_index = z_first + jnp.arange(plane_count, dtype=jnp.int32)[:, None, None]
    row_index = r_first + jnp.arange(height, dtype=jnp.int32)[None, :, None]
    col_index = jnp.arange(col_count, dtype=jnp.int32)[None, None, :]
    diff_z = jnp.concatenate([extended[1:] - extended[:-1], jnp.zeros_like(extended[:1])], axis=0)
    diff_z = jnp.where((z_index >= 0) & (z_index < zcount - 1), diff_z, 0.0)
    diff_r = jnp.concatenate(
        [extended[:, 1:] - extended[:, :-1], jnp.zeros_like(extended[:, :1])], axis=1
    )
    diff_r = jnp.where((row_index >= 0) & (row_index < rcount - 1), diff_r, 0.0)
    diff_c = jnp.concatenate(
        [extended[:, :, 1:] - extended[:, :, :-1], jnp.zeros_like(extended[:, :, :1])], axis=2
    )
    diff_c = jnp.where(col_index < col_count - 1, diff_c, 0.0)
    magnitude = jnp.sqrt(
        diff_z * diff_z + diff_r * diff_r + diff_c * diff_c + SMOOTH_EPS * SMOOTH_EPS
    )
    unit_z = diff_z / magnitude
    unit_r = diff_r / magnitude
    unit_c = diff_c / magnitude
    back_c = unit_c - jnp.concatenate([jnp.zeros_like(unit_c[:, :, :1]), unit_c[:, :, :-1]], axis=2)
    return (
        unit_z[1:-1, 1:-1]
        - unit_z[:-2, 1:-1]
        + (unit_r[1:-1, 1:-1] - unit_r[1:-1, :-2])
        + back_c[1:-1, 1:-1]
    )


def on_device(measured, drift, start_volume):
    wide_count = lax.axis_size("wide")
    groups = lax.axis_size("grp")
    slab_count, rows_tile, col_count = start_volume.shape
    rows_all = rows_tile * groups
    band_extent = rows_all // 2 + DMAX + 2
    per_device = measured.shape[0]
    total_angles = per_device * wide_count * groups
    global_scale = 1.0 / secant_sum(total_angles)
    z_first = lax.axis_index("wide") * slab_count - 1
    zcount = slab_count * wide_count
    local_measurement = lax.all_to_all(measured, "wide", split_axis=1, concat_axis=0, tiled=True)
    bin_position = jnp.arange(local_measurement.shape[0], dtype=jnp.int32)
    angle_ids = (
        bin_position // per_device * groups + lax.axis_index("grp")
    ) * per_device + bin_position % per_device
    weight_factors, residual_scale = local_geometry(
        angle_ids, drift, total_angles, rows_all, band_extent
    )
    own_tile = start_volume
    r_first = lax.axis_index("grp") * rows_tile - 1
    for sweep in range(ITERS):
        row_band_strip = lax.all_gather(own_tile, "grp", axis=1, tiled=True)
        volume_update = apply_correction(
            row_band_strip,
            local_measurement,
            weight_factors,
            residual_scale,
            global_scale,
            band_extent,
        )
        own_tile = own_tile + lax.psum_scatter(
            volume_update, "grp", scatter_dimension=1, tiled=True
        )
        extended = with_halo(own_tile, (("wide", 0), ("grp", 1)), 1)
        own_tile = own_tile + TV_STEP * divergence(extended, z_first, r_first, zcount, rows_all)
    return own_tile


LANES = 128
SUB = 8
HALO = 64


def tan_and_secant(total_angles):
    angle = TILT_MAX * (2.0 * np.arange(total_angles) / (total_angles - 1) - 1.0)
    return np.tan(angle), 1.0 / np.cos(angle)


def coords():
    wide, y = lax.axis_index("wide"), lax.axis_index("grp")
    return wide // 4, wide // 2 % 2, wide % 2, y


def move(value, target):
    pairs = []
    for z in range(4):
        for x in range(2):
            for c in range(2):
                for y in range(2):
                    tz, tx, tc, ty = target(z, x, c, y)
                    pairs.append((((z * 2 + x) * 2 + c) * 2 + y, ((tz * 2 + tx) * 2 + tc) * 2 + ty))
    return lax.ppermute(value, ("wide", "grp"), pairs)


def beside(z, x, c, y):
    if (z, x) in ((0, 0), (3, 1)):
        return z, x, 1 - c, y
    return (z + 1, 0, c, y) if x else (z - 1, 1, c, y)


def split_rows(value):
    high = value.astype(jnp.bfloat16).astype(jnp.float32)
    return jnp.concatenate([high, value - high], axis=0)


def left_terms(value):
    high = value.astype(jnp.bfloat16).astype(jnp.float32)
    return jnp.concatenate([high, high, value - high], axis=1)


def split_terms(value):
    high = value.astype(jnp.bfloat16)
    low = (value - high.astype(jnp.float32)).astype(jnp.bfloat16)
    return jnp.concatenate([high, low], axis=0)


def right_terms(value):
    high = value.astype(jnp.bfloat16)
    low = (value - high.astype(jnp.float32)).astype(jnp.bfloat16)
    return jnp.concatenate([high, low, high], axis=0)


def lane_iota(shape):
    return lax.broadcasted_iota(jnp.int32, shape, len(shape) - 1)


def row_iota(shape):
    return lax.broadcasted_iota(jnp.int32, shape, len(shape) - 2)


STEP = 3


def view_weights(views, rows, band, scale, tan_ref, drift_ref):
    z, x, c, y = coords()
    first_view = (((z * 2 + x) * 2 + c) * 2 + y) * views
    parts = 2 * band // STEP + 1
    shape = (parts * rows, STEP * views)
    lane, row = lane_iota(shape), row_iota(shape)
    view_of = lane_iota((1, STEP * views)) % views
    tan_lane = jnp.zeros((1, STEP * views), jnp.float32)
    drift_lane = tan_lane
    for a in range(views):
        tan_lane = jnp.where(view_of == a, tan_ref[first_view + a], tan_lane)
        drift_lane = jnp.where(view_of == a, drift_ref[first_view + a].astype(jnp.float32), drift_lane)
    shift = ((row % rows).astype(jnp.float32) - (rows - 1) / 2.0) * tan_lane - drift_lane
    offset = ((row // rows) * STEP + lane // views - band).astype(jnp.float32)
    weights = (scale / rows) * jnp.maximum(0.0, 1.0 - jnp.abs(shift - offset))
    return left_terms(weights).astype(jnp.bfloat16)


def back_project(views, rows, band, weights, load_strip, begin, out_ref, terms):
    count, _, width = terms.shape[0] // 2, *terms.shape[1:]
    out_cols = out_ref.shape[2]
    parts = 2 * band // STEP + 1
    for n in range(count):
        strip = load_strip(n)
        high = strip.astype(jnp.bfloat16)
        low = (strip - high.astype(jnp.float32)).astype(jnp.bfloat16)
        for j in range(STEP):
            moved = pltpu.roll(high, j, 1) if j else high
            terms[begin + n, j * views : (j + 1) * views] = moved
            terms[begin + n, (STEP + j) * views : (STEP + j + 1) * views] = pltpu.roll(low, j, 1) if j else low
            terms[begin + n, (2 * STEP + j) * views : (2 * STEP + j + 1) * views] = moved
    for n in range(count):
        spread = jnp.dot(weights, terms[begin + n], preferred_element_type=jnp.float32)
        total = None
        for i in range(parts):
            piece = pltpu.roll(spread[i * rows : (i + 1) * rows], width - HALO - band + STEP * i, 1)
            total = piece if total is None else total + piece
        out_ref[begin + n] = total[:, :out_cols]


def depth_partner(z, bits):
    return {0: z, 1: z + 1 - 2 * (z % 2), 2: (z + 2) % 4, 3: 3 - z}[bits]


def slice_place(half, kept, n):
    z, x, _, _ = coords()
    parity = x if kept else 1 - x
    four = depth_partner(z, (1, 0)[n // 4] if kept else (2, 3)[n // 4])
    group = jnp.where(half == 0, n // 4, four // 2)
    place = jnp.where(half == 0, 4 * (n // 2 % 2) + 2 * parity + n % 2, 4 * (four % 2) + n % 4)
    return group, place


def strip_loader(buf, half, kept, views, tiles):
    pitch = (tiles + 2) * SUB

    def load(n):
        group, place = slice_place(half, kept, n)
        first = half * SUB + place
        return jnp.concatenate(
            [buf[group, pl.ds(first + t * SUB, views, stride=pitch), :] for t in range(tiles + 1)], axis=1
        )

    return load


def volume_window(vol_ref, half, half_cols, vbuf):
    part, cols = vol_ref.shape[1:]
    vbuf[:, 0:LANES] = jnp.zeros((part, LANES), jnp.float32)
    vbuf[:, LANES : LANES + cols] = vol_ref[0]
    vbuf[:, LANES + cols :] = jnp.zeros((part, LANES), jnp.float32)
    width = half_cols + 2 * LANES
    window = vbuf[:, pl.ds(pl.multiple_of(half * half_cols, LANES), width)]
    return pltpu.roll(window, width - HALO, 1)[:, : half_cols + LANES]


def fetch_kernel(views, rows, band, scale, tan_hbm, drift_hbm, meas_hbm, vol_hbm, out_ref, own_buf, weights_ref, vol_ref,
                 tan_ref, drift_ref, sibling_buf, terms, vbuf, table_sem, sem):
    z, _, c, _ = coords()
    tiles = out_ref.shape[2] // LANES
    groups = sibling_buf.shape[0]

    def fetch(half, target, g, semaphore):
        return pltpu.make_async_copy(
            meas_hbm.at[:, g, pl.ds(half * (tiles - 2), tiles)], target.at[g, 0:views, 1 : tiles + 1], semaphore
        )

    tables = [
        pltpu.make_async_copy(tan_hbm, tan_ref, table_sem.at[0]),
        pltpu.make_async_copy(drift_hbm, drift_ref, table_sem.at[1]),
    ]
    vol_copy = pltpu.make_async_copy(vol_hbm, vol_ref, table_sem.at[2])
    soon = jnp.where(c == 0, 1 - z // 2, 0)
    first = [fetch(1 - c, sibling_buf, g, sem.at[0, g]) for g in (soon, 1 - soon)]
    later = [fetch(c, own_buf, g, sem.at[1, g]) for g in range(groups)]
    for copy in first[:1] + tables + first[1:] + [vol_copy] + later:
        copy.start()
    zero = jnp.zeros((views, SUB, LANES), jnp.float32)
    for g in range(groups):
        for target in (sibling_buf, own_buf):
            target[g, 0:views, 0] = zero
            target[g, 0:views, tiles + 1] = zero
    for copy in tables:
        copy.wait()
    weights = view_weights(views, rows, band, scale, tan_ref, drift_ref)
    weights_ref[...] = weights.astype(jnp.float32)
    load, load_kept = (strip_loader(flat_rows(sibling_buf), 1 - c, kept, views, tiles) for kept in (False, True))

    def load_strip(n):
        if n % 4 == 0:
            first[n // 4].wait()
        return load(n)

    count = terms.shape[0] // 2
    back_project(views, rows, band, weights, load_strip, 0, out_ref, terms)
    back_project(views, rows, band, weights, load_kept, count, out_ref, terms)
    vol_copy.wait()
    half_cols = out_ref.shape[2] - LANES
    part = vol_ref.shape[1]
    out_ref[2 * count, 0:part] = volume_window(vol_ref, 1 - c, half_cols, vbuf)
    out_ref[2 * count, part:] = jnp.zeros((rows - part, half_cols + LANES), jnp.float32)
    for copy in later:
        copy.wait()


def flat_rows(buf):
    groups, views, tiles, sub, lanes = buf.shape
    return buf.reshape(groups, views * tiles * sub, lanes)


def own_kernel(views, rows, band, buf, weights_ref, out_ref, terms):
    _, _, c, _ = coords()
    tiles = out_ref.shape[2] // LANES
    weights = weights_ref[...].astype(jnp.bfloat16)
    for kept in (False, True):
        load = strip_loader(flat_rows(buf), c, kept, views, tiles)
        back_project(views, rows, band, weights, load, terms.shape[0] // 2 if kept else 0, out_ref, terms)


def put_quarter(out, acc, py, tiles):
    for n in range(acc.shape[0]):
        for t in range(tiles):
            out[n * tiles + t] = acc[n, :, pl.ds(pl.multiple_of(((tiles - 1) * py + t) * LANES, LANES), LANES)]


def put_four(out, acc, first):
    tiles = acc.shape[2] // LANES
    for n in range(4):
        for t in range(tiles):
            out[n * tiles + t] = acc[first + n, :, t * LANES : (t + 1) * LANES]
    for t in range(4 * tiles, out.shape[0]):
        out[t] = jnp.zeros(out.shape[1:], jnp.float32)


def plane_pack_kernel(own_ref, got_ref, mine, send_1, send_2, send_3, passed, acc):
    count, _, half_width = passed.shape
    tiles = mine.shape[0] // count
    _, _, c, y = coords()
    passed[...] = own_ref[0:count] + got_ref[0:count]
    acc[...] = own_ref[count:] + got_ref[count : 2 * count]

    @pl.when(c == 0)
    def _():
        put_quarter(send_1, passed, 1 - y, tiles)
        put_quarter(send_2, acc, 1 - y, tiles)
        put_quarter(send_3, passed, y, tiles)
        put_quarter(mine, acc, y, tiles)

    @pl.when(c == 1)
    def _():
        put_four(send_1, passed, 0)
        put_four(send_2, passed, 4)
        put_four(send_3, acc, 0)
        put_four(mine, acc, 4)


def volume_pack_kernel(own_ref, got_ref, vol_ref, vol_mine, vol_to_y, both, vbuf):
    count, rows, half_width = own_ref.shape
    part = vol_ref.shape[1]
    _, _, c, y = coords()
    here = volume_window(vol_ref, c, half_width - LANES, vbuf)
    there = got_ref[count, 0:part]
    both[0:part] = jnp.where(c == 0, here, there)
    both[part:] = jnp.where(c == 0, there, here)
    width = vol_mine.shape[1]
    for vol, py in ((vol_mine, y), (vol_to_y, 1 - y)):
        vol[...] = both[:, pl.ds(pl.multiple_of(py * (width - LANES), LANES), width)]


def middle_pack_kernel(mine, got_1, got_2, got_3, own_pair, send_1, send_2, send_3, acc):
    z, x, c, y = coords()
    tiles = own_pair.shape[2] // LANES
    half_tiles = 2 * tiles - 1
    acc[...] = (mine[...] + got_1[...]) + (got_2[...] + got_3[...])

    def put(out, first, pitch):
        for i in range(2):
            for t in range(tiles):
                out[i, :, t * LANES : (t + 1) * LANES] = acc[first + i * pitch + t]

    for out, bits, px, py in ((own_pair, 0, x, y), (send_1, 3, 1 - x, 1 - y), (send_2, 2, 1 - x, y), (send_3, 1, x, 1 - y)):
        depth_first = 2 * tiles * depth_partner(z, bits)
        plane_first = 2 * half_tiles * px + (tiles - 1) * py
        put(out, jnp.where(c == 0, depth_first, plane_first), jnp.where(c == 0, tiles, half_tiles))


def gram_kernel(rows, band, scale, tan_ref, sec_ref, drift_ref, after_ref, conv_ref, low_ref, high_ref):
    views = tan_ref.shape[1]
    span = 2 * band + 1
    shape = (span * rows, views)
    row = row_iota(shape)
    shift = ((row % rows).astype(jnp.float32) - (rows - 1) / 2.0) * tan_ref[...] - drift_ref[...].astype(jnp.float32)
    hat = jnp.maximum(0.0, 1.0 - jnp.abs(shift - (row // rows - band).astype(jnp.float32)))
    gram = lax.dot_general(
        hat * ((scale / rows) * sec_ref[...]),
        hat,
        (((1,), (1,)), ((), ())),
        precision=lax.Precision.HIGHEST,
        preferred_element_type=jnp.float32,
    )
    edge = band * rows
    low_ref[...] = left_terms(gram[edge + rows :, edge + rows :])
    high_ref[...] = left_terms(gram[:edge, :edge])
    lanes = conv_ref.shape[1] // 3
    parts = conv_ref.shape[0] // rows
    width = lanes * parts
    padded = jnp.concatenate([gram, jnp.zeros((span * rows, width - span * rows), jnp.float32)], axis=1)
    total = jnp.zeros((rows, width), jnp.float32)
    for k in range(span):
        total = total + pltpu.roll(padded[k * rows : (k + 1) * rows], rows * (2 * band - k), 1)
    conv_ref[...] = left_terms(jnp.concatenate([total[:, i * lanes : (i + 1) * lanes] for i in range(parts)], axis=0))


def normal(volumes, conv, low_ref, high_ref, band, is_low, is_high):
    rows, width = volumes[0].shape
    step = conv.shape[1] // 3 // rows
    parts = conv.shape[0] // rows
    beyond = beyond_ends(volumes, low_ref, high_ref, band, is_low, is_high)
    zero = jnp.zeros((rows, width - 2 * LANES), jnp.float32)
    result = []
    for volume, piece in zip(volumes, beyond):
        moved = jnp.concatenate([pltpu.roll(volume, (2 * band - j) % width, 1) for j in range(step)], axis=0)
        spread = jnp.dot(conv, right_terms(moved), preferred_element_type=jnp.float32)
        total = spread[0:rows]
        for i in range(1, parts):
            total = total + pltpu.roll(spread[i * rows : (i + 1) * rows], width - step * i, 1)
        ends = [jnp.where(is_low, piece, 0.0), zero, jnp.where(is_high, piece, 0.0)]
        result.append(total - jnp.concatenate(ends, axis=1))
    return result


def beyond_ends(volumes, low_ref, high_ref, band, is_low, is_high):
    rows, width = volumes[0].shape
    pitch = LANES // len(volumes)
    lane = lane_iota((rows, LANES))
    tiles = [jnp.where(is_low, volume[:, :LANES], volume[:, width - LANES :]) for volume in volumes]
    offsets = [jnp.where(is_low, i + 1, i - band) for i in range(band)]
    moved = []
    for k in offsets:
        packed = jnp.zeros((rows, LANES), jnp.float32)
        for s, tile in enumerate(tiles):
            piece = pltpu.roll(tile, (s * pitch - (HALO - band) - k) % LANES, 1)
            packed = jnp.where((lane >= s * pitch) & (lane < (s + 1) * pitch), piece, packed)
        moved.append(packed)
    matrix = jnp.where(is_low, low_ref[...], high_ref[...]).astype(jnp.bfloat16)
    spread = jnp.dot(matrix, right_terms(jnp.concatenate(moved, axis=0)), preferred_element_type=jnp.float32)
    place = lane % pitch - jnp.where(is_low, 0, band)
    kept = [jnp.where((place >= 0) & (place < band), spread[i * rows : (i + 1) * rows], 0.0) for i in range(band)]
    near = (lane >= HALO - band) & (lane < HALO + band)
    result = []
    for s in range(len(volumes)):
        back = [pltpu.roll(kept[i], (HALO - band - s * pitch + k) % LANES, 1) for i, k in enumerate(offsets)]
        while len(back) > 1:
            back = [sum(back[i + 1 : i + 2], back[i]) for i in range(0, len(back), 2)]
        result.append(jnp.where(near, back[0], 0.0))
    return result


def block_place(width, total_cols):
    z, x, c, y = coords()
    block = width - 2 * HALO
    index = c * 2 + y
    return index * block - HALO, index == 0, index == total_cols // block - 1


def first_normal_kernel(band, total_cols, vol_mine, vol_got, conv_ref, low_ref, high_ref, out):
    _, is_low, is_high = block_place(vol_mine.shape[1], total_cols)
    _, _, _, y = coords()
    part = vol_mine.shape[0] // 2
    here, there = vol_mine[...], vol_got[...]
    upper = jnp.where(y == 0, here, there)
    lower = jnp.where(y == 0, there, here)
    volumes = [
        jnp.concatenate([upper[i * part : (i + 1) * part], lower[i * part : (i + 1) * part]], axis=0) for i in range(2)
    ]
    back = normal(volumes, conv_ref[...].astype(jnp.bfloat16), low_ref, high_ref, band, is_low, is_high)
    for i in range(2):
        out[i] = volumes[i] - back[i]


def half_pair_kernel(first_ref, own_pair, got_1, got_2, got_3, mine, to_x, to_diag, corr):
    _, x, _, _ = coords()
    corr[...] = (own_pair[...] + got_1[...]) + (got_2[...] + got_3[...])
    half = first_ref[...] + corr[...]
    mine[0:2] = half
    mine[2:4] = corr[...]
    to_x[0:2] = half
    to_x[2] = corr[1 - x]
    to_diag[0:2] = half
    to_diag[2] = corr[x]


def variation_step(half, z_of, first_col, depth, total_cols):
    rows, width = half[0].shape
    col = first_col + lane_iota((rows, width))
    row = row_iota((rows, width))
    inside = (col >= 0) & (col < total_cols - 1)
    units = []
    for w in range(len(half) - 1):
        v = half[w]
        keep = (z_of(w) >= 0) & (z_of(w) < depth - 1)
        dz = jnp.where(keep, half[w + 1] - v, 0.0)
        dr = jnp.where(row < rows - 1, pltpu.roll(v, rows - 1, 0) - v, 0.0)
        dc = jnp.where(inside, pltpu.roll(v, width - 1, 1) - v, 0.0)
        inverse = lax.rsqrt(dz * dz + dr * dr + dc * dc + SMOOTH_EPS * SMOOTH_EPS)
        units.append((dz * inverse, dr * inverse, dc * inverse))
    result = []
    for w in range(1, len(half) - 1):
        uz, ur, uc = units[w]
        div = (uz - units[w - 1][0]) + (ur - pltpu.roll(ur, 1, 0)) + (uc - pltpu.roll(uc, 1, 1))
        result.append(jnp.where((col >= 0) & (col < total_cols), half[w] + TV_STEP * div, 0.0))
    return result


def finish_kernel(
    band, depth, total_cols, mine, got_diag, got_x, conv_ref, low_ref, high_ref, keep_ref, send_ref
):
    width = mine.shape[2]
    first_col, is_low, is_high = block_place(width, total_cols)
    z, x, c, _ = coords()
    before = [jnp.where(x == 0, got_diag[i], got_x[i]) for i in range(3)]
    after = [jnp.where(x == 0, got_x[i], got_diag[i]) for i in range(3)]
    half = [before[0], before[1], mine[0], mine[1], after[0], after[1]]
    corr = [before[2], mine[2], mine[3], after[2]]
    slice_0 = 4 * z + 2 * x
    volumes = variation_step(half, lambda w: slice_0 - 2 + w, first_col, depth, total_cols)
    back = normal(volumes, conv_ref[...].astype(jnp.bfloat16), low_ref, high_ref, band, is_low, is_high)
    half = [volumes[s] + corr[s] - back[s] for s in range(4)]
    volumes = variation_step(half, lambda w: slice_0 - 1 + w, first_col, depth, total_cols)
    kept = jnp.where(c == 0, volumes[0], volumes[1])
    sent = jnp.where(c == 0, volumes[1], volumes[0])
    keep_ref[...] = pltpu.roll(kept, width - HALO, 1)[:, : width - LANES]
    send_ref[...] = pltpu.roll(sent, width - HALO, 1)[:, : width - LANES]


def result_pack_kernel(own_ref, got_ref, to_y):
    _, _, c, y = coords()
    part = to_y.shape[1]
    own, got = own_ref[...], got_ref[...]
    to_y[c] = jnp.where(y == 0, own[part:], own[:part])
    to_y[1 - c] = jnp.where(y == 0, got[part:], got[:part])


def result_kernel(own_ref, got_ref, got_y, out):
    _, _, c, y = coords()
    _, part, block = got_y.shape
    own, got = own_ref[...], got_ref[...]
    here = jnp.where(y == 0, own[:part], own[part:])
    there = jnp.where(y == 0, got[:part], got[part:])
    for value, h, q in ((here, c, y), (there, 1 - c, y), (got_y[0], 0, 1 - y), (got_y[1], 1, 1 - y)):
        out[0, :, pl.ds(pl.multiple_of((2 * h + q) * block, LANES), block)] = value


def f32(*shape):
    return jax.ShapeDtypeStruct(shape, jnp.float32)


VMEM_SPEC = pl.BlockSpec(memory_space=pltpu.VMEM)
SMEM_SPEC = pl.BlockSpec(memory_space=pltpu.SMEM)
ANY_SPEC = pl.BlockSpec(memory_space=pl.ANY)
HBM_SPEC = pl.BlockSpec(memory_space=pltpu.HBM)
PARAMS = pltpu.CompilerParams(vmem_limit_bytes=40 * 1024 * 1024)


def in_hbm(value):
    return pltpu.with_memory_space_constraint(value, pltpu.HBM)


def kernel_call(body, outs, in_specs, scratch, name, flops=0, size=0):
    many = isinstance(outs, (list, tuple))
    return pl.pallas_call(
        body,
        out_shape=outs,
        in_specs=in_specs,
        out_specs=[VMEM_SPEC] * len(outs) if many else VMEM_SPEC,
        scratch_shapes=scratch,
        compiler_params=PARAMS,
        name=name,
        cost_estimate=pl.CostEstimate(flops=flops, bytes_accessed=size, transcendentals=0),
    )


def summed_plan(measured, drift, start_volume):
    views, slices, cols = measured.shape
    part = start_volume.shape[1]
    rows = 2 * part
    band = rows // 2 + DMAX + 2
    total_angles = drift.shape[0]
    half_cols = cols // 2
    half_width = half_cols + LANES
    width = cols // 4 + 2 * HALO
    tangent, secant = tan_and_secant(total_angles)
    scale = float(1.0 / np.sum(secant))
    tangent, secant = tangent.astype(np.float32), secant.astype(np.float32)

    tiles = half_width // LANES
    groups = slices // SUB
    window = (groups, views + 1, tiles + 2, SUB, LANES)
    tiled = measured.reshape(views, groups, SUB, cols // LANES, LANES).transpose(0, 1, 3, 2, 4)
    table = ((2 * band // STEP + 1) * rows, 3 * STEP * views)
    count = slices // 2
    terms = pltpu.VMEM((slices, 3 * STEP * views, half_width + LANES), jnp.bfloat16)
    vbuf = pltpu.VMEM((part, cols + 2 * LANES), jnp.float32)
    half_of = f32(count, rows, half_width)
    sibling, own_buf, weights, volume = kernel_call(
        functools.partial(fetch_kernel, views, rows, band, scale),
        [f32(slices + 1, rows, half_width), f32(*window), f32(*table), f32(1, part, cols)],
        [HBM_SPEC] * 4,
        [
            pltpu.SMEM((total_angles,), jnp.float32),
            pltpu.SMEM((total_angles,), jnp.int32),
            pltpu.VMEM(window, jnp.float32),
            terms,
            vbuf,
            pltpu.SemaphoreType.DMA((3,)),
            pltpu.SemaphoreType.DMA((2, groups)),
        ],
        "other_share",
        flops=10**9,
    )(in_hbm(jnp.asarray(tangent)), in_hbm(drift), in_hbm(tiled), in_hbm(start_volume))
    got = move(sibling, lambda z, x, c, y: (z, x, 1 - c, y))
    own = kernel_call(
        functools.partial(own_kernel, views, rows, band),
        f32(slices, rows, half_width),
        [VMEM_SPEC] * 2,
        [terms],
        "own_share",
        flops=10**9,
    )(own_buf, weights)

    message = f32(count * width // LANES, rows, LANES)
    mine, send_1, send_2, send_3 = kernel_call(
        plane_pack_kernel,
        [message] * 4,
        [VMEM_SPEC] * 2,
        [pltpu.VMEM(half_of.shape, jnp.float32)] * 2,
        "plane_pack",
    )(own, got)
    vol_mine, vol_to_y = kernel_call(
        volume_pack_kernel,
        [f32(rows, width)] * 2,
        [ANY_SPEC, VMEM_SPEC, VMEM_SPEC],
        [pltpu.VMEM((rows, half_width), jnp.float32), vbuf],
        "volume_pack",
    )(own, got, volume)
    got_1 = move(send_1, lambda z, x, c, y: (z ^ 2, x, c, y) if c else (z, 1 - x, c, 1 - y))
    got_2 = move(send_2, lambda z, x, c, y: (z ^ 3, x, c, y) if c else (z, x, c, 1 - y))
    got_3 = move(send_3, lambda z, x, c, y: (z ^ 1, x, c, y) if c else (z, 1 - x, c, y))
    vol_got = move(vol_to_y, lambda z, x, c, y: (z, x, c, 1 - y))

    edge = band * rows
    conv, low, high = kernel_call(
        functools.partial(gram_kernel, rows, band, scale),
        [f32(6 * rows, 24 * rows), f32(edge, 3 * edge), f32(edge, 3 * edge)],
        [VMEM_SPEC] * 3 + [ANY_SPEC],
        [],
        "gram",
    )(tangent[None], secant[None], drift[None], mine)

    pair = f32(2, rows, width)
    own_pair, send_1, send_2, send_3 = kernel_call(
        middle_pack_kernel,
        [pair] * 4,
        [VMEM_SPEC] * 4,
        [pltpu.VMEM(message.shape, jnp.float32)],
        "middle_pack",
    )(mine, got_1, got_2, got_3)
    got_1 = move(send_1, lambda z, x, c, y: (z, 1 - x, c, 1 - y) if c else (z ^ 3, x, c, y))
    got_2 = move(send_2, lambda z, x, c, y: (z, 1 - x, c, y) if c else (z ^ 2, x, c, y))
    got_3 = move(send_3, lambda z, x, c, y: (z, x, c, 1 - y) if c else (z ^ 1, x, c, y))

    first = kernel_call(
        functools.partial(first_normal_kernel, band, cols),
        pair,
        [VMEM_SPEC] * 5,
        [],
        "first_normal",
        flops=10**9,
    )(vol_mine, vol_got, conv, low, high)

    three = f32(3, rows, width)
    mine, to_x, to_diag = kernel_call(
        half_pair_kernel,
        [f32(4, rows, width), three, three],
        [VMEM_SPEC] * 5,
        [pltpu.VMEM((2, rows, width), jnp.float32)],
        "half_pair",
    )(first, own_pair, got_1, got_2, got_3)
    got_diag = move(to_diag, beside)
    got_x = move(to_x, lambda z, x, c, y: (z, 1 - x, c, y))

    block = width - 2 * HALO
    quarter = f32(rows, block)
    keep, send = kernel_call(
        functools.partial(finish_kernel, band, slices, cols),
        [quarter, quarter],
        [VMEM_SPEC] * 6,
        [],
        "finish",
    )(mine, got_diag, got_x, conv, low, high)
    swapped = move(send, lambda z, x, c, y: (z, x, 1 - c, y))
    to_y = kernel_call(result_pack_kernel, f32(2, part, block), [VMEM_SPEC] * 2, [], "result_pack")(keep, swapped)
    got_y = move(to_y, lambda z, x, c, y: (z, x, c, 1 - y))
    return kernel_call(result_kernel, f32(1, part, cols), [VMEM_SPEC] * 3, [], "result")(keep, swapped, got_y)


def summed_plan_fits(mesh, measured, start_volume):
    rows = start_volume.shape[1]
    cols = measured.shape[2]
    return (
        ITERS == 2
        and dict(mesh.shape) == {"wide": 16, "grp": 2}
        and measured.shape[1] == start_volume.shape[0] == 16
        and rows == SUB
        and cols % (16 * LANES) == 0
        and measured.shape[0] % 256 == 0
    )


def solution(mesh):
    in_specs = (P(("wide", "grp"), None, None), P(), P("wide", "grp", None))
    out_specs = P("wide", "grp", None)

    def run(measured, drift, start_volume):
        plan = summed_plan if summed_plan_fits(mesh, measured, start_volume) else on_device
        return jax.shard_map(plan, mesh=mesh, in_specs=in_specs, out_specs=out_specs, check_vma=False)(
            measured, drift, start_volume
        )

    return run
```

```python
import functools
from functools import reduce
import math

import jax
import jax.numpy as jnp
import numpy as np
from jax import lax
from jax.experimental import pallas as pl
from jax.experimental.pallas import tpu as pltpu
from jax.sharding import PartitionSpec as P

ITERS = 2
DMAX = 4


TILT_MAX = math.pi / 4
SMOOTH_EPS = 0.05
TV_STEP = 0.1


def with_halo(block, sides, width):
    for axis, dim in sides:
        count = lax.axis_size(axis)
        forward = [(i, i + 1) for i in range(count - 1)]
        backward = [(target, source) for source, target in forward]
        low = lax.ppermute(
            lax.slice_in_dim(block, block.shape[dim] - width, None, axis=dim), axis, forward
        )
        high = lax.ppermute(lax.slice_in_dim(block, 0, width, axis=dim), axis, backward)
        block = jnp.concatenate([low, block, high], axis=dim)
    return block


def geometry(angle_ids, drift_vals, total_angles, rows, band_extent):
    angle_rad = TILT_MAX * (2.0 * angle_ids.astype(jnp.float32) / (total_angles - 1) - 1.0)
    secant = 1.0 / jnp.cos(angle_rad)
    height = jnp.arange(rows, dtype=jnp.float32) - (rows - 1) / 2.0
    offsets = jnp.arange(2 * band_extent + 1, dtype=jnp.float32) - band_extent
    shifts = height[None, :] * jnp.tan(angle_rad)[:, None] - drift_vals.astype(jnp.float32)[:, None]
    weight_factors = secant[:, None, None] * jnp.maximum(
        0.0, 1.0 - jnp.abs(shifts[:, :, None] - offsets[None, None, :])
    )
    return (weight_factors, jnp.cos(angle_rad) / rows)


def secant_sum(total_angles):
    angle_rad = TILT_MAX * (
        2.0 * jnp.arange(total_angles, dtype=jnp.float32) / (total_angles - 1) - 1.0
    )
    return jnp.sum(1.0 / jnp.cos(angle_rad))


def local_geometry(angle_ids, drift, total_angles, rows_all, band_extent):
    matches = angle_ids[:, None] == jnp.arange(total_angles, dtype=jnp.int32)[None, :]
    local_drift = jnp.sum(jnp.where(matches, drift[None, :], 0), axis=1)
    return geometry(angle_ids, local_drift, total_angles, rows_all, band_extent)


def apply_correction(
    row_band_strip, measurement_part, weight_factors, residual_scale, global_scale, band_extent
):
    col_count = row_band_strip.shape[2]
    span = 2 * band_extent + 1
    padded = jnp.pad(row_band_strip, ((0, 0), (0, 0), (band_extent, band_extent)))
    shifted = jnp.stack(
        [padded[:, :, shift_id : shift_id + col_count] for shift_id in range(span)], axis=2
    )
    forward_projected = jnp.einsum(
        "ark,zrku->azu", weight_factors, shifted, precision=lax.Precision.HIGHEST
    )
    residual_error = residual_scale[:, None, None] * (measurement_part - forward_projected)
    spread = jnp.einsum(
        "ark,azu->kzru", weight_factors, residual_error, precision=lax.Precision.HIGHEST
    )
    spread = jnp.pad(spread, ((0, 0), (0, 0), (0, 0), (band_extent, band_extent)))
    pieces = [
        spread[shift_id, :, :, 2 * band_extent - shift_id : 2 * band_extent - shift_id + col_count]
        for shift_id in range(span)
    ]
    return global_scale * reduce(lambda left, right: left + right, pieces)


def divergence(extended, z_first, r_first, zcount, rcount):
    plane_count, height, col_count = extended.shape
    z_index = z_first + jnp.arange(plane_count, dtype=jnp.int32)[:, None, None]
    row_index = r_first + jnp.arange(height, dtype=jnp.int32)[None, :, None]
    col_index = jnp.arange(col_count, dtype=jnp.int32)[None, None, :]
    diff_z = jnp.concatenate([extended[1:] - extended[:-1], jnp.zeros_like(extended[:1])], axis=0)
    diff_z = jnp.where((z_index >= 0) & (z_index < zcount - 1), diff_z, 0.0)
    diff_r = jnp.concatenate(
        [extended[:, 1:] - extended[:, :-1], jnp.zeros_like(extended[:, :1])], axis=1
    )
    diff_r = jnp.where((row_index >= 0) & (row_index < rcount - 1), diff_r, 0.0)
    diff_c = jnp.concatenate(
        [extended[:, :, 1:] - extended[:, :, :-1], jnp.zeros_like(extended[:, :, :1])], axis=2
    )
    diff_c = jnp.where(col_index < col_count - 1, diff_c, 0.0)
    magnitude = jnp.sqrt(
        diff_z * diff_z + diff_r * diff_r + diff_c * diff_c + SMOOTH_EPS * SMOOTH_EPS
    )
    unit_z = diff_z / magnitude
    unit_r = diff_r / magnitude
    unit_c = diff_c / magnitude
    back_c = unit_c - jnp.concatenate([jnp.zeros_like(unit_c[:, :, :1]), unit_c[:, :, :-1]], axis=2)
    return (
        unit_z[1:-1, 1:-1]
        - unit_z[:-2, 1:-1]
        + (unit_r[1:-1, 1:-1] - unit_r[1:-1, :-2])
        + back_c[1:-1, 1:-1]
    )


def on_device(measured, drift, start_volume):
    wide_count = lax.axis_size("wide")
    groups = lax.axis_size("grp")
    slab_count, rows_tile, col_count = start_volume.shape
    rows_all = rows_tile * groups
    band_extent = rows_all // 2 + DMAX + 2
    per_device = measured.shape[0]
    total_angles = per_device * wide_count * groups
    global_scale = 1.0 / secant_sum(total_angles)
    z_first = lax.axis_index("wide") * slab_count - 1
    zcount = slab_count * wide_count
    local_measurement = lax.all_to_all(measured, "wide", split_axis=1, concat_axis=0, tiled=True)
    bin_position = jnp.arange(local_measurement.shape[0], dtype=jnp.int32)
    angle_ids = (
        bin_position // per_device * groups + lax.axis_index("grp")
    ) * per_device + bin_position % per_device
    weight_factors, residual_scale = local_geometry(
        angle_ids, drift, total_angles, rows_all, band_extent
    )
    own_tile = start_volume
    r_first = lax.axis_index("grp") * rows_tile - 1
    for sweep in range(ITERS):
        row_band_strip = lax.all_gather(own_tile, "grp", axis=1, tiled=True)
        volume_update = apply_correction(
            row_band_strip,
            local_measurement,
            weight_factors,
            residual_scale,
            global_scale,
            band_extent,
        )
        own_tile = own_tile + lax.psum_scatter(
            volume_update, "grp", scatter_dimension=1, tiled=True
        )
        extended = with_halo(own_tile, (("wide", 0), ("grp", 1)), 1)
        own_tile = own_tile + TV_STEP * divergence(extended, z_first, r_first, zcount, rows_all)
    return own_tile


LANES = 128
SUB = 8
HALO = 64


def tan_and_secant(total_angles):
    angle = TILT_MAX * (2.0 * np.arange(total_angles) / (total_angles - 1) - 1.0)
    return np.tan(angle), 1.0 / np.cos(angle)


def coords():
    wide, y = lax.axis_index("wide"), lax.axis_index("grp")
    return wide // 4, wide // 2 % 2, wide % 2, y


def move(value, target):
    pairs = []
    for z in range(4):
        for x in range(2):
            for c in range(2):
                for y in range(2):
                    tz, tx, tc, ty = target(z, x, c, y)
                    pairs.append((((z * 2 + x) * 2 + c) * 2 + y, ((tz * 2 + tx) * 2 + tc) * 2 + ty))
    return lax.ppermute(value, ("wide", "grp"), pairs)


def beside(z, x, c, y):
    if (z, x) in ((0, 0), (3, 1)):
        return z, x, 1 - c, y
    return (z + 1, 0, c, y) if x else (z - 1, 1, c, y)


def split_rows(value):
    high = value.astype(jnp.bfloat16).astype(jnp.float32)
    return jnp.concatenate([high, value - high], axis=0)


def left_terms(value):
    high = value.astype(jnp.bfloat16).astype(jnp.float32)
    return jnp.concatenate([high, high, value - high], axis=1)


def split_terms(value):
    high = value.astype(jnp.bfloat16)
    low = (value - high.astype(jnp.float32)).astype(jnp.bfloat16)
    return jnp.concatenate([high, low], axis=0)


def right_terms(value):
    high = value.astype(jnp.bfloat16)
    low = (value - high.astype(jnp.float32)).astype(jnp.bfloat16)
    return jnp.concatenate([high, low, high], axis=0)


def lane_iota(shape):
    return lax.broadcasted_iota(jnp.int32, shape, len(shape) - 1)


def row_iota(shape):
    return lax.broadcasted_iota(jnp.int32, shape, len(shape) - 2)


STEP = 3


def view_weights(views, rows, band, scale, tan_ref, drift_ref):
    z, x, c, y = coords()
    first_view = (((z * 2 + x) * 2 + c) * 2 + y) * views
    parts = 2 * band // STEP + 1
    shape = (parts * rows, STEP * views)
    lane, row = lane_iota(shape), row_iota(shape)
    view_of = lane_iota((1, STEP * views)) % views
    tan_lane = jnp.zeros((1, STEP * views), jnp.float32)
    drift_lane = tan_lane
    for a in range(views):
        tan_lane = jnp.where(view_of == a, tan_ref[first_view + a], tan_lane)
        drift_lane = jnp.where(view_of == a, drift_ref[first_view + a].astype(jnp.float32), drift_lane)
    shift = ((row % rows).astype(jnp.float32) - (rows - 1) / 2.0) * tan_lane - drift_lane
    offset = ((row // rows) * STEP + lane // views - band).astype(jnp.float32)
    weights = (scale / rows) * jnp.maximum(0.0, 1.0 - jnp.abs(shift - offset))
    return left_terms(weights).astype(jnp.bfloat16)


def back_project(views, rows, band, weights, load_strip, begin, out_ref, terms):
    count, _, width = terms.shape[0] // 2, *terms.shape[1:]
    out_cols = out_ref.shape[2]
    parts = 2 * band // STEP + 1
    for n in range(count):
        strip = load_strip(n)
        high = strip.astype(jnp.bfloat16)
        low = (strip - high.astype(jnp.float32)).astype(jnp.bfloat16)
        for j in range(STEP):
            moved = pltpu.roll(high, j, 1) if j else high
            terms[begin + n, j * views : (j + 1) * views] = moved
            terms[begin + n, (STEP + j) * views : (STEP + j + 1) * views] = pltpu.roll(low, j, 1) if j else low
            terms[begin + n, (2 * STEP + j) * views : (2 * STEP + j + 1) * views] = moved
    for n in range(count):
        spread = jnp.dot(weights, terms[begin + n], preferred_element_type=jnp.float32)
        total = None
        for i in range(parts):
            piece = pltpu.roll(spread[i * rows : (i + 1) * rows], width - HALO - band + STEP * i, 1)
            total = piece if total is None else total + piece
        out_ref[begin + n] = total[:, :out_cols]


def depth_partner(z, bits):
    return {0: z, 1: z + 1 - 2 * (z % 2), 2: (z + 2) % 4, 3: 3 - z}[bits]


def slice_place(half, kept, n):
    z, x, _, _ = coords()
    parity = x if kept else 1 - x
    four = depth_partner(z, (1, 0)[n // 4] if kept else (2, 3)[n // 4])
    group = jnp.where(half == 0, n // 4, four // 2)
    place = jnp.where(half == 0, 4 * (n // 2 % 2) + 2 * parity + n % 2, 4 * (four % 2) + n % 4)
    return group, place


def strip_loader(buf, half, kept, views, tiles):
    pitch = (tiles + 2) * SUB

    def load(n):
        group, place = slice_place(half, kept, n)
        first = half * SUB + place
        return jnp.concatenate(
            [buf[group, pl.ds(first + t * SUB, views, stride=pitch), :] for t in range(tiles + 1)], axis=1
        )

    return load


def volume_window(vol_ref, half, half_cols, vbuf):
    part, cols = vol_ref.shape[1:]
    vbuf[:, 0:LANES] = jnp.zeros((part, LANES), jnp.float32)
    vbuf[:, LANES : LANES + cols] = vol_ref[0]
    vbuf[:, LANES + cols :] = jnp.zeros((part, LANES), jnp.float32)
    width = half_cols + 2 * LANES
    window = vbuf[:, pl.ds(pl.multiple_of(half * half_cols, LANES), width)]
    return pltpu.roll(window, width - HALO, 1)[:, : half_cols + LANES]


def fetch_kernel(views, rows, band, scale, tan_hbm, drift_hbm, meas_hbm, vol_hbm, out_ref, own_buf, weights_ref, vol_ref,
                 tan_ref, drift_ref, sibling_buf, terms, vbuf, table_sem, sem):
    z, _, c, _ = coords()
    tiles = out_ref.shape[2] // LANES
    groups = sibling_buf.shape[0]

    def fetch(half, target, g, semaphore):
        return pltpu.make_async_copy(
            meas_hbm.at[:, g, pl.ds(half * (tiles - 2), tiles)], target.at[g, 0:views, 1 : tiles + 1], semaphore
        )

    tables = [
        pltpu.make_async_copy(tan_hbm, tan_ref, table_sem.at[0]),
        pltpu.make_async_copy(drift_hbm, drift_ref, table_sem.at[1]),
    ]
    vol_copy = pltpu.make_async_copy(vol_hbm, vol_ref, table_sem.at[2])
    soon = jnp.where(c == 0, 1 - z // 2, 0)
    first = [fetch(1 - c, sibling_buf, g, sem.at[0, g]) for g in (soon, 1 - soon)]
    later = [fetch(c, own_buf, g, sem.at[1, g]) for g in range(groups)]
    for copy in first[:1] + tables + first[1:] + [vol_copy] + later:
        copy.start()
    zero = jnp.zeros((views, SUB, LANES), jnp.float32)
    for g in range(groups):
        for target in (sibling_buf, own_buf):
            target[g, 0:views, 0] = zero
            target[g, 0:views, tiles + 1] = zero
    for copy in tables:
        copy.wait()
    weights = view_weights(views, rows, band, scale, tan_ref, drift_ref)
    weights_ref[...] = weights.astype(jnp.float32)
    load, load_kept = (strip_loader(flat_rows(sibling_buf), 1 - c, kept, views, tiles) for kept in (False, True))

    def load_strip(n):
        if n % 4 == 0:
            first[n // 4].wait()
        return load(n)

    count = terms.shape[0] // 2
    back_project(views, rows, band, weights, load_strip, 0, out_ref, terms)
    back_project(views, rows, band, weights, load_kept, count, out_ref, terms)
    vol_copy.wait()
    half_cols = out_ref.shape[2] - LANES
    part = vol_ref.shape[1]
    out_ref[2 * count, 0:part] = volume_window(vol_ref, 1 - c, half_cols, vbuf)
    out_ref[2 * count, part:] = jnp.zeros((rows - part, half_cols + LANES), jnp.float32)
    for copy in later:
        copy.wait()


def flat_rows(buf):
    groups, views, tiles, sub, lanes = buf.shape
    return buf.reshape(groups, views * tiles * sub, lanes)


def own_kernel(views, rows, band, buf, weights_ref, out_ref, terms):
    _, _, c, _ = coords()
    tiles = out_ref.shape[2] // LANES
    weights = weights_ref[...].astype(jnp.bfloat16)
    for kept in (False, True):
        load = strip_loader(flat_rows(buf), c, kept, views, tiles)
        back_project(views, rows, band, weights, load, terms.shape[0] // 2 if kept else 0, out_ref, terms)


def put_quarter(out, acc, py, tiles):
    for n in range(acc.shape[0]):
        for t in range(tiles):
            out[n * tiles + t] = acc[n, :, pl.ds(pl.multiple_of(((tiles - 1) * py + t) * LANES, LANES), LANES)]


def put_four(out, acc, first):
    tiles = acc.shape[2] // LANES
    for n in range(4):
        for t in range(tiles):
            out[n * tiles + t] = acc[first + n, :, t * LANES : (t + 1) * LANES]
    for t in range(4 * tiles, out.shape[0]):
        out[t] = jnp.zeros(out.shape[1:], jnp.float32)


def plane_pack_kernel(own_ref, got_ref, mine, send_1, send_2, send_3, passed, acc):
    count, _, half_width = passed.shape
    tiles = mine.shape[0] // count
    _, _, c, y = coords()
    passed[...] = own_ref[0:count] + got_ref[0:count]
    acc[...] = own_ref[count:] + got_ref[count : 2 * count]

    @pl.when(c == 0)
    def _():
        put_quarter(send_1, passed, 1 - y, tiles)
        put_quarter(send_2, acc, 1 - y, tiles)
        put_quarter(send_3, passed, y, tiles)
        put_quarter(mine, acc, y, tiles)

    @pl.when(c == 1)
    def _():
        put_four(send_1, passed, 0)
        put_four(send_2, passed, 4)
        put_four(send_3, acc, 0)
        put_four(mine, acc, 4)


def volume_pack_kernel(own_ref, got_ref, vol_ref, vol_mine, vol_to_y, both, vbuf):
    count, rows, half_width = own_ref.shape
    part = vol_ref.shape[1]
    _, _, c, y = coords()
    here = volume_window(vol_ref, c, half_width - LANES, vbuf)
    there = got_ref[count, 0:part]
    both[0:part] = jnp.where(c == 0, here, there)
    both[part:] = jnp.where(c == 0, there, here)
    width = vol_mine.shape[1]
    for vol, py in ((vol_mine, y), (vol_to_y, 1 - y)):
        vol[...] = both[:, pl.ds(pl.multiple_of(py * (width - LANES), LANES), width)]


def middle_pack_kernel(mine, got_1, got_2, got_3, own_pair, send_1, send_2, send_3, acc):
    z, x, c, y = coords()
    tiles = own_pair.shape[2] // LANES
    half_tiles = 2 * tiles - 1
    acc[...] = (mine[...] + got_1[...]) + (got_2[...] + got_3[...])

    def put(out, first, pitch):
        for i in range(2):
            for t in range(tiles):
                out[i, :, t * LANES : (t + 1) * LANES] = acc[first + i * pitch + t]

    for out, bits, px, py in ((own_pair, 0, x, y), (send_1, 3, 1 - x, 1 - y), (send_2, 2, 1 - x, y), (send_3, 1, x, 1 - y)):
        depth_first = 2 * tiles * depth_partner(z, bits)
        plane_first = 2 * half_tiles * px + (tiles - 1) * py
        put(out, jnp.where(c == 0, depth_first, plane_first), jnp.where(c == 0, tiles, half_tiles))


def gram_kernel(rows, band, scale, tan_ref, sec_ref, drift_ref, after_ref, conv_ref, low_ref, high_ref):
    views = tan_ref.shape[1]
    span = 2 * band + 1
    shape = (span * rows, views)
    row = row_iota(shape)
    shift = ((row % rows).astype(jnp.float32) - (rows - 1) / 2.0) * tan_ref[...] - drift_ref[...].astype(jnp.float32)
    hat = jnp.maximum(0.0, 1.0 - jnp.abs(shift - (row // rows - band).astype(jnp.float32)))
    gram = lax.dot_general(
        hat * ((scale / rows) * sec_ref[...]),
        hat,
        (((1,), (1,)), ((), ())),
        precision=lax.Precision.HIGHEST,
        preferred_element_type=jnp.float32,
    )
    edge = band * rows
    low_ref[...] = left_terms(gram[edge + rows :, edge + rows :])
    high_ref[...] = left_terms(gram[:edge, :edge])
    lanes = conv_ref.shape[1] // 3
    parts = conv_ref.shape[0] // rows
    width = lanes * parts
    padded = jnp.concatenate([gram, jnp.zeros((span * rows, width - span * rows), jnp.float32)], axis=1)
    total = jnp.zeros((rows, width), jnp.float32)
    for k in range(span):
        total = total + pltpu.roll(padded[k * rows : (k + 1) * rows], rows * (2 * band - k), 1)
    conv_ref[...] = left_terms(jnp.concatenate([total[:, i * lanes : (i + 1) * lanes] for i in range(parts)], axis=0))


def normal(volumes, conv, low_ref, high_ref, band, is_low, is_high):
    rows, width = volumes[0].shape
    step = conv.shape[1] // 3 // rows
    parts = conv.shape[0] // rows
    beyond = beyond_ends(volumes, low_ref, high_ref, band, is_low, is_high)
    zero = jnp.zeros((rows, width - 2 * LANES), jnp.float32)
    result = []
    for volume, piece in zip(volumes, beyond):
        moved = jnp.concatenate([pltpu.roll(volume, (2 * band - j) % width, 1) for j in range(step)], axis=0)
        spread = jnp.dot(conv, right_terms(moved), preferred_element_type=jnp.float32)
        pieces = [spread[0:rows]]
        pieces += [pltpu.roll(spread[i * rows : (i + 1) * rows], width - step * i, 1) for i in range(1, parts)]
        total = (pieces[0] + pieces[1]) + (pieces[2] + pieces[3]) + sum(pieces[5:], pieces[4])
        ends = [jnp.where(is_low, piece, 0.0), zero, jnp.where(is_high, piece, 0.0)]
        result.append(total - jnp.concatenate(ends, axis=1))
    return result


def beyond_ends(volumes, low_ref, high_ref, band, is_low, is_high):
    rows, width = volumes[0].shape
    pitch = LANES // len(volumes)
    lane = lane_iota((rows, LANES))
    tiles = [jnp.where(is_low, volume[:, :LANES], volume[:, width - LANES :]) for volume in volumes]
    offsets = [jnp.where(is_low, i + 1, i - band) for i in range(band)]
    moved = []
    for k in offsets:
        packed = jnp.zeros((rows, LANES), jnp.float32)
        for s, tile in enumerate(tiles):
            piece = pltpu.roll(tile, (s * pitch - (HALO - band) - k) % LANES, 1)
            packed = jnp.where((lane >= s * pitch) & (lane < (s + 1) * pitch), piece, packed)
        moved.append(packed)
    matrix = jnp.where(is_low, low_ref[...], high_ref[...]).astype(jnp.bfloat16)
    spread = jnp.dot(matrix, right_terms(jnp.concatenate(moved, axis=0)), preferred_element_type=jnp.float32)
    place = lane % pitch - jnp.where(is_low, 0, band)
    kept = [jnp.where((place >= 0) & (place < band), spread[i * rows : (i + 1) * rows], 0.0) for i in range(band)]
    near = (lane >= HALO - band) & (lane < HALO + band)
    result = []
    for s in range(len(volumes)):
        back = [pltpu.roll(kept[i], (HALO - band - s * pitch + k) % LANES, 1) for i, k in enumerate(offsets)]
        while len(back) > 1:
            back = [sum(back[i + 1 : i + 2], back[i]) for i in range(0, len(back), 2)]
        result.append(jnp.where(near, back[0], 0.0))
    return result


def block_place(width, total_cols):
    z, x, c, y = coords()
    block = width - 2 * HALO
    index = c * 2 + y
    return index * block - HALO, index == 0, index == total_cols // block - 1


def first_normal_kernel(band, total_cols, vol_mine, vol_got, conv_ref, low_ref, high_ref, out):
    _, is_low, is_high = block_place(vol_mine.shape[1], total_cols)
    _, _, _, y = coords()
    part = vol_mine.shape[0] // 2
    here, there = vol_mine[...], vol_got[...]
    upper = jnp.where(y == 0, here, there)
    lower = jnp.where(y == 0, there, here)
    volumes = [
        jnp.concatenate([upper[i * part : (i + 1) * part], lower[i * part : (i + 1) * part]], axis=0) for i in range(2)
    ]
    back = normal(volumes, conv_ref[...].astype(jnp.bfloat16), low_ref, high_ref, band, is_low, is_high)
    for i in range(2):
        out[i] = volumes[i] - back[i]


def half_pair_kernel(first_ref, own_pair, got_1, got_2, got_3, mine, to_x, to_diag, corr):
    _, x, _, _ = coords()
    corr[...] = (own_pair[...] + got_1[...]) + (got_2[...] + got_3[...])
    half = first_ref[...] + corr[...]
    mine[0:2] = half
    mine[2:4] = corr[...]
    to_x[0:2] = half
    to_x[2] = corr[1 - x]
    to_diag[0:2] = half
    to_diag[2] = corr[x]


def variation_step(half, z_of, first_col, depth, total_cols):
    rows, width = half[0].shape
    col = first_col + lane_iota((rows, width))
    row = row_iota((rows, width))
    inside = (col >= 0) & (col < total_cols - 1)
    units = []
    for w in range(len(half) - 1):
        v = half[w]
        keep = (z_of(w) >= 0) & (z_of(w) < depth - 1)
        dz = jnp.where(keep, half[w + 1] - v, 0.0)
        dr = jnp.where(row < rows - 1, pltpu.roll(v, rows - 1, 0) - v, 0.0)
        dc = jnp.where(inside, pltpu.roll(v, width - 1, 1) - v, 0.0)
        inverse = lax.rsqrt(dz * dz + dr * dr + dc * dc + SMOOTH_EPS * SMOOTH_EPS)
        units.append((dz * inverse, dr * inverse, dc * inverse))
    result = []
    for w in range(1, len(half) - 1):
        uz, ur, uc = units[w]
        div = (uz - units[w - 1][0]) + (ur - pltpu.roll(ur, 1, 0)) + (uc - pltpu.roll(uc, 1, 1))
        result.append(jnp.where((col >= 0) & (col < total_cols), half[w] + TV_STEP * div, 0.0))
    return result


def finish_kernel(
    band, depth, total_cols, mine, got_diag, got_x, conv_ref, low_ref, high_ref, keep_ref, send_ref
):
    width = mine.shape[2]
    first_col, is_low, is_high = block_place(width, total_cols)
    z, x, c, _ = coords()
    before = [jnp.where(x == 0, got_diag[i], got_x[i]) for i in range(3)]
    after = [jnp.where(x == 0, got_x[i], got_diag[i]) for i in range(3)]
    half = [before[0], before[1], mine[0], mine[1], after[0], after[1]]
    corr = [before[2], mine[2], mine[3], after[2]]
    slice_0 = 4 * z + 2 * x
    volumes = variation_step(half, lambda w: slice_0 - 2 + w, first_col, depth, total_cols)
    back = normal(volumes, conv_ref[...].astype(jnp.bfloat16), low_ref, high_ref, band, is_low, is_high)
    half = [volumes[s] + corr[s] - back[s] for s in range(4)]
    volumes = variation_step(half, lambda w: slice_0 - 1 + w, first_col, depth, total_cols)
    kept = jnp.where(c == 0, volumes[0], volumes[1])
    sent = jnp.where(c == 0, volumes[1], volumes[0])
    keep_ref[...] = pltpu.roll(kept, width - HALO, 1)[:, : width - LANES]
    send_ref[...] = pltpu.roll(sent, width - HALO, 1)[:, : width - LANES]


def result_pack_kernel(own_ref, got_ref, to_y):
    _, _, c, y = coords()
    part = to_y.shape[1]
    own, got = own_ref[...], got_ref[...]
    to_y[c] = jnp.where(y == 0, own[part:], own[:part])
    to_y[1 - c] = jnp.where(y == 0, got[part:], got[:part])


def result_kernel(own_ref, got_ref, got_y, out):
    _, _, c, y = coords()
    _, part, block = got_y.shape
    own, got = own_ref[...], got_ref[...]
    here = jnp.where(y == 0, own[:part], own[part:])
    there = jnp.where(y == 0, got[:part], got[part:])
    for value, h, q in ((here, c, y), (there, 1 - c, y), (got_y[0], 0, 1 - y), (got_y[1], 1, 1 - y)):
        out[0, :, pl.ds(pl.multiple_of((2 * h + q) * block, LANES), block)] = value


def f32(*shape):
    return jax.ShapeDtypeStruct(shape, jnp.float32)


VMEM_SPEC = pl.BlockSpec(memory_space=pltpu.VMEM)
SMEM_SPEC = pl.BlockSpec(memory_space=pltpu.SMEM)
ANY_SPEC = pl.BlockSpec(memory_space=pl.ANY)
HBM_SPEC = pl.BlockSpec(memory_space=pltpu.HBM)
PARAMS = pltpu.CompilerParams(vmem_limit_bytes=40 * 1024 * 1024)


def in_hbm(value):
    return pltpu.with_memory_space_constraint(value, pltpu.HBM)


def kernel_call(body, outs, in_specs, scratch, name, flops=0, size=0):
    many = isinstance(outs, (list, tuple))
    return pl.pallas_call(
        body,
        out_shape=outs,
        in_specs=in_specs,
        out_specs=[VMEM_SPEC] * len(outs) if many else VMEM_SPEC,
        scratch_shapes=scratch,
        compiler_params=PARAMS,
        name=name,
        cost_estimate=pl.CostEstimate(flops=flops, bytes_accessed=size, transcendentals=0),
    )


def summed_plan(measured, drift, start_volume):
    views, slices, cols = measured.shape
    part = start_volume.shape[1]
    rows = 2 * part
    band = rows // 2 + DMAX + 2
    total_angles = drift.shape[0]
    half_cols = cols // 2
    half_width = half_cols + LANES
    width = cols // 4 + 2 * HALO
    tangent, secant = tan_and_secant(total_angles)
    scale = float(1.0 / np.sum(secant))
    tangent, secant = tangent.astype(np.float32), secant.astype(np.float32)

    tiles = half_width // LANES
    groups = slices // SUB
    window = (groups, views + 1, tiles + 2, SUB, LANES)
    tiled = measured.reshape(views, groups, SUB, cols // LANES, LANES).transpose(0, 1, 3, 2, 4)
    table = ((2 * band // STEP + 1) * rows, 3 * STEP * views)
    count = slices // 2
    terms = pltpu.VMEM((slices, 3 * STEP * views, half_width + LANES), jnp.bfloat16)
    vbuf = pltpu.VMEM((part, cols + 2 * LANES), jnp.float32)
    half_of = f32(count, rows, half_width)
    sibling, own_buf, weights, volume = kernel_call(
        functools.partial(fetch_kernel, views, rows, band, scale),
        [f32(slices + 1, rows, half_width), f32(*window), f32(*table), f32(1, part, cols)],
        [HBM_SPEC] * 4,
        [
            pltpu.SMEM((total_angles,), jnp.float32),
            pltpu.SMEM((total_angles,), jnp.int32),
            pltpu.VMEM(window, jnp.float32),
            terms,
            vbuf,
            pltpu.SemaphoreType.DMA((3,)),
            pltpu.SemaphoreType.DMA((2, groups)),
        ],
        "other_share",
        flops=10**9,
    )(in_hbm(jnp.asarray(tangent)), in_hbm(drift), in_hbm(tiled), in_hbm(start_volume))
    got = move(sibling, lambda z, x, c, y: (z, x, 1 - c, y))
    own = kernel_call(
        functools.partial(own_kernel, views, rows, band),
        f32(slices, rows, half_width),
        [VMEM_SPEC] * 2,
        [terms],
        "own_share",
        flops=10**9,
    )(own_buf, weights)

    message = f32(count * width // LANES, rows, LANES)
    mine, send_1, send_2, send_3 = kernel_call(
        plane_pack_kernel,
        [message] * 4,
        [VMEM_SPEC] * 2,
        [pltpu.VMEM(half_of.shape, jnp.float32)] * 2,
        "plane_pack",
    )(own, got)
    vol_mine, vol_to_y = kernel_call(
        volume_pack_kernel,
        [f32(rows, width)] * 2,
        [ANY_SPEC, VMEM_SPEC, VMEM_SPEC],
        [pltpu.VMEM((rows, half_width), jnp.float32), vbuf],
        "volume_pack",
    )(own, got, volume)
    got_1 = move(send_1, lambda z, x, c, y: (z ^ 2, x, c, y) if c else (z, 1 - x, c, 1 - y))
    got_2 = move(send_2, lambda z, x, c, y: (z ^ 3, x, c, y) if c else (z, x, c, 1 - y))
    got_3 = move(send_3, lambda z, x, c, y: (z ^ 1, x, c, y) if c else (z, 1 - x, c, y))
    vol_got = move(vol_to_y, lambda z, x, c, y: (z, x, c, 1 - y))

    edge = band * rows
    conv, low, high = kernel_call(
        functools.partial(gram_kernel, rows, band, scale),
        [f32(6 * rows, 24 * rows), f32(edge, 3 * edge), f32(edge, 3 * edge)],
        [VMEM_SPEC] * 3 + [ANY_SPEC],
        [],
        "gram",
    )(tangent[None], secant[None], drift[None], mine)

    pair = f32(2, rows, width)
    own_pair, send_1, send_2, send_3 = kernel_call(
        middle_pack_kernel,
        [pair] * 4,
        [VMEM_SPEC] * 4,
        [pltpu.VMEM(message.shape, jnp.float32)],
        "middle_pack",
    )(mine, got_1, got_2, got_3)
    got_1 = move(send_1, lambda z, x, c, y: (z, 1 - x, c, 1 - y) if c else (z ^ 3, x, c, y))
    got_2 = move(send_2, lambda z, x, c, y: (z, 1 - x, c, y) if c else (z ^ 2, x, c, y))
    got_3 = move(send_3, lambda z, x, c, y: (z, x, c, 1 - y) if c else (z ^ 1, x, c, y))

    first = kernel_call(
        functools.partial(first_normal_kernel, band, cols),
        pair,
        [VMEM_SPEC] * 5,
        [],
        "first_normal",
        flops=10**9,
    )(vol_mine, vol_got, conv, low, high)

    three = f32(3, rows, width)
    mine, to_x, to_diag = kernel_call(
        half_pair_kernel,
        [f32(4, rows, width), three, three],
        [VMEM_SPEC] * 5,
        [pltpu.VMEM((2, rows, width), jnp.float32)],
        "half_pair",
    )(first, own_pair, got_1, got_2, got_3)
    got_diag = move(to_diag, beside)
    got_x = move(to_x, lambda z, x, c, y: (z, 1 - x, c, y))

    block = width - 2 * HALO
    quarter = f32(rows, block)
    keep, send = kernel_call(
        functools.partial(finish_kernel, band, slices, cols),
        [quarter, quarter],
        [VMEM_SPEC] * 6,
        [],
        "finish",
    )(mine, got_diag, got_x, conv, low, high)
    swapped = move(send, lambda z, x, c, y: (z, x, 1 - c, y))
    to_y = kernel_call(result_pack_kernel, f32(2, part, block), [VMEM_SPEC] * 2, [], "result_pack")(keep, swapped)
    got_y = move(to_y, lambda z, x, c, y: (z, x, c, 1 - y))
    return kernel_call(result_kernel, f32(1, part, cols), [VMEM_SPEC] * 3, [], "result")(keep, swapped, got_y)


def summed_plan_fits(mesh, measured, start_volume):
    rows = start_volume.shape[1]
    cols = measured.shape[2]
    return (
        ITERS == 2
        and dict(mesh.shape) == {"wide": 16, "grp": 2}
        and measured.shape[1] == start_volume.shape[0] == 16
        and rows == SUB
        and cols % (16 * LANES) == 0
        and measured.shape[0] % 256 == 0
    )


def solution(mesh):
    in_specs = (P(("wide", "grp"), None, None), P(), P("wide", "grp", None))
    out_specs = P("wide", "grp", None)

    def run(measured, drift, start_volume):
        plan = summed_plan if summed_plan_fits(mesh, measured, start_volume) else on_device
        return jax.shard_map(plan, mesh=mesh, in_specs=in_specs, out_specs=out_specs, check_vma=False)(
            measured, drift, start_volume
        )

    return run
```
